32 devices in a mesh: seq: 2 (over y), blk: 16 (over z, x, core).
Axes of the slice: x: 2, y: 2, z: 4, core: 2. Of those that a mesh axis runs over, the one named last changes fastest.
Arguments:
- hidden: bfloat16 [2, 4096, 768], P('seq', 'blk'), may hold values from -6 to 6
- positions: int32 [2, 4096], P('seq', 'blk'), may hold values from 0 to 4095, as said below
- ln_attn_gain: bfloat16 [768], replicated, may hold values from 0.099609375 to 1.8984375
- ln_attn_bias: bfloat16 [768], replicated, may hold values from -4 to 4
- ln_mlp_gain: bfloat16 [768], replicated, may hold values from 0.099609375 to 1.8984375
- ln_mlp_bias: bfloat16 [768], replicated, may hold values from -4 to 4
- w_qkv: bfloat16 [768, 2304], replicated, may hold values from -0.21875 to 0.21875
- b_qkv: bfloat16 [2304], replicated, may hold values from -4 to 4
- w_dense: bfloat16 [768, 768], replicated, may hold values from -1.75 to 1.75
- b_dense: bfloat16 [768], replicated, may hold values from -4 to 4
- w_in: bfloat16 [768, 3072], replicated, may hold values from -0.21875 to 0.21875
- b_in: bfloat16 [3072], replicated, may hold values from -6 to 6
- w_out: bfloat16 [3072, 768], replicated, may hold values from -0.15625 to 0.15625
- b_out: bfloat16 [768], replicated, may hold values from -4 to 4
- out_grad: bfloat16 [2, 4096, 768], P('seq', 'blk'), may hold values from -6 to 6
Outputs:
- output: bfloat16 [2, 4096, 768], P('seq', 'blk')
- input_grad: bfloat16 [2, 4096, 768], P('seq', 'blk')
- ln_attn_gain_grad: float32 [768], replicated
- ln_attn_bias_grad: float32 [768], replicated
- ln_mlp_gain_grad: float32 [768], replicated
- ln_mlp_bias_grad: float32 [768], replicated
- w_qkv_grad: float32 [768, 2304], replicated
- b_qkv_grad: float32 [2304], replicated
- w_dense_grad: float32 [768, 768], replicated
- b_dense_grad: float32 [768], replicated
- w_in_grad: float32 [768, 3072], replicated
- b_in_grad: float32 [3072], replicated
- w_out_grad: float32 [3072, 768], replicated
- b_out_grad: float32 [768], replicated
The draws below stay inside these ranges and needn't reach their ends.
Inputs may be any that keep to these rules, and one draw needn't show every extreme that they name: In each sequence the positions are a permutation of 0 to 4095; the 256 rows of one device hold two runs of 128 consecutive positions, group c and group 32 - 1 - c for some c.
All inputs are finite; a program needn't handle non-finite values.
Results may differ from the reference program's by a relative error of at most 0.0093.
Values may be sent and summed in bfloat16 or wider, within the bound.
A program may use at most 384 MiB of HBM per device.

```python
import jax
import jax.numpy as jnp
from jax import lax

D = 768
HEADS = 12
HD = 64
FF = 3072
ROTARY = 16
GROUP = 128
GROUPS = 32
SEQ_LEN = 4096
SEQS = 2


def draw_positions(key, part):
    key = jax.random.fold_in(key, 17)
    keys = jax.random.split(key, SEQS)

    def one_order(single_key):
        return jax.random.permutation(single_key, GROUPS // 2).astype(jnp.int32)
    orders = jax.vmap(one_order)(keys)
    offsets = jnp.arange(GROUP, dtype=jnp.int32)
    lower_run = orders[:, :, None] * GROUP + offsets[None, None, :]
    upper_run = (GROUPS - 1 - orders)[:, :, None] * GROUP + offsets[None, None, :]
    return jnp.stack([lower_run, upper_run], axis=2).reshape(SEQS, SEQ_LEN).astype(jnp.int32)


def block_levels(own_key, shape, cuts, low, high):
    level = 1.0
    for axis_at, blocks in cuts:
        heights = jax.random.uniform(jax.random.fold_in(jax.random.fold_in(own_key, 6), axis_at), (blocks,), jnp.float32, low / len(cuts), high / len(cuts))
        level = level * jnp.repeat(jnp.exp(heights), shape[axis_at] // blocks).reshape((-1,) + (1,) * (len(shape) - 1 - axis_at))
    return level


def normal_values(own_key, shape, scale, limit, shards=(), held_as=jnp.bfloat16):
    array = scale * jax.random.normal(own_key, shape, jnp.float32)
    if shards:
        array = array * block_levels(own_key, shape, shards, -0.22, 0.18)
    return jnp.clip(array, -limit, limit).astype(held_as)


def setup_inputs(seed: int = 0) -> dict:
    arg_keys = jax.random.split(jax.random.key(seed), 16)
    hidden = normal_values(arg_keys[0], (SEQS, SEQ_LEN, D), 1.0, 6.0, ((0, 2), (1, 16)))
    positions = draw_positions(jax.random.fold_in(arg_keys[15], 71), 0)
    ln_attn_gain = jnp.clip(1.0 + 0.18 * jax.random.normal(arg_keys[2], (D,), jnp.float32), 0.099609375, 1.8984375).astype(jnp.bfloat16)
    ln_attn_bias = normal_values(arg_keys[3], (D,), 0.3, 4.0)
    ln_mlp_gain = jnp.clip(1.0 + 0.18 * jax.random.normal(arg_keys[4], (D,), jnp.float32), 0.099609375, 1.8984375).astype(jnp.bfloat16)
    ln_mlp_bias = normal_values(arg_keys[5], (D,), 0.3, 4.0)
    w_qkv = normal_values(arg_keys[6], (D, 3 * D), D ** -0.5, 0.21875)
    b_qkv = normal_values(arg_keys[7], (3 * D,), 0.3, 4.0)
    w_dense = normal_values(arg_keys[8], (D, D), (max(4, D * 64 // SEQ_LEN)) ** -0.5, 1.75)
    b_dense = normal_values(arg_keys[9], (D,), 0.3, 4.0)
    w_in = normal_values(arg_keys[10], (D, FF), D ** -0.5, 0.21875)
    b_in = normal_values(arg_keys[11], (FF,), 0.5, 6.0)
    w_out = normal_values(arg_keys[12], (FF, D), (FF // 2) ** -0.5, 0.15625)
    b_out = normal_values(arg_keys[13], (D,), 0.3, 4.0)
    out_grad = normal_values(arg_keys[14], (SEQS, SEQ_LEN, D), 1.0, 6.0, ((0, 2), (1, 16)))
    return {"hidden": hidden, "positions": positions, "ln_attn_gain": ln_attn_gain, "ln_attn_bias": ln_attn_bias, "ln_mlp_gain": ln_mlp_gain, "ln_mlp_bias": ln_mlp_bias, "w_qkv": w_qkv, "b_qkv": b_qkv, "w_dense": w_dense, "b_dense": b_dense, "w_in": w_in, "b_in": b_in, "w_out": w_out, "b_out": b_out, "out_grad": out_grad}


norm_epsilon = 1e-05
rotary_base = 10000.0
masked_fill = -1e+30
full_precision = lax.Precision.HIGHEST

@jax.custom_vjp
def low(v):
    return lax.optimization_barrier(v.astype(jnp.bfloat16)).astype(jnp.float32)

@jax.custom_vjp
def low_back(v):
    return v

def low_keep(v):
    return (low(v), None)

def low_pass(kept, grad):
    return (grad,)

def back_keep(v):
    return (v, None)

def back_low(kept, grad):
    return (low(grad),)
low.defvjp(low_keep, low_pass)
low_back.defvjp(back_keep, back_low)

def layer_norm(values, norm_gain, norm_shift):
    centre = values - lax.optimization_barrier(jnp.mean(values, axis=-1, keepdims=True))
    spread = lax.optimization_barrier(jnp.mean(centre * centre, axis=-1, keepdims=True))
    return centre * lax.rsqrt(spread + norm_epsilon) * norm_gain + norm_shift

def rotary_angles(position_ids):
    half_dims = ROTARY // 2
    inverse = jnp.power(rotary_base, -2.0 * jnp.arange(half_dims, dtype=jnp.float32) / ROTARY)
    return position_ids.astype(jnp.float32)[:, None] * inverse[None, :]

def rotate(values, angles):
    half_dims = angles.shape[-1]
    cosine = jnp.cos(angles)[:, None, :]
    sine_part = jnp.sin(angles)[:, None, :]
    first_half = values[..., :half_dims]
    second_half = values[..., half_dims:2 * half_dims]
    remainder = values[..., 2 * half_dims:]
    return jnp.concatenate([first_half * cosine - second_half * sine_part, second_half * cosine + first_half * sine_part, remainder], axis=-1)

def attend(query, key, value, position_ids):
    length = query.shape[0]
    block_size = 512 if length % 512 == 0 else length
    score_scale = HD ** (-0.5)

    def one_block(members):
        query_block, pos_block = members
        scores = low_back(jnp.einsum('qhd,khd->hqk', query_block, key, precision=full_precision) * score_scale)
        allowed = position_ids[None, None, :] <= pos_block[None, :, None]
        scores = jnp.where(allowed, scores, masked_fill)
        log_sum = jax.nn.logsumexp(scores, axis=-1, keepdims=True)
        attn_probs = low(jnp.exp(scores - log_sum))
        return jnp.einsum('hqk,khd->qhd', attn_probs, value, precision=full_precision)
    blocks = lax.map(jax.checkpoint(one_block), (query.reshape(length // block_size, block_size, HEADS, HD), position_ids.reshape(length // block_size, block_size)))
    return blocks.reshape(length, HEADS * HD)

def layer(hidden, position_ids, ln_attn_gain, ln_attn_bias, ln_mlp_gain, ln_mlp_bias, w_qkv, b_qkv, w_dense, b_dense, w_in, b_in, w_out, b_out):
    length = hidden.shape[0]
    normed_attn = low(layer_norm(hidden, ln_attn_gain, ln_attn_bias))
    mixed = low_back(jnp.dot(normed_attn, w_qkv, precision=full_precision) + b_qkv)
    angles = rotary_angles(position_ids)
    query = low(rotate(mixed[:, :D].reshape(length, HEADS, HD), angles))
    key = low(rotate(mixed[:, D:2 * D].reshape(length, HEADS, HD), angles))
    value = low(mixed[:, 2 * D:].reshape(length, HEADS, HD))
    attended = low(low_back(attend(query, key, value, position_ids)))
    attn_branch = jnp.dot(attended, w_dense, precision=full_precision) + b_dense
    normed_mlp = low(layer_norm(hidden, ln_mlp_gain, ln_mlp_bias))
    inner = low_back(jnp.dot(normed_mlp, w_in, precision=full_precision) + b_in)
    activated = low(jax.nn.gelu(inner, approximate=False))
    mlp_branch = jnp.dot(activated, w_out, precision=full_precision) + b_out
    return hidden + attn_branch + mlp_branch

def reference(hidden, positions, ln_attn_gain, ln_attn_bias, ln_mlp_gain, ln_mlp_bias, w_qkv, b_qkv, w_dense, b_dense, w_in, b_in, w_out, b_out, out_grad):
    params = tuple((member.astype(jnp.float32) for member in (ln_attn_gain, ln_attn_bias, ln_mlp_gain, ln_mlp_bias, w_qkv, b_qkv, w_dense, b_dense, w_in, b_in, w_out, b_out)))

    def one_sequence(totals, members):
        seq_rows, seq_pos, seq_cot = members

        def forward(rows_in, *weights):
            return layer(rows_in, seq_pos, *weights)
        result, pullback = jax.vjp(forward, seq_rows.astype(jnp.float32), *params)
        grads = pullback(seq_cot.astype(jnp.float32))
        totals = tuple((running + added for running, added in zip(totals, grads[1:])))
        return (totals, (result.astype(jnp.bfloat16), grads[0].astype(jnp.bfloat16)))
    initial = tuple((jnp.zeros(member.shape, jnp.float32) for member in params))
    totals, (output, input_grad) = lax.scan(one_sequence, initial, (hidden, positions, out_grad))
    return (output, input_grad, totals[0], totals[1], totals[2], totals[3], totals[4], totals[5], totals[6], totals[7], totals[8], totals[9], totals[10], totals[11])
```

```python
import functools

import jax
import jax.numpy as jnp
from jax import lax
from jax.experimental import pallas as pl
from jax.experimental.pallas import tpu as pltpu
from jax.sharding import PartitionSpec as P

HEADS = 12
HEAD_DIM = 64
ROTARY = 16
GROUP = 128
HEAD_GROUPS = 4
PER_GROUP = HEADS // HEAD_GROUPS
NORM_EPSILON = 1e-05
ROTARY_BASE = 10000.0
MASKED = -1e30
VMEM_BYTES = 58 * 1024 * 1024

F32 = jnp.float32
BF16 = jnp.bfloat16
IN_VMEM = pl.BlockSpec(memory_space=pltpu.VMEM)
IN_SMEM = pl.BlockSpec(memory_space=pltpu.SMEM)


def mm(a, b):
    return lax.dot_general(a, b, (((1,), (0,)), ((), ())), preferred_element_type=F32)


def mm_nt(a, b):
    return lax.dot_general(a, b, (((1,), (1,)), ((), ())), preferred_element_type=F32)


def mm_tn(a, b):
    return lax.dot_general(a, b, (((0,), (0,)), ((), ())), preferred_element_type=F32)


def normalise(rows):
    centre = rows - jnp.mean(rows, axis=-1, keepdims=True)
    spread = jnp.mean(centre * centre, axis=-1, keepdims=True)
    scale = lax.rsqrt(spread + NORM_EPSILON)
    return centre * scale, scale


def norm_back(grad, xhat, scale, gain):
    eg = grad * gain
    return scale * (
        eg
        - jnp.mean(eg, axis=-1, keepdims=True)
        - xhat * jnp.mean(eg * xhat, axis=-1, keepdims=True)
    )


def params():
    return pltpu.CompilerParams(vmem_limit_bytes=VMEM_BYTES)


def front_kernel(hid, og, gain, bias, wqkv, bqkv, wdense, cosw, sina, sinb, msg):
    rows = hid[...].astype(F32)
    xhat, _ = normalise(rows)
    normed = (xhat * gain[...].astype(F32) + bias[...].astype(F32)).astype(BF16)
    mixed = mm(normed, wqkv[...]) + bqkv[...].astype(F32)
    datt = mm_nt(og[...], wdense[...])
    width = hid.shape[1]
    lane = lax.broadcasted_iota(jnp.int32, (rows.shape[0], 128), 1)
    low = lane < HEAD_DIM
    ca, sa, sb = cosw[...], sina[...], sinb[...]

    def turned(u):
        return u * ca + pltpu.roll(u, 120, 1) * sa + pltpu.roll(u, 8, 1) * sb

    for tile in range(HEADS // 2):
        at = tile * 128
        q = turned(mixed[:, at : at + 128]) * (HEAD_DIM**-0.5)
        k = turned(mixed[:, width + at : width + at + 128])
        v = mixed[:, 2 * width + at : 2 * width + at + 128]
        d = datt[:, at : at + 128]
        for part, (one, two) in enumerate(((q, d), (k, v))):
            for odd in range(2):
                head = 2 * tile + odd
                if odd == 0:
                    packed = jnp.where(low, one, pltpu.roll(two, 64, 1))
                else:
                    packed = jnp.where(low, pltpu.roll(one, 64, 1), two)
                msg[head % PER_GROUP, head // PER_GROUP, part] = packed.astype(BF16)


def front(hid, og, gain, bias, wqkv, bqkv, wdense, tables):
    rows = hid.shape[0]
    return pl.pallas_call(
        front_kernel,
        out_shape=jax.ShapeDtypeStruct((PER_GROUP, HEAD_GROUPS, 2, rows, 128), BF16),
        in_specs=[IN_VMEM] * 10,
        out_specs=IN_VMEM,
        compiler_params=params(),
        name="front",
    )(hid, og, gain, bias, wqkv, bqkv, wdense, *tables)


def mlp_kernel(
    core, hid, og, again, abias, mgain, mbias, win, bin_, wout,
    grads, bin_grad, out_part, gn_part, normed_attn, normed_s,
):
    step = pl.program_id(0)

    @pl.when(step == 0)
    def _():
        xhat, _ = normalise(hid[...].astype(F32))
        normed_s[...] = (xhat * mgain[...].astype(F32) + mbias[...].astype(F32)).astype(BF16)
        normed_attn[...] = (xhat * again[...].astype(F32) + abias[...].astype(F32)).astype(BF16)
        out_part[...] = jnp.zeros_like(out_part)
        gn_part[...] = jnp.zeros_like(gn_part)

    x = normed_s[...]
    w1 = win[...]
    w2 = wout[...]
    inner = mm(x, w1) + bin_[...].astype(F32)
    cdf = 0.5 * (1.0 + lax.erf(inner * (0.5**0.5)))
    act = (inner * cdf).astype(BF16)
    pdf = jnp.exp(-0.5 * inner * inner) * (0.5 * 2.0**0.5 * 3.141592653589793**-0.5)
    gact = mm_nt(og[...], w2)
    ginner = (gact * (cdf + inner * pdf)).astype(BF16)
    bin_grad[...] = jnp.sum(ginner.astype(F32), axis=0, keepdims=True)
    grads[0] = mm_tn(ginner, x).astype(BF16)
    grads[1] = mm_tn(act, og[...]).astype(BF16)
    out_part[...] += mm(act, w2)
    gn_part[...] += mm_nt(ginner, w1)


def mlp(core, hid, og, again, abias, mgain, mbias, win, b_in, wout):
    rows, width = hid.shape
    half = win.shape[1] // 2
    chunk = 512
    steps = half // chunk
    whole = lambda i, c: (0, 0)
    return pl.pallas_call(
        mlp_kernel,
        grid_spec=pltpu.PrefetchScalarGridSpec(
            num_scalar_prefetch=1,
            grid=(steps,),
            in_specs=[
                pl.BlockSpec((rows, width), whole),
                pl.BlockSpec((rows, width), whole),
                pl.BlockSpec((1, width), whole),
                pl.BlockSpec((1, width), whole),
                pl.BlockSpec((1, width), whole),
                pl.BlockSpec((1, width), whole),
                pl.BlockSpec((width, chunk), lambda i, c: (0, c[0] * steps + i)),
                pl.BlockSpec((1, chunk), lambda i, c: (0, c[0] * steps + i)),
                pl.BlockSpec((chunk, width), lambda i, c: (c[0] * steps + i, 0)),
            ],
            out_specs=[
                pl.BlockSpec((2, chunk, width), lambda i, c: (0, i, 0)),
                pl.BlockSpec((1, chunk), lambda i, c: (0, i)),
                pl.BlockSpec((rows, width), whole),
                pl.BlockSpec((rows, width), whole),
                pl.BlockSpec((rows, width), whole),
            ],
            scratch_shapes=[pltpu.VMEM((rows, width), BF16)],
        ),
        out_shape=[
            jax.ShapeDtypeStruct((2, half, width), BF16),
            jax.ShapeDtypeStruct((1, half), F32),
            jax.ShapeDtypeStruct((rows, width), F32),
            jax.ShapeDtypeStruct((rows, width), F32),
            jax.ShapeDtypeStruct((rows, width), BF16),
        ],
        compiler_params=params(),
        name="mlp",
    )(core, hid, og, again, abias, mgain, mbias, win, b_in, wout)


def attention_kernel(blocks, pieces, n_query, *refs):
    tab = refs[0]
    qd_ref = refs[1]
    kv_refs = refs[2 : 2 + pieces]
    odq_ref = refs[2 + pieces]
    dkv_refs = refs[3 + pieces : 3 + 2 * pieces]
    kvs, kvt, sbuf, acc = refs[3 + 2 * pieces :]
    kb_rows = blocks
    per_piece = kv_refs[0].shape[0]
    n_run = pieces * per_piece

    def group_rows(g):
        return pl.ds(pl.multiple_of(g * GROUP, GROUP), GROUP)

    for piece in range(pieces):

        def place(i, _, piece=piece):
            rows = group_rows(tab[piece * per_piece + i])
            blk = kv_refs[piece][i]
            kvs[rows, :] = blk
            kvt[:, rows] = blk.T
            acc[rows, :] = jnp.zeros((GROUP, 128), F32)
            return 0

        lax.fori_loop(0, per_piece, place, 0, unroll=4)

    lane = lax.broadcasted_iota(jnp.int32, (2 * GROUP, 128), 1)
    row = lax.broadcasted_iota(jnp.int32, (128, 2 * GROUP), 0)
    qcol = lax.broadcasted_iota(jnp.int32, (1, 2 * GROUP), 1)
    krow = lax.broadcasted_iota(jnp.int32, (kb_rows, 1), 0)

    def pair_step(pair, _):
        i0 = tab[n_run + 2 * pair]
        i1 = tab[n_run + 2 * pair + 1]
        g0 = tab[n_run + n_query + 2 * pair]
        g1 = tab[n_run + n_query + 2 * pair + 1]
        qd = jnp.concatenate([qd_ref[i0], qd_ref[i1]], axis=0)
        zero = jnp.zeros_like(qd)
        w_keys = jnp.concatenate(
            [jnp.where(lane < HEAD_DIM, qd, zero), jnp.where(lane >= HEAD_DIM, qd, zero)], axis=0
        )
        qdt = qd.T
        zero_t = jnp.zeros_like(qdt)
        w_score = jnp.where(row < HEAD_DIM, qdt, zero_t)
        w_dprob = jnp.where(row >= HEAD_DIM, qdt, zero_t)
        qpos = jnp.where(qcol < GROUP, g0 * GROUP + qcol, (g1 - 1) * GROUP + qcol)
        n_full = (g0 * GROUP) // kb_rows
        n_all = (g1 * GROUP) // kb_rows + 1

        def block_rows(kb):
            return pl.ds(pl.multiple_of(kb * kb_rows, kb_rows), kb_rows)

        def score_step(kb, top, masked):
            rows = block_rows(kb)
            s = mm(kvs[rows, :], w_score)
            if masked:
                s = jnp.where(kb * kb_rows + krow <= qpos, s, MASKED)
            sbuf[rows, :] = s
            return jnp.maximum(top, jnp.max(s.reshape(kb_rows // 8, 8, 2 * GROUP), axis=0))

        top = jnp.full((8, 2 * GROUP), MASKED, F32)
        top = lax.fori_loop(0, n_full, lambda kb, c: score_step(kb, c, False), top)
        top = lax.fori_loop(n_full, n_all, lambda kb, c: score_step(kb, c, True), top)
        top = jnp.max(top, axis=0, keepdims=True)

        def value_step(kb, carry):
            total, out = carry
            rows = block_rows(kb)
            e = jnp.exp(sbuf[rows, :] - top)
            sbuf[rows, :] = e
            total = total + jnp.sum(e.reshape(kb_rows // 8, 8, 2 * GROUP), axis=0)
            return total, out + mm(kvt[HEAD_DIM:128, rows], e.astype(BF16))

        total, out = lax.fori_loop(
            0,
            n_all,
            value_step,
            (jnp.zeros((8, 2 * GROUP), F32), jnp.zeros((HEAD_DIM, 2 * GROUP), F32)),
        )
        inv = 1.0 / jnp.sum(total, axis=0, keepdims=True)
        out = out * inv
        delta = jnp.sum(out * qdt[HEAD_DIM:128, :].astype(F32), axis=0, keepdims=True)

        def grad_step(kb, dq):
            rows = block_rows(kb)
            p = sbuf[rows, :] * inv
            dp = mm(kvs[rows, :], w_dprob)
            ds = (p * (dp - delta)).astype(BF16)
            acc[rows, :] += mm(jnp.concatenate([ds, p.astype(BF16)], axis=1), w_keys)
            return dq + mm(kvt[0:HEAD_DIM, rows], ds)

        dq = lax.fori_loop(0, n_all, grad_step, jnp.zeros((HEAD_DIM, 2 * GROUP), F32))
        odq = jnp.concatenate([out, dq * (HEAD_DIM**-0.5)], axis=0).astype(BF16).T
        odq_ref[i0] = odq[:GROUP]
        odq_ref[i1] = odq[GROUP:]
        return 0

    lax.fori_loop(0, n_query // 2, pair_step, 0)

    for piece in range(pieces):

        def give(i, _, piece=piece):
            dkv_refs[piece][i] = acc[group_rows(tab[piece * per_piece + i]), :].astype(BF16)
            return 0

        lax.fori_loop(0, per_piece, give, 0, unroll=4)


def attention(tab, qd, kvs):
    pieces = len(kvs)
    n_query = qd.shape[0]
    n_key = pieces * kvs[0].shape[0] * GROUP
    blocks = 1024
    run = jax.ShapeDtypeStruct(kvs[0].shape, BF16)
    outs = pl.pallas_call(
        functools.partial(attention_kernel, blocks, pieces, n_query),
        out_shape=[jax.ShapeDtypeStruct(qd.shape, BF16)] + [run] * pieces,
        in_specs=[IN_SMEM] + [IN_VMEM] * (1 + pieces),
        out_specs=[IN_VMEM] * (1 + pieces),
        scratch_shapes=[
            pltpu.VMEM((n_key, 128), BF16),
            pltpu.VMEM((128, n_key), BF16),
            pltpu.VMEM((n_key, 2 * GROUP), F32),
            pltpu.VMEM((n_key, 128), F32),
        ],
        compiler_params=params(),
        name="attention",
    )(tab, qd, *kvs)
    return outs[0], outs[1:]


def tail_kernel(
    hi, odq, dkv, hid, og, again, mgain, wqkv, wdense, bdense, bout, mout, gn,
    cosw, sina, sinb, output, input_grad, send, small,
):
    rows = hid[...].astype(F32)
    count, width = rows.shape
    lane = lax.broadcasted_iota(jnp.int32, (count, 128), 1)
    low = lane < HEAD_DIM
    ca, sa, sb = cosw[...], sina[...], sinb[...]

    def turned_back(g):
        return g * ca - pltpu.roll(g, 120, 1) * sa - pltpu.roll(g, 8, 1) * sb

    def head(ref, a):
        at = lax.rem(a // PER_GROUP - hi[0] + HEAD_GROUPS, HEAD_GROUPS)
        return ref[a % PER_GROUP, at].astype(F32)

    outs, grads = [], [[], [], []]
    for tile in range(HEADS // 2):
        one, two = head(odq, 2 * tile), head(odq, 2 * tile + 1)
        outs.append(jnp.where(low, one, pltpu.roll(two, 64, 1)).astype(BF16))
        grads[0].append(turned_back(jnp.where(low, pltpu.roll(one, 64, 1), two)).astype(BF16))
        one, two = head(dkv, 2 * tile), head(dkv, 2 * tile + 1)
        grads[1].append(
            turned_back(jnp.where(low, one, pltpu.roll(two, 64, 1))).astype(BF16)
        )
        grads[2].append(jnp.where(low, pltpu.roll(one, 64, 1), two).astype(BF16))
    att = jnp.concatenate(outs, axis=1)
    dmixed = jnp.concatenate(grads[0] + grads[1] + grads[2], axis=1)
    half_m, half_a = dmixed.shape[1] // 2, width // 2
    for side in range(2):
        send[side, :, :half_m] = dmixed[:, side * half_m : (side + 1) * half_m]
        send[side, :, half_m:] = att[:, side * half_a : (side + 1) * half_a]
    branch = mm(att, wdense[...]) + bdense[...].astype(F32)
    output[...] = (rows + branch + (mout[...] + bout[...].astype(F32))).astype(BF16)
    gna = mm_nt(dmixed, wqkv[...])
    gnm = gn[...]
    xhat, scale = normalise(rows)
    cot = og[...].astype(F32)
    input_grad[...] = (
        cot
        + norm_back(gna, xhat, scale, again[...].astype(F32))
        + norm_back(gnm, xhat, scale, mgain[...].astype(F32))
    ).astype(BF16)
    small[0:1, :] = jnp.sum(gna * xhat, axis=0, keepdims=True)
    small[1:2, :] = jnp.sum(gna, axis=0, keepdims=True)
    small[2:3, :] = jnp.sum(gnm * xhat, axis=0, keepdims=True)
    small[3:4, :] = jnp.sum(gnm, axis=0, keepdims=True)
    for part in range(3):
        cols = dmixed[:, part * width : (part + 1) * width].astype(F32)
        small[4 + part : 5 + part, :] = jnp.sum(cols, axis=0, keepdims=True)
    small[7:8, :] = jnp.sum(cot, axis=0, keepdims=True)


def tail(hi, odq, dkv, hid, og, again, mgain, wqkv, wdense, bdense, bout, mout, gn, tables):
    rows, width = hid.shape
    return pl.pallas_call(
        tail_kernel,
        out_shape=[
            jax.ShapeDtypeStruct((rows, width), BF16),
            jax.ShapeDtypeStruct((rows, width), BF16),
            jax.ShapeDtypeStruct((2, rows, 2 * width), BF16),
            jax.ShapeDtypeStruct((8, width), F32),
        ],
        in_specs=[IN_SMEM] + [IN_VMEM] * 15,
        out_specs=[IN_VMEM] * 4,
        compiler_params=params(),
        name="tail",
    )(hi, odq, dkv, hid, og, again, mgain, wqkv, wdense, bdense, bout, mout, gn, *tables)


def weight_kernel(own, other, normed, og, grads):
    half_m = own.shape[1] * 3 // 4
    both = jnp.concatenate([own[...], other[...]], axis=0)
    grads[0:half_m, :] = mm_tn(both[:, :half_m], normed[...]).astype(BF16)
    grads[half_m:, :] = mm_tn(both[:, half_m:], og[...]).astype(BF16)


def weight_grads(own, other, normed, og):
    return pl.pallas_call(
        weight_kernel,
        out_shape=jax.ShapeDtypeStruct((own.shape[1], normed.shape[1]), BF16),
        in_specs=[IN_VMEM] * 4,
        out_specs=IN_VMEM,
        compiler_params=params(),
        name="weights",
    )(own, other, normed, og)


def rotary_tables(positions):
    lane = jnp.arange(128, dtype=jnp.int32) % HEAD_DIM
    half = ROTARY // 2
    inverse = jnp.power(ROTARY_BASE, -2.0 * (lane % half).astype(F32) / ROTARY)
    angles = positions.astype(F32)[:, None] * inverse[None, :]
    cosine, sine = jnp.cos(angles), jnp.sin(angles)
    lane = lane[None, :]
    return (
        jnp.where(lane < ROTARY, cosine, 1.0),
        jnp.where(lane < half, -sine, 0.0),
        jnp.where((lane >= half) & (lane < ROTARY), sine, 0.0),
    )


def solution(mesh):
    n_seq, n_blk = mesh.shape["seq"], mesh.shape["blk"]
    n_low = n_blk // HEAD_GROUPS
    low_bits = n_low.bit_length() - 1
    n_rest = n_blk // 4

    def permute(x, target):
        return lax.ppermute(x, "blk", [(b, target(b)) for b in range(n_blk)])

    def to_group(x, by):
        return permute(x, lambda b: ((b // n_low + by) % HEAD_GROUPS) * n_low + b % n_low)

    def flip(x, bit):
        return permute(x, lambda b: b ^ (1 << bit))

    def to_rest(x, by):
        return permute(x, lambda b: ((b // 4 + by) % n_rest) * 4 + b % 4)

    def to_seq(x):
        return lax.ppermute(x, "seq", [(s, (s + 1) % n_seq) for s in range(n_seq)])

    def pair_reduce(x, bit, swap):
        half = x.reshape((2, x.shape[0] // 2) + x.shape[1:])
        got = swap(lax.dynamic_index_in_dim(half, 1 - bit, 0, False))
        mine = lax.dynamic_index_in_dim(half, bit, 0, False)
        return (mine.astype(F32) + got.astype(F32)).astype(BF16)

    def pair_gather(x, bit, swap):
        got = swap(x)
        return jnp.concatenate([jnp.where(bit == 0, x, got), jnp.where(bit == 0, got, x)], axis=0)

    def rest_reduce(x, rest):
        parts = x.reshape((n_rest, x.shape[0] // n_rest) + x.shape[1:])
        total = lax.dynamic_index_in_dim(parts, rest, 0, False).astype(F32)
        for by in range(1, n_rest):
            part = lax.dynamic_index_in_dim(parts, lax.rem(rest + by, n_rest), 0, False)
            total = total + to_rest(part, by).astype(F32)
        return total.astype(BF16)

    def rest_gather(x, rest):
        got = [to_rest(x, by) for by in range(n_rest - 1, 0, -1)] + [x]
        both = jnp.concatenate(got + got[:-1], axis=0)
        start = (n_rest - 1 - rest) * x.shape[0]
        return lax.dynamic_slice_in_dim(both, start, n_rest * x.shape[0], 0)

    def sum_chips(x, order):
        b = lax.axis_index("blk")
        pairs = {
            "x": ((b >> 1) & 1, lambda v: flip(v, 1)),
            "y": (lax.axis_index("seq"), to_seq),
        }
        rest = b // 4
        for name in order:
            x = pair_reduce(x, *pairs[name])
        x = rest_reduce(x, rest)
        x = rest_gather(x, rest)
        for name in reversed(order):
            x = pair_gather(x, *pairs[name])
        return x

    def on_device(
        hidden, positions, ln_attn_gain, ln_attn_bias, ln_mlp_gain, ln_mlp_bias,
        w_qkv, b_qkv, w_dense, b_dense, w_in, b_in, w_out, b_out, out_grad,
    ):
        hid, og, pos = hidden[0], out_grad[0], positions[0]
        again, abias = ln_attn_gain[None], ln_attn_bias[None]
        mgain, mbias = ln_mlp_gain[None], ln_mlp_bias[None]
        tokens, width = hid.shape
        b = lax.axis_index("blk")
        core = b % 2
        hi = b // n_low
        tables = rotary_tables(pos)

        own_runs = pos[::GROUP] // GROUP
        line_runs = jnp.concatenate(
            [own_runs] + [to_group(own_runs, by) for by in range(1, HEAD_GROUPS)]
        )
        key_runs = [line_runs]
        for bit in range(low_bits - 1, -1, -1):
            key_runs = key_runs + [flip(r, bit) for r in key_runs]
        n_query = line_runs.shape[0]
        rank = jnp.sum(line_runs[:, None] > line_runs[None, :], axis=1)
        slots = rank[None, :] == jnp.arange(n_query)[:, None]
        order = jnp.sum(jnp.where(slots, jnp.arange(n_query)[None, :], 0), axis=1)
        ordered = jnp.sum(jnp.where(slots, line_runs[None, :], 0), axis=1)
        tab = jnp.concatenate(key_runs + [order, ordered]).astype(jnp.int32)

        hid2 = jnp.concatenate([hid, flip(hid, 0)], axis=0)
        og2 = jnp.concatenate([og, flip(og, 0)], axis=0)

        msg = front(hid, og, again, abias, w_qkv, b_qkv[None], w_dense, tables)

        arrived = []
        for j in range(PER_GROUP):
            got = []
            for by in range(HEAD_GROUPS):
                part = lax.dynamic_index_in_dim(msg[j], lax.rem(hi + by, HEAD_GROUPS), 0, False)
                got.append(part if by == 0 else to_group(part, by))
            qd = jnp.stack([g[0] for g in got])
            pieces = [jnp.stack([g[1] for g in got])]
            for bit in range(low_bits - 1, -1, -1):
                pieces = pieces + [flip(piece, bit) for piece in pieces]
            arrived.append((qd, pieces))

        mlp_grads, bin_half, out_part, gn_part, normed2 = mlp(
            core[None].astype(jnp.int32), hid2, og2, again, abias, mgain, mbias, w_in, b_in[None], w_out
        )
        mout = out_part[:tokens] + flip(out_part[tokens:], 0)
        gnm = gn_part[:tokens] + flip(gn_part[tokens:], 0)
        win_half = sum_chips(mlp_grads[0], "xy")
        wout_half = sum_chips(mlp_grads[1], "yx")

        back_odq, back_dkv = [], []
        for j in range(PER_GROUP):
            qd, pieces = arrived[j]
            runs = (HEAD_GROUPS * tokens // GROUP, GROUP, 128)
            odq, dkv = attention(tab, qd.reshape(runs), [p.reshape(runs) for p in pieces])
            for bit in range(low_bits):
                half = len(dkv) // 2
                dkv = [
                    (mine.astype(F32) + flip(theirs, bit).astype(F32)).astype(BF16)
                    for mine, theirs in zip(dkv[:half], dkv[half:])
                ]
            for kept, full in ((back_odq, odq), (back_dkv, dkv[0])):
                full = full.reshape(HEAD_GROUPS, tokens, 128)
                got = [full[0]] + [
                    to_group(full[by], HEAD_GROUPS - by) for by in range(1, HEAD_GROUPS)
                ]
                kept.append(jnp.stack(got))

        output, input_grad, send, small = tail(
            hi[None].astype(jnp.int32), jnp.stack(back_odq), jnp.stack(back_dkv), hid, og, again,
            mgain, w_qkv, w_dense, b_dense[None], b_out[None], mout, gnm, tables,
        )
        own = lax.dynamic_index_in_dim(send, core, 0, False)
        other = flip(lax.dynamic_index_in_dim(send, 1 - core, 0, False), 0)
        mixed_half = weight_grads(own, other, normed2, og2)
        half_rows = mixed_half.shape[0] // 2
        mixed_half = jnp.concatenate(
            [sum_chips(mixed_half[:half_rows], "xy"), sum_chips(mixed_half[half_rows:], "yx")]
        )

        def both_cores(x):
            got = flip(x, 0)
            return jnp.where(core == 0, x, got), jnp.where(core == 0, got, x)

        win_t = jnp.concatenate(both_cores(win_half), axis=0)
        wout = jnp.concatenate(both_cores(wout_half), axis=0)
        mixed = both_cores(mixed_half)
        cut = mixed_half.shape[0] * 3 // 4
        wqkv_t = jnp.concatenate([m[:cut] for m in mixed], axis=0)
        wdense = jnp.concatenate([m[cut:] for m in mixed], axis=0)

        zero = jnp.zeros_like(bin_half)
        bin_both = jnp.where(core == 0, jnp.concatenate([bin_half, zero], 1), jnp.concatenate([zero, bin_half], 1))
        vec = jnp.concatenate([small, bin_both.reshape(-1, width)], axis=0)
        for bit in range(2):
            vec = vec + flip(vec, bit)
        vec = vec + to_seq(vec)
        vec = vec + sum(to_rest(vec, by) for by in range(1, n_rest))
        return (
            output[None],
            input_grad[None],
            vec[0],
            vec[1],
            vec[2],
            vec[3],
            wqkv_t.T.astype(F32),
            vec[4:7].reshape(-1),
            wdense.astype(F32),
            vec[7],
            win_t.T.astype(F32),
            vec[8:].reshape(-1),
            wout.astype(F32),
            vec[7],
        )

    rows = P("seq", "blk", None)
    return jax.shard_map(
        on_device,
        mesh=mesh,
        in_specs=(rows, P("seq", "blk")) + (P(),) * 12 + (rows,),
        out_specs=(rows, rows) + (P(),) * 12,
        check_vma=False,
    )
```

```python
import functools

import jax
import jax.numpy as jnp
from jax import lax
from jax.experimental import pallas as pl
from jax.experimental.pallas import tpu as pltpu
from jax.sharding import PartitionSpec as P

HEADS = 12
HEAD_DIM = 64
ROTARY = 16
GROUP = 128
HEAD_GROUPS = 4
PER_GROUP = HEADS // HEAD_GROUPS
NORM_EPSILON = 1e-05
ROTARY_BASE = 10000.0
MASKED = -1e30
VMEM_BYTES = 62 * 1024 * 1024

F32 = jnp.float32
BF16 = jnp.bfloat16
IN_VMEM = pl.BlockSpec(memory_space=pltpu.VMEM)
IN_SMEM = pl.BlockSpec(memory_space=pltpu.SMEM)


def mm(a, b):
    return lax.dot_general(a, b, (((1,), (0,)), ((), ())), preferred_element_type=F32)


def mm_nt(a, b):
    return lax.dot_general(a, b, (((1,), (1,)), ((), ())), preferred_element_type=F32)


def mm_tn(a, b):
    return lax.dot_general(a, b, (((0,), (0,)), ((), ())), preferred_element_type=F32)


def normalise(rows):
    centre = rows - jnp.mean(rows, axis=-1, keepdims=True)
    spread = jnp.mean(centre * centre, axis=-1, keepdims=True)
    scale = lax.rsqrt(spread + NORM_EPSILON)
    return centre * scale, scale


def norm_back(grad, xhat, scale, gain):
    eg = grad * gain
    return scale * (
        eg
        - jnp.mean(eg, axis=-1, keepdims=True)
        - xhat * jnp.mean(eg * xhat, axis=-1, keepdims=True)
    )


def params():
    return pltpu.CompilerParams(vmem_limit_bytes=VMEM_BYTES)


def front_kernel(hid, og, gain, bias, wqkv, bqkv, wdense, cosw, sina, sinb, msg):
    rows = hid[...].astype(F32)
    xhat, _ = normalise(rows)
    normed = (xhat * gain[...].astype(F32) + bias[...].astype(F32)).astype(BF16)
    mixed = mm(normed, wqkv[...]) + bqkv[...].astype(F32)
    datt = mm_nt(og[...], wdense[...])
    width = hid.shape[1]
    lane = lax.broadcasted_iota(jnp.int32, (rows.shape[0], 128), 1)
    low = lane < HEAD_DIM
    ca, sa, sb = cosw[...], sina[...], sinb[...]

    def turned(u):
        return u * ca + pltpu.roll(u, 120, 1) * sa + pltpu.roll(u, 8, 1) * sb

    for tile in range(HEADS // 2):
        at = tile * 128
        q = turned(mixed[:, at : at + 128]) * (HEAD_DIM**-0.5)
        k = turned(mixed[:, width + at : width + at + 128])
        v = mixed[:, 2 * width + at : 2 * width + at + 128]
        d = datt[:, at : at + 128]
        for part, (one, two) in enumerate(((q, d), (k, v))):
            for odd in range(2):
                head = 2 * tile + odd
                if odd == 0:
                    packed = jnp.where(low, one, pltpu.roll(two, 64, 1))
                else:
                    packed = jnp.where(low, pltpu.roll(one, 64, 1), two)
                msg[head % PER_GROUP, head // PER_GROUP, part] = packed.astype(BF16)


def front(hid, og, gain, bias, wqkv, bqkv, wdense, tables):
    rows = hid.shape[0]
    return pl.pallas_call(
        front_kernel,
        out_shape=jax.ShapeDtypeStruct((PER_GROUP, HEAD_GROUPS, 2, rows, 128), BF16),
        in_specs=[IN_VMEM] * 10,
        out_specs=IN_VMEM,
        compiler_params=params(),
        name="front",
    )(hid, og, gain, bias, wqkv, bqkv, wdense, *tables)


def mlp_kernel(
    core, hid, og, again, abias, mgain, mbias, win, bin_, wout,
    grads, bin_grad, out_part, gn_part, normed_attn, normed_s,
):
    step = pl.program_id(0)

    @pl.when(step == 0)
    def _():
        xhat, _ = normalise(hid[...].astype(F32))
        normed_s[...] = (xhat * mgain[...].astype(F32) + mbias[...].astype(F32)).astype(BF16)
        normed_attn[...] = (xhat * again[...].astype(F32) + abias[...].astype(F32)).astype(BF16)
        out_part[...] = jnp.zeros_like(out_part)
        gn_part[...] = jnp.zeros_like(gn_part)

    x = normed_s[...]
    w1 = win[...]
    w2 = wout[...]
    inner = mm(x, w1) + bin_[...].astype(F32)
    cdf = 0.5 * (1.0 + lax.erf(inner * (0.5**0.5)))
    act = (inner * cdf).astype(BF16)
    pdf = jnp.exp(-0.5 * inner * inner) * (0.5 * 2.0**0.5 * 3.141592653589793**-0.5)
    gact = mm_nt(og[...], w2)
    ginner = (gact * (cdf + inner * pdf)).astype(BF16)
    bin_grad[...] = jnp.sum(ginner.astype(F32), axis=0, keepdims=True)
    grads[0] = mm_tn(ginner, x).astype(BF16)
    grads[1] = mm_tn(act, og[...]).astype(BF16)
    out_part[...] += mm(act, w2)
    gn_part[...] += mm_nt(ginner, w1)


def mlp(core, hid, og, again, abias, mgain, mbias, win, b_in, wout):
    rows, width = hid.shape
    half = win.shape[1] // 2
    chunk = 512
    steps = half // chunk
    whole = lambda i, c: (0, 0)
    return pl.pallas_call(
        mlp_kernel,
        grid_spec=pltpu.PrefetchScalarGridSpec(
            num_scalar_prefetch=1,
            grid=(steps,),
            in_specs=[
                pl.BlockSpec((rows, width), whole),
                pl.BlockSpec((rows, width), whole),
                pl.BlockSpec((1, width), whole),
                pl.BlockSpec((1, width), whole),
                pl.BlockSpec((1, width), whole),
                pl.BlockSpec((1, width), whole),
                pl.BlockSpec((width, chunk), lambda i, c: (0, c[0] * steps + i)),
                pl.BlockSpec((1, chunk), lambda i, c: (0, c[0] * steps + i)),
                pl.BlockSpec((chunk, width), lambda i, c: (c[0] * steps + i, 0)),
            ],
            out_specs=[
                pl.BlockSpec((2, chunk, width), lambda i, c: (0, i, 0)),
                pl.BlockSpec((1, chunk), lambda i, c: (0, i)),
                pl.BlockSpec((rows, width), whole),
                pl.BlockSpec((rows, width), whole),
                pl.BlockSpec((rows, width), whole),
            ],
            scratch_shapes=[pltpu.VMEM((rows, width), BF16)],
        ),
        out_shape=[
            jax.ShapeDtypeStruct((2, half, width), BF16),
            jax.ShapeDtypeStruct((1, half), F32),
            jax.ShapeDtypeStruct((rows, width), F32),
            jax.ShapeDtypeStruct((rows, width), F32),
            jax.ShapeDtypeStruct((rows, width), BF16),
        ],
        compiler_params=params(),
        name="mlp",
    )(core, hid, og, again, abias, mgain, mbias, win, b_in, wout)


def attention_kernel(blocks, pieces, n_query, *refs):
    tab = refs[0]
    qd_ref = refs[1]
    kv_refs = refs[2 : 2 + pieces]
    odq_ref = refs[2 + pieces]
    dkv_refs = refs[3 + pieces : 3 + 2 * pieces]
    kvs, kvt, sbuf, acc = refs[3 + 2 * pieces :]
    kb_rows = blocks
    per_piece = kv_refs[0].shape[0]
    n_run = pieces * per_piece

    def group_rows(g):
        return pl.ds(pl.multiple_of(g * GROUP, GROUP), GROUP)

    for piece in range(pieces):

        def place(i, _, piece=piece):
            rows = group_rows(tab[piece * per_piece + i])
            blk = kv_refs[piece][i]
            kvs[rows, :] = blk
            kvt[:, rows] = blk.T
            acc[rows, :] = jnp.zeros((GROUP, 128), F32)
            return 0

        lax.fori_loop(0, per_piece, place, 0, unroll=4)

    lane = lax.broadcasted_iota(jnp.int32, (2 * GROUP, 128), 1)
    row = lax.broadcasted_iota(jnp.int32, (128, 2 * GROUP), 0)
    qcol = lax.broadcasted_iota(jnp.int32, (1, 2 * GROUP), 1)
    krow = lax.broadcasted_iota(jnp.int32, (kb_rows, 1), 0)

    def pair_step(pair, _):
        i0 = tab[n_run + 2 * pair]
        i1 = tab[n_run + 2 * pair + 1]
        g0 = tab[n_run + n_query + 2 * pair]
        g1 = tab[n_run + n_query + 2 * pair + 1]
        qd = jnp.concatenate([qd_ref[i0], qd_ref[i1]], axis=0)
        zero = jnp.zeros_like(qd)
        w_keys = jnp.concatenate(
            [jnp.where(lane < HEAD_DIM, qd, zero), jnp.where(lane >= HEAD_DIM, qd, zero)], axis=0
        )
        qdt = qd.T
        zero_t = jnp.zeros_like(qdt)
        w_score = jnp.where(row < HEAD_DIM, qdt, zero_t)
        w_dprob = jnp.where(row >= HEAD_DIM, qdt, zero_t)
        qpos = jnp.where(qcol < GROUP, g0 * GROUP + qcol, (g1 - 1) * GROUP + qcol)
        n_full = (g0 * GROUP) // kb_rows
        n_all = (g1 * GROUP) // kb_rows + 1

        def block_rows(kb):
            return pl.ds(pl.multiple_of(kb * kb_rows, kb_rows), kb_rows)

        def score_step(kb, top, masked):
            rows = block_rows(kb)
            s = mm(kvs[rows, :], w_score)
            if masked:
                s = jnp.where(kb * kb_rows + krow <= qpos, s, MASKED)
            sbuf[rows, :] = s
            return jnp.maximum(top, jnp.max(s.reshape(kb_rows // 8, 8, 2 * GROUP), axis=0))

        top = jnp.full((8, 2 * GROUP), MASKED, F32)
        top = lax.fori_loop(0, n_full, lambda kb, c: score_step(kb, c, False), top)
        top = lax.fori_loop(n_full, n_all, lambda kb, c: score_step(kb, c, True), top)
        top = jnp.max(top, axis=0, keepdims=True)

        def value_step(kb, carry):
            total, out = carry
            rows = block_rows(kb)
            e = jnp.exp(sbuf[rows, :] - top)
            sbuf[rows, :] = e
            total = total + jnp.sum(e.reshape(kb_rows // 8, 8, 2 * GROUP), axis=0)
            return total, out + mm(kvt[HEAD_DIM:128, rows], e.astype(BF16))

        total, out = lax.fori_loop(
            0,
            n_all,
            value_step,
            (jnp.zeros((8, 2 * GROUP), F32), jnp.zeros((HEAD_DIM, 2 * GROUP), F32)),
        )
        inv = 1.0 / jnp.sum(total, axis=0, keepdims=True)
        out = out * inv
        delta = jnp.sum(out * qdt[HEAD_DIM:128, :].astype(F32), axis=0, keepdims=True)

        def grad_step(kb, dq):
            rows = block_rows(kb)
            p = sbuf[rows, :] * inv
            dp = mm(kvs[rows, :], w_dprob)
            ds = (p * (dp - delta)).astype(BF16)
            acc[rows, :] += mm(jnp.concatenate([ds, p.astype(BF16)], axis=1), w_keys)
            return dq + mm(kvt[0:HEAD_DIM, rows], ds)

        dq = lax.fori_loop(0, n_all, grad_step, jnp.zeros((HEAD_DIM, 2 * GROUP), F32))
        odq = jnp.concatenate([out, dq * (HEAD_DIM**-0.5)], axis=0).astype(BF16).T
        odq_ref[i0] = odq[:GROUP]
        odq_ref[i1] = odq[GROUP:]
        return 0

    lax.fori_loop(0, n_query // 2, pair_step, 0)

    for piece in range(pieces):

        def give(i, _, piece=piece):
            dkv_refs[piece][i] = acc[group_rows(tab[piece * per_piece + i]), :].astype(BF16)
            return 0

        lax.fori_loop(0, per_piece, give, 0, unroll=4)


def attention(tab, qd, kvs):
    pieces = len(kvs)
    n_query = qd.shape[0]
    n_key = pieces * kvs[0].shape[0] * GROUP
    blocks = 1024
    run = jax.ShapeDtypeStruct(kvs[0].shape, BF16)
    outs = pl.pallas_call(
        functools.partial(attention_kernel, blocks, pieces, n_query),
        out_shape=[jax.ShapeDtypeStruct(qd.shape, BF16)] + [run] * pieces,
        in_specs=[IN_SMEM] + [IN_VMEM] * (1 + pieces),
        out_specs=[IN_VMEM] * (1 + pieces),
        scratch_shapes=[
            pltpu.VMEM((n_key, 128), BF16),
            pltpu.VMEM((128, n_key), BF16),
            pltpu.VMEM((n_key, 2 * GROUP), F32),
            pltpu.VMEM((n_key, 128), F32),
        ],
        compiler_params=params(),
        name="attention",
    )(tab, qd, *kvs)
    return outs[0], outs[1:]


class Place:
    def __init__(self, n_seq, n_blk):
        self.n_seq, self.n_blk = n_seq, n_blk
        self.n_low = n_blk // HEAD_GROUPS
        self.n_rest = n_blk // 4
        self.s = lax.axis_index("seq")
        self.b = lax.axis_index("blk")
        self.core = self.b % 2
        self.x = (self.b // 2) % 2
        self.rest = self.b // 4
        self.hi = self.b // self.n_low

    def flip(self, bit):
        step = 1 << bit
        return (self.s, self.b + step - 2 * step * ((self.b // step) % 2))

    def to_seq(self):
        return ((self.s + 1) % self.n_seq, self.b)

    def to_rest(self, by):
        return (self.s, ((self.rest + by) % self.n_rest) * 4 + self.b % 4)

    def to_group(self, by):
        return (self.s, ((self.hi + by) % HEAD_GROUPS) * self.n_low + self.b % self.n_low)

    def partners(self):
        found = [self.flip(bit) for bit in range(self.n_low.bit_length() - 1)]
        found += [self.to_seq()]
        found += [self.to_rest(by) for by in range(1, self.n_rest)]
        if self.n_low != 4:
            found += [self.to_group(by) for by in range(1, HEAD_GROUPS)]
        return found

    def meet(self):
        barrier = pltpu.get_barrier_semaphore()
        partners = self.partners()
        for device in partners:
            pl.semaphore_signal(
                barrier, inc=1, device_id=device, device_id_type=pl.DeviceIdType.MESH
            )
        pl.semaphore_wait(barrier, len(partners))


class Wires:
    def __init__(self, sends, recvs):
        self.sends, self.recvs, self.used = sends, recvs, 0

    def copy(self, src, dst, device):
        at = self.used
        self.used += 1
        return pltpu.make_async_remote_copy(
            src_ref=src,
            dst_ref=dst,
            send_sem=self.sends.at[at],
            recv_sem=self.recvs.at[at],
            device_id=device,
            device_id_type=pl.DeviceIdType.MESH,
        )


def add_rows(dst, dst_at, others, count, out=None, out_at=0, lanes=slice(None), got_lanes=slice(None)):
    block = 16
    for size in (96, 64, 48, 32):
        if count % size == 0:
            block = size
            break
    out = dst if out is None else out

    def step(i, _):
        total = dst[pl.ds(pl.multiple_of(dst_at + i * block, 16), block), lanes].astype(F32)
        for ref, start in others:
            rows = pl.ds(pl.multiple_of(start + i * block, 16), block)
            total = total + ref[rows, got_lanes].astype(F32)
        out[pl.ds(pl.multiple_of(out_at + i * block, 16), block), lanes] = total.astype(BF16)
        return 0

    lax.fori_loop(0, count // block, step, 0)


def unit_copies(n_rest):
    return 2 * (2 + n_rest - 1) + 1


class Unit:
    def __init__(self, place, wires, data, base, size, order, got1, got2, got3, out, final, final_base, local):
        pairs = {"x": (place.x, place.flip(1)), "y": (place.s, place.to_seq())}
        (self.bit1, self.dev1), (self.bit2, self.dev2) = pairs[order[0]], pairs[order[1]]
        self.place, self.data, self.out = place, data, out
        self.base, self.size = base, size
        self.h, self.q = size // 2, size // 4
        n = place.n_rest
        self.cuts = 1 if (self.q // n) % 16 == 0 else 2
        self.e = self.q * self.cuts // n
        self.w = data.shape[1] // self.cuts
        self.base1 = base + self.bit1 * self.h
        self.base2 = self.base1 + self.bit2 * self.q
        self.got1, self.got2, self.got3 = got1, got2, got3
        self.fetch = None
        if local is not None:
            kept = pl.ds(pl.multiple_of(self.base1, 16), self.h)
            self.fetch = pltpu.make_async_copy(data.at[kept], out.at[kept], local)
        z = place.rest

        def cell(ref, start, index):
            at = pl.multiple_of(start + (index // self.cuts) * self.e, 16)
            if self.cuts == 1:
                return ref.at[pl.ds(at, self.e)]
            return ref.at[
                pl.ds(at, self.e), pl.ds(pl.multiple_of((index % self.cuts) * self.w, 128), self.w)
            ]

        def landing(by):
            slot = pl.ds((by - 1) * self.e, self.e)
            return got3.at[slot] if self.cuts == 1 else got3.at[slot, pl.ds(0, self.w)]

        def rows(ref, start, count):
            return ref.at[pl.ds(pl.multiple_of(start, 16), count)]

        self.rs1 = [wires.copy(rows(data, base + (1 - self.bit1) * self.h, self.h), got1, self.dev1)]
        self.rs2 = [wires.copy(rows(got1, (1 - self.bit2) * self.q, self.q), got2, self.dev2)]
        self.rs3 = [
            wires.copy(cell(got2, 0, (z + by) % n), landing(by), place.to_rest(by))
            for by in range(1, n)
        ]
        self.ag3 = [
            wires.copy(cell(out, self.base2, z), cell(out, self.base2, z), place.to_rest(by))
            for by in range(1, n)
        ]
        self.ag2 = [wires.copy(rows(out, self.base2, self.q), rows(out, self.base2, self.q), self.dev2)]
        self.ag1 = [wires.copy(rows(out, self.base1, self.h), rows(out, self.base1, self.h), self.dev1)]
        self.agc = [
            wires.copy(
                rows(out, base, size),
                final.at[place.core, pl.ds(final_base, size)],
                place.flip(0),
            )
        ]
        self.sent = []

    def start(self, copies):
        for copy in copies:
            copy.start()
        self.sent += copies

    def arrive(self, copies):
        for copy in copies:
            copy.wait_recv()

    def stage0(self):
        self.start(self.rs1)
        if self.fetch is not None:
            self.fetch.start()

    def stage1(self):
        self.arrive(self.rs1)
        if self.fetch is not None:
            self.fetch.wait()
        add_rows(self.got1, 0, [(self.data if self.fetch is None else self.out, self.base1)], self.h)
        self.start(self.rs2)

    def stage2(self):
        self.arrive(self.rs2)
        add_rows(self.got2, 0, [(self.got1, self.bit2 * self.q)], self.q)
        self.start(self.rs3)

    def stage3(self):
        self.arrive(self.rs3)
        others = [(self.got3, k * self.e) for k in range(self.place.n_rest - 1)]
        z = self.place.rest
        at = (z // self.cuts) * self.e
        lanes = got_lanes = slice(None)
        if self.cuts > 1:
            lanes = pl.ds(pl.multiple_of((z % self.cuts) * self.w, 128), self.w)
            got_lanes = pl.ds(0, self.w)
        add_rows(self.got2, at, others, self.e, self.out, self.base2 + at, lanes, got_lanes)
        self.start(self.ag3)

    def stage4(self):
        self.arrive(self.ag3)
        self.start(self.ag2)

    def stage5(self):
        self.arrive(self.ag2)
        self.start(self.ag1)

    def stage6(self):
        self.arrive(self.ag1)
        self.start(self.agc)

    def finish(self):
        self.arrive(self.agc)
        for copy in self.sent:
            copy.wait_send()


def tail_compute(
    odq, dkv, hi, hid, og, again, mgain, wqkv, wdense, bdense, bout, mout, gnm,
    cosw, sina, sinb, output, input_grad, send, small,
):
    rows = hid[...].astype(F32)
    count, width = rows.shape
    lane = lax.broadcasted_iota(jnp.int32, (count, 128), 1)
    low = lane < HEAD_DIM
    ca, sa, sb = cosw[...], sina[...], sinb[...]

    def turned_back(g):
        return g * ca - pltpu.roll(g, 120, 1) * sa - pltpu.roll(g, 8, 1) * sb

    def head(ref, a):
        at = (a // PER_GROUP - hi + HEAD_GROUPS) % HEAD_GROUPS
        return ref[a % PER_GROUP, at].astype(F32)

    outs, grads = [], [[], [], []]
    for tile in range(HEADS // 2):
        one, two = head(odq, 2 * tile), head(odq, 2 * tile + 1)
        outs.append(jnp.where(low, one, pltpu.roll(two, 64, 1)).astype(BF16))
        grads[0].append(turned_back(jnp.where(low, pltpu.roll(one, 64, 1), two)).astype(BF16))
        one, two = head(dkv, 2 * tile), head(dkv, 2 * tile + 1)
        grads[1].append(
            turned_back(jnp.where(low, one, pltpu.roll(two, 64, 1))).astype(BF16)
        )
        grads[2].append(jnp.where(low, pltpu.roll(one, 64, 1), two).astype(BF16))
    att = jnp.concatenate(outs, axis=1)
    dmixed = jnp.concatenate(grads[0] + grads[1] + grads[2], axis=1)
    half_m, half_a = dmixed.shape[1] // 2, width // 2
    for side in range(2):
        send[side, :, :half_m] = dmixed[:, side * half_m : (side + 1) * half_m]
        send[side, :, half_m:] = att[:, side * half_a : (side + 1) * half_a]
    branch = mm(att, wdense[...]) + bdense[...].astype(F32)
    output[...] = (rows + branch + (mout + bout[...].astype(F32))).astype(BF16)
    gna = mm_nt(dmixed, wqkv[...])
    xhat, scale = normalise(rows)
    cot = og[...].astype(F32)
    input_grad[...] = (
        cot
        + norm_back(gna, xhat, scale, again[...].astype(F32))
        + norm_back(gnm, xhat, scale, mgain[...].astype(F32))
    ).astype(BF16)
    small[0:1, :] = jnp.sum(gna * xhat, axis=0, keepdims=True)
    small[1:2, :] = jnp.sum(gna, axis=0, keepdims=True)
    small[2:3, :] = jnp.sum(gnm * xhat, axis=0, keepdims=True)
    small[3:4, :] = jnp.sum(gnm, axis=0, keepdims=True)
    for part in range(3):
        cols = dmixed[:, part * width : (part + 1) * width].astype(F32)
        small[4 + part : 5 + part, :] = jnp.sum(cols, axis=0, keepdims=True)
    small[7:8, :] = jnp.sum(cot, axis=0, keepdims=True)


def weight_compute(own, other, normed, og, grads):
    half_m = own.shape[1] * 3 // 4
    both = jnp.concatenate([own, other], axis=0)
    grads[0:half_m, :] = mm_tn(both[:, :half_m], normed[...]).astype(BF16)
    grads[half_m:, :] = mm_tn(both[:, half_m:], og[...]).astype(BF16)


def finish_kernel(
    n_seq, n_blk, units1, units2, pieces,
    odq0, odq1, odq2, *refs,
):
    dkvs = [refs[j * pieces : (j + 1) * pieces] for j in range(PER_GROUP)]
    (
        grads1, out_part, gn_part, hid, og, og2, normed2, bins, again, mgain, wqkv, wdense, bdense, bout,
        cosw, sina, sinb,
        output, input_grad, small_out, final,
        odq_all, dkv_all, dkv_got, mout_got, gn_got, send, other, grads2, small, small_got,
        got1, got2, got3, out1, out2, sends, recvs, local_sem,
    ) = refs[PER_GROUP * pieces :]
    place = Place(n_seq, n_blk)
    wires = Wires(sends, recvs)
    odqs = (odq0, odq1, odq2)
    tokens, width = hid.shape
    n_rest = place.n_rest
    rows1 = grads1.shape[0]
    place.meet()
    sent = []

    def go(copy):
        copy.start()
        sent.append(copy)
        return copy

    mout_copy = go(wires.copy(out_part.at[pl.ds(tokens, tokens)], mout_got, place.flip(0)))
    gn_copy = go(wires.copy(gn_part.at[pl.ds(tokens, tokens)], gn_got, place.flip(0)))
    low_bits = place.n_low.bit_length() - 1
    stage_copies = []
    for j in range(PER_GROUP):
        half = pieces // 2
        stage_copies.append([
            go(wires.copy(dkvs[j][half + i], dkv_got.at[j, i], place.flip(0))) for i in range(half)
        ])
    home = []
    for j in range(PER_GROUP):
        for by in range(1, HEAD_GROUPS):
            home.append(go(wires.copy(odqs[j].at[by], odq_all.at[j, by], place.to_group(HEAD_GROUPS - by))))
    units = []
    at = 0
    for base, size, order in units1:
        units.append(Unit(
            place, wires, grads1, base, size, order,
            got1.at[pl.ds(at // 2, size // 2)], got2.at[pl.ds(at // 4, size // 4)],
            got3.at[pl.ds(at // 2, size // 2)], out1, final, base, local_sem.at[2 + len(units)],
        ))
        at += size
    units_b = []
    for base, size, order in units2:
        units_b.append(Unit(
            place, wires, grads2, base, size, order,
            got1.at[pl.ds(at // 2, size // 2)], got2.at[pl.ds(at // 4, size // 4)],
            got3.at[pl.ds(at // 2, size // 2)], out2, final, rows1 + base, None,
        ))
        at += size
    for unit in units:
        unit.stage0()

    slot = 0
    half = pieces // 2
    for bit in range(low_bits):
        after = slot + half
        for j in range(PER_GROUP):
            for copy in stage_copies[j]:
                copy.wait_recv()
            for i in range(half):
                mine = dkvs[j][i][...] if bit == 0 else dkv_got[j, slot - 2 * half + i]
                dkv_got[j, slot + i] = (mine.astype(F32) + dkv_got[j, slot + i].astype(F32)).astype(BF16)
            if half > 1:
                stage_copies[j] = [
                    go(wires.copy(dkv_got.at[j, slot + half // 2 + i], dkv_got.at[j, after + i], place.flip(bit + 1)))
                    for i in range(half // 2)
                ]
            else:
                for by in range(1, HEAD_GROUPS):
                    home.append(go(wires.copy(
                        dkv_got.at[j, slot, by], dkv_all.at[j, by], place.to_group(HEAD_GROUPS - by)
                    )))
                dkv_all[j, 0] = dkv_got[j, slot, 0]
        slot = after
        half //= 2
    for j in range(PER_GROUP):
        odq_all[j, 0] = odqs[j][0]
    for unit in units:
        unit.stage1()
    for copy in home:
        copy.wait_recv()
    mout_copy.wait_recv()
    gn_copy.wait_recv()
    mout = out_part[0:tokens, :] + mout_got[...]
    gnm = gn_part[0:tokens, :] + gn_got[...]
    tail_compute(
        odq_all, dkv_all, place.hi, hid, og, again, mgain, wqkv, wdense, bdense, bout, mout, gnm,
        cosw, sina, sinb, output, input_grad, send, small,
    )
    other_copy = go(wires.copy(send.at[1 - place.core], other, place.flip(0)))
    for unit in units:
        unit.stage2()
    other_copy.wait_recv()
    weight_compute(send[place.core], other[...], normed2, og2, grads2)
    for unit in units_b:
        unit.stage0()
    small[8:, :] = bins[...]
    for unit in units:
        unit.stage3()
    for unit in units_b:
        unit.stage1()
    order = [[place.flip(0)], [place.flip(1)], [place.to_seq()], [place.to_rest(by) for by in range(1, n_rest)]]
    slot = 0
    for devices in order:
        copies = [wires.copy(small, small_got.at[slot + i], device) for i, device in enumerate(devices)]
        for copy in copies:
            copy.start()
        for copy in copies:
            copy.wait()
        total = small[...]
        for i in range(len(devices)):
            total = total + small_got[slot + i]
        small[...] = total
        slot += len(devices)
    small_out[...] = small[...]
    for unit in units:
        unit.stage4()
    for unit in units_b:
        unit.stage2()
    for unit in units:
        unit.stage5()
    for unit in units_b:
        unit.stage3()
    for unit in units:
        unit.stage6()
    for unit in units_b:
        unit.stage4()
    for unit in units_b:
        unit.stage5()
    for unit in units_b:
        unit.stage6()
    keep1 = pltpu.make_async_copy(out1, final.at[place.core, pl.ds(0, rows1)], local_sem.at[0])
    keep2 = pltpu.make_async_copy(out2, final.at[place.core, pl.ds(rows1, grads2.shape[0])], local_sem.at[1])
    keep1.start()
    keep2.start()
    for unit in units + units_b:
        unit.finish()
    for copy in sent:
        copy.wait_send()
    keep1.wait()
    keep2.wait()


def finish(mesh, odqs, dkvs, grads1, out_part, gn_part, hid, og, og2, normed2, bins, again, mgain, wqkv, wdense, bdense, bout, tables):
    n_seq, n_blk = mesh.shape["seq"], mesh.shape["blk"]
    n_rest = n_blk // 4
    tokens, width = hid.shape
    pieces = len(dkvs[0])
    rows1, rows2 = grads1.shape[0], 2 * width
    fine = (rows1 // 4) % (4 * n_rest * 16) == 0
    parts = 4 if fine else 2
    units1 = [(i * rows1 // parts, rows1 // parts, "xy" if 2 * i < parts else "yx") for i in range(parts)]
    parts = 2 if fine else 1
    units2 = [(i * rows2 // parts, rows2 // parts, "xy" if 2 * i < parts else "yx") for i in range(parts)]
    total = rows1 + rows2
    copies = (len(units1) + len(units2)) * unit_copies(n_rest)
    copies += 3 + PER_GROUP * (2 * (HEAD_GROUPS - 1) + pieces - 1) + 3 + n_rest - 1
    line = (HEAD_GROUPS, tokens, 128)
    n_small = 8 + bins.shape[0]
    inputs = list(odqs) + [p for d in dkvs for p in d] + [
        grads1, out_part, gn_part, hid, og, og2, normed2, bins, again, mgain, wqkv, wdense, bdense, bout, *tables,
    ]
    return pl.pallas_call(
        functools.partial(finish_kernel, n_seq, n_blk, units1, units2, pieces),
        out_shape=[
            jax.ShapeDtypeStruct((tokens, width), BF16),
            jax.ShapeDtypeStruct((tokens, width), BF16),
            jax.ShapeDtypeStruct((n_small, width), F32),
            jax.ShapeDtypeStruct((2, total, width), BF16),
        ],
        in_specs=[pl.BlockSpec(memory_space=pl.ANY) if v is grads1 else IN_VMEM for v in inputs],
        out_specs=[IN_VMEM] * 3 + [pl.BlockSpec(memory_space=pl.ANY)],
        scratch_shapes=[
            pltpu.VMEM((PER_GROUP,) + line, BF16),
            pltpu.VMEM((PER_GROUP,) + line, BF16),
            pltpu.VMEM((PER_GROUP, pieces - 1) + line, BF16),
            pltpu.VMEM((tokens, width), F32),
            pltpu.VMEM((tokens, width), F32),
            pltpu.VMEM((2, tokens, 2 * width), BF16),
            pltpu.VMEM((tokens, 2 * width), BF16),
            pltpu.VMEM((rows2, width), BF16),
            pltpu.VMEM((n_small, width), F32),
            pltpu.VMEM((3 + n_rest - 1, n_small, width), F32),
            pltpu.VMEM((total // 2, width), BF16),
            pltpu.VMEM((total // 4, width), BF16),
            pltpu.VMEM((total // 2, width), BF16),
            pltpu.VMEM((rows1, width), BF16),
            pltpu.VMEM((rows2, width), BF16),
            pltpu.SemaphoreType.DMA((copies,)),
            pltpu.SemaphoreType.DMA((copies,)),
            pltpu.SemaphoreType.DMA((2 + len(units1),)),
        ],
        compiler_params=pltpu.CompilerParams(
            vmem_limit_bytes=VMEM_BYTES, collective_id=1, has_side_effects=True
        ),
        name="finish",
    )(*inputs)


def expand_kernel(marks, block, *outs):
    step = pl.program_id(0)
    for out, (first, last, turn) in zip(outs, marks):

        @pl.when((step >= first) & (step < last))
        def _(out=out, turn=turn):
            rows = block[0].astype(F32)
            out[...] = rows.T if turn else rows


def expand(final, sizes):
    width = final.shape[2]
    block = width // 2
    marks, specs, shapes, firsts = [], [], [], []
    first = offset = 0
    for rows, turn in sizes:
        each = rows // block
        marks.append((first, first + 2 * each, turn))
        firsts.append((first, each, offset))

        def at(i, first=first, count=2 * each):
            return jnp.clip(i - first, 0, count - 1)

        if turn:
            specs.append(pl.BlockSpec((width, block), lambda i, at=at: (0, at(i))))
            shapes.append(jax.ShapeDtypeStruct((width, 2 * rows), F32))
        else:
            specs.append(pl.BlockSpec((block, width), lambda i, at=at: (at(i), 0)))
            shapes.append(jax.ShapeDtypeStruct((2 * rows, width), F32))
        first += 2 * each
        offset += each

    def source(i):
        core, row = 0, 0
        for begin, each, offset in firsts:
            here = (i >= begin) & (i < begin + 2 * each)
            core = jnp.where(here, (i - begin) // each, core)
            row = jnp.where(here, offset + (i - begin) % each, row)
        return (core, row, 0)

    return pl.pallas_call(
        functools.partial(expand_kernel, marks),
        grid=(first,),
        in_specs=[pl.BlockSpec((1, block, width), source)],
        out_specs=specs,
        out_shape=shapes,
        compiler_params=params(),
        name="expand",
    )(final)


def rotary_tables(positions):
    lane = jnp.arange(128, dtype=jnp.int32) % HEAD_DIM
    half = ROTARY // 2
    inverse = jnp.power(ROTARY_BASE, -2.0 * (lane % half).astype(F32) / ROTARY)
    angles = positions.astype(F32)[:, None] * inverse[None, :]
    cosine, sine = jnp.cos(angles), jnp.sin(angles)
    lane = lane[None, :]
    return (
        jnp.where(lane < ROTARY, cosine, 1.0),
        jnp.where(lane < half, -sine, 0.0),
        jnp.where((lane >= half) & (lane < ROTARY), sine, 0.0),
    )


def solution(mesh):
    n_seq, n_blk = mesh.shape["seq"], mesh.shape["blk"]
    n_low = n_blk // HEAD_GROUPS
    low_bits = n_low.bit_length() - 1
    def permute(x, target):
        return lax.ppermute(x, "blk", [(b, target(b)) for b in range(n_blk)])

    def to_group(x, by):
        return permute(x, lambda b: ((b // n_low + by) % HEAD_GROUPS) * n_low + b % n_low)

    def flip(x, bit):
        return permute(x, lambda b: b ^ (1 << bit))

    def on_device(
        hidden, positions, ln_attn_gain, ln_attn_bias, ln_mlp_gain, ln_mlp_bias,
        w_qkv, b_qkv, w_dense, b_dense, w_in, b_in, w_out, b_out, out_grad,
    ):
        hid, og, pos = hidden[0], out_grad[0], positions[0]
        again, abias = ln_attn_gain[None], ln_attn_bias[None]
        mgain, mbias = ln_mlp_gain[None], ln_mlp_bias[None]
        tokens, width = hid.shape
        b = lax.axis_index("blk")
        core = b % 2
        hi = b // n_low
        tables = rotary_tables(pos)

        own_runs = pos[::GROUP] // GROUP
        line_runs = jnp.concatenate(
            [own_runs] + [to_group(own_runs, by) for by in range(1, HEAD_GROUPS)]
        )
        key_runs = [line_runs]
        for bit in range(low_bits - 1, -1, -1):
            key_runs = key_runs + [flip(r, bit) for r in key_runs]
        n_query = line_runs.shape[0]
        rank = jnp.sum(line_runs[:, None] > line_runs[None, :], axis=1)
        slots = rank[None, :] == jnp.arange(n_query)[:, None]
        order = jnp.sum(jnp.where(slots, jnp.arange(n_query)[None, :], 0), axis=1)
        ordered = jnp.sum(jnp.where(slots, line_runs[None, :], 0), axis=1)
        tab = jnp.concatenate(key_runs + [order, ordered]).astype(jnp.int32)

        hid2 = jnp.concatenate([hid, flip(hid, 0)], axis=0)
        og2 = jnp.concatenate([og, flip(og, 0)], axis=0)

        msg = front(hid, og, again, abias, w_qkv, b_qkv[None], w_dense, tables)

        arrived = []
        for j in range(PER_GROUP):
            got = []
            for by in range(HEAD_GROUPS):
                part = lax.dynamic_index_in_dim(msg[j], lax.rem(hi + by, HEAD_GROUPS), 0, False)
                got.append(part if by == 0 else to_group(part, by))
            qd = jnp.stack([g[0] for g in got])
            pieces = [jnp.stack([g[1] for g in got])]
            for bit in range(low_bits - 1, -1, -1):
                pieces = pieces + [flip(piece, bit) for piece in pieces]
            arrived.append((qd, pieces))

        mlp_grads, bin_half, out_part, gn_part, normed2 = mlp(
            core[None].astype(jnp.int32), hid2, og2, again, abias, mgain, mbias, w_in, b_in[None], w_out
        )
        odqs, dkvs = [], []
        line = (HEAD_GROUPS, tokens, 128)
        for j in range(PER_GROUP):
            qd, pieces = arrived[j]
            runs = (HEAD_GROUPS * tokens // GROUP, GROUP, 128)
            odq, dkv = attention(tab, qd.reshape(runs), [p.reshape(runs) for p in pieces])
            odqs.append(odq.reshape(line))
            dkvs.append([d.reshape(line) for d in dkv])

        zero = jnp.zeros_like(bin_half)
        bins = jnp.where(
            core == 0, jnp.concatenate([bin_half, zero], 1), jnp.concatenate([zero, bin_half], 1)
        ).reshape(-1, width)
        half_ff = mlp_grads.shape[1]
        output, input_grad, vec, final = finish(
            mesh, odqs, dkvs, mlp_grads.reshape(2 * half_ff, width), out_part, gn_part, hid, og, og2,
            normed2, bins, again, mgain, w_qkv, w_dense, b_dense[None], b_out[None], tables,
        )
        win, wout, wqkv, wdense = expand(
            final, ((half_ff, True), (half_ff, False), (3 * width // 2, True), (width // 2, False))
        )
        return (
            output[None],
            input_grad[None],
            vec[0],
            vec[1],
            vec[2],
            vec[3],
            wqkv,
            vec[4:7].reshape(-1),
            wdense,
            vec[7],
            win,
            vec[8:].reshape(-1),
            wout,
            vec[7],
        )

    rows = P("seq", "blk", None)
    return jax.shard_map(
        on_device,
        mesh=mesh,
        in_specs=(rows, P("seq", "blk")) + (P(),) * 12 + (rows,),
        out_specs=(rows, rows) + (P(),) * 12,
        check_vma=False,
    )
```

```python
import functools

import jax
import jax.numpy as jnp
from jax import lax
from jax.experimental import pallas as pl
from jax.experimental.pallas import tpu as pltpu
from jax.sharding import PartitionSpec as P

HEADS = 12
HEAD_DIM = 64
ROTARY = 16
GROUP = 128
HEAD_GROUPS = 4
PER_GROUP = HEADS // HEAD_GROUPS
NORM_EPSILON = 1e-05
ROTARY_BASE = 10000.0
MASKED = -1e30
VMEM_BYTES = 62 * 1024 * 1024

F32 = jnp.float32
BF16 = jnp.bfloat16
IN_VMEM = pl.BlockSpec(memory_space=pltpu.VMEM)
IN_SMEM = pl.BlockSpec(memory_space=pltpu.SMEM)


def mm(a, b):
    return lax.dot_general(a, b, (((1,), (0,)), ((), ())), preferred_element_type=F32)


def mm_nt(a, b):
    return lax.dot_general(a, b, (((1,), (1,)), ((), ())), preferred_element_type=F32)


def mm_tn(a, b):
    return lax.dot_general(a, b, (((0,), (0,)), ((), ())), preferred_element_type=F32)


def normalise(rows):
    centre = rows - jnp.mean(rows, axis=-1, keepdims=True)
    spread = jnp.mean(centre * centre, axis=-1, keepdims=True)
    scale = lax.rsqrt(spread + NORM_EPSILON)
    return centre * scale, scale


def norm_back(grad, xhat, scale, gain):
    eg = grad * gain
    return scale * (
        eg
        - jnp.mean(eg, axis=-1, keepdims=True)
        - xhat * jnp.mean(eg * xhat, axis=-1, keepdims=True)
    )


def params():
    return pltpu.CompilerParams(vmem_limit_bytes=VMEM_BYTES)


def front_kernel(hid, og, gain, bias, wqkv, bqkv, wdense, cosw, sina, sinb, msg):
    rows = hid[...].astype(F32)
    xhat, _ = normalise(rows)
    normed = (xhat * gain[...].astype(F32) + bias[...].astype(F32)).astype(BF16)
    mixed = mm(normed, wqkv[...]) + bqkv[...].astype(F32)
    datt = mm_nt(og[...], wdense[...])
    width = hid.shape[1]
    lane = lax.broadcasted_iota(jnp.int32, (rows.shape[0], 128), 1)
    low = lane < HEAD_DIM
    ca, sa, sb = cosw[...], sina[...], sinb[...]

    def turned(u):
        return u * ca + pltpu.roll(u, 120, 1) * sa + pltpu.roll(u, 8, 1) * sb

    for tile in range(HEADS // 2):
        at = tile * 128
        q = turned(mixed[:, at : at + 128]) * (HEAD_DIM**-0.5)
        k = turned(mixed[:, width + at : width + at + 128])
        v = mixed[:, 2 * width + at : 2 * width + at + 128]
        d = datt[:, at : at + 128]
        for part, (one, two) in enumerate(((q, d), (k, v))):
            for odd in range(2):
                head = 2 * tile + odd
                if odd == 0:
                    packed = jnp.where(low, one, pltpu.roll(two, 64, 1))
                else:
                    packed = jnp.where(low, pltpu.roll(one, 64, 1), two)
                msg[head % PER_GROUP, head // PER_GROUP, part] = packed.astype(BF16)


def front(hid, og, gain, bias, wqkv, bqkv, wdense, tables):
    rows = hid.shape[0]
    return pl.pallas_call(
        front_kernel,
        out_shape=jax.ShapeDtypeStruct((PER_GROUP, HEAD_GROUPS, 2, rows, 128), BF16),
        in_specs=[IN_VMEM] * 10,
        out_specs=IN_VMEM,
        compiler_params=params(),
        name="front",
    )(hid, og, gain, bias, wqkv, bqkv, wdense, *tables)


def mlp_kernel(
    core, hid, og, again, abias, mgain, mbias, win, bin_, wout,
    grads, bin_grad, out_part, gn_part, normed_attn, normed_s,
):
    step = pl.program_id(0)

    @pl.when(step == 0)
    def _():
        xhat, _ = normalise(hid[...].astype(F32))
        normed_s[...] = (xhat * mgain[...].astype(F32) + mbias[...].astype(F32)).astype(BF16)
        normed_attn[...] = (xhat * again[...].astype(F32) + abias[...].astype(F32)).astype(BF16)
        out_part[...] = jnp.zeros_like(out_part)
        gn_part[...] = jnp.zeros_like(gn_part)

    x = normed_s[...]
    w1 = win[...]
    w2 = wout[...]
    inner = mm(x, w1) + bin_[...].astype(F32)
    cdf = 0.5 * (1.0 + lax.erf(inner * (0.5**0.5)))
    act = (inner * cdf).astype(BF16)
    pdf = jnp.exp(-0.5 * inner * inner) * (0.5 * 2.0**0.5 * 3.141592653589793**-0.5)
    gact = mm_nt(og[...], w2)
    ginner = (gact * (cdf + inner * pdf)).astype(BF16)
    bin_grad[...] = jnp.sum(ginner.astype(F32), axis=0, keepdims=True)
    grads[0] = mm_tn(ginner, x).astype(BF16)
    grads[1] = mm_tn(act, og[...]).astype(BF16)
    out_part[...] += mm(act, w2)
    gn_part[...] += mm_nt(ginner, w1)


def mlp(core, hid, og, again, abias, mgain, mbias, win, b_in, wout):
    rows, width = hid.shape
    half = win.shape[1] // 2
    chunk = 512
    steps = half // chunk
    whole = lambda i, c: (0, 0)
    return pl.pallas_call(
        mlp_kernel,
        grid_spec=pltpu.PrefetchScalarGridSpec(
            num_scalar_prefetch=1,
            grid=(steps,),
            in_specs=[
                pl.BlockSpec((rows, width), whole),
                pl.BlockSpec((rows, width), whole),
                pl.BlockSpec((1, width), whole),
                pl.BlockSpec((1, width), whole),
                pl.BlockSpec((1, width), whole),
                pl.BlockSpec((1, width), whole),
                pl.BlockSpec((width, chunk), lambda i, c: (0, c[0] * steps + i)),
                pl.BlockSpec((1, chunk), lambda i, c: (0, c[0] * steps + i)),
                pl.BlockSpec((chunk, width), lambda i, c: (c[0] * steps + i, 0)),
            ],
            out_specs=[
                pl.BlockSpec((2, chunk, width), lambda i, c: (0, i, 0)),
                pl.BlockSpec((1, chunk), lambda i, c: (0, i)),
                pl.BlockSpec((rows, width), whole),
                pl.BlockSpec((rows, width), whole),
                pl.BlockSpec((rows, width), whole),
            ],
            scratch_shapes=[pltpu.VMEM((rows, width), BF16)],
        ),
        out_shape=[
            jax.ShapeDtypeStruct((2, half, width), BF16),
            jax.ShapeDtypeStruct((1, half), F32),
            jax.ShapeDtypeStruct((rows, width), F32),
            jax.ShapeDtypeStruct((rows, width), F32),
            jax.ShapeDtypeStruct((rows, width), BF16),
        ],
        compiler_params=params(),
        name="mlp",
    )(core, hid, og, again, abias, mgain, mbias, win, b_in, wout)


def attention_kernel(blocks, pieces, n_query, *refs):
    tab = refs[0]
    qd_ref = refs[1]
    kv_refs = refs[2 : 2 + pieces]
    odq_ref = refs[2 + pieces]
    dkv_refs = refs[3 + pieces : 3 + 2 * pieces]
    kvs, kvt, sbuf, acc = refs[3 + 2 * pieces :]
    kb_rows = blocks
    per_piece = kv_refs[0].shape[0]
    n_run = pieces * per_piece

    def group_rows(g):
        return pl.ds(pl.multiple_of(g * GROUP, GROUP), GROUP)

    for piece in range(pieces):

        def place(i, _, piece=piece):
            rows = group_rows(tab[piece * per_piece + i])
            blk = kv_refs[piece][i]
            kvs[rows, :] = blk
            kvt[:, rows] = blk.T
            acc[rows, :] = jnp.zeros((GROUP, 128), F32)
            return 0

        lax.fori_loop(0, per_piece, place, 0, unroll=4)

    lane = lax.broadcasted_iota(jnp.int32, (2 * GROUP, 128), 1)
    row = lax.broadcasted_iota(jnp.int32, (128, 2 * GROUP), 0)
    qcol = lax.broadcasted_iota(jnp.int32, (1, 2 * GROUP), 1)
    krow = lax.broadcasted_iota(jnp.int32, (kb_rows, 1), 0)

    def pair_step(pair, _):
        i0 = tab[n_run + 2 * pair]
        i1 = tab[n_run + 2 * pair + 1]
        g0 = tab[n_run + n_query + 2 * pair]
        g1 = tab[n_run + n_query + 2 * pair + 1]
        qd = jnp.concatenate([qd_ref[i0], qd_ref[i1]], axis=0)
        zero = jnp.zeros_like(qd)
        w_keys = jnp.concatenate(
            [jnp.where(lane < HEAD_DIM, qd, zero), jnp.where(lane >= HEAD_DIM, qd, zero)], axis=0
        )
        qdt = qd.T
        zero_t = jnp.zeros_like(qdt)
        w_score = jnp.where(row < HEAD_DIM, qdt, zero_t)
        w_dprob = jnp.where(row >= HEAD_DIM, qdt, zero_t)
        qpos = jnp.where(qcol < GROUP, g0 * GROUP + qcol, (g1 - 1) * GROUP + qcol)
        n_full = (g0 * GROUP) // kb_rows
        n_all = (g1 * GROUP) // kb_rows + 1

        def block_rows(kb):
            return pl.ds(pl.multiple_of(kb * kb_rows, kb_rows), kb_rows)

        def score_step(kb, top, masked):
            rows = block_rows(kb)
            s = mm(kvs[rows, :], w_score)
            if masked:
                s = jnp.where(kb * kb_rows + krow <= qpos, s, MASKED)
            sbuf[rows, :] = s
            return jnp.maximum(top, jnp.max(s.reshape(kb_rows // 8, 8, 2 * GROUP), axis=0))

        top = jnp.full((8, 2 * GROUP), MASKED, F32)
        top = lax.fori_loop(0, n_full, lambda kb, c: score_step(kb, c, False), top)
        top = lax.fori_loop(n_full, n_all, lambda kb, c: score_step(kb, c, True), top)
        top = jnp.max(top, axis=0, keepdims=True)

        def value_step(kb, carry):
            total, out = carry
            rows = block_rows(kb)
            e = jnp.exp(sbuf[rows, :] - top)
            sbuf[rows, :] = e
            total = total + jnp.sum(e.reshape(kb_rows // 8, 8, 2 * GROUP), axis=0)
            return total, out + mm(kvt[HEAD_DIM:128, rows], e.astype(BF16))

        total, out = lax.fori_loop(
            0,
            n_all,
            value_step,
            (jnp.zeros((8, 2 * GROUP), F32), jnp.zeros((HEAD_DIM, 2 * GROUP), F32)),
        )
        inv = 1.0 / jnp.sum(total, axis=0, keepdims=True)
        out = out * inv
        delta = jnp.sum(out * qdt[HEAD_DIM:128, :].astype(F32), axis=0, keepdims=True)

        def grad_step(kb, dq):
            rows = block_rows(kb)
            p = sbuf[rows, :] * inv
            dp = mm(kvs[rows, :], w_dprob)
            ds = (p * (dp - delta)).astype(BF16)
            acc[rows, :] += mm(jnp.concatenate([ds, p.astype(BF16)], axis=1), w_keys)
            return dq + mm(kvt[0:HEAD_DIM, rows], ds)

        dq = lax.fori_loop(0, n_all, grad_step, jnp.zeros((HEAD_DIM, 2 * GROUP), F32))
        odq = jnp.concatenate([out, dq * (HEAD_DIM**-0.5)], axis=0).astype(BF16).T
        odq_ref[i0] = odq[:GROUP]
        odq_ref[i1] = odq[GROUP:]
        return 0

    lax.fori_loop(0, n_query // 2, pair_step, 0)

    for piece in range(pieces):

        def give(i, _, piece=piece):
            dkv_refs[piece][i] = acc[group_rows(tab[piece * per_piece + i]), :].astype(BF16)
            return 0

        lax.fori_loop(0, per_piece, give, 0, unroll=4)


def attention(tab, qd, kvs):
    pieces = len(kvs)
    n_query = qd.shape[0]
    n_key = pieces * kvs[0].shape[0] * GROUP
    blocks = 1024
    run = jax.ShapeDtypeStruct(kvs[0].shape, BF16)
    outs = pl.pallas_call(
        functools.partial(attention_kernel, blocks, pieces, n_query),
        out_shape=[jax.ShapeDtypeStruct(qd.shape, BF16)] + [run] * pieces,
        in_specs=[IN_SMEM] + [IN_VMEM] * (1 + pieces),
        out_specs=[IN_VMEM] * (1 + pieces),
        scratch_shapes=[
            pltpu.VMEM((n_key, 128), BF16),
            pltpu.VMEM((128, n_key), BF16),
            pltpu.VMEM((n_key, 2 * GROUP), F32),
            pltpu.VMEM((n_key, 128), F32),
        ],
        compiler_params=params(),
        name="attention",
    )(tab, qd, *kvs)
    return outs[0], outs[1:]


class Place:
    def __init__(self, n_seq, n_blk):
        self.n_seq, self.n_blk = n_seq, n_blk
        self.n_low = n_blk // HEAD_GROUPS
        self.n_rest = n_blk // 4
        self.s = lax.axis_index("seq")
        self.b = lax.axis_index("blk")
        self.core = self.b % 2
        self.x = (self.b // 2) % 2
        self.rest = self.b // 4
        self.hi = self.b // self.n_low

    def flip(self, bit):
        step = 1 << bit
        return (self.s, self.b + step - 2 * step * ((self.b // step) % 2))

    def to_seq(self):
        return ((self.s + 1) % self.n_seq, self.b)

    def to_rest(self, by):
        return (self.s, ((self.rest + by) % self.n_rest) * 4 + self.b % 4)

    def to_group(self, by):
        return (self.s, ((self.hi + by) % HEAD_GROUPS) * self.n_low + self.b % self.n_low)

    def partners(self):
        found = [self.flip(bit) for bit in range(self.n_low.bit_length() - 1)]
        found += [self.to_seq()]
        found += [self.to_rest(by) for by in range(1, self.n_rest)]
        if self.n_low != 4:
            found += [self.to_group(by) for by in range(1, HEAD_GROUPS)]
        return found

    def meet(self):
        barrier = pltpu.get_barrier_semaphore()
        partners = self.partners()
        for device in partners:
            pl.semaphore_signal(
                barrier, inc=1, device_id=device, device_id_type=pl.DeviceIdType.MESH
            )
        pl.semaphore_wait(barrier, len(partners))


class Wires:
    def __init__(self, sends, recvs):
        self.sends, self.recvs, self.used = sends, recvs, 0

    def copy(self, src, dst, device):
        at = self.used
        self.used += 1
        return pltpu.make_async_remote_copy(
            src_ref=src,
            dst_ref=dst,
            send_sem=self.sends.at[at],
            recv_sem=self.recvs.at[at],
            device_id=device,
            device_id_type=pl.DeviceIdType.MESH,
        )


def add_rows(dst, dst_at, others, count, out=None, out_at=0, lanes=slice(None), got_lanes=slice(None)):
    block = 16
    for size in (96, 64, 48, 32):
        if count % size == 0:
            block = size
            break
    out = dst if out is None else out

    def step(i, _):
        total = dst[pl.ds(pl.multiple_of(dst_at + i * block, 16), block), lanes].astype(F32)
        for ref, start in others:
            rows = pl.ds(pl.multiple_of(start + i * block, 16), block)
            total = total + ref[rows, got_lanes].astype(F32)
        out[pl.ds(pl.multiple_of(out_at + i * block, 16), block), lanes] = total.astype(BF16)
        return 0

    lax.fori_loop(0, count // block, step, 0)


def unit_copies(n_rest):
    return 2 * (2 + n_rest - 1) + 1


class Unit:
    def __init__(self, place, wires, data, base, size, order, got1, got2, got3, out, final, final_base, local):
        pairs = {"x": (place.x, place.flip(1)), "y": (place.s, place.to_seq())}
        (self.bit1, self.dev1), (self.bit2, self.dev2) = pairs[order[0]], pairs[order[1]]
        self.place, self.data, self.out = place, data, out
        self.base, self.size = base, size
        self.h, self.q = size // 2, size // 4
        n = place.n_rest
        self.cuts = 1 if (self.q // n) % 16 == 0 else 2
        self.e = self.q * self.cuts // n
        self.w = data.shape[1] // self.cuts
        self.base1 = base + self.bit1 * self.h
        self.base2 = self.base1 + self.bit2 * self.q
        self.got1, self.got2, self.got3 = got1, got2, got3
        self.fetch = None
        if local is not None:
            kept = pl.ds(pl.multiple_of(self.base1, 16), self.h)
            self.fetch = pltpu.make_async_copy(data.at[kept], out.at[kept], local)
        z = place.rest

        def cell(ref, start, index):
            at = pl.multiple_of(start + (index // self.cuts) * self.e, 16)
            if self.cuts == 1:
                return ref.at[pl.ds(at, self.e)]
            return ref.at[
                pl.ds(at, self.e), pl.ds(pl.multiple_of((index % self.cuts) * self.w, 128), self.w)
            ]

        def landing(by):
            slot = pl.ds((by - 1) * self.e, self.e)
            return got3.at[slot] if self.cuts == 1 else got3.at[slot, pl.ds(0, self.w)]

        def rows(ref, start, count):
            return ref.at[pl.ds(pl.multiple_of(start, 16), count)]

        self.rs1 = [wires.copy(rows(data, base + (1 - self.bit1) * self.h, self.h), got1, self.dev1)]
        self.rs2 = [wires.copy(rows(got1, (1 - self.bit2) * self.q, self.q), got2, self.dev2)]
        self.rs3 = [
            wires.copy(cell(got2, 0, (z + by) % n), landing(by), place.to_rest(by))
            for by in range(1, n)
        ]
        self.ag3 = [
            wires.copy(cell(out, self.base2, z), cell(out, self.base2, z), place.to_rest(by))
            for by in range(1, n)
        ]
        self.ag2 = [wires.copy(rows(out, self.base2, self.q), rows(out, self.base2, self.q), self.dev2)]
        self.ag1 = [wires.copy(rows(out, self.base1, self.h), rows(out, self.base1, self.h), self.dev1)]
        self.agc = [
            wires.copy(
                rows(out, base, size),
                final.at[place.core, pl.ds(final_base, size)],
                place.flip(0),
            )
        ]
        self.sent = []

    def start(self, copies):
        for copy in copies:
            copy.start()
        self.sent = self.sent + copies

    def arrive(self, copies):
        for copy in copies:
            copy.wait_recv()

    def stage0(self):
        self.start(self.rs1)
        if self.fetch is not None:
            self.fetch.start()

    def stage1(self):
        self.arrive(self.rs1)
        for copy in self.rs1:
            copy.wait_send()
        self.sent = [copy for copy in self.sent if not any(copy is gone for gone in self.rs1)]
        if self.fetch is not None:
            self.fetch.wait()
        add_rows(self.got1, 0, [(self.data if self.fetch is None else self.out, self.base1)], self.h)
        self.start(self.rs2)

    def stage2(self):
        self.arrive(self.rs2)
        add_rows(self.got2, 0, [(self.got1, self.bit2 * self.q)], self.q)
        self.start(self.rs3)

    def stage3(self):
        self.arrive(self.rs3)
        others = [(self.got3, k * self.e) for k in range(self.place.n_rest - 1)]
        z = self.place.rest
        at = (z // self.cuts) * self.e
        lanes = got_lanes = slice(None)
        if self.cuts > 1:
            lanes = pl.ds(pl.multiple_of((z % self.cuts) * self.w, 128), self.w)
            got_lanes = pl.ds(0, self.w)
        add_rows(self.got2, at, others, self.e, self.out, self.base2 + at, lanes, got_lanes)
        self.start(self.ag3)

    def stage4(self):
        self.arrive(self.ag3)
        self.start(self.ag2)

    def stage5(self):
        self.arrive(self.ag2)
        self.start(self.ag1)

    def stage6(self):
        self.arrive(self.ag1)
        self.start(self.agc)

    def finish(self):
        self.arrive(self.agc)
        for copy in self.sent:
            copy.wait_send()


def tail_compute(
    odq, dkv, hi, hid, og, again, mgain, wqkv, wdense, bdense, bout, mout, gnm,
    cosw, sina, sinb, output, input_grad, send, small,
):
    rows = hid[...].astype(F32)
    count, width = rows.shape
    lane = lax.broadcasted_iota(jnp.int32, (count, 128), 1)
    low = lane < HEAD_DIM
    ca, sa, sb = cosw[...], sina[...], sinb[...]

    def turned_back(g):
        return g * ca - pltpu.roll(g, 120, 1) * sa - pltpu.roll(g, 8, 1) * sb

    def head(ref, a):
        at = (a // PER_GROUP - hi + HEAD_GROUPS) % HEAD_GROUPS
        return ref[a % PER_GROUP, at].astype(F32)

    outs, grads = [], [[], [], []]
    for tile in range(HEADS // 2):
        one, two = head(odq, 2 * tile), head(odq, 2 * tile + 1)
        outs.append(jnp.where(low, one, pltpu.roll(two, 64, 1)).astype(BF16))
        grads[0].append(turned_back(jnp.where(low, pltpu.roll(one, 64, 1), two)).astype(BF16))
        one, two = head(dkv, 2 * tile), head(dkv, 2 * tile + 1)
        grads[1].append(
            turned_back(jnp.where(low, one, pltpu.roll(two, 64, 1))).astype(BF16)
        )
        grads[2].append(jnp.where(low, pltpu.roll(one, 64, 1), two).astype(BF16))
    att = jnp.concatenate(outs, axis=1)
    dmixed = jnp.concatenate(grads[0] + grads[1] + grads[2], axis=1)
    half_m, half_a = dmixed.shape[1] // 2, width // 2
    for side in range(2):
        send[side, :, :half_m] = dmixed[:, side * half_m : (side + 1) * half_m]
        send[side, :, half_m:] = att[:, side * half_a : (side + 1) * half_a]
    branch = mm(att, wdense[...]) + bdense[...].astype(F32)
    output[...] = (rows + branch + (mout + bout[...].astype(F32))).astype(BF16)
    gna = mm_nt(dmixed, wqkv[...])
    xhat, scale = normalise(rows)
    cot = og[...].astype(F32)
    input_grad[...] = (
        cot
        + norm_back(gna, xhat, scale, again[...].astype(F32))
        + norm_back(gnm, xhat, scale, mgain[...].astype(F32))
    ).astype(BF16)
    small[0:1, :] = jnp.sum(gna * xhat, axis=0, keepdims=True)
    small[1:2, :] = jnp.sum(gna, axis=0, keepdims=True)
    small[2:3, :] = jnp.sum(gnm * xhat, axis=0, keepdims=True)
    small[3:4, :] = jnp.sum(gnm, axis=0, keepdims=True)
    for part in range(3):
        cols = dmixed[:, part * width : (part + 1) * width].astype(F32)
        small[4 + part : 5 + part, :] = jnp.sum(cols, axis=0, keepdims=True)
    small[7:8, :] = jnp.sum(cot, axis=0, keepdims=True)


def weight_compute(own, other, normed, og, grads):
    half_m = own.shape[1] * 3 // 4
    both = jnp.concatenate([own, other], axis=0)
    grads[0:half_m, :] = mm_tn(both[:, :half_m], normed[...]).astype(BF16)
    grads[half_m:, :] = mm_tn(both[:, half_m:], og[...]).astype(BF16)


def finish_kernel(
    n_seq, n_blk, units1, units2, pieces,
    odq0, odq1, odq2, *refs,
):
    dkvs = [refs[j * pieces : (j + 1) * pieces] for j in range(PER_GROUP)]
    (
        grads1, out_part, gn_part, hid, og, og2, normed2, bins, again, mgain, wqkv, wdense, bdense, bout,
        cosw, sina, sinb,
        output, input_grad, small_out, final,
        odq_all, dkv_all, dkv_got, mout_got, gn_got, send, other, grads2, small, small_got,
        got1, got2, got3, out1, out2, sends, recvs, local_sem,
    ) = refs[PER_GROUP * pieces :]
    place = Place(n_seq, n_blk)
    wires = Wires(sends, recvs)
    odqs = (odq0, odq1, odq2)
    tokens, width = hid.shape
    n_rest = place.n_rest
    rows1 = grads1.shape[0]
    place.meet()
    sent = []

    def go(copy):
        copy.start()
        sent.append(copy)
        return copy

    mout_copy = go(wires.copy(out_part.at[pl.ds(tokens, tokens)], mout_got, place.flip(0)))
    gn_copy = go(wires.copy(gn_part.at[pl.ds(tokens, tokens)], gn_got, place.flip(0)))
    low_bits = place.n_low.bit_length() - 1
    stage_copies = []
    for j in range(PER_GROUP):
        half = pieces // 2
        stage_copies.append([
            go(wires.copy(dkvs[j][half + i], dkv_got.at[j, i], place.flip(0))) for i in range(half)
        ])
    home = []
    for j in range(PER_GROUP):
        for by in range(1, HEAD_GROUPS):
            home.append(go(wires.copy(odqs[j].at[by], odq_all.at[j, by], place.to_group(HEAD_GROUPS - by))))
    units = []
    at = 0
    for base, size, order in units1:
        units.append(Unit(
            place, wires, grads1, base, size, order,
            got1.at[pl.ds(at // 2, size // 2)], got2.at[pl.ds(at // 4, size // 4)],
            got3.at[pl.ds(at // 2, size // 2)], out1, final, base, local_sem.at[2 + len(units)],
        ))
        at += size
    units_b = []
    for base, size, order in units2:
        units_b.append(Unit(
            place, wires, grads2, base, size, order,
            got1.at[pl.ds(at // 2, size // 2)], got2.at[pl.ds(at // 4, size // 4)],
            got3.at[pl.ds(at // 2, size // 2)], out2, final, rows1 + base, None,
        ))
        at += size
    for unit in units:
        unit.stage0()

    slot = 0
    half = pieces // 2
    for bit in range(low_bits):
        after = slot + half
        for j in range(PER_GROUP):
            for copy in stage_copies[j]:
                copy.wait_recv()
            for i in range(half):
                mine = dkvs[j][i][...] if bit == 0 else dkv_got[j, slot - 2 * half + i]
                dkv_got[j, slot + i] = (mine.astype(F32) + dkv_got[j, slot + i].astype(F32)).astype(BF16)
            if half > 1:
                stage_copies[j] = [
                    go(wires.copy(dkv_got.at[j, slot + half // 2 + i], dkv_got.at[j, after + i], place.flip(bit + 1)))
                    for i in range(half // 2)
                ]
            else:
                for by in range(1, HEAD_GROUPS):
                    home.append(go(wires.copy(
                        dkv_got.at[j, slot, by], dkv_all.at[j, by], place.to_group(HEAD_GROUPS - by)
                    )))
                dkv_all[j, 0] = dkv_got[j, slot, 0]
        slot = after
        half //= 2
    for j in range(PER_GROUP):
        odq_all[j, 0] = odqs[j][0]
    for unit in units:
        unit.stage1()
    for copy in home:
        copy.wait_recv()
    mout_copy.wait_recv()
    gn_copy.wait_recv()
    mout = out_part[0:tokens, :] + mout_got[...]
    gnm = gn_part[0:tokens, :] + gn_got[...]
    tail_compute(
        odq_all, dkv_all, place.hi, hid, og, again, mgain, wqkv, wdense, bdense, bout, mout, gnm,
        cosw, sina, sinb, output, input_grad, send, small,
    )
    other_copy = go(wires.copy(send.at[1 - place.core], other, place.flip(0)))
    for unit in units:
        unit.stage2()
    other_copy.wait_recv()
    weight_compute(send[place.core], other[...], normed2, og2, grads2)
    for unit in units_b:
        unit.stage0()
    small[8:, :] = bins[...]
    for unit in units:
        unit.stage3()
    for unit in units_b:
        unit.stage1()
    order = [[place.flip(0)], [place.flip(1)], [place.to_seq()], [place.to_rest(by) for by in range(1, n_rest)]]
    slot = 0
    for devices in order:
        copies = [wires.copy(small, small_got.at[slot + i], device) for i, device in enumerate(devices)]
        for copy in copies:
            copy.start()
        for copy in copies:
            copy.wait()
        total = small[...]
        for i in range(len(devices)):
            total = total + small_got[slot + i]
        small[...] = total
        slot += len(devices)
    small_out[...] = small[...]
    for unit in units:
        unit.stage4()
    for unit in units_b:
        unit.stage2()
    for unit in units:
        unit.stage5()
    for unit in units_b:
        unit.stage3()
    for unit in units:
        unit.stage6()
    for unit in units_b:
        unit.stage4()
    for unit in units_b:
        unit.stage5()
    for unit in units_b:
        unit.stage6()
    keep1 = pltpu.make_async_copy(out1, final.at[place.core, pl.ds(0, rows1)], local_sem.at[0])
    keep2 = pltpu.make_async_copy(out2, final.at[place.core, pl.ds(rows1, grads2.shape[0])], local_sem.at[1])
    keep1.start()
    keep2.start()
    for unit in units + units_b:
        unit.finish()
    for copy in sent:
        copy.wait_send()
    keep1.wait()
    keep2.wait()


def finish(mesh, odqs, dkvs, grads1, out_part, gn_part, hid, og, og2, normed2, bins, again, mgain, wqkv, wdense, bdense, bout, tables):
    n_seq, n_blk = mesh.shape["seq"], mesh.shape["blk"]
    n_rest = n_blk // 4
    tokens, width = hid.shape
    pieces = len(dkvs[0])
    rows1, rows2 = grads1.shape[0], 2 * width
    fine = (rows1 // 4) % (4 * n_rest * 16) == 0
    parts = 4 if fine else 2
    units1 = [(i * rows1 // parts, rows1 // parts, "xy" if 2 * i < parts else "yx") for i in range(parts)]
    parts = 2 if fine else 1
    units2 = [(i * rows2 // parts, rows2 // parts, "xy" if 2 * i < parts else "yx") for i in range(parts)]
    total = rows1 + rows2
    copies = (len(units1) + len(units2)) * unit_copies(n_rest)
    copies += 3 + PER_GROUP * (2 * (HEAD_GROUPS - 1) + pieces - 1) + 3 + n_rest - 1
    line = (HEAD_GROUPS, tokens, 128)
    n_small = 8 + bins.shape[0]
    inputs = list(odqs) + [p for d in dkvs for p in d] + [
        grads1, out_part, gn_part, hid, og, og2, normed2, bins, again, mgain, wqkv, wdense, bdense, bout, *tables,
    ]
    return pl.pallas_call(
        functools.partial(finish_kernel, n_seq, n_blk, units1, units2, pieces),
        out_shape=[
            jax.ShapeDtypeStruct((tokens, width), BF16),
            jax.ShapeDtypeStruct((tokens, width), BF16),
            jax.ShapeDtypeStruct((n_small, width), F32),
            jax.ShapeDtypeStruct((2, total, width), BF16),
        ],
        in_specs=[pl.BlockSpec(memory_space=pl.ANY) if v is grads1 else IN_VMEM for v in inputs],
        out_specs=[IN_VMEM] * 3 + [pl.BlockSpec(memory_space=pl.ANY)],
        scratch_shapes=[
            pltpu.VMEM((PER_GROUP,) + line, BF16),
            pltpu.VMEM((PER_GROUP,) + line, BF16),
            pltpu.VMEM((PER_GROUP, pieces - 1) + line, BF16),
            pltpu.VMEM((tokens, width), F32),
            pltpu.VMEM((tokens, width), F32),
            pltpu.VMEM((2, tokens, 2 * width), BF16),
            pltpu.VMEM((tokens, 2 * width), BF16),
            pltpu.VMEM((rows2, width), BF16),
            pltpu.VMEM((n_small, width), F32),
            pltpu.VMEM((3 + n_rest - 1, n_small, width), F32),
            pltpu.VMEM((total // 2, width), BF16),
            pltpu.VMEM((total // 4, width), BF16),
            pltpu.VMEM((total // 2, width), BF16),
            pltpu.VMEM((rows1, width), BF16),
            pltpu.VMEM((rows2, width), BF16),
            pltpu.SemaphoreType.DMA((copies,)),
            pltpu.SemaphoreType.DMA((copies,)),
            pltpu.SemaphoreType.DMA((2 + len(units1),)),
        ],
        compiler_params=pltpu.CompilerParams(
            vmem_limit_bytes=VMEM_BYTES, collective_id=1, has_side_effects=True
        ),
        name="finish",
    )(*inputs)


def expand_kernel(marks, block, *outs):
    step = pl.program_id(0)
    for out, (first, last, turn) in zip(outs, marks):

        @pl.when((step >= first) & (step < last))
        def _(out=out, turn=turn):
            rows = block[0].astype(F32)
            out[...] = rows.T if turn else rows


def expand(final, sizes):
    width = final.shape[2]
    block = width // 2
    marks, specs, shapes, firsts = [], [], [], []
    first = offset = 0
    for rows, turn in sizes:
        each = rows // block
        marks.append((first, first + 2 * each, turn))
        firsts.append((first, each, offset))

        def at(i, first=first, count=2 * each):
            return jnp.clip(i - first, 0, count - 1)

        if turn:
            specs.append(pl.BlockSpec((width, block), lambda i, at=at: (0, at(i))))
            shapes.append(jax.ShapeDtypeStruct((width, 2 * rows), F32))
        else:
            specs.append(pl.BlockSpec((block, width), lambda i, at=at: (at(i), 0)))
            shapes.append(jax.ShapeDtypeStruct((2 * rows, width), F32))
        first += 2 * each
        offset += each

    def source(i):
        core, row = 0, 0
        for begin, each, offset in firsts:
            here = (i >= begin) & (i < begin + 2 * each)
            core = jnp.where(here, (i - begin) // each, core)
            row = jnp.where(here, offset + (i - begin) % each, row)
        return (core, row, 0)

    return pl.pallas_call(
        functools.partial(expand_kernel, marks),
        grid=(first,),
        in_specs=[pl.BlockSpec((1, block, width), source)],
        out_specs=specs,
        out_shape=shapes,
        compiler_params=params(),
        name="expand",
    )(final)


KEY_BLOCK = 2048


def half_rows(d):
    return pl.ds(pl.multiple_of(d * GROUP, GROUP), GROUP)


class Attention:
    def __init__(self, lines, devices, flags, kvl, kvtl, kvth, ksel, kselt, bias, sb, acc):
        self.lines, self.devices, self.flags = lines, devices, flags
        self.kvl, self.kvtl, self.kvth = kvl, kvtl, kvth
        self.ksel, self.kselt, self.bias, self.sb, self.acc = ksel, kselt, bias, sb, acc
        self.n = devices * GROUP
        self.block = min(KEY_BLOCK, self.n)

    def prepare(self, pieces):
        for p, ref in enumerate(pieces):

            def step(r, _, p=p, ref=ref):
                rows = half_rows(p * self.lines + r)
                low, high = ref[r, 0:GROUP, :], ref[r, GROUP : 2 * GROUP, :]
                self.kvl[rows, :] = low
                self.kvtl[:, rows] = low.T
                self.kvth[:, rows] = high.T
                self.acc[0, rows, :] = jnp.zeros((GROUP, 128), F32)
                self.acc[1, rows, :] = jnp.zeros((GROUP, 128), F32)
                return 0

            lax.fori_loop(0, self.lines, step, 0, unroll=self.lines)

    def select(self, i, slot, pieces):
        mine = self.flags[0, i]

        def choose(less, low, high):
            cut = (GROUP // 16, 16, 128)
            return jnp.where(less, low.reshape(cut), high.reshape(cut)).reshape(GROUP, 128)

        for p, ref in enumerate(pieces):

            def step(r, _, p=p, ref=ref):
                d = p * self.lines + r
                rows = half_rows(d)
                theirs = self.flags[p, r]
                less = jnp.broadcast_to((theirs < mine)[None], (GROUP // 16, 16, 128))
                self.ksel[slot, rows, :] = choose(less, ref[r, 0:GROUP, :], ref[r, GROUP : 2 * GROUP, :])
                self.kselt[slot, :, rows] = choose(less, self.kvtl[:, rows], self.kvth[:, rows])
                a, b = theirs.astype(F32)[0:8], mine.astype(F32)[0:8]
                self.bias[slot, d] = jnp.concatenate(
                    [jnp.where(a < b, 0.0, MASKED), jnp.where(a > b, 0.0, MASKED)], axis=1
                )
                return 0

            lax.fori_loop(0, self.lines, step, 0)

    def pair(self, first, qd_ref, pieces, odq_ref):
        own_kv = pieces[0]
        n, block = self.n, self.block
        steps = n // block
        per = block // GROUP
        wide = 2 * GROUP
        lane = lax.broadcasted_iota(jnp.int32, (GROUP, 128), 1)
        row = lax.broadcasted_iota(jnp.int32, (128, wide), 0)
        krow = lax.broadcasted_iota(jnp.int32, (wide, 1), 0)
        qcol = lax.broadcasted_iota(jnp.int32, (1, wide), 1)
        diagonal = (krow <= qcol) & ((krow < GROUP) == (qcol < GROUP))
        sb, ksel, kselt, kvl, kvtl, kvth = self.sb, self.ksel, self.kselt, self.kvl, self.kvtl, self.kvth

        def split(q):
            zero = jnp.zeros_like(q)
            return jnp.where(lane < HEAD_DIM, q, zero), jnp.where(lane >= HEAD_DIM, q, zero)

        w_score, w_dprob, w_keys, doutt, kvd, kvdt = [], [], [], [], [], []
        for slot in range(2):
            i = first + slot
            self.select(i, slot, pieces)
            qd = qd_ref[i]
            qdt = qd.T
            zero = jnp.zeros_like(qdt)
            w_score.append(jnp.where(row < HEAD_DIM, qdt, zero))
            w_dprob.append(jnp.where(row >= HEAD_DIM, qdt, zero))
            doutt.append(qdt[HEAD_DIM:128, :].astype(F32))
            w_keys.append([split(qd[at : at + GROUP]) for at in (0, GROUP)])
            kvd.append(own_kv[i])
            rows = half_rows(i)
            kvdt.append(jnp.concatenate([kvtl[:, rows], kvth[:, rows]], axis=1))

        def high(a, b):
            return jnp.concatenate([a[:, GROUP:], b[:, GROUP:]], axis=1)

        w_score.append(high(*w_score))
        w_dprob.append(high(*w_dprob))

        def key_rows(k):
            return pl.ds(pl.multiple_of(k * block, block), block)

        def keys(part, rows):
            return kvl[rows, :] if part == 2 else ksel[part, rows, :]

        def keys_t(part, rows, start, stop):
            return kvtl[start:stop, rows] if part == 2 else kselt[part, start:stop, rows]

        def top8(s):
            return jnp.max(s.reshape(s.shape[0] // 8, 8, wide), axis=0)

        def sum8(s):
            return jnp.sum(s.reshape(s.shape[0] // 8, 8, wide), axis=0)

        own = pl.ds(n, wide)
        tops = []
        for part in range(3):

            def score(k, top, part=part):
                rows = key_rows(k)
                s = mm(keys(part, rows), w_score[part])
                if part < 2:
                    bias = self.bias[part, pl.ds(k * per, per)]
                    s = (s.reshape(per, GROUP // 8, 8, wide) + bias[:, None]).reshape(block, wide)
                sb[part, rows, :] = s
                return jnp.maximum(top, top8(s))

            top = jnp.full((8, wide), MASKED, F32)
            if part < 2:
                s = jnp.where(diagonal, mm(kvd[part], w_score[part]), MASKED)
                sb[part, own, :] = s
                top = top8(s)
            top = lax.fori_loop(0, steps, score, top)
            tops.append(jnp.max(top, axis=0, keepdims=True))

        def join(base, extra, slot, combine):
            at = slot * GROUP
            return jnp.concatenate(
                [base[:, :GROUP], combine(base[:, GROUP:], extra[:, at : at + GROUP])], axis=1
            )

        tops = [join(tops[slot], tops[2], slot, jnp.maximum) for slot in range(2)]
        tops.append(high(*tops))
        totals, outs = [], []
        for part in range(3):

            def value(k, carry, part=part):
                total, out = carry
                rows = key_rows(k)
                e = jnp.exp(sb[part, rows, :] - tops[part])
                sb[part, rows, :] = e
                return total + sum8(e), out + mm(keys_t(part, rows, HEAD_DIM, 128), e.astype(BF16))

            total, out = jnp.zeros((8, wide), F32), jnp.zeros((HEAD_DIM, wide), F32)
            if part < 2:
                e = jnp.exp(sb[part, own, :] - tops[part])
                sb[part, own, :] = e
                total, out = sum8(e), mm(kvdt[part][HEAD_DIM:128], e.astype(BF16))
            total, out = lax.fori_loop(0, steps, value, (total, out))
            totals.append(jnp.sum(total, axis=0, keepdims=True))
            outs.append(out)
        yield
        add = lambda a, b: a + b
        invs = [1.0 / join(totals[slot], totals[2], slot, add) for slot in range(2)]
        outs = [join(outs[slot], outs[2], slot, add) * invs[slot] for slot in range(2)]
        deltas = [jnp.sum(outs[slot] * doutt[slot], axis=0, keepdims=True) for slot in range(2)]
        invs.append(high(*invs))
        deltas.append(high(*deltas))
        dqs = []
        for part in range(3):
            if part < 2:
                weights = [
                    (slice(at * GROUP, (at + 1) * GROUP), at, jnp.concatenate(w_keys[part][at], axis=0))
                    for at in range(2)
                ]
            else:
                (qa, da), (qb, db) = w_keys[0][1], w_keys[1][1]
                weights = [(slice(0, wide), 0, jnp.concatenate([qa, qb, da, db], axis=0))]

            def grad(k, dq, part=part, weights=weights):
                rows = key_rows(k)
                p = sb[part, rows, :] * invs[part]
                dp = mm(keys(part, rows), w_dprob[part])
                ds = (p * (dp - deltas[part])).astype(BF16)
                p = p.astype(BF16)
                for cols, side, w in weights:
                    self.acc[side, rows, :] += mm(jnp.concatenate([ds[:, cols], p[:, cols]], axis=1), w)
                return dq + mm(keys_t(part, rows, 0, HEAD_DIM), ds)

            dq = jnp.zeros((HEAD_DIM, wide), F32)
            if part < 2:
                p = sb[part, own, :] * invs[part]
                dp = mm(kvd[part], w_dprob[part])
                ds = (p * (dp - deltas[part])).astype(BF16)
                p = p.astype(BF16)
                rows = half_rows(first + part)
                for cols, side, w in weights:
                    pd = jnp.concatenate([ds[cols, cols], p[cols, cols]], axis=1)
                    self.acc[side, rows, :] += mm(pd, w)
                dq = mm(kvdt[part][0:HEAD_DIM], ds)
            dqs.append(lax.fori_loop(0, steps, grad, dq))
        for slot in range(2):
            dq = join(dqs[slot], dqs[2], slot, add) * (HEAD_DIM**-0.5)
            odq_ref[first + slot] = jnp.concatenate([outs[slot], dq], axis=0).astype(BF16).T

    def give(self, dkv_refs):
        for p, ref in enumerate(dkv_refs):

            def step(r, _, p=p, ref=ref):
                rows = half_rows(p * self.lines + r)
                ref[r, 0:GROUP, :] = self.acc[0, rows, :].astype(BF16)
                ref[r, GROUP : 2 * GROUP, :] = self.acc[1, rows, :].astype(BF16)
                return 0

            lax.fori_loop(0, self.lines, step, 0, unroll=self.lines)


def attention_scratch(lines, devices):
    n = devices * GROUP
    return [
        pltpu.VMEM((n, 128), BF16),
        pltpu.VMEM((128, n), BF16),
        pltpu.VMEM((128, n), BF16),
        pltpu.VMEM((2, n, 128), BF16),
        pltpu.VMEM((2, 128, n), BF16),
        pltpu.VMEM((2, devices, 8, 2 * GROUP), F32),
        pltpu.VMEM((3, n + 2 * GROUP, 2 * GROUP), F32),
        pltpu.VMEM((2, n, 128), F32),
    ]


class Chain:
    def __init__(self, place, wires, data, base, size, order, got, final, final_base, free):
        pairs = {
            "x": (place.x, place.flip(1)),
            "y": (place.s, place.to_seq()),
            "m": (place.rest % 2, place.flip(2)),
            "f": (place.rest // 2, place.flip(3)),
        }
        self.data, self.got, self.sizes, self.bases, self.bits = data, [], [size], [base], []
        at = 0
        self.down, self.up = [], []
        for level, name in enumerate(order):
            bit, device = pairs[name]
            half = self.sizes[-1] // 2
            got_here = got.at[pl.ds(at, half)]
            at += half
            source, start = (data, base) if level == 0 else (self.got[-1], 0)
            away = pl.ds(pl.multiple_of(start + (1 - bit) * half, 16), half)
            self.down.append(wires.copy(source.at[away], got_here, device))
            self.got.append(got_here)
            self.bits.append(bit)
            self.sizes.append(half)
            self.bases.append(self.bases[-1] + bit * half)
            kept = pl.ds(pl.multiple_of(self.bases[-1], 16), half)
            self.up.append(wires.copy(data.at[kept], data.at[kept], device))
        whole = pl.ds(base, size)
        self.up.insert(0, wires.copy(data.at[whole], final.at[place.core, pl.ds(final_base, size)], place.flip(0)))
        self.depth = len(order)
        self.free, self.first = free, pairs[order[0]][1]
        self.sent = []

    def start(self, copy):
        copy.start()
        self.sent.append(copy)

    def stage(self, number):
        depth = self.depth
        if number == 0:
            self.start(self.down[0])
        elif number <= depth:
            level = number - 1
            self.down[level].wait_recv()
            if level == 0:
                self.down[0].wait_send()
                self.sent.pop()
                pl.semaphore_signal(
                    self.free, inc=1, device_id=self.first, device_id_type=pl.DeviceIdType.MESH
                )
            half = self.sizes[number]
            source, start = (self.data, self.bases[0]) if level == 0 else (self.got[level - 1], 0)
            start = start + self.bits[level] * half
            if number < depth:
                add_rows(self.got[level], 0, [(source, start)], half)
                self.start(self.down[number])
            else:
                add_rows(self.got[level], 0, [(source, start)], half, self.data, self.bases[depth])
                self.start(self.up[depth])
        else:
            level = 2 * depth - number + 1
            self.up[level].wait_recv()
            if level == 2:
                pl.semaphore_wait(self.free, 1)
            self.start(self.up[level - 1])

    def finish(self):
        self.up[0].wait_recv()
        for copy in self.sent:
            copy.wait_send()


SCHEDULE = (
    "front", "send0", "send1", "send2", "mlp0", "u3.0", "u0.0", "mlp1", "u1.0", "u4.0", "mlp2", "line0", "spread0",
    "u5.0", "u0.1", "part", "u3.1", "u2.0", "fwd0", "line1", "u1.1", "spread1", "keys0", "a0", "u3.2", "a0", "u1.2",
    "line2", "u4.1", "spread2", "u3.3", "a0", "u5.1", "fwd1", "u1.3", "u3.4", "u4.2", "a0", "keys1", "fwd2", "u0.2",
    "u1.4", "u3.5", "a1", "u4.3", "core0", "u2.1", "keys2", "u5.2", "u0.3", "a1", "u3.6", "u1.5", "u4.4", "a1",
    "u5.3", "plane0", "u2.2", "u1.6", "u4.5", "u0.4", "a1", "u5.4", "u3.7", "a2", "core1", "u1.7", "u2.3", "u4.6",
    "a2", "u3.8", "u0.5", "a2", "plane1", "u5.5", "a2", "u4.7", "u0.6", "u1.8", "u2.4", "home0", "core2", "home1",
    "u5.6", "grad0", "grad1", "u4.8", "plane2", "u2.5", "u0.7", "u5.7", "v2.1", "v1.1", "v0.1", "home2", "u2.6",
    "tail", "vec0", "v2.2", "v1.2", "u0.8", "v3.1", "grad2", "v1.3", "u5.8", "vec1", "u2.7", "v0.2", "v2.3", "v1.4",
    "v3.2", "v0.3", "v4.1", "v1.5", "v3.3", "v0.4", "v5.1", "vec2", "v1.6", "v3.4", "v4.2", "v0.5", "v5.2", "v1.7",
    "v3.5", "u2.8", "v4.3", "v2.4", "v0.6", "vec3", "v3.6", "v5.3", "v4.4", "v3.7", "v1.8", "v2.5", "v5.4", "v4.5",
    "v0.7", "v2.6", "v5.5", "v4.6", "v3.8", "v5.6", "v0.8", "v2.7", "v4.7", "v5.7", "v2.8", "v4.8", "v5.8",
)
FF_CHUNK = 256
ORDERS = ("xymf", "yxmf", "yxmf", "yxmf", "yxmf", "yxmf", "xymf", "yxmf", "mfxy", "yxmf", "yxmf", "xmyf")


def joined_kernel(
    n_seq, n_blk, units1, units2,
    hid, og, marks, again, abias, mgain, mbias, bqkv, bdense, bout, bin_, cosw, sina, sinb,
    wqkv_hbm, wdense_hbm, win_hbm, wout_hbm,
    output, input_grad, vec_out, final,
    wqkv, wdense, win, wout, hid2, og2, normed2, normed_m, qd_msg, kv_msg, qd_line, keys, flags,
    kvl, kvtl, kvth, ksel, kselt, bias, sb, acc,
    dkv_got, odq_all, dkv_all, out_part, gn_part, mout_got, gn_got, mine, other, bins,
    grads1, grads2, got, small, small_got, sends, recvs, load_sem, chunk_sem, keep_sem, free_sem,
):
    def row(ref):
        return ref[...].astype(F32).reshape(1, ref.shape[0])

    place = Place(n_seq, n_blk)
    wires = Wires(sends, recvs)
    tokens, width = hid.shape
    n_rest = place.n_rest
    core, hi = place.core, place.hi
    half_ff = win_hbm.shape[1] // 2
    chunks = half_ff // FF_CHUNK
    rows1 = grads1.shape[0]
    pieces = place.n_low
    sent, waiting = [], {}
    todo = {}

    def go(name, src, dst, device):
        copy = wires.copy(src, dst, device)
        copy.start()
        sent.append(copy)
        waiting.setdefault(name, []).append(copy)

    def arrive(name):
        for copy in waiting.pop(name):
            copy.wait_recv()

    loads = [
        pltpu.make_async_copy(wqkv_hbm, wqkv, load_sem.at[0]),
        pltpu.make_async_copy(wdense_hbm, wdense, load_sem.at[1]),
    ]
    for load in loads:
        load.start()

    def chunk_loads(f):
        slot = f % 2
        at = pl.multiple_of(core * half_ff + f * FF_CHUNK, FF_CHUNK)
        return [
            pltpu.make_async_copy(win_hbm.at[:, pl.ds(at, FF_CHUNK)], win.at[slot], chunk_sem.at[0, slot]),
            pltpu.make_async_copy(wout_hbm.at[pl.ds(at, FF_CHUNK), :], wout.at[slot], chunk_sem.at[1, slot]),
        ]

    for f in range(2):
        for load in chunk_loads(f):
            load.start()

    turned_rows = jnp.broadcast_to((marks[1] > 0)[None], (GROUP // 16, 16, 128))
    cut = (GROUP // 16, 16, 128)
    for src, dst in ((hid, hid2), (og, og2)):
        for at in range(0, width, 128):
            cols = slice(at, at + 128)
            one, two = src[0:GROUP, cols].reshape(cut), src[GROUP : 2 * GROUP, cols].reshape(cut)
            dst[0:GROUP, cols] = jnp.where(turned_rows, two, one).reshape(GROUP, 128)
            dst[GROUP : 2 * GROUP, cols] = jnp.where(turned_rows, one, two).reshape(GROUP, 128)
    flags[0, 0] = marks[0]
    place.meet()
    for by in range(1, HEAD_GROUPS):
        go("flags", flags.at[0, 0], flags.at[0, by], place.to_group(by))
    for ref in (hid2, og2):
        go("rows", ref.at[pl.ds(0, tokens)], ref.at[pl.ds(tokens, tokens)], place.flip(0))

    lane = lax.broadcasted_iota(jnp.int32, (tokens, 128), 1)
    low = lane < HEAD_DIM

    def front():
        xhat, _ = normalise(hid2[0:tokens, :].astype(F32))
        normed = (xhat * row(again) + row(abias)).astype(BF16)
        for load in loads:
            load.wait()
        mixed = mm(normed, wqkv[...]) + row(bqkv)
        datt = mm_nt(og2[0:tokens, :], wdense[...])
        ca, sa, sb_ = cosw[...], sina[...], sinb[...]

        def turned(u):
            return u * ca + pltpu.roll(u, 120, 1) * sa + pltpu.roll(u, 8, 1) * sb_

        for tile in range(HEADS // 2):
            at = tile * 128
            q = turned(mixed[:, at : at + 128]) * (HEAD_DIM**-0.5)
            k = turned(mixed[:, width + at : width + at + 128])
            v = mixed[:, 2 * width + at : 2 * width + at + 128]
            d = datt[:, at : at + 128]
            for msg, one, two in ((qd_msg, q, d), (kv_msg, k, v)):
                for odd in range(2):
                    head = 2 * tile + odd
                    if odd == 0:
                        packed = jnp.where(low, one, pltpu.roll(two, 64, 1))
                    else:
                        packed = jnp.where(low, pltpu.roll(one, 64, 1), two)
                    msg[head % PER_GROUP, head // PER_GROUP] = packed.astype(BF16)
        arrive("flags")
        go("flag_x", flags.at[0], flags.at[1], place.flip(1))
        go("flag_c", flags.at[0], flags.at[2], place.flip(0))

    def send(j):
        for msg, line, name in ((kv_msg, keys.at[j, 0], "line"), (qd_msg, qd_line.at[j], "line")):
            for by in range(1, HEAD_GROUPS):
                go(name + str(j), msg.at[j, (hi + by) % HEAD_GROUPS], line.at[by], place.to_group(by))
        keys[j, 0, 0] = kv_msg[j, hi]
        qd_line[j, 0] = qd_msg[j, hi]

    def mlp_group(g):
        if g == 0:
            arrive("rows")
            xhat, _ = normalise(hid2[...].astype(F32))
            normed_m[...] = (xhat * row(mgain) + row(mbias)).astype(BF16)
            normed2[...] = (xhat * row(again) + row(abias)).astype(BF16)
            out_part[...] = jnp.zeros_like(out_part)
            gn_part[...] = jnp.zeros_like(gn_part)
        per = chunks // 3

        def step(f, _):
            slot = f % 2
            for load in chunk_loads(f):
                load.wait()
            x, w1, w2 = normed_m[...], win[slot], wout[slot]
            at = pl.multiple_of(f * FF_CHUNK, FF_CHUNK)
            bias_at = pl.ds(pl.multiple_of(core * half_ff + f * FF_CHUNK, FF_CHUNK), FF_CHUNK)
            inner = mm(x, w1) + bin_[bias_at].astype(F32).reshape(1, FF_CHUNK)
            cdf = 0.5 * (1.0 + lax.erf(inner * (0.5**0.5)))
            act = (inner * cdf).astype(BF16)
            pdf = jnp.exp(-0.5 * inner * inner) * (0.5 * 2.0**0.5 * 3.141592653589793**-0.5)
            gact = mm_nt(og2[...], w2)
            ginner = (gact * (cdf + inner * pdf)).astype(BF16)
            bins[0:1, pl.ds(at, FF_CHUNK)] = jnp.sum(ginner.astype(F32), axis=0, keepdims=True)
            grads1[pl.ds(at, FF_CHUNK), :] = mm_tn(ginner, x).astype(BF16)
            grads1[pl.ds(pl.multiple_of(half_ff + at, FF_CHUNK), FF_CHUNK), :] = mm_tn(act, og2[...]).astype(BF16)
            out_part[...] += mm(act, w2)
            gn_part[...] += mm_nt(ginner, w1)

            @pl.when(f + 2 < chunks)
            def _():
                for load in chunk_loads(f + 2):
                    load.start()

            return 0

        lax.fori_loop(g * per, (g + 1) * per, step, 0)

    def part():
        go("part", out_part.at[pl.ds(tokens, tokens)], mout_got, place.flip(0))
        go("part", gn_part.at[pl.ds(tokens, tokens)], gn_got, place.flip(0))

    def spread(j):
        go("x" + str(j), keys.at[j, 0], keys.at[j, 1], place.flip(1))
        go("c" + str(j), keys.at[j, 0], keys.at[j, 2], place.flip(0))

    def forward(j):
        arrive("x" + str(j))
        go("c" + str(j), keys.at[j, 1], keys.at[j, 3], place.flip(0))
        if j == 0:
            arrive("flag_x")
            go("flag_c", flags.at[1], flags.at[3], place.flip(0))

    def keys_there(j):
        arrive("c" + str(j))
        if j == 0:
            arrive("flag_c")

    attention = Attention(HEAD_GROUPS, HEAD_GROUPS * pieces, flags, kvl, kvtl, kvth, ksel, kselt, bias, sb, acc)

    def attend(j):
        sources = [keys.at[j, p] for p in range(pieces)]
        attention.prepare(sources)
        for first in range(0, HEAD_GROUPS, 2):
            yield from attention.pair(first, qd_line.at[j], sources, qd_line.at[j])
            if first + 2 < HEAD_GROUPS:
                yield
        for copy in leaving[j]:
            copy.wait_send()
        attention.give(sources)
        for by in range(1, HEAD_GROUPS):
            go("home" + str(j), qd_line.at[j, by], odq_all.at[j, by], place.to_group(HEAD_GROUPS - by))
        for i in range(2):
            go("core" + str(j), keys.at[j, 2 + i], dkv_got.at[j, i], place.flip(0))
        yield

    leaving = {}

    def core_sum(j):
        arrive("core" + str(j))
        for i in range(2):
            dkv_got[j, i] = (keys[j, i].astype(F32) + dkv_got[j, i].astype(F32)).astype(BF16)
        go("plane" + str(j), dkv_got.at[j, 1], dkv_got.at[j, 2], place.flip(1))

    def plane_sum(j):
        arrive("plane" + str(j))
        dkv_got[j, 2] = (dkv_got[j, 0].astype(F32) + dkv_got[j, 2].astype(F32)).astype(BF16)
        for by in range(1, HEAD_GROUPS):
            go("home" + str(j), dkv_got.at[j, 2, by], dkv_all.at[j, by], place.to_group(HEAD_GROUPS - by))
        odq_all[j, 0] = qd_line[j, 0]
        dkv_all[j, 0] = dkv_got[j, 2, 0]

    def home(j):
        arrive("home" + str(j))
        ca, sa, sb_ = cosw[...], sina[...], sinb[...]

        def turned_back(g):
            return g * ca - pltpu.roll(g, 120, 1) * sa - pltpu.roll(g, 8, 1) * sb_

        for g in range(HEAD_GROUPS):
            at = (g - hi + HEAD_GROUPS) % HEAD_GROUPS
            a, b = odq_all[j, at].astype(F32), dkv_all[j, at].astype(F32)
            mine[j, g, :, 0:128] = jnp.where(low, a, turned_back(a)).astype(BF16)
            mine[j, g, :, 128:256] = jnp.where(low, turned_back(b), b).astype(BF16)
        half = HEAD_GROUPS // 2
        go("other" + str(j), mine.at[j, pl.ds((1 - core) * half, half)], other.at[j], place.flip(0))

    def grad(j):
        arrive("other" + str(j))
        half = HEAD_GROUPS // 2
        normed, cot = normed2[...], og2[...]
        from_out = lax.broadcasted_iota(jnp.int32, (128, width), 0) < HEAD_DIM
        for g in range(half):
            both = jnp.concatenate([mine[j, core * half + g], other[j, g]], axis=0)
            base = (j * half + g) * 256
            by_normed = mm_tn(both, normed)
            by_cot = mm_tn(both[:, 0:128], cot)
            grads2[base : base + 128, :] = jnp.where(from_out, by_cot, by_normed[0:128]).astype(BF16)
            grads2[base + 128 : base + 256, :] = by_normed[128:256].astype(BF16)
        per = len(units2) // PER_GROUP
        for unit in second[j * per : (j + 1) * per]:
            unit.stage(0)

    def tail():
        arrive("part")
        rows = hid2[0:tokens, :].astype(F32)

        def parts(a):
            return mine[a % PER_GROUP, a // PER_GROUP].astype(F32)

        outs, grads = [], [[], [], []]
        for tile in range(HEADS // 2):
            one, two = parts(2 * tile), parts(2 * tile + 1)
            a1, b1, a2, b2 = one[:, 0:128], one[:, 128:256], two[:, 0:128], two[:, 128:256]
            outs.append(jnp.where(low, a1, pltpu.roll(a2, 64, 1)).astype(BF16))
            grads[0].append(jnp.where(low, pltpu.roll(a1, 64, 1), a2).astype(BF16))
            grads[1].append(jnp.where(low, b1, pltpu.roll(b2, 64, 1)).astype(BF16))
            grads[2].append(jnp.where(low, pltpu.roll(b1, 64, 1), b2).astype(BF16))
        att = jnp.concatenate(outs, axis=1)
        dmixed = jnp.concatenate(grads[0] + grads[1] + grads[2], axis=1)
        branch = mm(att, wdense[...]) + row(bdense)
        mout = out_part[0:tokens, :] + mout_got[...]
        output[...] = (rows + branch + (mout + row(bout))).astype(BF16)
        gna = mm_nt(dmixed, wqkv[...])
        gnm = gn_part[0:tokens, :] + gn_got[...]
        xhat, scale = normalise(rows)
        cot = og2[0:tokens, :].astype(F32)
        input_grad[...] = (
            cot
            + norm_back(gna, xhat, scale, row(again))
            + norm_back(gnm, xhat, scale, row(mgain))
        ).astype(BF16)
        small[0:1, :] = jnp.sum(gna * xhat, axis=0, keepdims=True)
        small[1:2, :] = jnp.sum(gna, axis=0, keepdims=True)
        small[2:3, :] = jnp.sum(gnm * xhat, axis=0, keepdims=True)
        small[3:4, :] = jnp.sum(gnm, axis=0, keepdims=True)
        for k in range(3):
            cols = dmixed[:, k * width : (k + 1) * width].astype(F32)
            small[4 + k : 5 + k, :] = jnp.sum(cols, axis=0, keepdims=True)
        small[7:8, :] = jnp.sum(cot, axis=0, keepdims=True)
        per = half_ff // width
        for side in range(2):
            here = (1 - core if side == 0 else core).astype(F32)
            for k in range(per):
                at = 8 + side * per + k
                small[at : at + 1, :] = bins[0:1, k * width : (k + 1) * width] * here

    rounds = [
        [place.flip(0)],
        [place.flip(1)],
        [place.to_seq()],
        [place.to_rest(by) for by in range(1, n_rest)],
    ]

    def vec_start(r):
        for i, device in enumerate(rounds[r]):
            go("vec" + str(r), small.at[pl.ds(0, small.shape[0])] if r == 0 else small_got.at[8 + r], small_got.at[2 * r if r < 3 else 5 + i], device)

    def vec(r):
        if r == 0:
            vec_start(0)
            return
        arrive("vec" + str(r - 1))
        source = small[...] if r == 1 else small_got[8 + r - 1]
        small_got[8 + r] = source + small_got[2 * (r - 1)]
        vec_start(r)

    def vec_end():
        arrive("vec3")
        total = small_got[8 + 3]
        for i in range(n_rest - 1):
            total = total + small_got[5 + i]
        vec_out[...] = total

    first, second = [], []
    at = 0
    for found, units, data, offset in ((first, units1, grads1, 0), (second, units2, grads2, rows1)):
        for base, size, order in units:
            found.append(Chain(
                place, wires, data, base, size, order, got.at[pl.ds(at, size)], final, offset + base,
                free_sem.at[len(first) + len(second)],
            ))
            at += size

    todo = {"front": front, "part": part, "tail": tail}
    for g in range(3):
        todo["mlp" + str(g)] = functools.partial(mlp_group, g)
    for r in range(4):
        todo["vec" + str(r)] = functools.partial(vec, r)
    runs = {}
    for j in range(PER_GROUP):
        for name, action in (
            ("send", send), ("line", lambda j: arrive("line" + str(j))), ("spread", spread), ("fwd", forward),
            ("keys", keys_there), ("core", core_sum), ("plane", plane_sum), ("home", home), ("grad", grad),
        ):
            todo[name + str(j)] = functools.partial(action, j)
        runs[j] = attend(j)
        todo["a" + str(j)] = functools.partial(next, runs[j])
    for name, units in (("u", first), ("v", second)):
        for i, unit in enumerate(units):
            for stage in range(2 * unit.depth + 1):
                todo[name + str(i) + "." + str(stage)] = functools.partial(unit.stage, stage)
    for j in range(PER_GROUP):
        leaving[j] = []
    for token in SCHEDULE:
        before = len(sent)
        todo[token]()
        if token[:-1] in ("spread", "fwd"):
            leaving[int(token[-1])] += sent[before:]
            del sent[before:]
    vec_end()
    keeps = [
        pltpu.make_async_copy(grads1, final.at[core, pl.ds(0, rows1)], keep_sem.at[0]),
        pltpu.make_async_copy(grads2, final.at[core, pl.ds(rows1, grads2.shape[0])], keep_sem.at[1]),
    ]
    for keep in keeps:
        keep.start()
    for unit in first + second:
        if unit.sent:
            unit.finish()
    for copy in sent:
        copy.wait_send()
    for keep in keeps:
        keep.wait()


def joined(mesh, hid, og, marks, again, abias, mgain, mbias, bqkv, bdense, bout, b_in, tables, wqkv, wdense, win, wout):
    n_seq, n_blk = mesh.shape["seq"], mesh.shape["blk"]
    n_low, n_rest = n_blk // HEAD_GROUPS, n_blk // 4
    tokens, width = hid.shape
    half_ff = win.shape[1] // 2
    rows1, rows2 = 2 * half_ff, 2 * width
    size = half_ff // 3
    units1 = [(i * size, size, order) for i, order in enumerate(ORDERS[:6])]
    size = rows2 // 6
    units2 = [(i * size, size, order) for i, order in enumerate(ORDERS[6:])]
    total = rows1 + rows2
    copies = 9 * (len(units1) + len(units2)) + 128
    line = (HEAD_GROUPS, tokens, 128)
    n_small = 8 + 2 * half_ff // width
    devices = HEAD_GROUPS * n_low
    per = PER_GROUP
    inputs = [hid, og, marks, again, abias, mgain, mbias, bqkv, bdense, bout, b_in, *tables, wqkv, wdense, win, wout]
    return pl.pallas_call(
        functools.partial(joined_kernel, n_seq, n_blk, units1, units2),
        out_shape=[
            jax.ShapeDtypeStruct((tokens, width), BF16),
            jax.ShapeDtypeStruct((tokens, width), BF16),
            jax.ShapeDtypeStruct((n_small, width), F32),
            jax.ShapeDtypeStruct((2, total, width), BF16),
        ],
        in_specs=[IN_VMEM] * (len(inputs) - 4) + [pl.BlockSpec(memory_space=pl.ANY)] * 4,
        out_specs=[IN_VMEM] * 3 + [pl.BlockSpec(memory_space=pl.ANY)],
        scratch_shapes=[
            pltpu.VMEM(wqkv.shape, BF16),
            pltpu.VMEM(wdense.shape, BF16),
            pltpu.VMEM((2, width, FF_CHUNK), BF16),
            pltpu.VMEM((2, FF_CHUNK, width), BF16),
            pltpu.VMEM((2 * tokens, width), BF16),
            pltpu.VMEM((2 * tokens, width), BF16),
            pltpu.VMEM((2 * tokens, width), BF16),
            pltpu.VMEM((2 * tokens, width), BF16),
            pltpu.VMEM((per,) + line, BF16),
            pltpu.VMEM((per,) + line, BF16),
            pltpu.VMEM((per,) + line, BF16),
            pltpu.VMEM((per, n_low) + line, BF16),
            pltpu.VMEM((n_low, HEAD_GROUPS, 16, 128), BF16),
            *attention_scratch(HEAD_GROUPS, devices),
            pltpu.VMEM((per, 3) + line, BF16),
            pltpu.VMEM((per,) + line, BF16),
            pltpu.VMEM((per,) + line, BF16),
            pltpu.VMEM((2 * tokens, width), F32),
            pltpu.VMEM((2 * tokens, width), F32),
            pltpu.VMEM((tokens, width), F32),
            pltpu.VMEM((tokens, width), F32),
            pltpu.VMEM((per, HEAD_GROUPS, tokens, 256), BF16),
            pltpu.VMEM((per, HEAD_GROUPS // 2, tokens, 256), BF16),
            pltpu.VMEM((1, half_ff), F32),
            pltpu.VMEM((rows1, width), BF16),
            pltpu.VMEM((rows2, width), BF16),
            pltpu.VMEM((total, width), BF16),
            pltpu.VMEM((n_small, width), F32),
            pltpu.VMEM((12, n_small, width), F32),
            pltpu.SemaphoreType.DMA((copies,)),
            pltpu.SemaphoreType.DMA((copies,)),
            pltpu.SemaphoreType.DMA((2,)),
            pltpu.SemaphoreType.DMA((2, 2)),
            pltpu.SemaphoreType.DMA((2,)),
            pltpu.SemaphoreType.REGULAR((len(units1) + len(units2),)),
        ],
        compiler_params=pltpu.CompilerParams(
            vmem_limit_bytes=VMEM_BYTES, collective_id=2, has_side_effects=True
        ),
        name="joined",
    )(*inputs)


def spread_kernel(
    final, vec, out_rows, grad_rows, marks,
    output, input_grad, win, wout, wqkv, wdense, again, abias, mgain, mbias, bqkv, bdense, bin_, bout,
):
    half_ff = win.shape[1] // 2

    @pl.when(pl.program_id(0) == 0)
    def _():
        width = vec.shape[1]
        turned_rows = jnp.broadcast_to((marks[1] > 0)[None], (GROUP // 16, 16, 128))
        cut = (GROUP // 16, 16, 128)
        for src, dst in ((out_rows, output), (grad_rows, input_grad)):
            for at in range(0, width, 128):
                cols = slice(at, at + 128)
                one, two = src[0:GROUP, cols].reshape(cut), src[GROUP : 2 * GROUP, cols].reshape(cut)
                dst[0:GROUP, cols] = jnp.where(turned_rows, two, one).reshape(GROUP, 128)
                dst[GROUP : 2 * GROUP, cols] = jnp.where(turned_rows, one, two).reshape(GROUP, 128)
        for ref, at in ((again, 0), (abias, 1), (mgain, 2), (mbias, 3), (bqkv, 4), (bdense, 7), (bout, 7), (bin_, 8)):
            for k in range(ref.shape[0] // width):
                ref[k * width : (k + 1) * width] = vec[at + k : at + k + 1, :].reshape(width)

    for core in range(2):
        win[:, core * half_ff : (core + 1) * half_ff] = final[core, 0:half_ff, :].T.astype(F32)
        wout[core * half_ff : (core + 1) * half_ff, :] = final[core, half_ff : 2 * half_ff, :].astype(F32)

    def segment(head, part):
        group, j = head // PER_GROUP, head % PER_GROUP
        half = HEAD_GROUPS // 2
        at = 2 * half_ff + (j * half + group % half) * 256 + part * HEAD_DIM
        return final[group // half, at : at + HEAD_DIM, :]

    width = wdense.shape[0]
    for tile in range(HEADS // 2):
        for part in range(4):
            both = jnp.concatenate([segment(2 * tile, part), segment(2 * tile + 1, part)], axis=0)
            if part == 0:
                wdense[tile * 128 : tile * 128 + 128, :] = both.astype(F32)
            else:
                at = (part - 1) * width + tile * 128
                wqkv[:, at : at + 128] = both.T.astype(F32)


def spread_out(final, vec, out_rows, grad_rows, marks, ff):
    total, width = final.shape[1:]
    lanes = 128

    def whole(x):
        return pl.BlockSpec(x.shape, lambda i: (0,) * len(x.shape))

    vectors = [jax.ShapeDtypeStruct((n,), F32) for n in (width, width, width, width, 3 * width, width, ff, width)]
    rows = jax.ShapeDtypeStruct(out_rows.shape, BF16)
    return pl.pallas_call(
        spread_kernel,
        grid=(width // lanes,),
        in_specs=[pl.BlockSpec((2, total, lanes), lambda i: (0, 0, i))]
        + [whole(x) for x in (vec, out_rows, grad_rows, marks)],
        out_specs=[
            whole(rows),
            whole(rows),
            pl.BlockSpec((lanes, ff), lambda i: (i, 0)),
            pl.BlockSpec((ff, lanes), lambda i: (0, i)),
            pl.BlockSpec((lanes, 3 * width), lambda i: (i, 0)),
            pl.BlockSpec((width, lanes), lambda i: (0, i)),
        ]
        + [whole(x) for x in vectors],
        out_shape=[
            rows,
            rows,
            jax.ShapeDtypeStruct((width, ff), F32),
            jax.ShapeDtypeStruct((ff, width), F32),
            jax.ShapeDtypeStruct((width, 3 * width), F32),
            jax.ShapeDtypeStruct((width, width), F32),
        ]
        + vectors,
        compiler_params=params(),
        name="spread",
    )(final, vec, out_rows, grad_rows, marks)


def rotary_tables(positions):
    lane = jnp.arange(128, dtype=jnp.int32) % HEAD_DIM
    half = ROTARY // 2
    inverse = jnp.power(ROTARY_BASE, -2.0 * (lane % half).astype(F32) / ROTARY)
    angles = positions.astype(F32)[:, None] * inverse[None, :]
    cosine, sine = jnp.cos(angles), jnp.sin(angles)
    lane = lane[None, :]
    return (
        jnp.where(lane < ROTARY, cosine, 1.0),
        jnp.where(lane < half, -sine, 0.0),
        jnp.where((lane >= half) & (lane < ROTARY), sine, 0.0),
    )


def solution(mesh):
    n_seq, n_blk = mesh.shape["seq"], mesh.shape["blk"]
    n_low = n_blk // HEAD_GROUPS
    low_bits = n_low.bit_length() - 1
    def permute(x, target):
        return lax.ppermute(x, "blk", [(b, target(b)) for b in range(n_blk)])

    def to_group(x, by):
        return permute(x, lambda b: ((b // n_low + by) % HEAD_GROUPS) * n_low + b % n_low)

    def flip(x, bit):
        return permute(x, lambda b: b ^ (1 << bit))

    def on_device(
        hidden, positions, ln_attn_gain, ln_attn_bias, ln_mlp_gain, ln_mlp_bias,
        w_qkv, b_qkv, w_dense, b_dense, w_in, b_in, w_out, b_out, out_grad,
    ):
        hid, og, pos = hidden[0], out_grad[0], positions[0]
        again, abias = ln_attn_gain[None], ln_attn_bias[None]
        mgain, mbias = ln_mlp_gain[None], ln_mlp_bias[None]
        tokens, width = hid.shape
        if n_low == 4:
            group = pos[0] // GROUP
            mirror = 2 * n_blk - 1 - group
            turn = group > mirror
            shown = jnp.stack([jnp.minimum(group, mirror), turn.astype(group.dtype)]).astype(BF16)
            marks = jnp.broadcast_to(shown[:, None, None], (2, 16, 128))

            def ordered(rows):
                return jnp.where(turn, jnp.roll(rows, GROUP, axis=0), rows)

            output, input_grad, vec, final = joined(
                mesh, hid, og, marks, ln_attn_gain, ln_attn_bias, ln_mlp_gain, ln_mlp_bias, b_qkv, b_dense, b_out, b_in,
                rotary_tables(ordered(pos)), w_qkv, w_dense, w_in, w_out,
            )
            output, input_grad, win, wout, wqkv, wdense, *vectors = spread_out(
                final, vec, output, input_grad, marks, w_in.shape[1]
            )
            dgain, dbias, dmgain, dmbias, dbqkv, dbdense, dbin, dbout = vectors
            return (
                output[None], input_grad[None], dgain, dbias, dmgain, dmbias,
                wqkv, dbqkv, wdense, dbdense, win, dbin, wout, dbout,
            )
        b = lax.axis_index("blk")
        core = b % 2
        hi = b // n_low
        tables = rotary_tables(pos)

        own_runs = pos[::GROUP] // GROUP
        line_runs = jnp.concatenate(
            [own_runs] + [to_group(own_runs, by) for by in range(1, HEAD_GROUPS)]
        )
        key_runs = [line_runs]
        for bit in range(low_bits - 1, -1, -1):
            key_runs = key_runs + [flip(r, bit) for r in key_runs]
        n_query = line_runs.shape[0]
        rank = jnp.sum(line_runs[:, None] > line_runs[None, :], axis=1)
        slots = rank[None, :] == jnp.arange(n_query)[:, None]
        order = jnp.sum(jnp.where(slots, jnp.arange(n_query)[None, :], 0), axis=1)
        ordered = jnp.sum(jnp.where(slots, line_runs[None, :], 0), axis=1)
        tab = jnp.concatenate(key_runs + [order, ordered]).astype(jnp.int32)

        hid2 = jnp.concatenate([hid, flip(hid, 0)], axis=0)
        og2 = jnp.concatenate([og, flip(og, 0)], axis=0)

        msg = front(hid, og, again, abias, w_qkv, b_qkv[None], w_dense, tables)

        arrived = []
        for j in range(PER_GROUP):
            got = []
            for by in range(HEAD_GROUPS):
                part = lax.dynamic_index_in_dim(msg[j], lax.rem(hi + by, HEAD_GROUPS), 0, False)
                got.append(part if by == 0 else to_group(part, by))
            qd = jnp.stack([g[0] for g in got])
            pieces = [jnp.stack([g[1] for g in got])]
            for bit in range(low_bits - 1, -1, -1):
                pieces = pieces + [flip(piece, bit) for piece in pieces]
            arrived.append((qd, pieces))

        mlp_grads, bin_half, out_part, gn_part, normed2 = mlp(
            core[None].astype(jnp.int32), hid2, og2, again, abias, mgain, mbias, w_in, b_in[None], w_out
        )
        odqs, dkvs = [], []
        line = (HEAD_GROUPS, tokens, 128)
        for j in range(PER_GROUP):
            qd, pieces = arrived[j]
            runs = (HEAD_GROUPS * tokens // GROUP, GROUP, 128)
            odq, dkv = attention(tab, qd.reshape(runs), [p.reshape(runs) for p in pieces])
            odqs.append(odq.reshape(line))
            dkvs.append([d.reshape(line) for d in dkv])

        zero = jnp.zeros_like(bin_half)
        bins = jnp.where(
            core == 0, jnp.concatenate([bin_half, zero], 1), jnp.concatenate([zero, bin_half], 1)
        ).reshape(-1, width)
        half_ff = mlp_grads.shape[1]
        output, input_grad, vec, final = finish(
            mesh, odqs, dkvs, mlp_grads.reshape(2 * half_ff, width), out_part, gn_part, hid, og, og2,
            normed2, bins, again, mgain, w_qkv, w_dense, b_dense[None], b_out[None], tables,
        )
        win, wout, wqkv, wdense = expand(
            final, ((half_ff, True), (half_ff, False), (3 * width // 2, True), (width // 2, False))
        )
        return (
            output[None],
            input_grad[None],
            vec[0],
            vec[1],
            vec[2],
            vec[3],
            wqkv,
            vec[4:7].reshape(-1),
            wdense,
            vec[7],
            win,
            vec[8:].reshape(-1),
            wout,
            vec[7],
        )

    rows = P("seq", "blk", None)
    return jax.shard_map(
        on_device,
        mesh=mesh,
        in_specs=(rows, P("seq", "blk")) + (P(),) * 12 + (rows,),
        out_specs=(rows, rows) + (P(),) * 12,
        check_vma=False,
    )
```

```python
import functools

import jax
import jax.numpy as jnp
import numpy as np
from jax import lax
from jax.experimental import pallas as pl
from jax.experimental.pallas import tpu as pltpu
from jax.sharding import PartitionSpec as P

HEADS = 12
HEAD_DIM = 64
ROTARY = 16
GROUP = 128
HEAD_GROUPS = 4
PER_GROUP = HEADS // HEAD_GROUPS
NORM_EPSILON = 1e-05
ROTARY_BASE = 10000.0
MASKED = -1e30
VMEM_BYTES = 62 * 1024 * 1024

F32 = jnp.float32
BF16 = jnp.bfloat16
IN_VMEM = pl.BlockSpec(memory_space=pltpu.VMEM)
IN_SMEM = pl.BlockSpec(memory_space=pltpu.SMEM)


def mm(a, b):
    return lax.dot_general(a, b, (((1,), (0,)), ((), ())), preferred_element_type=F32)


def mm_nt(a, b):
    return lax.dot_general(a, b, (((1,), (1,)), ((), ())), preferred_element_type=F32)


def mm_tn(a, b):
    return lax.dot_general(a, b, (((0,), (0,)), ((), ())), preferred_element_type=F32)


def normalise(rows):
    centre = rows - jnp.mean(rows, axis=-1, keepdims=True)
    spread = jnp.mean(centre * centre, axis=-1, keepdims=True)
    scale = lax.rsqrt(spread + NORM_EPSILON)
    return centre * scale, scale


def norm_back(grad, xhat, scale, gain):
    eg = grad * gain
    return scale * (
        eg
        - jnp.mean(eg, axis=-1, keepdims=True)
        - xhat * jnp.mean(eg * xhat, axis=-1, keepdims=True)
    )


def params():
    return pltpu.CompilerParams(vmem_limit_bytes=VMEM_BYTES)


def front_kernel(hid, og, gain, bias, wqkv, bqkv, wdense, cosw, sina, sinb, msg):
    rows = hid[...].astype(F32)
    xhat, _ = normalise(rows)
    normed = (xhat * gain[...].astype(F32) + bias[...].astype(F32)).astype(BF16)
    mixed = mm(normed, wqkv[...]) + bqkv[...].astype(F32)
    datt = mm_nt(og[...], wdense[...])
    width = hid.shape[1]
    lane = lax.broadcasted_iota(jnp.int32, (rows.shape[0], 128), 1)
    low = lane < HEAD_DIM
    ca, sa, sb = cosw[...], sina[...], sinb[...]

    def turned(u):
        return u * ca + pltpu.roll(u, 120, 1) * sa + pltpu.roll(u, 8, 1) * sb

    for tile in range(HEADS // 2):
        at = tile * 128
        q = turned(mixed[:, at : at + 128]) * (HEAD_DIM**-0.5)
        k = turned(mixed[:, width + at : width + at + 128])
        v = mixed[:, 2 * width + at : 2 * width + at + 128]
        d = datt[:, at : at + 128]
        for part, (one, two) in enumerate(((q, d), (k, v))):
            for odd in range(2):
                head = 2 * tile + odd
                if odd == 0:
                    packed = jnp.where(low, one, pltpu.roll(two, 64, 1))
                else:
                    packed = jnp.where(low, pltpu.roll(one, 64, 1), two)
                msg[head % PER_GROUP, head // PER_GROUP, part] = packed.astype(BF16)


def front(hid, og, gain, bias, wqkv, bqkv, wdense, tables):
    rows = hid.shape[0]
    return pl.pallas_call(
        front_kernel,
        out_shape=jax.ShapeDtypeStruct((PER_GROUP, HEAD_GROUPS, 2, rows, 128), BF16),
        in_specs=[IN_VMEM] * 10,
        out_specs=IN_VMEM,
        compiler_params=params(),
        name="front",
    )(hid, og, gain, bias, wqkv, bqkv, wdense, *tables)


def mlp_kernel(
    core, hid, og, again, abias, mgain, mbias, win, bin_, wout,
    grads, bin_grad, out_part, gn_part, normed_attn, normed_s,
):
    step = pl.program_id(0)

    @pl.when(step == 0)
    def _():
        xhat, _ = normalise(hid[...].astype(F32))
        normed_s[...] = (xhat * mgain[...].astype(F32) + mbias[...].astype(F32)).astype(BF16)
        normed_attn[...] = (xhat * again[...].astype(F32) + abias[...].astype(F32)).astype(BF16)
        out_part[...] = jnp.zeros_like(out_part)
        gn_part[...] = jnp.zeros_like(gn_part)

    x = normed_s[...]
    w1 = win[...]
    w2 = wout[...]
    inner = mm(x, w1) + bin_[...].astype(F32)
    cdf = 0.5 * (1.0 + lax.erf(inner * (0.5**0.5)))
    act = (inner * cdf).astype(BF16)
    pdf = jnp.exp(-0.5 * inner * inner) * (0.5 * 2.0**0.5 * 3.141592653589793**-0.5)
    gact = mm_nt(og[...], w2)
    ginner = (gact * (cdf + inner * pdf)).astype(BF16)
    bin_grad[...] = jnp.sum(ginner.astype(F32), axis=0, keepdims=True)
    grads[0] = mm_tn(ginner, x).astype(BF16)
    grads[1] = mm_tn(act, og[...]).astype(BF16)
    out_part[...] += mm(act, w2)
    gn_part[...] += mm_nt(ginner, w1)


def mlp(core, hid, og, again, abias, mgain, mbias, win, b_in, wout):
    rows, width = hid.shape
    half = win.shape[1] // 2
    chunk = 512
    steps = half // chunk
    whole = lambda i, c: (0, 0)
    return pl.pallas_call(
        mlp_kernel,
        grid_spec=pltpu.PrefetchScalarGridSpec(
            num_scalar_prefetch=1,
            grid=(steps,),
            in_specs=[
                pl.BlockSpec((rows, width), whole),
                pl.BlockSpec((rows, width), whole),
                pl.BlockSpec((1, width), whole),
                pl.BlockSpec((1, width), whole),
                pl.BlockSpec((1, width), whole),
                pl.BlockSpec((1, width), whole),
                pl.BlockSpec((width, chunk), lambda i, c: (0, c[0] * steps + i)),
                pl.BlockSpec((1, chunk), lambda i, c: (0, c[0] * steps + i)),
                pl.BlockSpec((chunk, width), lambda i, c: (c[0] * steps + i, 0)),
            ],
            out_specs=[
                pl.BlockSpec((2, chunk, width), lambda i, c: (0, i, 0)),
                pl.BlockSpec((1, chunk), lambda i, c: (0, i)),
                pl.BlockSpec((rows, width), whole),
                pl.BlockSpec((rows, width), whole),
                pl.BlockSpec((rows, width), whole),
            ],
            scratch_shapes=[pltpu.VMEM((rows, width), BF16)],
        ),
        out_shape=[
            jax.ShapeDtypeStruct((2, half, width), BF16),
            jax.ShapeDtypeStruct((1, half), F32),
            jax.ShapeDtypeStruct((rows, width), F32),
            jax.ShapeDtypeStruct((rows, width), F32),
            jax.ShapeDtypeStruct((rows, width), BF16),
        ],
        compiler_params=params(),
        name="mlp",
    )(core, hid, og, again, abias, mgain, mbias, win, b_in, wout)


def attention_kernel(blocks, pieces, n_query, *refs):
    tab = refs[0]
    qd_ref = refs[1]
    kv_refs = refs[2 : 2 + pieces]
    odq_ref = refs[2 + pieces]
    dkv_refs = refs[3 + pieces : 3 + 2 * pieces]
    kvs, kvt, sbuf, acc = refs[3 + 2 * pieces :]
    kb_rows = blocks
    per_piece = kv_refs[0].shape[0]
    n_run = pieces * per_piece

    def group_rows(g):
        return pl.ds(pl.multiple_of(g * GROUP, GROUP), GROUP)

    for piece in range(pieces):

        def place(i, _, piece=piece):
            rows = group_rows(tab[piece * per_piece + i])
            blk = kv_refs[piece][i]
            kvs[rows, :] = blk
            kvt[:, rows] = blk.T
            acc[rows, :] = jnp.zeros((GROUP, 128), F32)
            return 0

        lax.fori_loop(0, per_piece, place, 0, unroll=4)

    lane = lax.broadcasted_iota(jnp.int32, (2 * GROUP, 128), 1)
    row = lax.broadcasted_iota(jnp.int32, (128, 2 * GROUP), 0)
    qcol = lax.broadcasted_iota(jnp.int32, (1, 2 * GROUP), 1)
    krow = lax.broadcasted_iota(jnp.int32, (kb_rows, 1), 0)

    def pair_step(pair, _):
        i0 = tab[n_run + 2 * pair]
        i1 = tab[n_run + 2 * pair + 1]
        g0 = tab[n_run + n_query + 2 * pair]
        g1 = tab[n_run + n_query + 2 * pair + 1]
        qd = jnp.concatenate([qd_ref[i0], qd_ref[i1]], axis=0)
        zero = jnp.zeros_like(qd)
        w_keys = jnp.concatenate(
            [jnp.where(lane < HEAD_DIM, qd, zero), jnp.where(lane >= HEAD_DIM, qd, zero)], axis=0
        )
        qdt = qd.T
        zero_t = jnp.zeros_like(qdt)
        w_score = jnp.where(row < HEAD_DIM, qdt, zero_t)
        w_dprob = jnp.where(row >= HEAD_DIM, qdt, zero_t)
        qpos = jnp.where(qcol < GROUP, g0 * GROUP + qcol, (g1 - 1) * GROUP + qcol)
        n_full = (g0 * GROUP) // kb_rows
        n_all = (g1 * GROUP) // kb_rows + 1

        def block_rows(kb):
            return pl.ds(pl.multiple_of(kb * kb_rows, kb_rows), kb_rows)

        def score_step(kb, top, masked):
            rows = block_rows(kb)
            s = mm(kvs[rows, :], w_score)
            if masked:
                s = jnp.where(kb * kb_rows + krow <= qpos, s, MASKED)
            sbuf[rows, :] = s
            return jnp.maximum(top, jnp.max(s.reshape(kb_rows // 8, 8, 2 * GROUP), axis=0))

        top = jnp.full((8, 2 * GROUP), MASKED, F32)
        top = lax.fori_loop(0, n_full, lambda kb, c: score_step(kb, c, False), top)
        top = lax.fori_loop(n_full, n_all, lambda kb, c: score_step(kb, c, True), top)
        top = jnp.max(top, axis=0, keepdims=True)

        def value_step(kb, carry):
            total, out = carry
            rows = block_rows(kb)
            e = jnp.exp(sbuf[rows, :] - top)
            sbuf[rows, :] = e
            total = total + jnp.sum(e.reshape(kb_rows // 8, 8, 2 * GROUP), axis=0)
            return total, out + mm(kvt[HEAD_DIM:128, rows], e.astype(BF16))

        total, out = lax.fori_loop(
            0,
            n_all,
            value_step,
            (jnp.zeros((8, 2 * GROUP), F32), jnp.zeros((HEAD_DIM, 2 * GROUP), F32)),
        )
        inv = 1.0 / jnp.sum(total, axis=0, keepdims=True)
        out = out * inv
        delta = jnp.sum(out * qdt[HEAD_DIM:128, :].astype(F32), axis=0, keepdims=True)

        def grad_step(kb, dq):
            rows = block_rows(kb)
            p = sbuf[rows, :] * inv
            dp = mm(kvs[rows, :], w_dprob)
            ds = (p * (dp - delta)).astype(BF16)
            acc[rows, :] += mm(jnp.concatenate([ds, p.astype(BF16)], axis=1), w_keys)
            return dq + mm(kvt[0:HEAD_DIM, rows], ds)

        dq = lax.fori_loop(0, n_all, grad_step, jnp.zeros((HEAD_DIM, 2 * GROUP), F32))
        odq = jnp.concatenate([out, dq * (HEAD_DIM**-0.5)], axis=0).astype(BF16).T
        odq_ref[i0] = odq[:GROUP]
        odq_ref[i1] = odq[GROUP:]
        return 0

    lax.fori_loop(0, n_query // 2, pair_step, 0)

    for piece in range(pieces):

        def give(i, _, piece=piece):
            dkv_refs[piece][i] = acc[group_rows(tab[piece * per_piece + i]), :].astype(BF16)
            return 0

        lax.fori_loop(0, per_piece, give, 0, unroll=4)


def attention(tab, qd, kvs):
    pieces = len(kvs)
    n_query = qd.shape[0]
    n_key = pieces * kvs[0].shape[0] * GROUP
    blocks = 1024
    run = jax.ShapeDtypeStruct(kvs[0].shape, BF16)
    outs = pl.pallas_call(
        functools.partial(attention_kernel, blocks, pieces, n_query),
        out_shape=[jax.ShapeDtypeStruct(qd.shape, BF16)] + [run] * pieces,
        in_specs=[IN_SMEM] + [IN_VMEM] * (1 + pieces),
        out_specs=[IN_VMEM] * (1 + pieces),
        scratch_shapes=[
            pltpu.VMEM((n_key, 128), BF16),
            pltpu.VMEM((128, n_key), BF16),
            pltpu.VMEM((n_key, 2 * GROUP), F32),
            pltpu.VMEM((n_key, 128), F32),
        ],
        compiler_params=params(),
        name="attention",
    )(tab, qd, *kvs)
    return outs[0], outs[1:]


class Place:
    def __init__(self, n_seq, n_blk):
        self.n_seq, self.n_blk = n_seq, n_blk
        self.n_low = n_blk // HEAD_GROUPS
        self.n_rest = n_blk // 4
        self.s = lax.axis_index("seq")
        self.b = lax.axis_index("blk")
        self.core = self.b % 2
        self.x = (self.b // 2) % 2
        self.rest = self.b // 4
        self.hi = self.b // self.n_low

    def flip(self, bit):
        step = 1 << bit
        return (self.s, self.b + step - 2 * step * ((self.b // step) % 2))

    def to_seq(self):
        return ((self.s + 1) % self.n_seq, self.b)

    def to_rest(self, by):
        return (self.s, ((self.rest + by) % self.n_rest) * 4 + self.b % 4)

    def to_group(self, by):
        return (self.s, ((self.hi + by) % HEAD_GROUPS) * self.n_low + self.b % self.n_low)

    def partners(self):
        found = [self.flip(bit) for bit in range(self.n_low.bit_length() - 1)]
        found += [self.to_seq()]
        found += [self.to_rest(by) for by in range(1, self.n_rest)]
        if self.n_low != 4:
            found += [self.to_group(by) for by in range(1, HEAD_GROUPS)]
        return found

    def meet(self):
        barrier = pltpu.get_barrier_semaphore()
        partners = self.partners()
        for device in partners:
            pl.semaphore_signal(
                barrier, inc=1, device_id=device, device_id_type=pl.DeviceIdType.MESH
            )
        pl.semaphore_wait(barrier, len(partners))


class Wires:
    def __init__(self, sends, recvs):
        self.sends, self.recvs, self.used = sends, recvs, 0

    def copy(self, src, dst, device):
        at = self.used
        self.used += 1
        return pltpu.make_async_remote_copy(
            src_ref=src,
            dst_ref=dst,
            send_sem=self.sends.at[at],
            recv_sem=self.recvs.at[at],
            device_id=device,
            device_id_type=pl.DeviceIdType.MESH,
        )


def add_rows(dst, dst_at, others, count, out=None, out_at=0, lanes=slice(None), got_lanes=slice(None)):
    block = 16
    for size in (96, 64, 48, 32):
        if count % size == 0:
            block = size
            break
    out = dst if out is None else out

    def step(i, _):
        total = dst[pl.ds(pl.multiple_of(dst_at + i * block, 16), block), lanes].astype(F32)
        for ref, start in others:
            rows = pl.ds(pl.multiple_of(start + i * block, 16), block)
            total = total + ref[rows, got_lanes].astype(F32)
        out[pl.ds(pl.multiple_of(out_at + i * block, 16), block), lanes] = total.astype(BF16)
        return 0

    lax.fori_loop(0, count // block, step, 0)


def unit_copies(n_rest):
    return 2 * (2 + n_rest - 1) + 1


class Unit:
    def __init__(self, place, wires, data, base, size, order, got1, got2, got3, out, final, final_base, local):
        pairs = {"x": (place.x, place.flip(1)), "y": (place.s, place.to_seq())}
        (self.bit1, self.dev1), (self.bit2, self.dev2) = pairs[order[0]], pairs[order[1]]
        self.place, self.data, self.out = place, data, out
        self.base, self.size = base, size
        self.h, self.q = size // 2, size // 4
        n = place.n_rest
        self.cuts = 1 if (self.q // n) % 16 == 0 else 2
        self.e = self.q * self.cuts // n
        self.w = data.shape[1] // self.cuts
        self.base1 = base + self.bit1 * self.h
        self.base2 = self.base1 + self.bit2 * self.q
        self.got1, self.got2, self.got3 = got1, got2, got3
        self.fetch = None
        if local is not None:
            kept = pl.ds(pl.multiple_of(self.base1, 16), self.h)
            self.fetch = pltpu.make_async_copy(data.at[kept], out.at[kept], local)
        z = place.rest

        def cell(ref, start, index):
            at = pl.multiple_of(start + (index // self.cuts) * self.e, 16)
            if self.cuts == 1:
                return ref.at[pl.ds(at, self.e)]
            return ref.at[
                pl.ds(at, self.e), pl.ds(pl.multiple_of((index % self.cuts) * self.w, 128), self.w)
            ]

        def landing(by):
            slot = pl.ds((by - 1) * self.e, self.e)
            return got3.at[slot] if self.cuts == 1 else got3.at[slot, pl.ds(0, self.w)]

        def rows(ref, start, count):
            return ref.at[pl.ds(pl.multiple_of(start, 16), count)]

        self.rs1 = [wires.copy(rows(data, base + (1 - self.bit1) * self.h, self.h), got1, self.dev1)]
        self.rs2 = [wires.copy(rows(got1, (1 - self.bit2) * self.q, self.q), got2, self.dev2)]
        self.rs3 = [
            wires.copy(cell(got2, 0, (z + by) % n), landing(by), place.to_rest(by))
            for by in range(1, n)
        ]
        self.ag3 = [
            wires.copy(cell(out, self.base2, z), cell(out, self.base2, z), place.to_rest(by))
            for by in range(1, n)
        ]
        self.ag2 = [wires.copy(rows(out, self.base2, self.q), rows(out, self.base2, self.q), self.dev2)]
        self.ag1 = [wires.copy(rows(out, self.base1, self.h), rows(out, self.base1, self.h), self.dev1)]
        self.agc = [
            wires.copy(
                rows(out, base, size),
                final.at[place.core, pl.ds(final_base, size)],
                place.flip(0),
            )
        ]
        self.sent = []

    def start(self, copies):
        for copy in copies:
            copy.start()
        self.sent = self.sent + copies

    def arrive(self, copies):
        for copy in copies:
            copy.wait_recv()

    def stage0(self):
        self.start(self.rs1)
        if self.fetch is not None:
            self.fetch.start()

    def stage1(self):
        self.arrive(self.rs1)
        for copy in self.rs1:
            copy.wait_send()
        self.sent = [copy for copy in self.sent if not any(copy is gone for gone in self.rs1)]
        if self.fetch is not None:
            self.fetch.wait()
        add_rows(self.got1, 0, [(self.data if self.fetch is None else self.out, self.base1)], self.h)
        self.start(self.rs2)

    def stage2(self):
        self.arrive(self.rs2)
        add_rows(self.got2, 0, [(self.got1, self.bit2 * self.q)], self.q)
        self.start(self.rs3)

    def stage3(self):
        self.arrive(self.rs3)
        others = [(self.got3, k * self.e) for k in range(self.place.n_rest - 1)]
        z = self.place.rest
        at = (z // self.cuts) * self.e
        lanes = got_lanes = slice(None)
        if self.cuts > 1:
            lanes = pl.ds(pl.multiple_of((z % self.cuts) * self.w, 128), self.w)
            got_lanes = pl.ds(0, self.w)
        add_rows(self.got2, at, others, self.e, self.out, self.base2 + at, lanes, got_lanes)
        self.start(self.ag3)

    def stage4(self):
        self.arrive(self.ag3)
        self.start(self.ag2)

    def stage5(self):
        self.arrive(self.ag2)
        self.start(self.ag1)

    def stage6(self):
        self.arrive(self.ag1)
        self.start(self.agc)

    def finish(self):
        self.arrive(self.agc)
        for copy in self.sent:
            copy.wait_send()


def tail_compute(
    odq, dkv, hi, hid, og, again, mgain, wqkv, wdense, bdense, bout, mout, gnm,
    cosw, sina, sinb, output, input_grad, send, small,
):
    rows = hid[...].astype(F32)
    count, width = rows.shape
    lane = lax.broadcasted_iota(jnp.int32, (count, 128), 1)
    low = lane < HEAD_DIM
    ca, sa, sb = cosw[...], sina[...], sinb[...]

    def turned_back(g):
        return g * ca - pltpu.roll(g, 120, 1) * sa - pltpu.roll(g, 8, 1) * sb

    def head(ref, a):
        at = (a // PER_GROUP - hi + HEAD_GROUPS) % HEAD_GROUPS
        return ref[a % PER_GROUP, at].astype(F32)

    outs, grads = [], [[], [], []]
    for tile in range(HEADS // 2):
        one, two = head(odq, 2 * tile), head(odq, 2 * tile + 1)
        outs.append(jnp.where(low, one, pltpu.roll(two, 64, 1)).astype(BF16))
        grads[0].append(turned_back(jnp.where(low, pltpu.roll(one, 64, 1), two)).astype(BF16))
        one, two = head(dkv, 2 * tile), head(dkv, 2 * tile + 1)
        grads[1].append(
            turned_back(jnp.where(low, one, pltpu.roll(two, 64, 1))).astype(BF16)
        )
        grads[2].append(jnp.where(low, pltpu.roll(one, 64, 1), two).astype(BF16))
    att = jnp.concatenate(outs, axis=1)
    dmixed = jnp.concatenate(grads[0] + grads[1] + grads[2], axis=1)
    half_m, half_a = dmixed.shape[1] // 2, width // 2
    for side in range(2):
        send[side, :, :half_m] = dmixed[:, side * half_m : (side + 1) * half_m]
        send[side, :, half_m:] = att[:, side * half_a : (side + 1) * half_a]
    branch = mm(att, wdense[...]) + bdense[...].astype(F32)
    output[...] = (rows + branch + (mout + bout[...].astype(F32))).astype(BF16)
    gna = mm_nt(dmixed, wqkv[...])
    xhat, scale = normalise(rows)
    cot = og[...].astype(F32)
    input_grad[...] = (
        cot
        + norm_back(gna, xhat, scale, again[...].astype(F32))
        + norm_back(gnm, xhat, scale, mgain[...].astype(F32))
    ).astype(BF16)
    small[0:1, :] = jnp.sum(gna * xhat, axis=0, keepdims=True)
    small[1:2, :] = jnp.sum(gna, axis=0, keepdims=True)
    small[2:3, :] = jnp.sum(gnm * xhat, axis=0, keepdims=True)
    small[3:4, :] = jnp.sum(gnm, axis=0, keepdims=True)
    for part in range(3):
        cols = dmixed[:, part * width : (part + 1) * width].astype(F32)
        small[4 + part : 5 + part, :] = jnp.sum(cols, axis=0, keepdims=True)
    small[7:8, :] = jnp.sum(cot, axis=0, keepdims=True)


def weight_compute(own, other, normed, og, grads):
    half_m = own.shape[1] * 3 // 4
    both = jnp.concatenate([own, other], axis=0)
    grads[0:half_m, :] = mm_tn(both[:, :half_m], normed[...]).astype(BF16)
    grads[half_m:, :] = mm_tn(both[:, half_m:], og[...]).astype(BF16)


def finish_kernel(
    n_seq, n_blk, units1, units2, pieces,
    odq0, odq1, odq2, *refs,
):
    dkvs = [refs[j * pieces : (j + 1) * pieces] for j in range(PER_GROUP)]
    (
        grads1, out_part, gn_part, hid, og, og2, normed2, bins, again, mgain, wqkv, wdense, bdense, bout,
        cosw, sina, sinb,
        output, input_grad, small_out, final,
        odq_all, dkv_all, dkv_got, mout_got, gn_got, send, other, grads2, small, small_got,
        got1, got2, got3, out1, out2, sends, recvs, local_sem,
    ) = refs[PER_GROUP * pieces :]
    place = Place(n_seq, n_blk)
    wires = Wires(sends, recvs)
    odqs = (odq0, odq1, odq2)
    tokens, width = hid.shape
    n_rest = place.n_rest
    rows1 = grads1.shape[0]
    place.meet()
    sent = []

    def go(copy):
        copy.start()
        sent.append(copy)
        return copy

    mout_copy = go(wires.copy(out_part.at[pl.ds(tokens, tokens)], mout_got, place.flip(0)))
    gn_copy = go(wires.copy(gn_part.at[pl.ds(tokens, tokens)], gn_got, place.flip(0)))
    low_bits = place.n_low.bit_length() - 1
    stage_copies = []
    for j in range(PER_GROUP):
        half = pieces // 2
        stage_copies.append([
            go(wires.copy(dkvs[j][half + i], dkv_got.at[j, i], place.flip(0))) for i in range(half)
        ])
    home = []
    for j in range(PER_GROUP):
        for by in range(1, HEAD_GROUPS):
            home.append(go(wires.copy(odqs[j].at[by], odq_all.at[j, by], place.to_group(HEAD_GROUPS - by))))
    units = []
    at = 0
    for base, size, order in units1:
        units.append(Unit(
            place, wires, grads1, base, size, order,
            got1.at[pl.ds(at // 2, size // 2)], got2.at[pl.ds(at // 4, size // 4)],
            got3.at[pl.ds(at // 2, size // 2)], out1, final, base, local_sem.at[2 + len(units)],
        ))
        at += size
    units_b = []
    for base, size, order in units2:
        units_b.append(Unit(
            place, wires, grads2, base, size, order,
            got1.at[pl.ds(at // 2, size // 2)], got2.at[pl.ds(at // 4, size // 4)],
            got3.at[pl.ds(at // 2, size // 2)], out2, final, rows1 + base, None,
        ))
        at += size
    for unit in units:
        unit.stage0()

    slot = 0
    half = pieces // 2
    for bit in range(low_bits):
        after = slot + half
        for j in range(PER_GROUP):
            for copy in stage_copies[j]:
                copy.wait_recv()
            for i in range(half):
                mine = dkvs[j][i][...] if bit == 0 else dkv_got[j, slot - 2 * half + i]
                dkv_got[j, slot + i] = (mine.astype(F32) + dkv_got[j, slot + i].astype(F32)).astype(BF16)
            if half > 1:
                stage_copies[j] = [
                    go(wires.copy(dkv_got.at[j, slot + half // 2 + i], dkv_got.at[j, after + i], place.flip(bit + 1)))
                    for i in range(half // 2)
                ]
            else:
                for by in range(1, HEAD_GROUPS):
                    home.append(go(wires.copy(
                        dkv_got.at[j, slot, by], dkv_all.at[j, by], place.to_group(HEAD_GROUPS - by)
                    )))
                dkv_all[j, 0] = dkv_got[j, slot, 0]
        slot = after
        half //= 2
    for j in range(PER_GROUP):
        odq_all[j, 0] = odqs[j][0]
    for unit in units:
        unit.stage1()
    for copy in home:
        copy.wait_recv()
    mout_copy.wait_recv()
    gn_copy.wait_recv()
    mout = out_part[0:tokens, :] + mout_got[...]
    gnm = gn_part[0:tokens, :] + gn_got[...]
    tail_compute(
        odq_all, dkv_all, place.hi, hid, og, again, mgain, wqkv, wdense, bdense, bout, mout, gnm,
        cosw, sina, sinb, output, input_grad, send, small,
    )
    other_copy = go(wires.copy(send.at[1 - place.core], other, place.flip(0)))
    for unit in units:
        unit.stage2()
    other_copy.wait_recv()
    weight_compute(send[place.core], other[...], normed2, og2, grads2)
    for unit in units_b:
        unit.stage0()
    small[8:, :] = bins[...]
    for unit in units:
        unit.stage3()
    for unit in units_b:
        unit.stage1()
    order = [[place.flip(0)], [place.flip(1)], [place.to_seq()], [place.to_rest(by) for by in range(1, n_rest)]]
    slot = 0
    for devices in order:
        copies = [wires.copy(small, small_got.at[slot + i], device) for i, device in enumerate(devices)]
        for copy in copies:
            copy.start()
        for copy in copies:
            copy.wait()
        total = small[...]
        for i in range(len(devices)):
            total = total + small_got[slot + i]
        small[...] = total
        slot += len(devices)
    small_out[...] = small[...]
    for unit in units:
        unit.stage4()
    for unit in units_b:
        unit.stage2()
    for unit in units:
        unit.stage5()
    for unit in units_b:
        unit.stage3()
    for unit in units:
        unit.stage6()
    for unit in units_b:
        unit.stage4()
    for unit in units_b:
        unit.stage5()
    for unit in units_b:
        unit.stage6()
    keep1 = pltpu.make_async_copy(out1, final.at[place.core, pl.ds(0, rows1)], local_sem.at[0])
    keep2 = pltpu.make_async_copy(out2, final.at[place.core, pl.ds(rows1, grads2.shape[0])], local_sem.at[1])
    keep1.start()
    keep2.start()
    for unit in units + units_b:
        unit.finish()
    for copy in sent:
        copy.wait_send()
    keep1.wait()
    keep2.wait()


def finish(mesh, odqs, dkvs, grads1, out_part, gn_part, hid, og, og2, normed2, bins, again, mgain, wqkv, wdense, bdense, bout, tables):
    n_seq, n_blk = mesh.shape["seq"], mesh.shape["blk"]
    n_rest = n_blk // 4
    tokens, width = hid.shape
    pieces = len(dkvs[0])
    rows1, rows2 = grads1.shape[0], 2 * width
    fine = (rows1 // 4) % (4 * n_rest * 16) == 0
    parts = 4 if fine else 2
    units1 = [(i * rows1 // parts, rows1 // parts, "xy" if 2 * i < parts else "yx") for i in range(parts)]
    parts = 2 if fine else 1
    units2 = [(i * rows2 // parts, rows2 // parts, "xy" if 2 * i < parts else "yx") for i in range(parts)]
    total = rows1 + rows2
    copies = (len(units1) + len(units2)) * unit_copies(n_rest)
    copies += 3 + PER_GROUP * (2 * (HEAD_GROUPS - 1) + pieces - 1) + 3 + n_rest - 1
    line = (HEAD_GROUPS, tokens, 128)
    n_small = 8 + bins.shape[0]
    inputs = list(odqs) + [p for d in dkvs for p in d] + [
        grads1, out_part, gn_part, hid, og, og2, normed2, bins, again, mgain, wqkv, wdense, bdense, bout, *tables,
    ]
    return pl.pallas_call(
        functools.partial(finish_kernel, n_seq, n_blk, units1, units2, pieces),
        out_shape=[
            jax.ShapeDtypeStruct((tokens, width), BF16),
            jax.ShapeDtypeStruct((tokens, width), BF16),
            jax.ShapeDtypeStruct((n_small, width), F32),
            jax.ShapeDtypeStruct((2, total, width), BF16),
        ],
        in_specs=[pl.BlockSpec(memory_space=pl.ANY) if v is grads1 else IN_VMEM for v in inputs],
        out_specs=[IN_VMEM] * 3 + [pl.BlockSpec(memory_space=pl.ANY)],
        scratch_shapes=[
            pltpu.VMEM((PER_GROUP,) + line, BF16),
            pltpu.VMEM((PER_GROUP,) + line, BF16),
            pltpu.VMEM((PER_GROUP, pieces - 1) + line, BF16),
            pltpu.VMEM((tokens, width), F32),
            pltpu.VMEM((tokens, width), F32),
            pltpu.VMEM((2, tokens, 2 * width), BF16),
            pltpu.VMEM((tokens, 2 * width), BF16),
            pltpu.VMEM((rows2, width), BF16),
            pltpu.VMEM((n_small, width), F32),
            pltpu.VMEM((3 + n_rest - 1, n_small, width), F32),
            pltpu.VMEM((total // 2, width), BF16),
            pltpu.VMEM((total // 4, width), BF16),
            pltpu.VMEM((total // 2, width), BF16),
            pltpu.VMEM((rows1, width), BF16),
            pltpu.VMEM((rows2, width), BF16),
            pltpu.SemaphoreType.DMA((copies,)),
            pltpu.SemaphoreType.DMA((copies,)),
            pltpu.SemaphoreType.DMA((2 + len(units1),)),
        ],
        compiler_params=pltpu.CompilerParams(
            vmem_limit_bytes=VMEM_BYTES, collective_id=1, has_side_effects=True
        ),
        name="finish",
    )(*inputs)


def expand_kernel(marks, block, *outs):
    step = pl.program_id(0)
    for out, (first, last, turn) in zip(outs, marks):

        @pl.when((step >= first) & (step < last))
        def _(out=out, turn=turn):
            rows = block[0].astype(F32)
            out[...] = rows.T if turn else rows


def expand(final, sizes):
    width = final.shape[2]
    block = width // 2
    marks, specs, shapes, firsts = [], [], [], []
    first = offset = 0
    for rows, turn in sizes:
        each = rows // block
        marks.append((first, first + 2 * each, turn))
        firsts.append((first, each, offset))

        def at(i, first=first, count=2 * each):
            return jnp.clip(i - first, 0, count - 1)

        if turn:
            specs.append(pl.BlockSpec((width, block), lambda i, at=at: (0, at(i))))
            shapes.append(jax.ShapeDtypeStruct((width, 2 * rows), F32))
        else:
            specs.append(pl.BlockSpec((block, width), lambda i, at=at: (at(i), 0)))
            shapes.append(jax.ShapeDtypeStruct((2 * rows, width), F32))
        first += 2 * each
        offset += each

    def source(i):
        core, row = 0, 0
        for begin, each, offset in firsts:
            here = (i >= begin) & (i < begin + 2 * each)
            core = jnp.where(here, (i - begin) // each, core)
            row = jnp.where(here, offset + (i - begin) % each, row)
        return (core, row, 0)

    return pl.pallas_call(
        functools.partial(expand_kernel, marks),
        grid=(first,),
        in_specs=[pl.BlockSpec((1, block, width), source)],
        out_specs=specs,
        out_shape=shapes,
        compiler_params=params(),
        name="expand",
    )(final)


KEY_BLOCK = 2048


def half_rows(d):
    return pl.ds(pl.multiple_of(d * GROUP, GROUP), GROUP)


class Attention:
    def __init__(self, lines, devices, flags, kvl, kvtl, kvth, ksel, kselt, bias, sb, acc):
        self.lines, self.devices, self.flags = lines, devices, flags
        self.kvl, self.kvtl, self.kvth = kvl, kvtl, kvth
        self.ksel, self.kselt, self.bias, self.sb, self.acc = ksel, kselt, bias, sb, acc
        self.n = devices * GROUP
        self.block = min(KEY_BLOCK, self.n)

    def prepare(self, pieces):
        for p, ref in enumerate(pieces):

            def step(r, _, p=p, ref=ref):
                rows = half_rows(p * self.lines + r)
                low, high = ref[r, 0:GROUP, :], ref[r, GROUP : 2 * GROUP, :]
                self.kvl[rows, :] = low
                self.kvtl[:, rows] = low.T
                self.kvth[:, rows] = high.T
                self.acc[0, rows, :] = jnp.zeros((GROUP, 128), F32)
                self.acc[1, rows, :] = jnp.zeros((GROUP, 128), F32)
                return 0

            lax.fori_loop(0, self.lines, step, 0, unroll=self.lines)

    def select(self, i, slot, pieces):
        mine = self.flags[0, i]

        def choose(less, low, high):
            cut = (GROUP // 16, 16, 128)
            return jnp.where(less, low.reshape(cut), high.reshape(cut)).reshape(GROUP, 128)

        for p, ref in enumerate(pieces):

            def step(r, _, p=p, ref=ref):
                d = p * self.lines + r
                rows = half_rows(d)
                theirs = self.flags[p, r]
                less = jnp.broadcast_to((theirs < mine)[None], (GROUP // 16, 16, 128))
                self.ksel[slot, rows, :] = choose(less, ref[r, 0:GROUP, :], ref[r, GROUP : 2 * GROUP, :])
                self.kselt[slot, :, rows] = choose(less, self.kvtl[:, rows], self.kvth[:, rows])
                a, b = theirs.astype(F32)[0:8], mine.astype(F32)[0:8]
                self.bias[slot, d] = jnp.concatenate(
                    [jnp.where(a < b, 0.0, MASKED), jnp.where(a > b, 0.0, MASKED)], axis=1
                )
                return 0

            lax.fori_loop(0, self.lines, step, 0)

    def pair(self, first, qd_ref, pieces, odq_ref):
        own_kv = pieces[0]
        n, block = self.n, self.block
        steps = n // block
        per = block // GROUP
        wide = 2 * GROUP
        lane = lax.broadcasted_iota(jnp.int32, (GROUP, 128), 1)
        row = lax.broadcasted_iota(jnp.int32, (128, wide), 0)
        krow = lax.broadcasted_iota(jnp.int32, (wide, 1), 0)
        qcol = lax.broadcasted_iota(jnp.int32, (1, wide), 1)
        diagonal = (krow <= qcol) & ((krow < GROUP) == (qcol < GROUP))
        sb, ksel, kselt, kvl, kvtl, kvth = self.sb, self.ksel, self.kselt, self.kvl, self.kvtl, self.kvth

        def split(q):
            zero = jnp.zeros_like(q)
            return jnp.where(lane < HEAD_DIM, q, zero), jnp.where(lane >= HEAD_DIM, q, zero)

        w_score, w_dprob, w_keys, doutt, kvd, kvdt = [], [], [], [], [], []
        for slot in range(2):
            i = first + slot
            self.select(i, slot, pieces)
            qd = qd_ref[i]
            qdt = qd.T
            zero = jnp.zeros_like(qdt)
            w_score.append(jnp.where(row < HEAD_DIM, qdt, zero))
            w_dprob.append(jnp.where(row >= HEAD_DIM, qdt, zero))
            doutt.append(qdt[HEAD_DIM:128, :].astype(F32))
            w_keys.append([split(qd[at : at + GROUP]) for at in (0, GROUP)])
            kvd.append(own_kv[i])
            rows = half_rows(i)
            kvdt.append(jnp.concatenate([kvtl[:, rows], kvth[:, rows]], axis=1))

        def high(a, b):
            return jnp.concatenate([a[:, GROUP:], b[:, GROUP:]], axis=1)

        w_score.append(high(*w_score))
        w_dprob.append(high(*w_dprob))

        def key_rows(k):
            return pl.ds(pl.multiple_of(k * block, block), block)

        def keys(part, rows):
            return kvl[rows, :] if part == 2 else ksel[part, rows, :]

        def keys_t(part, rows, start, stop):
            return kvtl[start:stop, rows] if part == 2 else kselt[part, start:stop, rows]

        def top8(s):
            return jnp.max(s.reshape(s.shape[0] // 8, 8, wide), axis=0)

        def sum8(s):
            return jnp.sum(s.reshape(s.shape[0] // 8, 8, wide), axis=0)

        own = pl.ds(n, wide)
        tops = []
        for part in range(3):

            def score(k, top, part=part):
                rows = key_rows(k)
                s = mm(keys(part, rows), w_score[part])
                if part < 2:
                    bias = self.bias[part, pl.ds(k * per, per)]
                    s = (s.reshape(per, GROUP // 8, 8, wide) + bias[:, None]).reshape(block, wide)
                sb[part, rows, :] = s
                return jnp.maximum(top, top8(s))

            top = jnp.full((8, wide), MASKED, F32)
            if part < 2:
                s = jnp.where(diagonal, mm(kvd[part], w_score[part]), MASKED)
                sb[part, own, :] = s
                top = top8(s)
            top = lax.fori_loop(0, steps, score, top)
            tops.append(jnp.max(top, axis=0, keepdims=True))

        def join(base, extra, slot, combine):
            at = slot * GROUP
            return jnp.concatenate(
                [base[:, :GROUP], combine(base[:, GROUP:], extra[:, at : at + GROUP])], axis=1
            )

        tops = [join(tops[slot], tops[2], slot, jnp.maximum) for slot in range(2)]
        tops.append(high(*tops))
        totals, outs = [], []
        for part in range(3):

            def value(k, carry, part=part):
                total, out = carry
                rows = key_rows(k)
                e = jnp.exp(sb[part, rows, :] - tops[part])
                sb[part, rows, :] = e
                return total + sum8(e), out + mm(keys_t(part, rows, HEAD_DIM, 128), e.astype(BF16))

            total, out = jnp.zeros((8, wide), F32), jnp.zeros((HEAD_DIM, wide), F32)
            if part < 2:
                e = jnp.exp(sb[part, own, :] - tops[part])
                sb[part, own, :] = e
                total, out = sum8(e), mm(kvdt[part][HEAD_DIM:128], e.astype(BF16))
            total, out = lax.fori_loop(0, steps, value, (total, out))
            totals.append(jnp.sum(total, axis=0, keepdims=True))
            outs.append(out)
        yield
        add = lambda a, b: a + b
        invs = [1.0 / join(totals[slot], totals[2], slot, add) for slot in range(2)]
        outs = [join(outs[slot], outs[2], slot, add) * invs[slot] for slot in range(2)]
        deltas = [jnp.sum(outs[slot] * doutt[slot], axis=0, keepdims=True) for slot in range(2)]
        invs.append(high(*invs))
        deltas.append(high(*deltas))
        dqs = []
        for part in range(3):
            if part < 2:
                weights = [
                    (slice(at * GROUP, (at + 1) * GROUP), at, jnp.concatenate(w_keys[part][at], axis=0))
                    for at in range(2)
                ]
            else:
                (qa, da), (qb, db) = w_keys[0][1], w_keys[1][1]
                weights = [(slice(0, wide), 0, jnp.concatenate([qa, qb, da, db], axis=0))]

            def grad(k, dq, part=part, weights=weights):
                rows = key_rows(k)
                p = sb[part, rows, :] * invs[part]
                dp = mm(keys(part, rows), w_dprob[part])
                ds = (p * (dp - deltas[part])).astype(BF16)
                p = p.astype(BF16)
                for cols, side, w in weights:
                    self.acc[side, rows, :] += mm(jnp.concatenate([ds[:, cols], p[:, cols]], axis=1), w)
                return dq + mm(keys_t(part, rows, 0, HEAD_DIM), ds)

            dq = jnp.zeros((HEAD_DIM, wide), F32)
            if part < 2:
                p = sb[part, own, :] * invs[part]
                dp = mm(kvd[part], w_dprob[part])
                ds = (p * (dp - deltas[part])).astype(BF16)
                p = p.astype(BF16)
                rows = half_rows(first + part)
                for cols, side, w in weights:
                    pd = jnp.concatenate([ds[cols, cols], p[cols, cols]], axis=1)
                    self.acc[side, rows, :] += mm(pd, w)
                dq = mm(kvdt[part][0:HEAD_DIM], ds)
            dqs.append(lax.fori_loop(0, steps, grad, dq))
        for slot in range(2):
            dq = join(dqs[slot], dqs[2], slot, add) * (HEAD_DIM**-0.5)
            odq_ref[first + slot] = jnp.concatenate([outs[slot], dq], axis=0).astype(BF16).T

    def give(self, dkv_refs):
        for p, ref in enumerate(dkv_refs):

            def step(r, _, p=p, ref=ref):
                rows = half_rows(p * self.lines + r)
                ref[r, 0:GROUP, :] = self.acc[0, rows, :].astype(BF16)
                ref[r, GROUP : 2 * GROUP, :] = self.acc[1, rows, :].astype(BF16)
                return 0

            lax.fori_loop(0, self.lines, step, 0, unroll=self.lines)


def attention_scratch(lines, devices):
    n = devices * GROUP
    return [
        pltpu.VMEM((n, 128), BF16),
        pltpu.VMEM((128, n), BF16),
        pltpu.VMEM((128, n), BF16),
        pltpu.VMEM((2, n, 128), BF16),
        pltpu.VMEM((2, 128, n), BF16),
        pltpu.VMEM((2, devices, 8, 2 * GROUP), F32),
        pltpu.VMEM((3, n + 2 * GROUP, 2 * GROUP), F32),
        pltpu.VMEM((2, n, 128), F32),
    ]


class Chain:
    def __init__(self, place, wires, data, base, size, order, got, final, final_base, free, keep):
        pairs = {
            "x": (place.x, place.flip(1)),
            "y": (place.s, place.to_seq()),
            "m": (place.rest % 2, place.flip(2)),
            "f": (place.rest // 2, place.flip(3)),
        }
        self.data, self.got, self.sizes, self.bases, self.bits = data, [], [size], [base], []
        at = 0
        self.down, self.up = [], []
        for level, name in enumerate(order):
            bit, device = pairs[name]
            half = self.sizes[-1] // 2
            got_here = got.at[pl.ds(at, half)]
            at += half
            source, start = (data, base) if level == 0 else (self.got[-1], 0)
            away = pl.ds(pl.multiple_of(start + (1 - bit) * half, 16), half)
            self.down.append(wires.copy(source.at[away], got_here, device))
            self.got.append(got_here)
            self.bits.append(bit)
            self.sizes.append(half)
            self.bases.append(self.bases[-1] + bit * half)
            kept = pl.ds(pl.multiple_of(self.bases[-1], 16), half)
            self.up.append(wires.copy(data.at[kept], data.at[kept], device))
        whole = pl.ds(base, size)
        self.up.insert(0, wires.copy(data.at[whole], final.at[place.core, pl.ds(final_base, size)], place.flip(0)))
        self.depth = len(order)
        self.keep = pltpu.make_async_copy(data.at[whole], final.at[place.core, pl.ds(final_base, size)], keep)
        self.free, self.first = free, pairs[order[0]][1]
        self.sent = []

    def start(self, copy):
        copy.start()
        self.sent.append(copy)

    def stage(self, number):
        depth = self.depth
        if number == 0:
            self.start(self.down[0])
        elif number <= depth:
            level = number - 1
            self.down[level].wait_recv()
            if level == 0:
                self.down[0].wait_send()
                self.sent.pop()
                pl.semaphore_signal(
                    self.free, inc=1, device_id=self.first, device_id_type=pl.DeviceIdType.MESH
                )
            half = self.sizes[number]
            source, start = (self.data, self.bases[0]) if level == 0 else (self.got[level - 1], 0)
            start = start + self.bits[level] * half
            if number < depth:
                add_rows(self.got[level], 0, [(source, start)], half)
                self.start(self.down[number])
            else:
                add_rows(self.got[level], 0, [(source, start)], half, self.data, self.bases[depth])
                self.start(self.up[depth])
        else:
            level = 2 * depth - number + 1
            self.up[level].wait_recv()
            if level == 2:
                pl.semaphore_wait(self.free, 1)
            self.start(self.up[level - 1])
            if level == 1:
                self.keep.start()

    def finish(self):
        self.up[0].wait_recv()
        self.keep.wait()
        for copy in self.sent:
            copy.wait_send()


SCHEDULE = (
    "front", "send0", "mlp0", "u3.0", "u0.0", "mlp1", "send1", "send2", "line0", "spread0", "u3.1", "u0.1", "u4.0",
    "mlp2", "u5.0", "fwd0", "u0.2", "u1.0", "u2.0", "keys0", "a0", "a0", "line1", "spread1", "u0.3", "u4.1", "a0",
    "u3.2", "a0", "u1.1", "u2.1", "fwd1", "line2", "u0.4", "core0", "u5.1", "keys1", "u4.2", "a1", "u2.2", "u4.3",
    "u0.5", "u3.3", "a1", "u4.4", "plane0", "spread2", "a1", "u4.5", "u2.3", "a1", "home0", "fwd2", "u5.2", "u3.4",
    "u4.6", "u1.2", "u2.4", "u0.6", "core1", "grad0", "keys2", "a2", "u5.3", "u4.7", "a2", "u0.7", "u2.5", "plane1",
    "a2", "u5.4", "a2", "u2.6", "v0.1", "home1", "core2", "v1.1", "grad1", "u3.5", "u1.3", "v1.2", "u3.6", "u5.5",
    "part", "plane2", "v1.3", "v2.1", "v0.2", "v1.4", "u3.7", "u5.6", "u1.4", "v2.2", "v1.5", "home2", "v3.1", "v0.3",
    "u1.5", "grad2", "v2.3", "tail", "v1.6", "v4.1", "v3.2", "u4.8", "v2.4", "v0.4", "u1.6", "v5.1", "v3.3", "v4.2",
    "v2.5", "u5.7", "vec0", "v5.2", "v0.5", "v3.4", "v2.6", "v4.3", "u2.7", "v5.3", "v1.7", "v0.6", "u0.8", "v5.4",
    "v2.7", "v4.4", "v3.5", "v5.5", "vec1", "v4.5", "u5.8", "u1.7", "v5.6", "v4.6", "v2.8", "v0.7", "v3.6", "v5.7",
    "u3.8", "vec2", "v4.7", "u2.8", "v1.8", "v3.7", "u1.8", "vec3", "v0.8", "v5.8", "v4.8", "v3.8",
)
FF_CHUNK = 256
ORDERS = ("xymf", "mxyf", "xymf", "yxmf", "yxmf", "yxmf", "yxmf", "myfx", "yxmf", "yxmf", "mxyf", "xymf")


def runs_of(positions, n_blk):
    group = positions[0, 0] // GROUP
    mirror = 2 * n_blk - 1 - group
    turn = jnp.full((16, 128), (group - mirror).astype(F32), F32).astype(BF16) > 0
    return jnp.minimum(group, mirror), jnp.broadcast_to(turn[None], (GROUP // 16, 16, 128))


def rotary_rows(low_group, n_blk):
    shape = (2 * GROUP, 2 * HEAD_DIM)
    row = lax.broadcasted_iota(jnp.int32, shape, 0)
    lane = lax.broadcasted_iota(jnp.int32, shape, 1) % HEAD_DIM
    half = ROTARY // 2
    at = jnp.where(row < GROUP, low_group * GROUP + row, (2 * n_blk - 2 - low_group) * GROUP + row)
    inverse = jnp.zeros(shape, F32)
    for i in range(half):
        inverse = jnp.where(lane % half == i, float(np.float32(ROTARY_BASE ** (-2.0 * i / ROTARY))), inverse)
    angles = at.astype(F32) * inverse
    cosine, sine = jnp.cos(angles), jnp.sin(angles)
    return (
        jnp.where(lane < ROTARY, cosine, 1.0),
        jnp.where(lane < half, -sine, 0.0),
        jnp.where((lane >= half) & (lane < ROTARY), sine, 0.0),
    )


def joined_kernel(
    n_seq, n_blk, units1, units2,
    positions, hid, og, again, abias, mgain, mbias, bqkv, bdense, bout, bin_,
    wqkv_hbm, wdense_hbm, win_hbm, wout_hbm,
    output, input_grad, vec_out, final,
    wqkv, wdense, win, wout, cosw, sina, sinb, hid2, og2, normed2, normed_m, qd_msg, kv_msg, qd_line, keys, flags,
    kvl, kvtl, kvth, ksel, kselt, bias, sb, acc,
    dkv_got, odq_all, dkv_all, out_part, gn_part, mout_got, gn_got, mine, other, bins,
    grads1, grads2, got, small, small_got, sends, recvs, load_sem, chunk_sem, keep_sem, free_sem,
):
    def row(ref):
        return ref[...].astype(F32).reshape(1, ref.shape[0])

    place = Place(n_seq, n_blk)
    wires = Wires(sends, recvs)
    tokens, width = hid.shape
    n_rest = place.n_rest
    core, hi = place.core, place.hi
    half_ff = win_hbm.shape[1] // 2
    chunks = half_ff // FF_CHUNK
    rows1 = grads1.shape[0]
    pieces = place.n_low
    sent, waiting = [], {}
    todo = {}

    def go(name, src, dst, device):
        copy = wires.copy(src, dst, device)
        copy.start()
        sent.append(copy)
        waiting.setdefault(name, []).append(copy)

    def arrive(name):
        for copy in waiting.pop(name):
            copy.wait_recv()

    loads = [
        pltpu.make_async_copy(wqkv_hbm, wqkv, load_sem.at[0]),
        pltpu.make_async_copy(wdense_hbm, wdense, load_sem.at[1]),
    ]
    for load in loads:
        load.start()

    def chunk_loads(f):
        slot = f % 2
        at = pl.multiple_of(core * half_ff + f * FF_CHUNK, FF_CHUNK)
        return [
            pltpu.make_async_copy(win_hbm.at[:, pl.ds(at, FF_CHUNK)], win.at[slot], chunk_sem.at[0, slot]),
            pltpu.make_async_copy(wout_hbm.at[pl.ds(at, FF_CHUNK), :], wout.at[slot], chunk_sem.at[1, slot]),
        ]

    for f in range(2):
        for load in chunk_loads(f):
            load.start()

    low_group, turned_rows = runs_of(positions, n_blk)
    cut = (GROUP // 16, 16, 128)
    for src, dst in ((hid, hid2), (og, og2)):
        for at in range(0, width, 128):
            cols = slice(at, at + 128)
            one, two = src[0:GROUP, cols].reshape(cut), src[GROUP : 2 * GROUP, cols].reshape(cut)
            dst[0:GROUP, cols] = jnp.where(turned_rows, two, one).reshape(GROUP, 128)
            dst[GROUP : 2 * GROUP, cols] = jnp.where(turned_rows, one, two).reshape(GROUP, 128)
    flags[0, 0] = jnp.full((16, 128), low_group.astype(F32), F32).astype(BF16)
    cosw[...], sina[...], sinb[...] = rotary_rows(low_group, n_blk)
    place.meet()
    for by in range(1, HEAD_GROUPS):
        go("flags", flags.at[0, 0], flags.at[0, by], place.to_group(by))
    for ref in (hid2, og2):
        go("rows", ref.at[pl.ds(0, tokens)], ref.at[pl.ds(tokens, tokens)], place.flip(0))

    lane = lax.broadcasted_iota(jnp.int32, (tokens, 128), 1)
    low = lane < HEAD_DIM

    def front():
        xhat, _ = normalise(hid2[0:tokens, :].astype(F32))
        normed = (xhat * row(again) + row(abias)).astype(BF16)
        for load in loads:
            load.wait()
        mixed = mm(normed, wqkv[...]) + row(bqkv)
        datt = mm_nt(og2[0:tokens, :], wdense[...])
        ca, sa, sb_ = cosw[...], sina[...], sinb[...]

        def turned(u):
            return u * ca + pltpu.roll(u, 120, 1) * sa + pltpu.roll(u, 8, 1) * sb_

        for tile in range(HEADS // 2):
            at = tile * 128
            q = turned(mixed[:, at : at + 128]) * (HEAD_DIM**-0.5)
            k = turned(mixed[:, width + at : width + at + 128])
            v = mixed[:, 2 * width + at : 2 * width + at + 128]
            d = datt[:, at : at + 128]
            for msg, one, two in ((qd_msg, q, d), (kv_msg, k, v)):
                for odd in range(2):
                    head = 2 * tile + odd
                    if odd == 0:
                        packed = jnp.where(low, one, pltpu.roll(two, 64, 1))
                    else:
                        packed = jnp.where(low, pltpu.roll(one, 64, 1), two)
                    msg[head % PER_GROUP, head // PER_GROUP] = packed.astype(BF16)
        arrive("flags")
        go("flag_x", flags.at[0], flags.at[1], place.flip(1))
        go("flag_c", flags.at[0], flags.at[2], place.flip(0))

    def send(j):
        for msg, line, name in ((kv_msg, keys.at[j, 0], "line"), (qd_msg, qd_line.at[j], "line")):
            for by in range(1, HEAD_GROUPS):
                go(name + str(j), msg.at[j, (hi + by) % HEAD_GROUPS], line.at[by], place.to_group(by))
        keys[j, 0, 0] = kv_msg[j, hi]
        qd_line[j, 0] = qd_msg[j, hi]

    def mlp_group(g):
        if g == 0:
            arrive("rows")
            xhat, _ = normalise(hid2[...].astype(F32))
            normed_m[...] = (xhat * row(mgain) + row(mbias)).astype(BF16)
            normed2[...] = (xhat * row(again) + row(abias)).astype(BF16)
            out_part[...] = jnp.zeros_like(out_part)
            gn_part[...] = jnp.zeros_like(gn_part)
        per = chunks // 3

        def step(f, _):
            slot = f % 2
            for load in chunk_loads(f):
                load.wait()
            x, w1, w2 = normed_m[...], win[slot], wout[slot]
            at = pl.multiple_of(f * FF_CHUNK, FF_CHUNK)
            bias_at = pl.ds(pl.multiple_of(core * half_ff + f * FF_CHUNK, FF_CHUNK), FF_CHUNK)
            inner = mm(x, w1) + bin_[bias_at].astype(F32).reshape(1, FF_CHUNK)
            cdf = 0.5 * (1.0 + lax.erf(inner * (0.5**0.5)))
            act = (inner * cdf).astype(BF16)
            pdf = jnp.exp(-0.5 * inner * inner) * (0.5 * 2.0**0.5 * 3.141592653589793**-0.5)
            gact = mm_nt(og2[...], w2)
            ginner = (gact * (cdf + inner * pdf)).astype(BF16)
            bins[0:1, pl.ds(at, FF_CHUNK)] = jnp.sum(ginner.astype(F32), axis=0, keepdims=True)
            grads1[pl.ds(at, FF_CHUNK), :] = mm_tn(ginner, x).astype(BF16)
            grads1[pl.ds(pl.multiple_of(half_ff + at, FF_CHUNK), FF_CHUNK), :] = mm_tn(act, og2[...]).astype(BF16)
            out_part[...] += mm(act, w2)
            gn_part[...] += mm_nt(ginner, w1)

            @pl.when(f + 2 < chunks)
            def _():
                for load in chunk_loads(f + 2):
                    load.start()

            return 0

        lax.fori_loop(g * per, (g + 1) * per, step, 0)

    def part():
        go("part", out_part.at[pl.ds(tokens, tokens)], mout_got, place.flip(0))
        go("part", gn_part.at[pl.ds(tokens, tokens)], gn_got, place.flip(0))

    def spread(j):
        go("x" + str(j), keys.at[j, 0], keys.at[j, 1], place.flip(1))
        go("c" + str(j), keys.at[j, 0], keys.at[j, 2], place.flip(0))

    def forward(j):
        arrive("x" + str(j))
        go("c" + str(j), keys.at[j, 1], keys.at[j, 3], place.flip(0))
        if j == 0:
            arrive("flag_x")
            go("flag_c", flags.at[1], flags.at[3], place.flip(0))

    def keys_there(j):
        arrive("c" + str(j))
        if j == 0:
            arrive("flag_c")

    attention = Attention(HEAD_GROUPS, HEAD_GROUPS * pieces, flags, kvl, kvtl, kvth, ksel, kselt, bias, sb, acc)

    def attend(j):
        sources = [keys.at[j, p] for p in range(pieces)]
        attention.prepare(sources)
        for first in range(0, HEAD_GROUPS, 2):
            yield from attention.pair(first, qd_line.at[j], sources, qd_line.at[j])
            if first + 2 < HEAD_GROUPS:
                yield
        for copy in leaving[j]:
            copy.wait_send()
        attention.give(sources)
        for by in range(1, HEAD_GROUPS):
            go("home" + str(j), qd_line.at[j, by], odq_all.at[j, by], place.to_group(HEAD_GROUPS - by))
        for i in range(2):
            go("core" + str(j), keys.at[j, 2 + i], dkv_got.at[j, i], place.flip(0))
        yield

    leaving = {}

    def core_sum(j):
        arrive("core" + str(j))
        for i in range(2):
            dkv_got[j, i] = (keys[j, i].astype(F32) + dkv_got[j, i].astype(F32)).astype(BF16)
        go("plane" + str(j), dkv_got.at[j, 1], dkv_got.at[j, 2], place.flip(1))

    def plane_sum(j):
        arrive("plane" + str(j))
        dkv_got[j, 2] = (dkv_got[j, 0].astype(F32) + dkv_got[j, 2].astype(F32)).astype(BF16)
        for by in range(1, HEAD_GROUPS):
            go("home" + str(j), dkv_got.at[j, 2, by], dkv_all.at[j, by], place.to_group(HEAD_GROUPS - by))
        odq_all[j, 0] = qd_line[j, 0]
        dkv_all[j, 0] = dkv_got[j, 2, 0]

    def home(j):
        arrive("home" + str(j))
        ca, sa, sb_ = cosw[...], sina[...], sinb[...]

        def turned_back(g):
            return g * ca - pltpu.roll(g, 120, 1) * sa - pltpu.roll(g, 8, 1) * sb_

        for g in range(HEAD_GROUPS):
            at = (g - hi + HEAD_GROUPS) % HEAD_GROUPS
            a, b = odq_all[j, at].astype(F32), dkv_all[j, at].astype(F32)
            mine[j, g, :, 0:128] = jnp.where(low, a, turned_back(a)).astype(BF16)
            mine[j, g, :, 128:256] = jnp.where(low, turned_back(b), b).astype(BF16)
        half = HEAD_GROUPS // 2
        go("other" + str(j), mine.at[j, pl.ds((1 - core) * half, half)], other.at[j], place.flip(0))

    def grad(j):
        arrive("other" + str(j))
        half = HEAD_GROUPS // 2
        normed, cot = normed2[...], og2[...]
        from_out = lax.broadcasted_iota(jnp.int32, (128, width), 0) < HEAD_DIM
        for g in range(half):
            both = jnp.concatenate([mine[j, core * half + g], other[j, g]], axis=0)
            base = (j * half + g) * 256
            by_normed = mm_tn(both, normed)
            by_cot = mm_tn(both[:, 0:128], cot)
            grads2[base : base + 128, :] = jnp.where(from_out, by_cot, by_normed[0:128]).astype(BF16)
            grads2[base + 128 : base + 256, :] = by_normed[128:256].astype(BF16)
        per = len(units2) // PER_GROUP
        for unit in second[j * per : (j + 1) * per]:
            unit.stage(0)

    def tail():
        arrive("part")
        rows = hid2[0:tokens, :].astype(F32)

        def parts(a):
            return mine[a % PER_GROUP, a // PER_GROUP].astype(F32)

        outs, grads = [], [[], [], []]
        for tile in range(HEADS // 2):
            one, two = parts(2 * tile), parts(2 * tile + 1)
            a1, b1, a2, b2 = one[:, 0:128], one[:, 128:256], two[:, 0:128], two[:, 128:256]
            outs.append(jnp.where(low, a1, pltpu.roll(a2, 64, 1)).astype(BF16))
            grads[0].append(jnp.where(low, pltpu.roll(a1, 64, 1), a2).astype(BF16))
            grads[1].append(jnp.where(low, b1, pltpu.roll(b2, 64, 1)).astype(BF16))
            grads[2].append(jnp.where(low, pltpu.roll(b1, 64, 1), b2).astype(BF16))
        att = jnp.concatenate(outs, axis=1)
        dmixed = jnp.concatenate(grads[0] + grads[1] + grads[2], axis=1)
        branch = mm(att, wdense[...]) + row(bdense)
        mout = out_part[0:tokens, :] + mout_got[...]
        output[...] = (rows + branch + (mout + row(bout))).astype(BF16)
        gna = mm_nt(dmixed, wqkv[...])
        gnm = gn_part[0:tokens, :] + gn_got[...]
        xhat, scale = normalise(rows)
        cot = og2[0:tokens, :].astype(F32)
        input_grad[...] = (
            cot
            + norm_back(gna, xhat, scale, row(again))
            + norm_back(gnm, xhat, scale, row(mgain))
        ).astype(BF16)
        small[0:1, :] = jnp.sum(gna * xhat, axis=0, keepdims=True)
        small[1:2, :] = jnp.sum(gna, axis=0, keepdims=True)
        small[2:3, :] = jnp.sum(gnm * xhat, axis=0, keepdims=True)
        small[3:4, :] = jnp.sum(gnm, axis=0, keepdims=True)
        for k in range(3):
            cols = dmixed[:, k * width : (k + 1) * width].astype(F32)
            small[4 + k : 5 + k, :] = jnp.sum(cols, axis=0, keepdims=True)
        small[7:8, :] = jnp.sum(cot, axis=0, keepdims=True)
        per = half_ff // width
        for side in range(2):
            here = (1 - core if side == 0 else core).astype(F32)
            for k in range(per):
                at = 8 + side * per + k
                small[at : at + 1, :] = bins[0:1, k * width : (k + 1) * width] * here

    rounds = [
        [place.flip(0)],
        [place.flip(1)],
        [place.to_seq()],
        [place.to_rest(by) for by in range(1, n_rest)],
    ]

    def vec_start(r):
        for i, device in enumerate(rounds[r]):
            go("vec" + str(r), small.at[pl.ds(0, small.shape[0])] if r == 0 else small_got.at[8 + r], small_got.at[2 * r if r < 3 else 5 + i], device)

    def vec(r):
        if r == 0:
            vec_start(0)
            return
        arrive("vec" + str(r - 1))
        source = small[...] if r == 1 else small_got[8 + r - 1]
        small_got[8 + r] = source + small_got[2 * (r - 1)]
        vec_start(r)

    def vec_end():
        arrive("vec3")
        total = small_got[8 + 3]
        for i in range(n_rest - 1):
            total = total + small_got[5 + i]
        vec_out[...] = total

    first, second = [], []
    at = 0
    for found, units, data, offset in ((first, units1, grads1, 0), (second, units2, grads2, rows1)):
        for base, size, order in units:
            found.append(Chain(
                place, wires, data, base, size, order, got.at[pl.ds(at, size)], final, offset + base,
                free_sem.at[len(first) + len(second)], keep_sem.at[len(first) + len(second)],
            ))
            at += size

    todo = {"front": front, "part": part, "tail": tail}
    for g in range(3):
        todo["mlp" + str(g)] = functools.partial(mlp_group, g)
    for r in range(4):
        todo["vec" + str(r)] = functools.partial(vec, r)
    runs = {}
    for j in range(PER_GROUP):
        for name, action in (
            ("send", send), ("line", lambda j: arrive("line" + str(j))), ("spread", spread), ("fwd", forward),
            ("keys", keys_there), ("core", core_sum), ("plane", plane_sum), ("home", home), ("grad", grad),
        ):
            todo[name + str(j)] = functools.partial(action, j)
        runs[j] = attend(j)
        todo["a" + str(j)] = functools.partial(next, runs[j])
    for name, units in (("u", first), ("v", second)):
        for i, unit in enumerate(units):
            for stage in range(2 * unit.depth + 1):
                todo[name + str(i) + "." + str(stage)] = functools.partial(unit.stage, stage)
    for j in range(PER_GROUP):
        leaving[j] = []
    for token in SCHEDULE:
        before = len(sent)
        todo[token]()
        if token[:-1] in ("spread", "fwd"):
            leaving[int(token[-1])] += sent[before:]
            del sent[before:]
    vec_end()
    for unit in first + second:
        if unit.sent:
            unit.finish()
    for copy in sent:
        copy.wait_send()


def joined(mesh, positions, hid, og, again, abias, mgain, mbias, bqkv, bdense, bout, b_in, wqkv, wdense, win, wout):
    n_seq, n_blk = mesh.shape["seq"], mesh.shape["blk"]
    n_low, n_rest = n_blk // HEAD_GROUPS, n_blk // 4
    tokens, width = hid.shape
    half_ff = win.shape[1] // 2
    rows1, rows2 = 2 * half_ff, 2 * width
    size = half_ff // 3
    units1 = [(i * size, size, order) for i, order in enumerate(ORDERS[:6])]
    size = rows2 // 6
    units2 = [(i * size, size, order) for i, order in enumerate(ORDERS[6:])]
    total = rows1 + rows2
    copies = 9 * (len(units1) + len(units2)) + 128
    line = (HEAD_GROUPS, tokens, 128)
    n_small = 8 + 2 * half_ff // width
    devices = HEAD_GROUPS * n_low
    per = PER_GROUP
    inputs = [positions, hid, og, again, abias, mgain, mbias, bqkv, bdense, bout, b_in, wqkv, wdense, win, wout]
    return pl.pallas_call(
        functools.partial(joined_kernel, n_seq, n_blk, units1, units2),
        out_shape=[
            jax.ShapeDtypeStruct((tokens, width), BF16),
            jax.ShapeDtypeStruct((tokens, width), BF16),
            jax.ShapeDtypeStruct((n_small, width), F32),
            jax.ShapeDtypeStruct((2, total, width), BF16),
        ],
        in_specs=[IN_SMEM] + [IN_VMEM] * (len(inputs) - 5) + [pl.BlockSpec(memory_space=pl.ANY)] * 4,
        out_specs=[IN_VMEM] * 3 + [pl.BlockSpec(memory_space=pl.ANY)],
        scratch_shapes=[
            pltpu.VMEM(wqkv.shape, BF16),
            pltpu.VMEM(wdense.shape, BF16),
            pltpu.VMEM((2, width, FF_CHUNK), BF16),
            pltpu.VMEM((2, FF_CHUNK, width), BF16),
            pltpu.VMEM((tokens, 2 * HEAD_DIM), F32),
            pltpu.VMEM((tokens, 2 * HEAD_DIM), F32),
            pltpu.VMEM((tokens, 2 * HEAD_DIM), F32),
            pltpu.VMEM((2 * tokens, width), BF16),
            pltpu.VMEM((2 * tokens, width), BF16),
            pltpu.VMEM((2 * tokens, width), BF16),
            pltpu.VMEM((2 * tokens, width), BF16),
            pltpu.VMEM((per,) + line, BF16),
            pltpu.VMEM((per,) + line, BF16),
            pltpu.VMEM((per,) + line, BF16),
            pltpu.VMEM((per, n_low) + line, BF16),
            pltpu.VMEM((n_low, HEAD_GROUPS, 16, 128), BF16),
            *attention_scratch(HEAD_GROUPS, devices),
            pltpu.VMEM((per, 3) + line, BF16),
            pltpu.VMEM((per,) + line, BF16),
            pltpu.VMEM((per,) + line, BF16),
            pltpu.VMEM((2 * tokens, width), F32),
            pltpu.VMEM((2 * tokens, width), F32),
            pltpu.VMEM((tokens, width), F32),
            pltpu.VMEM((tokens, width), F32),
            pltpu.VMEM((per, HEAD_GROUPS, tokens, 256), BF16),
            pltpu.VMEM((per, HEAD_GROUPS // 2, tokens, 256), BF16),
            pltpu.VMEM((1, half_ff), F32),
            pltpu.VMEM((rows1, width), BF16),
            pltpu.VMEM((rows2, width), BF16),
            pltpu.VMEM((total, width), BF16),
            pltpu.VMEM((n_small, width), F32),
            pltpu.VMEM((12, n_small, width), F32),
            pltpu.SemaphoreType.DMA((copies,)),
            pltpu.SemaphoreType.DMA((copies,)),
            pltpu.SemaphoreType.DMA((2,)),
            pltpu.SemaphoreType.DMA((2, 2)),
            pltpu.SemaphoreType.DMA((len(units1) + len(units2),)),
            pltpu.SemaphoreType.REGULAR((len(units1) + len(units2),)),
        ],
        compiler_params=pltpu.CompilerParams(
            vmem_limit_bytes=VMEM_BYTES, collective_id=2, has_side_effects=True
        ),
        name="joined",
    )(*inputs)


def spread_kernel(
    n_blk, positions, final, vec, out_rows, grad_rows,
    output, input_grad, win, wout, wqkv, wdense, again, abias, mgain, mbias, bqkv, bdense, bin_, bout,
):
    half_ff = win.shape[1] // 2

    @pl.when(pl.program_id(0) == 0)
    def _():
        width = vec.shape[1]
        _, turned_rows = runs_of(positions, n_blk)
        cut = (GROUP // 16, 16, 128)
        for src, dst in ((out_rows, output), (grad_rows, input_grad)):
            for at in range(0, width, 128):
                cols = slice(at, at + 128)
                one, two = src[0:GROUP, cols].reshape(cut), src[GROUP : 2 * GROUP, cols].reshape(cut)
                dst[0:GROUP, cols] = jnp.where(turned_rows, two, one).reshape(GROUP, 128)
                dst[GROUP : 2 * GROUP, cols] = jnp.where(turned_rows, one, two).reshape(GROUP, 128)
        for ref, at in ((again, 0), (abias, 1), (mgain, 2), (mbias, 3), (bqkv, 4), (bdense, 7), (bout, 7), (bin_, 8)):
            for k in range(ref.shape[0] // width):
                ref[k * width : (k + 1) * width] = vec[at + k : at + k + 1, :].reshape(width)

    for core in range(2):
        win[:, core * half_ff : (core + 1) * half_ff] = final[core, 0:half_ff, :].T.astype(F32)
        wout[core * half_ff : (core + 1) * half_ff, :] = final[core, half_ff : 2 * half_ff, :].astype(F32)

    def segment(head, part):
        group, j = head // PER_GROUP, head % PER_GROUP
        half = HEAD_GROUPS // 2
        at = 2 * half_ff + (j * half + group % half) * 256 + part * HEAD_DIM
        return final[group // half, at : at + HEAD_DIM, :]

    width = wdense.shape[0]
    for tile in range(HEADS // 2):
        for part in range(4):
            both = jnp.concatenate([segment(2 * tile, part), segment(2 * tile + 1, part)], axis=0)
            if part == 0:
                wdense[tile * 128 : tile * 128 + 128, :] = both.astype(F32)
            else:
                at = (part - 1) * width + tile * 128
                wqkv[:, at : at + 128] = both.T.astype(F32)


def spread_out(n_blk, positions, final, vec, out_rows, grad_rows, ff):
    total, width = final.shape[1:]
    lanes = 128

    def whole(x):
        return pl.BlockSpec(x.shape, lambda i: (0,) * len(x.shape))

    vectors = [jax.ShapeDtypeStruct((n,), F32) for n in (width, width, width, width, 3 * width, width, ff, width)]
    rows = jax.ShapeDtypeStruct(out_rows.shape, BF16)
    return pl.pallas_call(
        functools.partial(spread_kernel, n_blk),
        grid=(width // lanes,),
        in_specs=[IN_SMEM, pl.BlockSpec((2, total, lanes), lambda i: (0, 0, i))]
        + [whole(x) for x in (vec, out_rows, grad_rows)],
        out_specs=[
            whole(rows),
            whole(rows),
            pl.BlockSpec((lanes, ff), lambda i: (i, 0)),
            pl.BlockSpec((ff, lanes), lambda i: (0, i)),
            pl.BlockSpec((lanes, 3 * width), lambda i: (i, 0)),
            pl.BlockSpec((width, lanes), lambda i: (0, i)),
        ]
        + [whole(x) for x in vectors],
        out_shape=[
            rows,
            rows,
            jax.ShapeDtypeStruct((width, ff), F32),
            jax.ShapeDtypeStruct((ff, width), F32),
            jax.ShapeDtypeStruct((width, 3 * width), F32),
            jax.ShapeDtypeStruct((width, width), F32),
        ]
        + vectors,
        compiler_params=params(),
        name="spread",
    )(positions, final, vec, out_rows, grad_rows)


def rotary_tables(positions):
    lane = jnp.arange(128, dtype=jnp.int32) % HEAD_DIM
    half = ROTARY // 2
    inverse = jnp.power(ROTARY_BASE, -2.0 * (lane % half).astype(F32) / ROTARY)
    angles = positions.astype(F32)[:, None] * inverse[None, :]
    cosine, sine = jnp.cos(angles), jnp.sin(angles)
    lane = lane[None, :]
    return (
        jnp.where(lane < ROTARY, cosine, 1.0),
        jnp.where(lane < half, -sine, 0.0),
        jnp.where((lane >= half) & (lane < ROTARY), sine, 0.0),
    )


def solution(mesh):
    n_seq, n_blk = mesh.shape["seq"], mesh.shape["blk"]
    n_low = n_blk // HEAD_GROUPS
    low_bits = n_low.bit_length() - 1
    def permute(x, target):
        return lax.ppermute(x, "blk", [(b, target(b)) for b in range(n_blk)])

    def to_group(x, by):
        return permute(x, lambda b: ((b // n_low + by) % HEAD_GROUPS) * n_low + b % n_low)

    def flip(x, bit):
        return permute(x, lambda b: b ^ (1 << bit))

    def on_device(
        hidden, positions, ln_attn_gain, ln_attn_bias, ln_mlp_gain, ln_mlp_bias,
        w_qkv, b_qkv, w_dense, b_dense, w_in, b_in, w_out, b_out, out_grad,
    ):
        hid, og, pos = hidden[0], out_grad[0], positions[0]
        again, abias = ln_attn_gain[None], ln_attn_bias[None]
        mgain, mbias = ln_mlp_gain[None], ln_mlp_bias[None]
        tokens, width = hid.shape
        if n_low == 4:
            output, input_grad, vec, final = joined(
                mesh, positions, hid, og, ln_attn_gain, ln_attn_bias, ln_mlp_gain, ln_mlp_bias, b_qkv, b_dense, b_out,
                b_in, w_qkv, w_dense, w_in, w_out,
            )
            output, input_grad, win, wout, wqkv, wdense, *vectors = spread_out(
                n_blk, positions, final, vec, output, input_grad, w_in.shape[1]
            )
            dgain, dbias, dmgain, dmbias, dbqkv, dbdense, dbin, dbout = vectors
            return (
                output[None], input_grad[None], dgain, dbias, dmgain, dmbias,
                wqkv, dbqkv, wdense, dbdense, win, dbin, wout, dbout,
            )
        b = lax.axis_index("blk")
        core = b % 2
        hi = b // n_low
        tables = rotary_tables(pos)

        own_runs = pos[::GROUP] // GROUP
        line_runs = jnp.concatenate(
            [own_runs] + [to_group(own_runs, by) for by in range(1, HEAD_GROUPS)]
        )
        key_runs = [line_runs]
        for bit in range(low_bits - 1, -1, -1):
            key_runs = key_runs + [flip(r, bit) for r in key_runs]
        n_query = line_runs.shape[0]
        rank = jnp.sum(line_runs[:, None] > line_runs[None, :], axis=1)
        slots = rank[None, :] == jnp.arange(n_query)[:, None]
        order = jnp.sum(jnp.where(slots, jnp.arange(n_query)[None, :], 0), axis=1)
        ordered = jnp.sum(jnp.where(slots, line_runs[None, :], 0), axis=1)
        tab = jnp.concatenate(key_runs + [order, ordered]).astype(jnp.int32)

        hid2 = jnp.concatenate([hid, flip(hid, 0)], axis=0)
        og2 = jnp.concatenate([og, flip(og, 0)], axis=0)

        msg = front(hid, og, again, abias, w_qkv, b_qkv[None], w_dense, tables)

        arrived = []
        for j in range(PER_GROUP):
            got = []
            for by in range(HEAD_GROUPS):
                part = lax.dynamic_index_in_dim(msg[j], lax.rem(hi + by, HEAD_GROUPS), 0, False)
                got.append(part if by == 0 else to_group(part, by))
            qd = jnp.stack([g[0] for g in got])
            pieces = [jnp.stack([g[1] for g in got])]
            for bit in range(low_bits - 1, -1, -1):
                pieces = pieces + [flip(piece, bit) for piece in pieces]
            arrived.append((qd, pieces))

        mlp_grads, bin_half, out_part, gn_part, normed2 = mlp(
            core[None].astype(jnp.int32), hid2, og2, again, abias, mgain, mbias, w_in, b_in[None], w_out
        )
        odqs, dkvs = [], []
        line = (HEAD_GROUPS, tokens, 128)
        for j in range(PER_GROUP):
            qd, pieces = arrived[j]
            runs = (HEAD_GROUPS * tokens // GROUP, GROUP, 128)
            odq, dkv = attention(tab, qd.reshape(runs), [p.reshape(runs) for p in pieces])
            odqs.append(odq.reshape(line))
            dkvs.append([d.reshape(line) for d in dkv])

        zero = jnp.zeros_like(bin_half)
        bins = jnp.where(
            core == 0, jnp.concatenate([bin_half, zero], 1), jnp.concatenate([zero, bin_half], 1)
        ).reshape(-1, width)
        half_ff = mlp_grads.shape[1]
        output, input_grad, vec, final = finish(
            mesh, odqs, dkvs, mlp_grads.reshape(2 * half_ff, width), out_part, gn_part, hid, og, og2,
            normed2, bins, again, mgain, w_qkv, w_dense, b_dense[None], b_out[None], tables,
        )
        win, wout, wqkv, wdense = expand(
            final, ((half_ff, True), (half_ff, False), (3 * width // 2, True), (width // 2, False))
        )
        return (
            output[None],
            input_grad[None],
            vec[0],
            vec[1],
            vec[2],
            vec[3],
            wqkv,
            vec[4:7].reshape(-1),
            wdense,
            vec[7],
            win,
            vec[8:].reshape(-1),
            wout,
            vec[7],
        )

    rows = P("seq", "blk", None)
    return jax.shard_map(
        on_device,
        mesh=mesh,
        in_specs=(rows, P("seq", "blk")) + (P(),) * 12 + (rows,),
        out_specs=(rows, rows) + (P(),) * 12,
        check_vma=False,
    )
```

```python
import functools

import jax
import jax.numpy as jnp
import numpy as np
from jax import lax
from jax.experimental import pallas as pl
from jax.experimental.pallas import tpu as pltpu
from jax.sharding import PartitionSpec as P

HEADS = 12
HEAD_DIM = 64
ROTARY = 16
GROUP = 128
HEAD_GROUPS = 4
PER_GROUP = HEADS // HEAD_GROUPS
NORM_EPSILON = 1e-05
ROTARY_BASE = 10000.0
MASKED = -1e30
VMEM_BYTES = 62 * 1024 * 1024

F32 = jnp.float32
BF16 = jnp.bfloat16
IN_VMEM = pl.BlockSpec(memory_space=pltpu.VMEM)
IN_SMEM = pl.BlockSpec(memory_space=pltpu.SMEM)


def mm(a, b):
    return lax.dot_general(a, b, (((1,), (0,)), ((), ())), preferred_element_type=F32)


def mm_nt(a, b):
    return lax.dot_general(a, b, (((1,), (1,)), ((), ())), preferred_element_type=F32)


def mm_tn(a, b):
    return lax.dot_general(a, b, (((0,), (0,)), ((), ())), preferred_element_type=F32)


def normalise(rows):
    centre = rows - jnp.mean(rows, axis=-1, keepdims=True)
    spread = jnp.mean(centre * centre, axis=-1, keepdims=True)
    scale = lax.rsqrt(spread + NORM_EPSILON)
    return centre * scale, scale


def norm_back(grad, xhat, scale, gain):
    eg = grad * gain
    return scale * (
        eg
        - jnp.mean(eg, axis=-1, keepdims=True)
        - xhat * jnp.mean(eg * xhat, axis=-1, keepdims=True)
    )


def params():
    return pltpu.CompilerParams(vmem_limit_bytes=VMEM_BYTES)


def front_kernel(hid, og, gain, bias, wqkv, bqkv, wdense, cosw, sina, sinb, msg):
    rows = hid[...].astype(F32)
    xhat, _ = normalise(rows)
    normed = (xhat * gain[...].astype(F32) + bias[...].astype(F32)).astype(BF16)
    mixed = mm(normed, wqkv[...]) + bqkv[...].astype(F32)
    datt = mm_nt(og[...], wdense[...])
    width = hid.shape[1]
    lane = lax.broadcasted_iota(jnp.int32, (rows.shape[0], 128), 1)
    low = lane < HEAD_DIM
    ca, sa, sb = cosw[...], sina[...], sinb[...]

    def turned(u):
        return u * ca + pltpu.roll(u, 120, 1) * sa + pltpu.roll(u, 8, 1) * sb

    for tile in range(HEADS // 2):
        at = tile * 128
        q = turned(mixed[:, at : at + 128]) * (HEAD_DIM**-0.5)
        k = turned(mixed[:, width + at : width + at + 128])
        v = mixed[:, 2 * width + at : 2 * width + at + 128]
        d = datt[:, at : at + 128]
        for part, (one, two) in enumerate(((q, d), (k, v))):
            for odd in range(2):
                head = 2 * tile + odd
                if odd == 0:
                    packed = jnp.where(low, one, pltpu.roll(two, 64, 1))
                else:
                    packed = jnp.where(low, pltpu.roll(one, 64, 1), two)
                msg[head % PER_GROUP, head // PER_GROUP, part] = packed.astype(BF16)


def front(hid, og, gain, bias, wqkv, bqkv, wdense, tables):
    rows = hid.shape[0]
    return pl.pallas_call(
        front_kernel,
        out_shape=jax.ShapeDtypeStruct((PER_GROUP, HEAD_GROUPS, 2, rows, 128), BF16),
        in_specs=[IN_VMEM] * 10,
        out_specs=IN_VMEM,
        compiler_params=params(),
        name="front",
    )(hid, og, gain, bias, wqkv, bqkv, wdense, *tables)


def mlp_kernel(
    core, hid, og, again, abias, mgain, mbias, win, bin_, wout,
    grads, bin_grad, out_part, gn_part, normed_attn, normed_s,
):
    step = pl.program_id(0)

    @pl.when(step == 0)
    def _():
        xhat, _ = normalise(hid[...].astype(F32))
        normed_s[...] = (xhat * mgain[...].astype(F32) + mbias[...].astype(F32)).astype(BF16)
        normed_attn[...] = (xhat * again[...].astype(F32) + abias[...].astype(F32)).astype(BF16)
        out_part[...] = jnp.zeros_like(out_part)
        gn_part[...] = jnp.zeros_like(gn_part)

    x = normed_s[...]
    w1 = win[...]
    w2 = wout[...]
    inner = mm(x, w1) + bin_[...].astype(F32)
    cdf = 0.5 * (1.0 + lax.erf(inner * (0.5**0.5)))
    act = (inner * cdf).astype(BF16)
    pdf = jnp.exp(-0.5 * inner * inner) * (0.5 * 2.0**0.5 * 3.141592653589793**-0.5)
    gact = mm_nt(og[...], w2)
    ginner = (gact * (cdf + inner * pdf)).astype(BF16)
    bin_grad[...] = jnp.sum(ginner.astype(F32), axis=0, keepdims=True)
    grads[0] = mm_tn(ginner, x).astype(BF16)
    grads[1] = mm_tn(act, og[...]).astype(BF16)
    out_part[...] += mm(act, w2)
    gn_part[...] += mm_nt(ginner, w1)


def mlp(core, hid, og, again, abias, mgain, mbias, win, b_in, wout):
    rows, width = hid.shape
    half = win.shape[1] // 2
    chunk = 512
    steps = half // chunk
    whole = lambda i, c: (0, 0)
    return pl.pallas_call(
        mlp_kernel,
        grid_spec=pltpu.PrefetchScalarGridSpec(
            num_scalar_prefetch=1,
            grid=(steps,),
            in_specs=[
                pl.BlockSpec((rows, width), whole),
                pl.BlockSpec((rows, width), whole),
                pl.BlockSpec((1, width), whole),
                pl.BlockSpec((1, width), whole),
                pl.BlockSpec((1, width), whole),
                pl.BlockSpec((1, width), whole),
                pl.BlockSpec((width, chunk), lambda i, c: (0, c[0] * steps + i)),
                pl.BlockSpec((1, chunk), lambda i, c: (0, c[0] * steps + i)),
                pl.BlockSpec((chunk, width), lambda i, c: (c[0] * steps + i, 0)),
            ],
            out_specs=[
                pl.BlockSpec((2, chunk, width), lambda i, c: (0, i, 0)),
                pl.BlockSpec((1, chunk), lambda i, c: (0, i)),
                pl.BlockSpec((rows, width), whole),
                pl.BlockSpec((rows, width), whole),
                pl.BlockSpec((rows, width), whole),
            ],
            scratch_shapes=[pltpu.VMEM((rows, width), BF16)],
        ),
        out_shape=[
            jax.ShapeDtypeStruct((2, half, width), BF16),
            jax.ShapeDtypeStruct((1, half), F32),
            jax.ShapeDtypeStruct((rows, width), F32),
            jax.ShapeDtypeStruct((rows, width), F32),
            jax.ShapeDtypeStruct((rows, width), BF16),
        ],
        compiler_params=params(),
        name="mlp",
    )(core, hid, og, again, abias, mgain, mbias, win, b_in, wout)


def attention_kernel(blocks, pieces, n_query, *refs):
    tab = refs[0]
    qd_ref = refs[1]
    kv_refs = refs[2 : 2 + pieces]
    odq_ref = refs[2 + pieces]
    dkv_refs = refs[3 + pieces : 3 + 2 * pieces]
    kvs, kvt, sbuf, acc = refs[3 + 2 * pieces :]
    kb_rows = blocks
    per_piece = kv_refs[0].shape[0]
    n_run = pieces * per_piece

    def group_rows(g):
        return pl.ds(pl.multiple_of(g * GROUP, GROUP), GROUP)

    for piece in range(pieces):

        def place(i, _, piece=piece):
            rows = group_rows(tab[piece * per_piece + i])
            blk = kv_refs[piece][i]
            kvs[rows, :] = blk
            kvt[:, rows] = blk.T
            acc[rows, :] = jnp.zeros((GROUP, 128), F32)
            return 0

        lax.fori_loop(0, per_piece, place, 0, unroll=4)

    lane = lax.broadcasted_iota(jnp.int32, (2 * GROUP, 128), 1)
    row = lax.broadcasted_iota(jnp.int32, (128, 2 * GROUP), 0)
    qcol = lax.broadcasted_iota(jnp.int32, (1, 2 * GROUP), 1)
    krow = lax.broadcasted_iota(jnp.int32, (kb_rows, 1), 0)

    def pair_step(pair, _):
        i0 = tab[n_run + 2 * pair]
        i1 = tab[n_run + 2 * pair + 1]
        g0 = tab[n_run + n_query + 2 * pair]
        g1 = tab[n_run + n_query + 2 * pair + 1]
        qd = jnp.concatenate([qd_ref[i0], qd_ref[i1]], axis=0)
        zero = jnp.zeros_like(qd)
        w_keys = jnp.concatenate(
            [jnp.where(lane < HEAD_DIM, qd, zero), jnp.where(lane >= HEAD_DIM, qd, zero)], axis=0
        )
        qdt = qd.T
        zero_t = jnp.zeros_like(qdt)
        w_score = jnp.where(row < HEAD_DIM, qdt, zero_t)
        w_dprob = jnp.where(row >= HEAD_DIM, qdt, zero_t)
        qpos = jnp.where(qcol < GROUP, g0 * GROUP + qcol, (g1 - 1) * GROUP + qcol)
        n_full = (g0 * GROUP) // kb_rows
        n_all = (g1 * GROUP) // kb_rows + 1

        def block_rows(kb):
            return pl.ds(pl.multiple_of(kb * kb_rows, kb_rows), kb_rows)

        def score_step(kb, top, masked):
            rows = block_rows(kb)
            s = mm(kvs[rows, :], w_score)
            if masked:
                s = jnp.where(kb * kb_rows + krow <= qpos, s, MASKED)
            sbuf[rows, :] = s
            return jnp.maximum(top, jnp.max(s.reshape(kb_rows // 8, 8, 2 * GROUP), axis=0))

        top = jnp.full((8, 2 * GROUP), MASKED, F32)
        top = lax.fori_loop(0, n_full, lambda kb, c: score_step(kb, c, False), top)
        top = lax.fori_loop(n_full, n_all, lambda kb, c: score_step(kb, c, True), top)
        top = jnp.max(top, axis=0, keepdims=True)

        def value_step(kb, carry):
            total, out = carry
            rows = block_rows(kb)
            e = jnp.exp(sbuf[rows, :] - top)
            sbuf[rows, :] = e
            total = total + jnp.sum(e.reshape(kb_rows // 8, 8, 2 * GROUP), axis=0)
            return total, out + mm(kvt[HEAD_DIM:128, rows], e.astype(BF16))

        total, out = lax.fori_loop(
            0,
            n_all,
            value_step,
            (jnp.zeros((8, 2 * GROUP), F32), jnp.zeros((HEAD_DIM, 2 * GROUP), F32)),
        )
        inv = 1.0 / jnp.sum(total, axis=0, keepdims=True)
        out = out * inv
        delta = jnp.sum(out * qdt[HEAD_DIM:128, :].astype(F32), axis=0, keepdims=True)

        def grad_step(kb, dq):
            rows = block_rows(kb)
            p = sbuf[rows, :] * inv
            dp = mm(kvs[rows, :], w_dprob)
            ds = (p * (dp - delta)).astype(BF16)
            acc[rows, :] += mm(jnp.concatenate([ds, p.astype(BF16)], axis=1), w_keys)
            return dq + mm(kvt[0:HEAD_DIM, rows], ds)

        dq = lax.fori_loop(0, n_all, grad_step, jnp.zeros((HEAD_DIM, 2 * GROUP), F32))
        odq = jnp.concatenate([out, dq * (HEAD_DIM**-0.5)], axis=0).astype(BF16).T
        odq_ref[i0] = odq[:GROUP]
        odq_ref[i1] = odq[GROUP:]
        return 0

    lax.fori_loop(0, n_query // 2, pair_step, 0)

    for piece in range(pieces):

        def give(i, _, piece=piece):
            dkv_refs[piece][i] = acc[group_rows(tab[piece * per_piece + i]), :].astype(BF16)
            return 0

        lax.fori_loop(0, per_piece, give, 0, unroll=4)


def attention(tab, qd, kvs):
    pieces = len(kvs)
    n_query = qd.shape[0]
    n_key = pieces * kvs[0].shape[0] * GROUP
    blocks = 1024
    run = jax.ShapeDtypeStruct(kvs[0].shape, BF16)
    outs = pl.pallas_call(
        functools.partial(attention_kernel, blocks, pieces, n_query),
        out_shape=[jax.ShapeDtypeStruct(qd.shape, BF16)] + [run] * pieces,
        in_specs=[IN_SMEM] + [IN_VMEM] * (1 + pieces),
        out_specs=[IN_VMEM] * (1 + pieces),
        scratch_shapes=[
            pltpu.VMEM((n_key, 128), BF16),
            pltpu.VMEM((128, n_key), BF16),
            pltpu.VMEM((n_key, 2 * GROUP), F32),
            pltpu.VMEM((n_key, 128), F32),
        ],
        compiler_params=params(),
        name="attention",
    )(tab, qd, *kvs)
    return outs[0], outs[1:]


class Place:
    def __init__(self, n_seq, n_blk):
        self.n_seq, self.n_blk = n_seq, n_blk
        self.n_low = n_blk // HEAD_GROUPS
        self.n_rest = n_blk // 4
        self.s = lax.axis_index("seq")
        self.b = lax.axis_index("blk")
        self.core = self.b % 2
        self.x = (self.b // 2) % 2
        self.rest = self.b // 4
        self.hi = self.b // self.n_low

    def flip(self, bit):
        step = 1 << bit
        return (self.s, self.b + step - 2 * step * ((self.b // step) % 2))

    def to_seq(self):
        return ((self.s + 1) % self.n_seq, self.b)

    def to_rest(self, by):
        return (self.s, ((self.rest + by) % self.n_rest) * 4 + self.b % 4)

    def to_group(self, by):
        return (self.s, ((self.hi + by) % HEAD_GROUPS) * self.n_low + self.b % self.n_low)

    def partners(self):
        found = [self.flip(bit) for bit in range(self.n_low.bit_length() - 1)]
        found += [self.to_seq()]
        found += [self.to_rest(by) for by in range(1, self.n_rest)]
        if self.n_low != 4:
            found += [self.to_group(by) for by in range(1, HEAD_GROUPS)]
        return found

    def meet(self):
        barrier = pltpu.get_barrier_semaphore()
        partners = self.partners()
        for device in partners:
            pl.semaphore_signal(
                barrier, inc=1, device_id=device, device_id_type=pl.DeviceIdType.MESH
            )
        pl.semaphore_wait(barrier, len(partners))


class Wires:
    def __init__(self, sends, recvs):
        self.sends, self.recvs, self.used = sends, recvs, 0

    def copy(self, src, dst, device):
        at = self.used
        self.used += 1
        return pltpu.make_async_remote_copy(
            src_ref=src,
            dst_ref=dst,
            send_sem=self.sends.at[at],
            recv_sem=self.recvs.at[at],
            device_id=device,
            device_id_type=pl.DeviceIdType.MESH,
        )


def add_rows(dst, dst_at, others, count, out=None, out_at=0, lanes=slice(None), got_lanes=slice(None)):
    block = 16
    for size in (96, 64, 48, 32):
        if count % size == 0:
            block = size
            break
    out = dst if out is None else out

    def step(i, _):
        total = dst[pl.ds(pl.multiple_of(dst_at + i * block, 16), block), lanes].astype(F32)
        for ref, start in others:
            rows = pl.ds(pl.multiple_of(start + i * block, 16), block)
            total = total + ref[rows, got_lanes].astype(F32)
        out[pl.ds(pl.multiple_of(out_at + i * block, 16), block), lanes] = total.astype(BF16)
        return 0

    lax.fori_loop(0, count // block, step, 0)


def unit_copies(n_rest):
    return 2 * (2 + n_rest - 1) + 1


class Unit:
    def __init__(self, place, wires, data, base, size, order, got1, got2, got3, out, final, final_base, local):
        pairs = {"x": (place.x, place.flip(1)), "y": (place.s, place.to_seq())}
        (self.bit1, self.dev1), (self.bit2, self.dev2) = pairs[order[0]], pairs[order[1]]
        self.place, self.data, self.out = place, data, out
        self.base, self.size = base, size
        self.h, self.q = size // 2, size // 4
        n = place.n_rest
        self.cuts = 1 if (self.q // n) % 16 == 0 else 2
        self.e = self.q * self.cuts // n
        self.w = data.shape[1] // self.cuts
        self.base1 = base + self.bit1 * self.h
        self.base2 = self.base1 + self.bit2 * self.q
        self.got1, self.got2, self.got3 = got1, got2, got3
        self.fetch = None
        if local is not None:
            kept = pl.ds(pl.multiple_of(self.base1, 16), self.h)
            self.fetch = pltpu.make_async_copy(data.at[kept], out.at[kept], local)
        z = place.rest

        def cell(ref, start, index):
            at = pl.multiple_of(start + (index // self.cuts) * self.e, 16)
            if self.cuts == 1:
                return ref.at[pl.ds(at, self.e)]
            return ref.at[
                pl.ds(at, self.e), pl.ds(pl.multiple_of((index % self.cuts) * self.w, 128), self.w)
            ]

        def landing(by):
            slot = pl.ds((by - 1) * self.e, self.e)
            return got3.at[slot] if self.cuts == 1 else got3.at[slot, pl.ds(0, self.w)]

        def rows(ref, start, count):
            return ref.at[pl.ds(pl.multiple_of(start, 16), count)]

        self.rs1 = [wires.copy(rows(data, base + (1 - self.bit1) * self.h, self.h), got1, self.dev1)]
        self.rs2 = [wires.copy(rows(got1, (1 - self.bit2) * self.q, self.q), got2, self.dev2)]
        self.rs3 = [
            wires.copy(cell(got2, 0, (z + by) % n), landing(by), place.to_rest(by))
            for by in range(1, n)
        ]
        self.ag3 = [
            wires.copy(cell(out, self.base2, z), cell(out, self.base2, z), place.to_rest(by))
            for by in range(1, n)
        ]
        self.ag2 = [wires.copy(rows(out, self.base2, self.q), rows(out, self.base2, self.q), self.dev2)]
        self.ag1 = [wires.copy(rows(out, self.base1, self.h), rows(out, self.base1, self.h), self.dev1)]
        self.agc = [
            wires.copy(
                rows(out, base, size),
                final.at[place.core, pl.ds(final_base, size)],
                place.flip(0),
            )
        ]
        self.sent = []

    def start(self, copies):
        for copy in copies:
            copy.start()
        self.sent = self.sent + copies

    def arrive(self, copies):
        for copy in copies:
            copy.wait_recv()

    def stage0(self):
        self.start(self.rs1)
        if self.fetch is not None:
            self.fetch.start()

    def stage1(self):
        self.arrive(self.rs1)
        for copy in self.rs1:
            copy.wait_send()
        self.sent = [copy for copy in self.sent if not any(copy is gone for gone in self.rs1)]
        if self.fetch is not None:
            self.fetch.wait()
        add_rows(self.got1, 0, [(self.data if self.fetch is None else self.out, self.base1)], self.h)
        self.start(self.rs2)

    def stage2(self):
        self.arrive(self.rs2)
        add_rows(self.got2, 0, [(self.got1, self.bit2 * self.q)], self.q)
        self.start(self.rs3)

    def stage3(self):
        self.arrive(self.rs3)
        others = [(self.got3, k * self.e) for k in range(self.place.n_rest - 1)]
        z = self.place.rest
        at = (z // self.cuts) * self.e
        lanes = got_lanes = slice(None)
        if self.cuts > 1:
            lanes = pl.ds(pl.multiple_of((z % self.cuts) * self.w, 128), self.w)
            got_lanes = pl.ds(0, self.w)
        add_rows(self.got2, at, others, self.e, self.out, self.base2 + at, lanes, got_lanes)
        self.start(self.ag3)

    def stage4(self):
        self.arrive(self.ag3)
        self.start(self.ag2)

    def stage5(self):
        self.arrive(self.ag2)
        self.start(self.ag1)

    def stage6(self):
        self.arrive(self.ag1)
        self.start(self.agc)

    def finish(self):
        self.arrive(self.agc)
        for copy in self.sent:
            copy.wait_send()


def tail_compute(
    odq, dkv, hi, hid, og, again, mgain, wqkv, wdense, bdense, bout, mout, gnm,
    cosw, sina, sinb, output, input_grad, send, small,
):
    rows = hid[...].astype(F32)
    count, width = rows.shape
    lane = lax.broadcasted_iota(jnp.int32, (count, 128), 1)
    low = lane < HEAD_DIM
    ca, sa, sb = cosw[...], sina[...], sinb[...]

    def turned_back(g):
        return g * ca - pltpu.roll(g, 120, 1) * sa - pltpu.roll(g, 8, 1) * sb

    def head(ref, a):
        at = (a // PER_GROUP - hi + HEAD_GROUPS) % HEAD_GROUPS
        return ref[a % PER_GROUP, at].astype(F32)

    outs, grads = [], [[], [], []]
    for tile in range(HEADS // 2):
        one, two = head(odq, 2 * tile), head(odq, 2 * tile + 1)
        outs.append(jnp.where(low, one, pltpu.roll(two, 64, 1)).astype(BF16))
        grads[0].append(turned_back(jnp.where(low, pltpu.roll(one, 64, 1), two)).astype(BF16))
        one, two = head(dkv, 2 * tile), head(dkv, 2 * tile + 1)
        grads[1].append(
            turned_back(jnp.where(low, one, pltpu.roll(two, 64, 1))).astype(BF16)
        )
        grads[2].append(jnp.where(low, pltpu.roll(one, 64, 1), two).astype(BF16))
    att = jnp.concatenate(outs, axis=1)
    dmixed = jnp.concatenate(grads[0] + grads[1] + grads[2], axis=1)
    half_m, half_a = dmixed.shape[1] // 2, width // 2
    for side in range(2):
        send[side, :, :half_m] = dmixed[:, side * half_m : (side + 1) * half_m]
        send[side, :, half_m:] = att[:, side * half_a : (side + 1) * half_a]
    branch = mm(att, wdense[...]) + bdense[...].astype(F32)
    output[...] = (rows + branch + (mout + bout[...].astype(F32))).astype(BF16)
    gna = mm_nt(dmixed, wqkv[...])
    xhat, scale = normalise(rows)
    cot = og[...].astype(F32)
    input_grad[...] = (
        cot
        + norm_back(gna, xhat, scale, again[...].astype(F32))
        + norm_back(gnm, xhat, scale, mgain[...].astype(F32))
    ).astype(BF16)
    small[0:1, :] = jnp.sum(gna * xhat, axis=0, keepdims=True)
    small[1:2, :] = jnp.sum(gna, axis=0, keepdims=True)
    small[2:3, :] = jnp.sum(gnm * xhat, axis=0, keepdims=True)
    small[3:4, :] = jnp.sum(gnm, axis=0, keepdims=True)
    for part in range(3):
        cols = dmixed[:, part * width : (part + 1) * width].astype(F32)
        small[4 + part : 5 + part, :] = jnp.sum(cols, axis=0, keepdims=True)
    small[7:8, :] = jnp.sum(cot, axis=0, keepdims=True)


def weight_compute(own, other, normed, og, grads):
    half_m = own.shape[1] * 3 // 4
    both = jnp.concatenate([own, other], axis=0)
    grads[0:half_m, :] = mm_tn(both[:, :half_m], normed[...]).astype(BF16)
    grads[half_m:, :] = mm_tn(both[:, half_m:], og[...]).astype(BF16)


def finish_kernel(
    n_seq, n_blk, units1, units2, pieces,
    odq0, odq1, odq2, *refs,
):
    dkvs = [refs[j * pieces : (j + 1) * pieces] for j in range(PER_GROUP)]
    (
        grads1, out_part, gn_part, hid, og, og2, normed2, bins, again, mgain, wqkv, wdense, bdense, bout,
        cosw, sina, sinb,
        output, input_grad, small_out, final,
        odq_all, dkv_all, dkv_got, mout_got, gn_got, send, other, grads2, small, small_got,
        got1, got2, got3, out1, out2, sends, recvs, local_sem,
    ) = refs[PER_GROUP * pieces :]
    place = Place(n_seq, n_blk)
    wires = Wires(sends, recvs)
    odqs = (odq0, odq1, odq2)
    tokens, width = hid.shape
    n_rest = place.n_rest
    rows1 = grads1.shape[0]
    place.meet()
    sent = []

    def go(copy):
        copy.start()
        sent.append(copy)
        return copy

    mout_copy = go(wires.copy(out_part.at[pl.ds(tokens, tokens)], mout_got, place.flip(0)))
    gn_copy = go(wires.copy(gn_part.at[pl.ds(tokens, tokens)], gn_got, place.flip(0)))
    low_bits = place.n_low.bit_length() - 1
    stage_copies = []
    for j in range(PER_GROUP):
        half = pieces // 2
        stage_copies.append([
            go(wires.copy(dkvs[j][half + i], dkv_got.at[j, i], place.flip(0))) for i in range(half)
        ])
    home = []
    for j in range(PER_GROUP):
        for by in range(1, HEAD_GROUPS):
            home.append(go(wires.copy(odqs[j].at[by], odq_all.at[j, by], place.to_group(HEAD_GROUPS - by))))
    units = []
    at = 0
    for base, size, order in units1:
        units.append(Unit(
            place, wires, grads1, base, size, order,
            got1.at[pl.ds(at // 2, size // 2)], got2.at[pl.ds(at // 4, size // 4)],
            got3.at[pl.ds(at // 2, size // 2)], out1, final, base, local_sem.at[2 + len(units)],
        ))
        at += size
    units_b = []
    for base, size, order in units2:
        units_b.append(Unit(
            place, wires, grads2, base, size, order,
            got1.at[pl.ds(at // 2, size // 2)], got2.at[pl.ds(at // 4, size // 4)],
            got3.at[pl.ds(at // 2, size // 2)], out2, final, rows1 + base, None,
        ))
        at += size
    for unit in units:
        unit.stage0()

    slot = 0
    half = pieces // 2
    for bit in range(low_bits):
        after = slot + half
        for j in range(PER_GROUP):
            for copy in stage_copies[j]:
                copy.wait_recv()
            for i in range(half):
                mine = dkvs[j][i][...] if bit == 0 else dkv_got[j, slot - 2 * half + i]
                dkv_got[j, slot + i] = (mine.astype(F32) + dkv_got[j, slot + i].astype(F32)).astype(BF16)
            if half > 1:
                stage_copies[j] = [
                    go(wires.copy(dkv_got.at[j, slot + half // 2 + i], dkv_got.at[j, after + i], place.flip(bit + 1)))
                    for i in range(half // 2)
                ]
            else:
                for by in range(1, HEAD_GROUPS):
                    home.append(go(wires.copy(
                        dkv_got.at[j, slot, by], dkv_all.at[j, by], place.to_group(HEAD_GROUPS - by)
                    )))
                dkv_all[j, 0] = dkv_got[j, slot, 0]
        slot = after
        half //= 2
    for j in range(PER_GROUP):
        odq_all[j, 0] = odqs[j][0]
    for unit in units:
        unit.stage1()
    for copy in home:
        copy.wait_recv()
    mout_copy.wait_recv()
    gn_copy.wait_recv()
    mout = out_part[0:tokens, :] + mout_got[...]
    gnm = gn_part[0:tokens, :] + gn_got[...]
    tail_compute(
        odq_all, dkv_all, place.hi, hid, og, again, mgain, wqkv, wdense, bdense, bout, mout, gnm,
        cosw, sina, sinb, output, input_grad, send, small,
    )
    other_copy = go(wires.copy(send.at[1 - place.core], other, place.flip(0)))
    for unit in units:
        unit.stage2()
    other_copy.wait_recv()
    weight_compute(send[place.core], other[...], normed2, og2, grads2)
    for unit in units_b:
        unit.stage0()
    small[8:, :] = bins[...]
    for unit in units:
        unit.stage3()
    for unit in units_b:
        unit.stage1()
    order = [[place.flip(0)], [place.flip(1)], [place.to_seq()], [place.to_rest(by) for by in range(1, n_rest)]]
    slot = 0
    for devices in order:
        copies = [wires.copy(small, small_got.at[slot + i], device) for i, device in enumerate(devices)]
        for copy in copies:
            copy.start()
        for copy in copies:
            copy.wait()
        total = small[...]
        for i in range(len(devices)):
            total = total + small_got[slot + i]
        small[...] = total
        slot += len(devices)
    small_out[...] = small[...]
    for unit in units:
        unit.stage4()
    for unit in units_b:
        unit.stage2()
    for unit in units:
        unit.stage5()
    for unit in units_b:
        unit.stage3()
    for unit in units:
        unit.stage6()
    for unit in units_b:
        unit.stage4()
    for unit in units_b:
        unit.stage5()
    for unit in units_b:
        unit.stage6()
    keep1 = pltpu.make_async_copy(out1, final.at[place.core, pl.ds(0, rows1)], local_sem.at[0])
    keep2 = pltpu.make_async_copy(out2, final.at[place.core, pl.ds(rows1, grads2.shape[0])], local_sem.at[1])
    keep1.start()
    keep2.start()
    for unit in units + units_b:
        unit.finish()
    for copy in sent:
        copy.wait_send()
    keep1.wait()
    keep2.wait()


def finish(mesh, odqs, dkvs, grads1, out_part, gn_part, hid, og, og2, normed2, bins, again, mgain, wqkv, wdense, bdense, bout, tables):
    n_seq, n_blk = mesh.shape["seq"], mesh.shape["blk"]
    n_rest = n_blk // 4
    tokens, width = hid.shape
    pieces = len(dkvs[0])
    rows1, rows2 = grads1.shape[0], 2 * width
    fine = (rows1 // 4) % (4 * n_rest * 16) == 0
    parts = 4 if fine else 2
    units1 = [(i * rows1 // parts, rows1 // parts, "xy" if 2 * i < parts else "yx") for i in range(parts)]
    parts = 2 if fine else 1
    units2 = [(i * rows2 // parts, rows2 // parts, "xy" if 2 * i < parts else "yx") for i in range(parts)]
    total = rows1 + rows2
    copies = (len(units1) + len(units2)) * unit_copies(n_rest)
    copies += 3 + PER_GROUP * (2 * (HEAD_GROUPS - 1) + pieces - 1) + 3 + n_rest - 1
    line = (HEAD_GROUPS, tokens, 128)
    n_small = 8 + bins.shape[0]
    inputs = list(odqs) + [p for d in dkvs for p in d] + [
        grads1, out_part, gn_part, hid, og, og2, normed2, bins, again, mgain, wqkv, wdense, bdense, bout, *tables,
    ]
    return pl.pallas_call(
        functools.partial(finish_kernel, n_seq, n_blk, units1, units2, pieces),
        out_shape=[
            jax.ShapeDtypeStruct((tokens, width), BF16),
            jax.ShapeDtypeStruct((tokens, width), BF16),
            jax.ShapeDtypeStruct((n_small, width), F32),
            jax.ShapeDtypeStruct((2, total, width), BF16),
        ],
        in_specs=[pl.BlockSpec(memory_space=pl.ANY) if v is grads1 else IN_VMEM for v in inputs],
        out_specs=[IN_VMEM] * 3 + [pl.BlockSpec(memory_space=pl.ANY)],
        scratch_shapes=[
            pltpu.VMEM((PER_GROUP,) + line, BF16),
            pltpu.VMEM((PER_GROUP,) + line, BF16),
            pltpu.VMEM((PER_GROUP, pieces - 1) + line, BF16),
            pltpu.VMEM((tokens, width), F32),
            pltpu.VMEM((tokens, width), F32),
            pltpu.VMEM((2, tokens, 2 * width), BF16),
            pltpu.VMEM((tokens, 2 * width), BF16),
            pltpu.VMEM((rows2, width), BF16),
            pltpu.VMEM((n_small, width), F32),
            pltpu.VMEM((3 + n_rest - 1, n_small, width), F32),
            pltpu.VMEM((total // 2, width), BF16),
            pltpu.VMEM((total // 4, width), BF16),
            pltpu.VMEM((total // 2, width), BF16),
            pltpu.VMEM((rows1, width), BF16),
            pltpu.VMEM((rows2, width), BF16),
            pltpu.SemaphoreType.DMA((copies,)),
            pltpu.SemaphoreType.DMA((copies,)),
            pltpu.SemaphoreType.DMA((2 + len(units1),)),
        ],
        compiler_params=pltpu.CompilerParams(
            vmem_limit_bytes=VMEM_BYTES, collective_id=1, has_side_effects=True
        ),
        name="finish",
    )(*inputs)


def expand_kernel(marks, block, *outs):
    step = pl.program_id(0)
    for out, (first, last, turn) in zip(outs, marks):

        @pl.when((step >= first) & (step < last))
        def _(out=out, turn=turn):
            rows = block[0].astype(F32)
            out[...] = rows.T if turn else rows


def expand(final, sizes):
    width = final.shape[2]
    block = width // 2
    marks, specs, shapes, firsts = [], [], [], []
    first = offset = 0
    for rows, turn in sizes:
        each = rows // block
        marks.append((first, first + 2 * each, turn))
        firsts.append((first, each, offset))

        def at(i, first=first, count=2 * each):
            return jnp.clip(i - first, 0, count - 1)

        if turn:
            specs.append(pl.BlockSpec((width, block), lambda i, at=at: (0, at(i))))
            shapes.append(jax.ShapeDtypeStruct((width, 2 * rows), F32))
        else:
            specs.append(pl.BlockSpec((block, width), lambda i, at=at: (at(i), 0)))
            shapes.append(jax.ShapeDtypeStruct((2 * rows, width), F32))
        first += 2 * each
        offset += each

    def source(i):
        core, row = 0, 0
        for begin, each, offset in firsts:
            here = (i >= begin) & (i < begin + 2 * each)
            core = jnp.where(here, (i - begin) // each, core)
            row = jnp.where(here, offset + (i - begin) % each, row)
        return (core, row, 0)

    return pl.pallas_call(
        functools.partial(expand_kernel, marks),
        grid=(first,),
        in_specs=[pl.BlockSpec((1, block, width), source)],
        out_specs=specs,
        out_shape=shapes,
        compiler_params=params(),
        name="expand",
    )(final)


def half_rows(d):
    return pl.ds(pl.multiple_of(d * GROUP, GROUP), GROUP)


class Attention:
    def __init__(self, lines, devices, flags, kk, vv, kkt, vvt, sb, acc):
        self.lines, self.devices, self.flags = lines, devices, flags
        self.kk, self.vv, self.kkt, self.vvt = kk, vv, kkt, vvt
        self.sb, self.acc = sb, acc
        self.n = devices * GROUP

    def prepare(self, pieces):
        low_lanes = lax.broadcasted_iota(jnp.int32, (GROUP, 128), 1) < HEAD_DIM
        for p, ref in enumerate(pieces):

            def step(r, _, p=p, ref=ref):
                rows = half_rows(p * self.lines + r)
                low, high = ref[r, 0:GROUP, :], ref[r, GROUP : 2 * GROUP, :]
                lowt, hight = low.T, high.T
                low, high = low.astype(F32), high.astype(F32)
                self.kk[rows, :] = jnp.where(low_lanes, low, pltpu.roll(high, 64, 1)).astype(BF16)
                self.vv[rows, :] = jnp.where(low_lanes, pltpu.roll(low, 64, 1), high).astype(BF16)
                self.kkt[0:HEAD_DIM, rows] = lowt[0:HEAD_DIM]
                self.kkt[HEAD_DIM:128, rows] = hight[0:HEAD_DIM]
                self.vvt[0:HEAD_DIM, rows] = lowt[HEAD_DIM:128]
                self.vvt[HEAD_DIM:128, rows] = hight[HEAD_DIM:128]
                self.acc[0, rows, :] = jnp.zeros((GROUP, 128), F32)
                self.acc[1, rows, :] = jnp.zeros((GROUP, 128), F32)
                return 0

            lax.fori_loop(0, self.lines, step, 0, unroll=self.lines)

    def masks(self, i):
        all_flags = self.flags[...].reshape(self.devices, 16, 128)
        mine = all_flags[i : i + 1]
        one, nil = jnp.ones(mine.shape, BF16), jnp.zeros(mine.shape, BF16)
        low, high = [], []
        for d in range(self.devices):
            theirs = all_flags[d : d + 1]
            low.append(one if d == i else jnp.where(theirs < mine, one, nil))
            high.append(nil if d == i else jnp.where(theirs > mine, one, nil))
        return jnp.concatenate(low + [nil], axis=0), jnp.concatenate(high + [one], axis=0)

    def pair(self, first, qd_ref, odq_ref):
        n, blocks = self.n, self.devices + 1
        wide = 2 * GROUP
        lane = lax.broadcasted_iota(jnp.int32, (GROUP, 128), 1)
        krow = lax.broadcasted_iota(jnp.int32, (GROUP, wide), 0)
        qcol = lax.broadcasted_iota(jnp.int32, (GROUP, wide), 1)
        seen = krow <= qcol % GROUP
        sb, kk, vv = self.sb, self.kk, self.vv
        masks, low_t, high_t, keys_w, both_w = [], [], [], [], []
        for slot in range(2):
            masks.append(self.masks(first + slot))
            qd = qd_ref[first + slot]
            qdt = qd.T
            low_t.append(qdt[:, 0:GROUP])
            high_t.append(qdt[:, GROUP:wide])
            low, high = qd[0:GROUP], qd[GROUP:wide]
            zero = jnp.zeros_like(low)
            ql, qh = jnp.where(lane < HEAD_DIM, low, zero), jnp.where(lane < HEAD_DIM, high, zero)
            dl, dh = jnp.where(lane < HEAD_DIM, zero, low), jnp.where(lane < HEAD_DIM, zero, high)
            keys_w.append(jnp.concatenate([jnp.concatenate([ql, qh], axis=1), jnp.concatenate([dl, dh], axis=1)], axis=0))
            both_w.append((qh, dh))
        none = jnp.zeros((128, GROUP), BF16)

        def diagonal(rows):
            own = [jnp.concatenate([low_t[k][rows], high_t[k][rows]], axis=0) for k in range(2)]
            return jnp.concatenate(
                [jnp.concatenate([own[0], none], axis=1), jnp.concatenate([none, own[1]], axis=1)], axis=0
            )

        def highs(rows):
            got = jnp.concatenate([high_t[0][rows], high_t[1][rows]], axis=1)
            return jnp.concatenate([got, jnp.zeros_like(got)], axis=0)

        q_rows, d_rows = slice(0, HEAD_DIM), slice(HEAD_DIM, 128)
        w_score, w_dprob = diagonal(q_rows), diagonal(d_rows)
        h_score, h_dprob = highs(q_rows), highs(d_rows)
        dout_low = jnp.concatenate([low_t[0][d_rows], low_t[1][d_rows]], axis=1).astype(F32)
        dout_high = jnp.concatenate([high_t[0][d_rows], high_t[1][d_rows]], axis=1).astype(F32)
        weights_all = jnp.concatenate([both_w[0][0], both_w[1][0], both_w[0][1], both_w[1][1]], axis=0)
        less = jnp.concatenate([low.astype(F32)[:, 0:8] for low, _ in masks], axis=2)
        low_lanes = lax.broadcasted_iota(jnp.int32, (blocks, 16, 128), 2) < HEAD_DIM

        def rows_seen(held):
            found = []
            for slot, (low, high) in enumerate(masks):
                lanes = jnp.where(low_lanes, low.astype(F32), high.astype(F32)).astype(BF16)
                x = jnp.concatenate([held[...], held[half_rows(first + slot), :]], axis=0)
                x = x.reshape(blocks, GROUP // 16, 16, 128) * lanes[:, None]
                found.append(x.reshape(blocks * GROUP, 128))
            return jnp.concatenate(found, axis=1)

        def columns_seen(held):
            found = []
            for slot, pair in enumerate(masks):
                for half, mask in enumerate(pair):
                    rows = slice(half * HEAD_DIM, half * HEAD_DIM + HEAD_DIM)
                    x = jnp.concatenate([held[rows, :], held[rows, half_rows(first + slot)]], axis=1)
                    line = jnp.concatenate([mask[d] for d in range(blocks)], axis=1)
                    x = x.reshape(HEAD_DIM // 16, 16, blocks * GROUP) * line[None]
                    found.append(x.reshape(HEAD_DIM, blocks * GROUP))
            return jnp.concatenate(found, axis=0)

        own, rest = pl.ds(0, blocks * GROUP), pl.ds(blocks * GROUP, n)

        def cut(x):
            return x.reshape(x.shape[0] // GROUP, GROUP // 8, 8, wide)

        def spread(low, high):
            return jnp.where(less > 0, low, high)[:, None]

        s = cut(mm(rows_seen(kk), w_score))
        hide = cut(jnp.where(seen, 0.0, MASKED))
        left = cut(jnp.where(seen | (qcol >= GROUP), 0.0, MASKED))
        right = cut(jnp.where(seen | (qcol < GROUP), 0.0, MASKED))
        s = [s[:first], s[first : first + 1] + left, s[first + 1 : first + 2] + right, s[first + 2 : -1], s[blocks - 1 :] + hide]
        s = jnp.concatenate([x for x in s if x.shape[0]], axis=0)
        sb[own, :] = s.reshape(blocks * GROUP, wide)
        tops = jnp.max(s, axis=1)
        s = mm(kk[...], h_score)
        sb[rest, :] = s
        top_low = jnp.max(jnp.max(jnp.where(less > 0, tops, MASKED), axis=0), axis=0, keepdims=True)
        top_high = jnp.maximum(
            jnp.max(jnp.where(less > 0, MASKED, tops), axis=0), jnp.max(s.reshape(n // 8, 8, wide), axis=0)
        )
        top_high = jnp.max(top_high, axis=0, keepdims=True)

        e = jnp.exp(cut(sb[own, :]) - spread(top_low, top_high))
        sums = jnp.sum(e, axis=1)
        e = e.reshape(blocks * GROUP, wide)
        sb[own, :] = e
        out = mm(columns_seen(self.vvt), e.astype(BF16))
        e = jnp.exp(sb[rest, :] - top_high)
        sb[rest, :] = e
        out_high = mm(self.vvt[0:HEAD_DIM, :], e.astype(BF16))
        total_low = jnp.sum(jnp.sum(jnp.where(less > 0, sums, 0.0), axis=0), axis=0, keepdims=True)
        total_high = jnp.sum(jnp.where(less > 0, 0.0, sums), axis=0) + jnp.sum(e.reshape(n // 8, 8, wide), axis=0)
        total_high = jnp.sum(total_high, axis=0, keepdims=True)

        def parts(x):
            low = jnp.concatenate([x[0:64, 0:GROUP], x[128:192, GROUP:wide]], axis=1)
            high = jnp.concatenate([x[64:128, 0:GROUP], x[192:256, GROUP:wide]], axis=1)
            return low, high

        yield
        inv_low, inv_high = 1.0 / total_low, 1.0 / total_high
        out_low, more = parts(out)
        out_low, out_high = out_low * inv_low, (out_high + more) * inv_high
        delta_low = jnp.sum(out_low * dout_low, axis=0, keepdims=True)
        delta_high = jnp.sum(out_high * dout_high, axis=0, keepdims=True)

        p = cut(sb[own, :]) * spread(inv_low, inv_high)
        dp = cut(mm(rows_seen(vv), w_dprob))
        ds = (p * (dp - spread(delta_low, delta_high))).reshape(blocks * GROUP, wide).astype(BF16)
        p = p.reshape(blocks * GROUP, wide).astype(BF16)
        dq = mm(columns_seen(self.kkt), ds)
        for slot in range(2):
            cols = slice(slot * GROUP, slot * GROUP + GROUP)
            got = mm(jnp.concatenate([ds[:, cols], p[:, cols]], axis=1), keys_w[slot])
            here = less[:, :, cols][:, None] > 0
            got = got.reshape(blocks, GROUP // 8, 8, wide)
            low = jnp.where(here, got[..., 0:128], 0.0).reshape(blocks * GROUP, 128)
            high = jnp.where(here, 0.0, got[..., 128:256]).reshape(blocks * GROUP, 128)
            self.acc[0] += low[0:n]
            self.acc[1] += high[0:n]
            self.acc[1, half_rows(first + slot), :] += high[n:]
        p = sb[rest, :] * inv_high
        dp = mm(vv[...], h_dprob)
        ds = (p * (dp - delta_high)).astype(BF16)
        self.acc[0] += mm(jnp.concatenate([ds, p.astype(BF16)], axis=1), weights_all)
        dq_low, dq_high = parts(dq)
        dq_high = dq_high + mm(self.kkt[0:HEAD_DIM, :], ds)
        for slot in range(2):
            cols = slice(slot * GROUP, slot * GROUP + GROUP)
            scale = HEAD_DIM**-0.5
            low = jnp.concatenate([out_low[:, cols], dq_low[:, cols] * scale], axis=0).astype(BF16).T
            high = jnp.concatenate([out_high[:, cols], dq_high[:, cols] * scale], axis=0).astype(BF16).T
            odq_ref[first + slot] = jnp.concatenate([low, high], axis=0)

    def give(self, dkv_refs):
        for p, ref in enumerate(dkv_refs):

            def step(r, _, p=p, ref=ref):
                rows = half_rows(p * self.lines + r)
                ref[r, 0:GROUP, :] = self.acc[0, rows, :].astype(BF16)
                ref[r, GROUP : 2 * GROUP, :] = self.acc[1, rows, :].astype(BF16)
                return 0

            lax.fori_loop(0, self.lines, step, 0, unroll=2)


def attention_scratch(lines, devices):
    n = devices * GROUP
    more = n + GROUP
    return [
        pltpu.VMEM((n, 128), BF16),
        pltpu.VMEM((n, 128), BF16),
        pltpu.VMEM((128, n), BF16),
        pltpu.VMEM((128, n), BF16),
        pltpu.VMEM((n + more, 256), F32),
        pltpu.VMEM((2, n, 128), F32),
    ]


class Chain:
    def __init__(self, place, wires, data, base, size, order, got, final, final_base, free, keep):
        pairs = {
            "x": (place.x, place.flip(1)),
            "y": (place.s, place.to_seq()),
            "m": (place.rest % 2, place.flip(2)),
            "f": (place.rest // 2, place.flip(3)),
        }
        self.data, self.got, self.sizes, self.bases, self.bits = data, [], [size], [base], []
        at = 0
        self.down, self.up = [], []
        for level, name in enumerate(order):
            bit, device = pairs[name]
            half = self.sizes[-1] // 2
            got_here = got.at[pl.ds(at, half)]
            at += half
            source, start = (data, base) if level == 0 else (self.got[-1], 0)
            away = pl.ds(pl.multiple_of(start + (1 - bit) * half, 16), half)
            self.down.append(wires.copy(source.at[away], got_here, device))
            self.got.append(got_here)
            self.bits.append(bit)
            self.sizes.append(half)
            self.bases.append(self.bases[-1] + bit * half)
            kept = pl.ds(pl.multiple_of(self.bases[-1], 16), half)
            self.up.append(wires.copy(data.at[kept], data.at[kept], device))
        whole = pl.ds(base, size)
        self.up.insert(0, wires.copy(data.at[whole], final.at[place.core, pl.ds(final_base, size)], place.flip(0)))
        self.depth = len(order)
        self.keep = pltpu.make_async_copy(data.at[whole], final.at[place.core, pl.ds(final_base, size)], keep)
        self.free, self.first = free, pairs[order[0]][1]
        self.sent = []

    def start(self, copy):
        copy.start()
        self.sent.append(copy)

    def stage(self, number):
        depth = self.depth
        if number == 0:
            self.start(self.down[0])
        elif number <= depth:
            level = number - 1
            self.down[level].wait_recv()
            if level == 0:
                self.down[0].wait_send()
                self.sent.pop()
                pl.semaphore_signal(
                    self.free, inc=1, device_id=self.first, device_id_type=pl.DeviceIdType.MESH
                )
            half = self.sizes[number]
            source, start = (self.data, self.bases[0]) if level == 0 else (self.got[level - 1], 0)
            start = start + self.bits[level] * half
            if number < depth:
                add_rows(self.got[level], 0, [(source, start)], half)
                self.start(self.down[number])
            else:
                add_rows(self.got[level], 0, [(source, start)], half, self.data, self.bases[depth])
                self.start(self.up[depth])
        else:
            level = 2 * depth - number + 1
            self.up[level].wait_recv()
            if level == 2:
                pl.semaphore_wait(self.free, 1)
            self.start(self.up[level - 1])
            if level == 1:
                self.keep.start()

    def finish(self):
        self.up[0].wait_recv()
        self.keep.wait()
        for copy in self.sent:
            copy.wait_send()


SCHEDULE = (
    "front", "send0", "mlp0", "u0.0", "u3.0", "mlp1", "mlp2", "u5.0", "send1", "line0", "spread0", "u0.1", "fwd0",
    "u4.0", "u3.1", "send2", "u5.1", "line1", "spread1", "keys0", "a0", "a0", "u0.2", "u4.1", "u5.2", "a0", "fwd1",
    "line2", "u3.2", "u0.3", "spread2", "u5.3", "a0", "u4.2", "u2.0", "keys1", "a1", "u5.4", "u3.3", "a1", "u1.0",
    "fwd2", "a1", "u0.4", "core0", "u5.5", "a1", "u2.1", "u5.6", "u3.4", "keys2", "a2", "u0.5", "core1", "a2",
    "plane0", "u1.1", "u4.3", "u5.7", "u0.6", "u3.5", "a2", "a2", "u2.2", "home0", "u3.6", "plane1", "u4.4", "u1.2",
    "core2", "grad0", "u0.7", "v0.1", "plane2", "home1", "u4.5", "u1.3", "grad1", "v0.2", "v1.1", "u2.3", "home2",
    "u4.6", "part", "u1.4", "v0.3", "v3.1", "v2.1", "u2.4", "grad2", "u1.5", "v0.4", "v3.2", "u4.7", "u1.6", "v0.5",
    "u3.7", "v2.2", "u2.5", "v3.3", "tail", "v4.1", "v3.4", "v5.1", "v2.3", "v0.6", "u2.6", "v1.2", "vec0", "u1.7",
    "v3.5", "v2.4", "u0.8", "v1.3", "v1.4", "u4.8", "u2.7", "v4.2", "u3.8", "v1.5", "v5.2", "v3.6", "v0.7", "v2.5",
    "v4.3", "v5.3", "u5.8", "v5.4", "v1.6", "v2.6", "v4.4", "v3.7", "u1.8", "v5.5", "v4.5", "v4.6", "v5.6", "v2.7",
    "vec1", "v0.8", "u2.8", "v4.7", "v5.7", "v1.7", "v3.8", "v2.8", "vec2", "v4.8", "v5.8", "vec3", "v1.8",
)
FF_CHUNK = 256
ORDERS = ("yxmf", "yxmf", "xymf", "xymf", "yxmf", "yxmf", "yxmf", "xymf", "yxmf", "xymf", "xymf", "yxmf")


def runs_of(positions, n_blk):
    group = positions[0, 0] // GROUP
    mirror = 2 * n_blk - 1 - group
    turn = jnp.full((16, 128), (group - mirror).astype(F32), F32).astype(BF16) > 0
    return jnp.minimum(group, mirror), jnp.broadcast_to(turn[None], (GROUP // 16, 16, 128))


def rotary_rows(low_group, n_blk):
    shape = (2 * GROUP, 2 * HEAD_DIM)
    row = lax.broadcasted_iota(jnp.int32, shape, 0)
    lane = lax.broadcasted_iota(jnp.int32, shape, 1) % HEAD_DIM
    half = ROTARY // 2
    at = jnp.where(row < GROUP, low_group * GROUP + row, (2 * n_blk - 2 - low_group) * GROUP + row)
    inverse = jnp.zeros(shape, F32)
    for i in range(half):
        inverse = jnp.where(lane % half == i, float(np.float32(ROTARY_BASE ** (-2.0 * i / ROTARY))), inverse)
    angles = at.astype(F32) * inverse
    cosine, sine = jnp.cos(angles), jnp.sin(angles)
    return (
        jnp.where(lane < ROTARY, cosine, 1.0),
        jnp.where(lane < half, -sine, 0.0),
        jnp.where((lane >= half) & (lane < ROTARY), sine, 0.0),
    )


def joined_kernel(
    n_seq, n_blk, units1, units2,
    positions, hid, og, again, abias, mgain, mbias, bqkv, bdense, bout, bin_,
    wqkv_hbm, wdense_hbm, win_hbm, wout_hbm,
    output, input_grad, vec_out, final,
    wqkv, wdense, win, wout, cosw, sina, sinb, hid2, og2, normed2, normed_m, qd_msg, kv_msg, qd_line, keys, flags,
    kk, vv, kkt, vvt, sb, acc,
    dkv_got, odq_all, dkv_all, out_part, gn_part, mout_got, gn_got, mine, other, bins,
    grads1, grads2, got, small, small_got, sends, recvs, load_sem, chunk_sem, keep_sem, free_sem,
):
    def row(ref):
        return ref[...].astype(F32).reshape(1, ref.shape[0])

    place = Place(n_seq, n_blk)
    wires = Wires(sends, recvs)
    tokens, width = hid.shape
    n_rest = place.n_rest
    core, hi = place.core, place.hi
    half_ff = win_hbm.shape[1] // 2
    chunks = half_ff // FF_CHUNK
    rows1 = grads1.shape[0]
    pieces = place.n_low
    sent, waiting = [], {}
    todo = {}

    def go(name, src, dst, device):
        copy = wires.copy(src, dst, device)
        copy.start()
        sent.append(copy)
        waiting.setdefault(name, []).append(copy)

    def arrive(name):
        for copy in waiting.pop(name):
            copy.wait_recv()

    loads = [
        pltpu.make_async_copy(wqkv_hbm, wqkv, load_sem.at[0]),
        pltpu.make_async_copy(wdense_hbm, wdense, load_sem.at[1]),
    ]
    for load in loads:
        load.start()

    def chunk_loads(f):
        slot = f % 2
        at = pl.multiple_of(core * half_ff + f * FF_CHUNK, FF_CHUNK)
        return [
            pltpu.make_async_copy(win_hbm.at[:, pl.ds(at, FF_CHUNK)], win.at[slot], chunk_sem.at[0, slot]),
            pltpu.make_async_copy(wout_hbm.at[pl.ds(at, FF_CHUNK), :], wout.at[slot], chunk_sem.at[1, slot]),
        ]

    for f in range(2):
        for load in chunk_loads(f):
            load.start()

    low_group, turned_rows = runs_of(positions, n_blk)
    cut = (GROUP // 16, 16, 128)
    for src, dst in ((hid, hid2), (og, og2)):
        for at in range(0, width, 128):
            cols = slice(at, at + 128)
            one, two = src[0:GROUP, cols].reshape(cut), src[GROUP : 2 * GROUP, cols].reshape(cut)
            dst[0:GROUP, cols] = jnp.where(turned_rows, two, one).reshape(GROUP, 128)
            dst[GROUP : 2 * GROUP, cols] = jnp.where(turned_rows, one, two).reshape(GROUP, 128)
    flags[0, 0] = jnp.full((16, 128), low_group.astype(F32), F32).astype(BF16)
    cosw[...], sina[...], sinb[...] = rotary_rows(low_group, n_blk)
    place.meet()
    for by in range(1, HEAD_GROUPS):
        go("flags", flags.at[0, 0], flags.at[0, by], place.to_group(by))
    for ref in (hid2, og2):
        go("rows", ref.at[pl.ds(0, tokens)], ref.at[pl.ds(tokens, tokens)], place.flip(0))

    lane = lax.broadcasted_iota(jnp.int32, (tokens, 128), 1)
    low = lane < HEAD_DIM

    def front():
        xhat, _ = normalise(hid2[0:tokens, :].astype(F32))
        normed = (xhat * row(again) + row(abias)).astype(BF16)
        for load in loads:
            load.wait()
        mixed = mm(normed, wqkv[...]) + row(bqkv)
        datt = mm_nt(og2[0:tokens, :], wdense[...])
        ca, sa, sb_ = cosw[...], sina[...], sinb[...]

        def turned(u):
            return u * ca + pltpu.roll(u, 120, 1) * sa + pltpu.roll(u, 8, 1) * sb_

        for tile in range(HEADS // 2):
            at = tile * 128
            q = turned(mixed[:, at : at + 128]) * (HEAD_DIM**-0.5)
            k = turned(mixed[:, width + at : width + at + 128])
            v = mixed[:, 2 * width + at : 2 * width + at + 128]
            d = datt[:, at : at + 128]
            for msg, one, two in ((qd_msg, q, d), (kv_msg, k, v)):
                for odd in range(2):
                    head = 2 * tile + odd
                    if odd == 0:
                        packed = jnp.where(low, one, pltpu.roll(two, 64, 1))
                    else:
                        packed = jnp.where(low, pltpu.roll(one, 64, 1), two)
                    msg[head % PER_GROUP, head // PER_GROUP] = packed.astype(BF16)
        arrive("flags")
        go("flag_x", flags.at[0], flags.at[1], place.flip(1))
        go("flag_c", flags.at[0], flags.at[2], place.flip(0))

    def send(j):
        for msg, line, name in ((kv_msg, keys.at[j, 0], "line"), (qd_msg, qd_line.at[j], "query")):
            for by in range(1, HEAD_GROUPS):
                go(name + str(j), msg.at[j, (hi + by) % HEAD_GROUPS], line.at[by], place.to_group(by))
        keys[j, 0, 0] = kv_msg[j, hi]
        qd_line[j, 0] = qd_msg[j, hi]

    def mlp_group(g):
        if g == 0:
            arrive("rows")
            xhat, _ = normalise(hid2[...].astype(F32))
            normed_m[...] = (xhat * row(mgain) + row(mbias)).astype(BF16)
            normed2[...] = (xhat * row(again) + row(abias)).astype(BF16)
            out_part[...] = jnp.zeros_like(out_part)
            gn_part[...] = jnp.zeros_like(gn_part)
        per = chunks // 3

        def step(f, _):
            slot = f % 2
            for load in chunk_loads(f):
                load.wait()
            x, w1, w2 = normed_m[...], win[slot], wout[slot]
            at = pl.multiple_of(f * FF_CHUNK, FF_CHUNK)
            bias_at = pl.ds(pl.multiple_of(core * half_ff + f * FF_CHUNK, FF_CHUNK), FF_CHUNK)
            inner = mm(x, w1) + bin_[bias_at].astype(F32).reshape(1, FF_CHUNK)
            cdf = 0.5 * (1.0 + lax.erf(inner * (0.5**0.5)))
            act = (inner * cdf).astype(BF16)
            pdf = jnp.exp(-0.5 * inner * inner) * (0.5 * 2.0**0.5 * 3.141592653589793**-0.5)
            gact = mm_nt(og2[...], w2)
            ginner = (gact * (cdf + inner * pdf)).astype(BF16)
            bins[0:1, pl.ds(at, FF_CHUNK)] = jnp.sum(ginner.astype(F32), axis=0, keepdims=True)
            grads1[pl.ds(at, FF_CHUNK), :] = mm_tn(ginner, x).astype(BF16)
            grads1[pl.ds(pl.multiple_of(half_ff + at, FF_CHUNK), FF_CHUNK), :] = mm_tn(act, og2[...]).astype(BF16)
            out_part[...] += mm(act, w2)
            gn_part[...] += mm_nt(ginner, w1)

            @pl.when(f + 2 < chunks)
            def _():
                for load in chunk_loads(f + 2):
                    load.start()

            return 0

        lax.fori_loop(g * per, (g + 1) * per, step, 0)

    def part():
        go("part", out_part.at[pl.ds(tokens, tokens)], mout_got, place.flip(0))
        go("part", gn_part.at[pl.ds(tokens, tokens)], gn_got, place.flip(0))

    def spread(j):
        go("x" + str(j), keys.at[j, 0], keys.at[j, 1], place.flip(1))
        go("c" + str(j), keys.at[j, 0], keys.at[j, 2], place.flip(0))

    def forward(j):
        arrive("x" + str(j))
        go("c" + str(j), keys.at[j, 1], keys.at[j, 3], place.flip(0))
        if j == 0:
            arrive("flag_x")
            go("flag_c", flags.at[1], flags.at[3], place.flip(0))

    def keys_there(j):
        arrive("c" + str(j))
        arrive("query" + str(j))
        if j == 0:
            arrive("flag_c")

    attention = Attention(HEAD_GROUPS, HEAD_GROUPS * pieces, flags, kk, vv, kkt, vvt, sb, acc)

    def attend(j):
        sources = [keys.at[j, p] for p in range(pieces)]
        attention.prepare(sources)
        for first in range(0, HEAD_GROUPS, 2):
            yield from attention.pair(first, qd_line.at[j], qd_line.at[j])
            if first + 2 < HEAD_GROUPS:
                yield
        for copy in leaving[j]:
            copy.wait_send()
        attention.give(sources)
        for by in range(1, HEAD_GROUPS):
            go("home" + str(j), qd_line.at[j, by], odq_all.at[j, by], place.to_group(HEAD_GROUPS - by))
        for i in range(2):
            go("core" + str(j), keys.at[j, 2 + i], dkv_got.at[j, i], place.flip(0))
        yield

    leaving = {}

    def core_sum(j):
        arrive("core" + str(j))
        for i in range(2):
            dkv_got[j, i] = (keys[j, i].astype(F32) + dkv_got[j, i].astype(F32)).astype(BF16)
        go("plane" + str(j), dkv_got.at[j, 1], dkv_got.at[j, 2], place.flip(1))

    def plane_sum(j):
        arrive("plane" + str(j))
        dkv_got[j, 2] = (dkv_got[j, 0].astype(F32) + dkv_got[j, 2].astype(F32)).astype(BF16)
        for by in range(1, HEAD_GROUPS):
            go("home" + str(j), dkv_got.at[j, 2, by], dkv_all.at[j, by], place.to_group(HEAD_GROUPS - by))
        odq_all[j, 0] = qd_line[j, 0]
        dkv_all[j, 0] = dkv_got[j, 2, 0]

    def home(j):
        arrive("home" + str(j))
        ca, sa, sb_ = cosw[...], sina[...], sinb[...]

        def turned_back(g):
            return g * ca - pltpu.roll(g, 120, 1) * sa - pltpu.roll(g, 8, 1) * sb_

        for g in range(HEAD_GROUPS):
            at = (g - hi + HEAD_GROUPS) % HEAD_GROUPS
            a, b = odq_all[j, at].astype(F32), dkv_all[j, at].astype(F32)
            mine[j, g, :, 0:128] = jnp.where(low, a, turned_back(a)).astype(BF16)
            mine[j, g, :, 128:256] = jnp.where(low, turned_back(b), b).astype(BF16)
        half = HEAD_GROUPS // 2
        go("other" + str(j), mine.at[j, pl.ds((1 - core) * half, half)], other.at[j], place.flip(0))

    def grad(j):
        arrive("other" + str(j))
        half = HEAD_GROUPS // 2
        normed, cot = normed2[...], og2[...]
        from_out = lax.broadcasted_iota(jnp.int32, (128, width), 0) < HEAD_DIM
        for g in range(half):
            both = jnp.concatenate([mine[j, core * half + g], other[j, g]], axis=0)
            base = (j * half + g) * 256
            by_normed = mm_tn(both, normed)
            by_cot = mm_tn(both[:, 0:128], cot)
            grads2[base : base + 128, :] = jnp.where(from_out, by_cot, by_normed[0:128]).astype(BF16)
            grads2[base + 128 : base + 256, :] = by_normed[128:256].astype(BF16)
        per = len(units2) // PER_GROUP
        for unit in second[j * per : (j + 1) * per]:
            unit.stage(0)

    def tail():
        arrive("part")
        rows = hid2[0:tokens, :].astype(F32)

        def parts(a):
            return mine[a % PER_GROUP, a // PER_GROUP].astype(F32)

        outs, grads = [], [[], [], []]
        for tile in range(HEADS // 2):
            one, two = parts(2 * tile), parts(2 * tile + 1)
            a1, b1, a2, b2 = one[:, 0:128], one[:, 128:256], two[:, 0:128], two[:, 128:256]
            outs.append(jnp.where(low, a1, pltpu.roll(a2, 64, 1)).astype(BF16))
            grads[0].append(jnp.where(low, pltpu.roll(a1, 64, 1), a2).astype(BF16))
            grads[1].append(jnp.where(low, b1, pltpu.roll(b2, 64, 1)).astype(BF16))
            grads[2].append(jnp.where(low, pltpu.roll(b1, 64, 1), b2).astype(BF16))
        att = jnp.concatenate(outs, axis=1)
        dmixed = jnp.concatenate(grads[0] + grads[1] + grads[2], axis=1)
        branch = mm(att, wdense[...]) + row(bdense)
        mout = out_part[0:tokens, :] + mout_got[...]
        output[...] = (rows + branch + (mout + row(bout))).astype(BF16)
        gna = mm_nt(dmixed, wqkv[...])
        gnm = gn_part[0:tokens, :] + gn_got[...]
        xhat, scale = normalise(rows)
        cot = og2[0:tokens, :].astype(F32)
        input_grad[...] = (
            cot
            + norm_back(gna, xhat, scale, row(again))
            + norm_back(gnm, xhat, scale, row(mgain))
        ).astype(BF16)
        small[0:1, :] = jnp.sum(gna * xhat, axis=0, keepdims=True)
        small[1:2, :] = jnp.sum(gna, axis=0, keepdims=True)
        small[2:3, :] = jnp.sum(gnm * xhat, axis=0, keepdims=True)
        small[3:4, :] = jnp.sum(gnm, axis=0, keepdims=True)
        for k in range(3):
            cols = dmixed[:, k * width : (k + 1) * width].astype(F32)
            small[4 + k : 5 + k, :] = jnp.sum(cols, axis=0, keepdims=True)
        small[7:8, :] = jnp.sum(cot, axis=0, keepdims=True)
        per = half_ff // width
        for side in range(2):
            here = (1 - core if side == 0 else core).astype(F32)
            for k in range(per):
                at = 8 + side * per + k
                small[at : at + 1, :] = bins[0:1, k * width : (k + 1) * width] * here

    rounds = [
        [place.flip(0)],
        [place.flip(1)],
        [place.to_seq()],
        [place.to_rest(by) for by in range(1, n_rest)],
    ]

    def vec_start(r):
        for i, device in enumerate(rounds[r]):
            go("vec" + str(r), small.at[pl.ds(0, small.shape[0])] if r == 0 else small_got.at[8 + r], small_got.at[2 * r if r < 3 else 5 + i], device)

    def vec(r):
        if r == 0:
            vec_start(0)
            return
        arrive("vec" + str(r - 1))
        source = small[...] if r == 1 else small_got[8 + r - 1]
        small_got[8 + r] = source + small_got[2 * (r - 1)]
        vec_start(r)

    def vec_end():
        arrive("vec3")
        total = small_got[8 + 3]
        for i in range(n_rest - 1):
            total = total + small_got[5 + i]
        vec_out[...] = total

    first, second = [], []
    at = 0
    for found, units, data, offset in ((first, units1, grads1, 0), (second, units2, grads2, rows1)):
        for base, size, order in units:
            found.append(Chain(
                place, wires, data, base, size, order, got.at[pl.ds(at, size)], final, offset + base,
                free_sem.at[len(first) + len(second)], keep_sem.at[len(first) + len(second)],
            ))
            at += size

    todo = {"front": front, "part": part, "tail": tail}
    for g in range(3):
        todo["mlp" + str(g)] = functools.partial(mlp_group, g)
    for r in range(4):
        todo["vec" + str(r)] = functools.partial(vec, r)
    runs = {}
    for j in range(PER_GROUP):
        for name, action in (
            ("send", send), ("line", lambda j: arrive("line" + str(j))), ("spread", spread), ("fwd", forward),
            ("keys", keys_there), ("core", core_sum), ("plane", plane_sum), ("home", home), ("grad", grad),
        ):
            todo[name + str(j)] = functools.partial(action, j)
        runs[j] = attend(j)
        todo["a" + str(j)] = functools.partial(next, runs[j])
    for name, units in (("u", first), ("v", second)):
        for i, unit in enumerate(units):
            for stage in range(2 * unit.depth + 1):
                todo[name + str(i) + "." + str(stage)] = functools.partial(unit.stage, stage)
    for j in range(PER_GROUP):
        leaving[j] = []
    for token in SCHEDULE:
        before = len(sent)
        todo[token]()
        if token[:-1] in ("spread", "fwd"):
            leaving[int(token[-1])] += sent[before:]
            del sent[before:]
    vec_end()
    for unit in first + second:
        if unit.sent:
            unit.finish()
    for copy in sent:
        copy.wait_send()


def joined(mesh, positions, hid, og, again, abias, mgain, mbias, bqkv, bdense, bout, b_in, wqkv, wdense, win, wout):
    n_seq, n_blk = mesh.shape["seq"], mesh.shape["blk"]
    n_low, n_rest = n_blk // HEAD_GROUPS, n_blk // 4
    tokens, width = hid.shape
    half_ff = win.shape[1] // 2
    rows1, rows2 = 2 * half_ff, 2 * width
    size = half_ff // 3
    units1 = [(i * size, size, order) for i, order in enumerate(ORDERS[:6])]
    size = rows2 // 6
    units2 = [(i * size, size, order) for i, order in enumerate(ORDERS[6:])]
    total = rows1 + rows2
    copies = 9 * (len(units1) + len(units2)) + 128
    line = (HEAD_GROUPS, tokens, 128)
    n_small = 8 + 2 * half_ff // width
    devices = HEAD_GROUPS * n_low
    per = PER_GROUP
    inputs = [positions, hid, og, again, abias, mgain, mbias, bqkv, bdense, bout, b_in, wqkv, wdense, win, wout]
    return pl.pallas_call(
        functools.partial(joined_kernel, n_seq, n_blk, units1, units2),
        out_shape=[
            jax.ShapeDtypeStruct((tokens, width), BF16),
            jax.ShapeDtypeStruct((tokens, width), BF16),
            jax.ShapeDtypeStruct((n_small, width), F32),
            jax.ShapeDtypeStruct((2, total, width), BF16),
        ],
        in_specs=[IN_SMEM] + [IN_VMEM] * (len(inputs) - 5) + [pl.BlockSpec(memory_space=pl.ANY)] * 4,
        out_specs=[IN_VMEM] * 3 + [pl.BlockSpec(memory_space=pl.ANY)],
        scratch_shapes=[
            pltpu.VMEM(wqkv.shape, BF16),
            pltpu.VMEM(wdense.shape, BF16),
            pltpu.VMEM((2, width, FF_CHUNK), BF16),
            pltpu.VMEM((2, FF_CHUNK, width), BF16),
            pltpu.VMEM((tokens, 2 * HEAD_DIM), F32),
            pltpu.VMEM((tokens, 2 * HEAD_DIM), F32),
            pltpu.VMEM((tokens, 2 * HEAD_DIM), F32),
            pltpu.VMEM((2 * tokens, width), BF16),
            pltpu.VMEM((2 * tokens, width), BF16),
            pltpu.VMEM((2 * tokens, width), BF16),
            pltpu.VMEM((2 * tokens, width), BF16),
            pltpu.VMEM((per,) + line, BF16),
            pltpu.VMEM((per,) + line, BF16),
            pltpu.VMEM((per,) + line, BF16),
            pltpu.VMEM((per, n_low) + line, BF16),
            pltpu.VMEM((n_low, HEAD_GROUPS, 16, 128), BF16),
            *attention_scratch(HEAD_GROUPS, devices),
            pltpu.VMEM((per, 3) + line, BF16),
            pltpu.VMEM((per,) + line, BF16),
            pltpu.VMEM((per,) + line, BF16),
            pltpu.VMEM((2 * tokens, width), F32),
            pltpu.VMEM((2 * tokens, width), F32),
            pltpu.VMEM((tokens, width), F32),
            pltpu.VMEM((tokens, width), F32),
            pltpu.VMEM((per, HEAD_GROUPS, tokens, 256), BF16),
            pltpu.VMEM((per, HEAD_GROUPS // 2, tokens, 256), BF16),
            pltpu.VMEM((1, half_ff), F32),
            pltpu.VMEM((rows1, width), BF16),
            pltpu.VMEM((rows2, width), BF16),
            pltpu.VMEM((total, width), BF16),
            pltpu.VMEM((n_small, width), F32),
            pltpu.VMEM((12, n_small, width), F32),
            pltpu.SemaphoreType.DMA((copies,)),
            pltpu.SemaphoreType.DMA((copies,)),
            pltpu.SemaphoreType.DMA((2,)),
            pltpu.SemaphoreType.DMA((2, 2)),
            pltpu.SemaphoreType.DMA((len(units1) + len(units2),)),
            pltpu.SemaphoreType.REGULAR((len(units1) + len(units2),)),
        ],
        compiler_params=pltpu.CompilerParams(
            vmem_limit_bytes=VMEM_BYTES, collective_id=2, has_side_effects=True
        ),
        name="joined",
    )(*inputs)


def spread_kernel(
    n_blk, positions, final, vec, out_rows, grad_rows,
    output, input_grad, win, wout, wqkv, wdense, again, abias, mgain, mbias, bqkv, bdense, bin_, bout,
):
    half_ff = win.shape[1] // 2

    @pl.when(pl.program_id(0) == 0)
    def _():
        width = vec.shape[1]
        _, turned_rows = runs_of(positions, n_blk)
        cut = (GROUP // 16, 16, 128)
        for src, dst in ((out_rows, output), (grad_rows, input_grad)):
            for at in range(0, width, 128):
                cols = slice(at, at + 128)
                one, two = src[0:GROUP, cols].reshape(cut), src[GROUP : 2 * GROUP, cols].reshape(cut)
                dst[0:GROUP, cols] = jnp.where(turned_rows, two, one).reshape(GROUP, 128)
                dst[GROUP : 2 * GROUP, cols] = jnp.where(turned_rows, one, two).reshape(GROUP, 128)
        for ref, at in ((again, 0), (abias, 1), (mgain, 2), (mbias, 3), (bqkv, 4), (bdense, 7), (bout, 7), (bin_, 8)):
            for k in range(ref.shape[0] // width):
                ref[k * width : (k + 1) * width] = vec[at + k : at + k + 1, :].reshape(width)

    for core in range(2):
        win[:, core * half_ff : (core + 1) * half_ff] = final[core, 0:half_ff, :].T.astype(F32)
        wout[core * half_ff : (core + 1) * half_ff, :] = final[core, half_ff : 2 * half_ff, :].astype(F32)

    def segment(head, part):
        group, j = head // PER_GROUP, head % PER_GROUP
        half = HEAD_GROUPS // 2
        at = 2 * half_ff + (j * half + group % half) * 256 + part * HEAD_DIM
        return final[group // half, at : at + HEAD_DIM, :]

    width = wdense.shape[0]
    for tile in range(HEADS // 2):
        for part in range(4):
            both = jnp.concatenate([segment(2 * tile, part), segment(2 * tile + 1, part)], axis=0)
            if part == 0:
                wdense[tile * 128 : tile * 128 + 128, :] = both.astype(F32)
            else:
                at = (part - 1) * width + tile * 128
                wqkv[:, at : at + 128] = both.T.astype(F32)


def spread_out(n_blk, positions, final, vec, out_rows, grad_rows, ff):
    total, width = final.shape[1:]
    lanes = 128

    def whole(x):
        return pl.BlockSpec(x.shape, lambda i: (0,) * len(x.shape))

    vectors = [jax.ShapeDtypeStruct((n,), F32) for n in (width, width, width, width, 3 * width, width, ff, width)]
    rows = jax.ShapeDtypeStruct(out_rows.shape, BF16)
    return pl.pallas_call(
        functools.partial(spread_kernel, n_blk),
        grid=(width // lanes,),
        in_specs=[IN_SMEM, pl.BlockSpec((2, total, lanes), lambda i: (0, 0, i))]
        + [whole(x) for x in (vec, out_rows, grad_rows)],
        out_specs=[
            whole(rows),
            whole(rows),
            pl.BlockSpec((lanes, ff), lambda i: (i, 0)),
            pl.BlockSpec((ff, lanes), lambda i: (0, i)),
            pl.BlockSpec((lanes, 3 * width), lambda i: (i, 0)),
            pl.BlockSpec((width, lanes), lambda i: (0, i)),
        ]
        + [whole(x) for x in vectors],
        out_shape=[
            rows,
            rows,
            jax.ShapeDtypeStruct((width, ff), F32),
            jax.ShapeDtypeStruct((ff, width), F32),
            jax.ShapeDtypeStruct((width, 3 * width), F32),
            jax.ShapeDtypeStruct((width, width), F32),
        ]
        + vectors,
        compiler_params=params(),
        name="spread",
    )(positions, final, vec, out_rows, grad_rows)


def rotary_tables(positions):
    lane = jnp.arange(128, dtype=jnp.int32) % HEAD_DIM
    half = ROTARY // 2
    inverse = jnp.power(ROTARY_BASE, -2.0 * (lane % half).astype(F32) / ROTARY)
    angles = positions.astype(F32)[:, None] * inverse[None, :]
    cosine, sine = jnp.cos(angles), jnp.sin(angles)
    lane = lane[None, :]
    return (
        jnp.where(lane < ROTARY, cosine, 1.0),
        jnp.where(lane < half, -sine, 0.0),
        jnp.where((lane >= half) & (lane < ROTARY), sine, 0.0),
    )


def solution(mesh):
    n_seq, n_blk = mesh.shape["seq"], mesh.shape["blk"]
    n_low = n_blk // HEAD_GROUPS
    low_bits = n_low.bit_length() - 1
    def permute(x, target):
        return lax.ppermute(x, "blk", [(b, target(b)) for b in range(n_blk)])

    def to_group(x, by):
        return permute(x, lambda b: ((b // n_low + by) % HEAD_GROUPS) * n_low + b % n_low)

    def flip(x, bit):
        return permute(x, lambda b: b ^ (1 << bit))

    def on_device(
        hidden, positions, ln_attn_gain, ln_attn_bias, ln_mlp_gain, ln_mlp_bias,
        w_qkv, b_qkv, w_dense, b_dense, w_in, b_in, w_out, b_out, out_grad,
    ):
        hid, og, pos = hidden[0], out_grad[0], positions[0]
        again, abias = ln_attn_gain[None], ln_attn_bias[None]
        mgain, mbias = ln_mlp_gain[None], ln_mlp_bias[None]
        tokens, width = hid.shape
        if n_low == 4:
            output, input_grad, vec, final = joined(
                mesh, positions, hid, og, ln_attn_gain, ln_attn_bias, ln_mlp_gain, ln_mlp_bias, b_qkv, b_dense, b_out,
                b_in, w_qkv, w_dense, w_in, w_out,
            )
            output, input_grad, win, wout, wqkv, wdense, *vectors = spread_out(
                n_blk, positions, final, vec, output, input_grad, w_in.shape[1]
            )
            dgain, dbias, dmgain, dmbias, dbqkv, dbdense, dbin, dbout = vectors
            return (
                output[None], input_grad[None], dgain, dbias, dmgain, dmbias,
                wqkv, dbqkv, wdense, dbdense, win, dbin, wout, dbout,
            )
        b = lax.axis_index("blk")
        core = b % 2
        hi = b // n_low
        tables = rotary_tables(pos)

        own_runs = pos[::GROUP] // GROUP
        line_runs = jnp.concatenate(
            [own_runs] + [to_group(own_runs, by) for by in range(1, HEAD_GROUPS)]
        )
        key_runs = [line_runs]
        for bit in range(low_bits - 1, -1, -1):
            key_runs = key_runs + [flip(r, bit) for r in key_runs]
        n_query = line_runs.shape[0]
        rank = jnp.sum(line_runs[:, None] > line_runs[None, :], axis=1)
        slots = rank[None, :] == jnp.arange(n_query)[:, None]
        order = jnp.sum(jnp.where(slots, jnp.arange(n_query)[None, :], 0), axis=1)
        ordered = jnp.sum(jnp.where(slots, line_runs[None, :], 0), axis=1)
        tab = jnp.concatenate(key_runs + [order, ordered]).astype(jnp.int32)

        hid2 = jnp.concatenate([hid, flip(hid, 0)], axis=0)
        og2 = jnp.concatenate([og, flip(og, 0)], axis=0)

        msg = front(hid, og, again, abias, w_qkv, b_qkv[None], w_dense, tables)

        arrived = []
        for j in range(PER_GROUP):
            got = []
            for by in range(HEAD_GROUPS):
                part = lax.dynamic_index_in_dim(msg[j], lax.rem(hi + by, HEAD_GROUPS), 0, False)
                got.append(part if by == 0 else to_group(part, by))
            qd = jnp.stack([g[0] for g in got])
            pieces = [jnp.stack([g[1] for g in got])]
            for bit in range(low_bits - 1, -1, -1):
                pieces = pieces + [flip(piece, bit) for piece in pieces]
            arrived.append((qd, pieces))

        mlp_grads, bin_half, out_part, gn_part, normed2 = mlp(
            core[None].astype(jnp.int32), hid2, og2, again, abias, mgain, mbias, w_in, b_in[None], w_out
        )
        odqs, dkvs = [], []
        line = (HEAD_GROUPS, tokens, 128)
        for j in range(PER_GROUP):
            qd, pieces = arrived[j]
            runs = (HEAD_GROUPS * tokens // GROUP, GROUP, 128)
            odq, dkv = attention(tab, qd.reshape(runs), [p.reshape(runs) for p in pieces])
            odqs.append(odq.reshape(line))
            dkvs.append([d.reshape(line) for d in dkv])

        zero = jnp.zeros_like(bin_half)
        bins = jnp.where(
            core == 0, jnp.concatenate([bin_half, zero], 1), jnp.concatenate([zero, bin_half], 1)
        ).reshape(-1, width)
        half_ff = mlp_grads.shape[1]
        output, input_grad, vec, final = finish(
            mesh, odqs, dkvs, mlp_grads.reshape(2 * half_ff, width), out_part, gn_part, hid, og, og2,
            normed2, bins, again, mgain, w_qkv, w_dense, b_dense[None], b_out[None], tables,
        )
        win, wout, wqkv, wdense = expand(
            final, ((half_ff, True), (half_ff, False), (3 * width // 2, True), (width // 2, False))
        )
        return (
            output[None],
            input_grad[None],
            vec[0],
            vec[1],
            vec[2],
            vec[3],
            wqkv,
            vec[4:7].reshape(-1),
            wdense,
            vec[7],
            win,
            vec[8:].reshape(-1),
            wout,
            vec[7],
        )

    rows = P("seq", "blk", None)
    return jax.shard_map(
        on_device,
        mesh=mesh,
        in_specs=(rows, P("seq", "blk")) + (P(),) * 12 + (rows,),
        out_specs=(rows, rows) + (P(),) * 12,
        check_vma=False,
    )
```

```python
import functools

import jax
import jax.numpy as jnp
import numpy as np
from jax import lax
from jax.experimental import pallas as pl
from jax.experimental.pallas import tpu as pltpu
from jax.sharding import PartitionSpec as P

HEADS = 12
HEAD_DIM = 64
ROTARY = 16
GROUP = 128
HEAD_GROUPS = 4
PER_GROUP = HEADS // HEAD_GROUPS
NORM_EPSILON = 1e-05
ROTARY_BASE = 10000.0
MASKED = -1e30
VMEM_BYTES = 62 * 1024 * 1024

F32 = jnp.float32
BF16 = jnp.bfloat16
IN_VMEM = pl.BlockSpec(memory_space=pltpu.VMEM)
IN_SMEM = pl.BlockSpec(memory_space=pltpu.SMEM)


def mm(a, b):
    return lax.dot_general(a, b, (((1,), (0,)), ((), ())), preferred_element_type=F32)


def mm_nt(a, b):
    return lax.dot_general(a, b, (((1,), (1,)), ((), ())), preferred_element_type=F32)


def mm_tn(a, b):
    return lax.dot_general(a, b, (((0,), (0,)), ((), ())), preferred_element_type=F32)


def normalise(rows):
    centre = rows - jnp.mean(rows, axis=-1, keepdims=True)
    spread = jnp.mean(centre * centre, axis=-1, keepdims=True)
    scale = lax.rsqrt(spread + NORM_EPSILON)
    return centre * scale, scale


def norm_back(grad, xhat, scale, gain):
    eg = grad * gain
    return scale * (
        eg
        - jnp.mean(eg, axis=-1, keepdims=True)
        - xhat * jnp.mean(eg * xhat, axis=-1, keepdims=True)
    )


def params():
    return pltpu.CompilerParams(vmem_limit_bytes=VMEM_BYTES)


def front_kernel(hid, og, gain, bias, wqkv, bqkv, wdense, cosw, sina, sinb, msg):
    rows = hid[...].astype(F32)
    xhat, _ = normalise(rows)
    normed = (xhat * gain[...].astype(F32) + bias[...].astype(F32)).astype(BF16)
    mixed = mm(normed, wqkv[...]) + bqkv[...].astype(F32)
    datt = mm_nt(og[...], wdense[...])
    width = hid.shape[1]
    lane = lax.broadcasted_iota(jnp.int32, (rows.shape[0], 128), 1)
    low = lane < HEAD_DIM
    ca, sa, sb = cosw[...], sina[...], sinb[...]

    def turned(u):
        return u * ca + pltpu.roll(u, 120, 1) * sa + pltpu.roll(u, 8, 1) * sb

    for tile in range(HEADS // 2):
        at = tile * 128
        q = turned(mixed[:, at : at + 128]) * (HEAD_DIM**-0.5)
        k = turned(mixed[:, width + at : width + at + 128])
        v = mixed[:, 2 * width + at : 2 * width + at + 128]
        d = datt[:, at : at + 128]
        for part, (one, two) in enumerate(((q, d), (k, v))):
            for odd in range(2):
                head = 2 * tile + odd
                if odd == 0:
                    packed = jnp.where(low, one, pltpu.roll(two, 64, 1))
                else:
                    packed = jnp.where(low, pltpu.roll(one, 64, 1), two)
                msg[head % PER_GROUP, head // PER_GROUP, part] = packed.astype(BF16)


def front(hid, og, gain, bias, wqkv, bqkv, wdense, tables):
    rows = hid.shape[0]
    return pl.pallas_call(
        front_kernel,
        out_shape=jax.ShapeDtypeStruct((PER_GROUP, HEAD_GROUPS, 2, rows, 128), BF16),
        in_specs=[IN_VMEM] * 10,
        out_specs=IN_VMEM,
        compiler_params=params(),
        name="front",
    )(hid, og, gain, bias, wqkv, bqkv, wdense, *tables)


def mlp_kernel(
    core, hid, og, again, abias, mgain, mbias, win, bin_, wout,
    grads, bin_grad, out_part, gn_part, normed_attn, normed_s,
):
    step = pl.program_id(0)

    @pl.when(step == 0)
    def _():
        xhat, _ = normalise(hid[...].astype(F32))
        normed_s[...] = (xhat * mgain[...].astype(F32) + mbias[...].astype(F32)).astype(BF16)
        normed_attn[...] = (xhat * again[...].astype(F32) + abias[...].astype(F32)).astype(BF16)
        out_part[...] = jnp.zeros_like(out_part)
        gn_part[...] = jnp.zeros_like(gn_part)

    x = normed_s[...]
    w1 = win[...]
    w2 = wout[...]
    inner = mm(x, w1) + bin_[...].astype(F32)
    cdf = 0.5 * (1.0 + lax.erf(inner * (0.5**0.5)))
    act = (inner * cdf).astype(BF16)
    pdf = jnp.exp(-0.5 * inner * inner) * (0.5 * 2.0**0.5 * 3.141592653589793**-0.5)
    gact = mm_nt(og[...], w2)
    ginner = (gact * (cdf + inner * pdf)).astype(BF16)
    bin_grad[...] = jnp.sum(ginner.astype(F32), axis=0, keepdims=True)
    grads[0] = mm_tn(ginner, x).astype(BF16)
    grads[1] = mm_tn(act, og[...]).astype(BF16)
    out_part[...] += mm(act, w2)
    gn_part[...] += mm_nt(ginner, w1)


def mlp(core, hid, og, again, abias, mgain, mbias, win, b_in, wout):
    rows, width = hid.shape
    half = win.shape[1] // 2
    chunk = 512
    steps = half // chunk
    whole = lambda i, c: (0, 0)
    return pl.pallas_call(
        mlp_kernel,
        grid_spec=pltpu.PrefetchScalarGridSpec(
            num_scalar_prefetch=1,
            grid=(steps,),
            in_specs=[
                pl.BlockSpec((rows, width), whole),
                pl.BlockSpec((rows, width), whole),
                pl.BlockSpec((1, width), whole),
                pl.BlockSpec((1, width), whole),
                pl.BlockSpec((1, width), whole),
                pl.BlockSpec((1, width), whole),
                pl.BlockSpec((width, chunk), lambda i, c: (0, c[0] * steps + i)),
                pl.BlockSpec((1, chunk), lambda i, c: (0, c[0] * steps + i)),
                pl.BlockSpec((chunk, width), lambda i, c: (c[0] * steps + i, 0)),
            ],
            out_specs=[
                pl.BlockSpec((2, chunk, width), lambda i, c: (0, i, 0)),
                pl.BlockSpec((1, chunk), lambda i, c: (0, i)),
                pl.BlockSpec((rows, width), whole),
                pl.BlockSpec((rows, width), whole),
                pl.BlockSpec((rows, width), whole),
            ],
            scratch_shapes=[pltpu.VMEM((rows, width), BF16)],
        ),
        out_shape=[
            jax.ShapeDtypeStruct((2, half, width), BF16),
            jax.ShapeDtypeStruct((1, half), F32),
            jax.ShapeDtypeStruct((rows, width), F32),
            jax.ShapeDtypeStruct((rows, width), F32),
            jax.ShapeDtypeStruct((rows, width), BF16),
        ],
        compiler_params=params(),
        name="mlp",
    )(core, hid, og, again, abias, mgain, mbias, win, b_in, wout)


def attention_kernel(blocks, pieces, n_query, *refs):
    tab = refs[0]
    qd_ref = refs[1]
    kv_refs = refs[2 : 2 + pieces]
    odq_ref = refs[2 + pieces]
    dkv_refs = refs[3 + pieces : 3 + 2 * pieces]
    kvs, kvt, sbuf, acc = refs[3 + 2 * pieces :]
    kb_rows = blocks
    per_piece = kv_refs[0].shape[0]
    n_run = pieces * per_piece

    def group_rows(g):
        return pl.ds(pl.multiple_of(g * GROUP, GROUP), GROUP)

    for piece in range(pieces):

        def place(i, _, piece=piece):
            rows = group_rows(tab[piece * per_piece + i])
            blk = kv_refs[piece][i]
            kvs[rows, :] = blk
            kvt[:, rows] = blk.T
            acc[rows, :] = jnp.zeros((GROUP, 128), F32)
            return 0

        lax.fori_loop(0, per_piece, place, 0, unroll=4)

    lane = lax.broadcasted_iota(jnp.int32, (2 * GROUP, 128), 1)
    row = lax.broadcasted_iota(jnp.int32, (128, 2 * GROUP), 0)
    qcol = lax.broadcasted_iota(jnp.int32, (1, 2 * GROUP), 1)
    krow = lax.broadcasted_iota(jnp.int32, (kb_rows, 1), 0)

    def pair_step(pair, _):
        i0 = tab[n_run + 2 * pair]
        i1 = tab[n_run + 2 * pair + 1]
        g0 = tab[n_run + n_query + 2 * pair]
        g1 = tab[n_run + n_query + 2 * pair + 1]
        qd = jnp.concatenate([qd_ref[i0], qd_ref[i1]], axis=0)
        zero = jnp.zeros_like(qd)
        w_keys = jnp.concatenate(
            [jnp.where(lane < HEAD_DIM, qd, zero), jnp.where(lane >= HEAD_DIM, qd, zero)], axis=0
        )
        qdt = qd.T
        zero_t = jnp.zeros_like(qdt)
        w_score = jnp.where(row < HEAD_DIM, qdt, zero_t)
        w_dprob = jnp.where(row >= HEAD_DIM, qdt, zero_t)
        qpos = jnp.where(qcol < GROUP, g0 * GROUP + qcol, (g1 - 1) * GROUP + qcol)
        n_full = (g0 * GROUP) // kb_rows
        n_all = (g1 * GROUP) // kb_rows + 1

        def block_rows(kb):
            return pl.ds(pl.multiple_of(kb * kb_rows, kb_rows), kb_rows)

        def score_step(kb, top, masked):
            rows = block_rows(kb)
            s = mm(kvs[rows, :], w_score)
            if masked:
                s = jnp.where(kb * kb_rows + krow <= qpos, s, MASKED)
            sbuf[rows, :] = s
            return jnp.maximum(top, jnp.max(s.reshape(kb_rows // 8, 8, 2 * GROUP), axis=0))

        top = jnp.full((8, 2 * GROUP), MASKED, F32)
        top = lax.fori_loop(0, n_full, lambda kb, c: score_step(kb, c, False), top)
        top = lax.fori_loop(n_full, n_all, lambda kb, c: score_step(kb, c, True), top)
        top = jnp.max(top, axis=0, keepdims=True)

        def value_step(kb, carry):
            total, out = carry
            rows = block_rows(kb)
            e = jnp.exp(sbuf[rows, :] - top)
            sbuf[rows, :] = e
            total = total + jnp.sum(e.reshape(kb_rows // 8, 8, 2 * GROUP), axis=0)
            return total, out + mm(kvt[HEAD_DIM:128, rows], e.astype(BF16))

        total, out = lax.fori_loop(
            0,
            n_all,
            value_step,
            (jnp.zeros((8, 2 * GROUP), F32), jnp.zeros((HEAD_DIM, 2 * GROUP), F32)),
        )
        inv = 1.0 / jnp.sum(total, axis=0, keepdims=True)
        out = out * inv
        delta = jnp.sum(out * qdt[HEAD_DIM:128, :].astype(F32), axis=0, keepdims=True)

        def grad_step(kb, dq):
            rows = block_rows(kb)
            p = sbuf[rows, :] * inv
            dp = mm(kvs[rows, :], w_dprob)
            ds = (p * (dp - delta)).astype(BF16)
            acc[rows, :] += mm(jnp.concatenate([ds, p.astype(BF16)], axis=1), w_keys)
            return dq + mm(kvt[0:HEAD_DIM, rows], ds)

        dq = lax.fori_loop(0, n_all, grad_step, jnp.zeros((HEAD_DIM, 2 * GROUP), F32))
        odq = jnp.concatenate([out, dq * (HEAD_DIM**-0.5)], axis=0).astype(BF16).T
        odq_ref[i0] = odq[:GROUP]
        odq_ref[i1] = odq[GROUP:]
        return 0

    lax.fori_loop(0, n_query // 2, pair_step, 0)

    for piece in range(pieces):

        def give(i, _, piece=piece):
            dkv_refs[piece][i] = acc[group_rows(tab[piece * per_piece + i]), :].astype(BF16)
            return 0

        lax.fori_loop(0, per_piece, give, 0, unroll=4)


def attention(tab, qd, kvs):
    pieces = len(kvs)
    n_query = qd.shape[0]
    n_key = pieces * kvs[0].shape[0] * GROUP
    blocks = 1024
    run = jax.ShapeDtypeStruct(kvs[0].shape, BF16)
    outs = pl.pallas_call(
        functools.partial(attention_kernel, blocks, pieces, n_query),
        out_shape=[jax.ShapeDtypeStruct(qd.shape, BF16)] + [run] * pieces,
        in_specs=[IN_SMEM] + [IN_VMEM] * (1 + pieces),
        out_specs=[IN_VMEM] * (1 + pieces),
        scratch_shapes=[
            pltpu.VMEM((n_key, 128), BF16),
            pltpu.VMEM((128, n_key), BF16),
            pltpu.VMEM((n_key, 2 * GROUP), F32),
            pltpu.VMEM((n_key, 128), F32),
        ],
        compiler_params=params(),
        name="attention",
    )(tab, qd, *kvs)
    return outs[0], outs[1:]


class Place:
    def __init__(self, n_seq, n_blk):
        self.n_seq, self.n_blk = n_seq, n_blk
        self.n_low = n_blk // HEAD_GROUPS
        self.n_rest = n_blk // 4
        self.s = lax.axis_index("seq")
        self.b = lax.axis_index("blk")
        self.core = self.b % 2
        self.x = (self.b // 2) % 2
        self.rest = self.b // 4
        self.hi = self.b // self.n_low

    def flip(self, bit):
        step = 1 << bit
        return (self.s, self.b + step - 2 * step * ((self.b // step) % 2))

    def to_seq(self):
        return ((self.s + 1) % self.n_seq, self.b)

    def to_rest(self, by):
        return (self.s, ((self.rest + by) % self.n_rest) * 4 + self.b % 4)

    def to_group(self, by):
        return (self.s, ((self.hi + by) % HEAD_GROUPS) * self.n_low + self.b % self.n_low)

    def partners(self):
        found = [self.flip(bit) for bit in range(self.n_low.bit_length() - 1)]
        found += [self.to_seq()]
        found += [self.to_rest(by) for by in range(1, self.n_rest)]
        if self.n_low != 4:
            found += [self.to_group(by) for by in range(1, HEAD_GROUPS)]
        return found

    def meet(self):
        barrier = pltpu.get_barrier_semaphore()
        partners = self.partners()
        for device in partners:
            pl.semaphore_signal(
                barrier, inc=1, device_id=device, device_id_type=pl.DeviceIdType.MESH
            )
        pl.semaphore_wait(barrier, len(partners))


class Wires:
    def __init__(self, sends, recvs):
        self.sends, self.recvs, self.used = sends, recvs, 0

    def copy(self, src, dst, device):
        at = self.used
        self.used += 1
        return pltpu.make_async_remote_copy(
            src_ref=src,
            dst_ref=dst,
            send_sem=self.sends.at[at],
            recv_sem=self.recvs.at[at],
            device_id=device,
            device_id_type=pl.DeviceIdType.MESH,
        )


def add_rows(dst, dst_at, others, count, out=None, out_at=0, lanes=slice(None), got_lanes=slice(None)):
    block = 16
    for size in (96, 64, 48, 32):
        if count % size == 0:
            block = size
            break
    out = dst if out is None else out

    def step(i, _):
        total = dst[pl.ds(pl.multiple_of(dst_at + i * block, 16), block), lanes].astype(F32)
        for ref, start in others:
            rows = pl.ds(pl.multiple_of(start + i * block, 16), block)
            total = total + ref[rows, got_lanes].astype(F32)
        out[pl.ds(pl.multiple_of(out_at + i * block, 16), block), lanes] = total.astype(BF16)
        return 0

    lax.fori_loop(0, count // block, step, 0)


def unit_copies(n_rest):
    return 2 * (2 + n_rest - 1) + 1


class Unit:
    def __init__(self, place, wires, data, base, size, order, got1, got2, got3, out, final, final_base, local):
        pairs = {"x": (place.x, place.flip(1)), "y": (place.s, place.to_seq())}
        (self.bit1, self.dev1), (self.bit2, self.dev2) = pairs[order[0]], pairs[order[1]]
        self.place, self.data, self.out = place, data, out
        self.base, self.size = base, size
        self.h, self.q = size // 2, size // 4
        n = place.n_rest
        self.cuts = 1 if (self.q // n) % 16 == 0 else 2
        self.e = self.q * self.cuts // n
        self.w = data.shape[1] // self.cuts
        self.base1 = base + self.bit1 * self.h
        self.base2 = self.base1 + self.bit2 * self.q
        self.got1, self.got2, self.got3 = got1, got2, got3
        self.fetch = None
        if local is not None:
            kept = pl.ds(pl.multiple_of(self.base1, 16), self.h)
            self.fetch = pltpu.make_async_copy(data.at[kept], out.at[kept], local)
        z = place.rest

        def cell(ref, start, index):
            at = pl.multiple_of(start + (index // self.cuts) * self.e, 16)
            if self.cuts == 1:
                return ref.at[pl.ds(at, self.e)]
            return ref.at[
                pl.ds(at, self.e), pl.ds(pl.multiple_of((index % self.cuts) * self.w, 128), self.w)
            ]

        def landing(by):
            slot = pl.ds((by - 1) * self.e, self.e)
            return got3.at[slot] if self.cuts == 1 else got3.at[slot, pl.ds(0, self.w)]

        def rows(ref, start, count):
            return ref.at[pl.ds(pl.multiple_of(start, 16), count)]

        self.rs1 = [wires.copy(rows(data, base + (1 - self.bit1) * self.h, self.h), got1, self.dev1)]
        self.rs2 = [wires.copy(rows(got1, (1 - self.bit2) * self.q, self.q), got2, self.dev2)]
        self.rs3 = [
            wires.copy(cell(got2, 0, (z + by) % n), landing(by), place.to_rest(by))
            for by in range(1, n)
        ]
        self.ag3 = [
            wires.copy(cell(out, self.base2, z), cell(out, self.base2, z), place.to_rest(by))
            for by in range(1, n)
        ]
        self.ag2 = [wires.copy(rows(out, self.base2, self.q), rows(out, self.base2, self.q), self.dev2)]
        self.ag1 = [wires.copy(rows(out, self.base1, self.h), rows(out, self.base1, self.h), self.dev1)]
        self.agc = [
            wires.copy(
                rows(out, base, size),
                final.at[place.core, pl.ds(final_base, size)],
                place.flip(0),
            )
        ]
        self.sent = []

    def start(self, copies):
        for copy in copies:
            copy.start()
        self.sent = self.sent + copies

    def arrive(self, copies):
        for copy in copies:
            copy.wait_recv()

    def stage0(self):
        self.start(self.rs1)
        if self.fetch is not None:
            self.fetch.start()

    def stage1(self):
        self.arrive(self.rs1)
        for copy in self.rs1:
            copy.wait_send()
        self.sent = [copy for copy in self.sent if not any(copy is gone for gone in self.rs1)]
        if self.fetch is not None:
            self.fetch.wait()
        add_rows(self.got1, 0, [(self.data if self.fetch is None else self.out, self.base1)], self.h)
        self.start(self.rs2)

    def stage2(self):
        self.arrive(self.rs2)
        add_rows(self.got2, 0, [(self.got1, self.bit2 * self.q)], self.q)
        self.start(self.rs3)

    def stage3(self):
        self.arrive(self.rs3)
        others = [(self.got3, k * self.e) for k in range(self.place.n_rest - 1)]
        z = self.place.rest
        at = (z // self.cuts) * self.e
        lanes = got_lanes = slice(None)
        if self.cuts > 1:
            lanes = pl.ds(pl.multiple_of((z % self.cuts) * self.w, 128), self.w)
            got_lanes = pl.ds(0, self.w)
        add_rows(self.got2, at, others, self.e, self.out, self.base2 + at, lanes, got_lanes)
        self.start(self.ag3)

    def stage4(self):
        self.arrive(self.ag3)
        self.start(self.ag2)

    def stage5(self):
        self.arrive(self.ag2)
        self.start(self.ag1)

    def stage6(self):
        self.arrive(self.ag1)
        self.start(self.agc)

    def finish(self):
        self.arrive(self.agc)
        for copy in self.sent:
            copy.wait_send()


def tail_compute(
    odq, dkv, hi, hid, og, again, mgain, wqkv, wdense, bdense, bout, mout, gnm,
    cosw, sina, sinb, output, input_grad, send, small,
):
    rows = hid[...].astype(F32)
    count, width = rows.shape
    lane = lax.broadcasted_iota(jnp.int32, (count, 128), 1)
    low = lane < HEAD_DIM
    ca, sa, sb = cosw[...], sina[...], sinb[...]

    def turned_back(g):
        return g * ca - pltpu.roll(g, 120, 1) * sa - pltpu.roll(g, 8, 1) * sb

    def head(ref, a):
        at = (a // PER_GROUP - hi + HEAD_GROUPS) % HEAD_GROUPS
        return ref[a % PER_GROUP, at].astype(F32)

    outs, grads = [], [[], [], []]
    for tile in range(HEADS // 2):
        one, two = head(odq, 2 * tile), head(odq, 2 * tile + 1)
        outs.append(jnp.where(low, one, pltpu.roll(two, 64, 1)).astype(BF16))
        grads[0].append(turned_back(jnp.where(low, pltpu.roll(one, 64, 1), two)).astype(BF16))
        one, two = head(dkv, 2 * tile), head(dkv, 2 * tile + 1)
        grads[1].append(
            turned_back(jnp.where(low, one, pltpu.roll(two, 64, 1))).astype(BF16)
        )
        grads[2].append(jnp.where(low, pltpu.roll(one, 64, 1), two).astype(BF16))
    att = jnp.concatenate(outs, axis=1)
    dmixed = jnp.concatenate(grads[0] + grads[1] + grads[2], axis=1)
    half_m, half_a = dmixed.shape[1] // 2, width // 2
    for side in range(2):
        send[side, :, :half_m] = dmixed[:, side * half_m : (side + 1) * half_m]
        send[side, :, half_m:] = att[:, side * half_a : (side + 1) * half_a]
    branch = mm(att, wdense[...]) + bdense[...].astype(F32)
    output[...] = (rows + branch + (mout + bout[...].astype(F32))).astype(BF16)
    gna = mm_nt(dmixed, wqkv[...])
    xhat, scale = normalise(rows)
    cot = og[...].astype(F32)
    input_grad[...] = (
        cot
        + norm_back(gna, xhat, scale, again[...].astype(F32))
        + norm_back(gnm, xhat, scale, mgain[...].astype(F32))
    ).astype(BF16)
    small[0:1, :] = jnp.sum(gna * xhat, axis=0, keepdims=True)
    small[1:2, :] = jnp.sum(gna, axis=0, keepdims=True)
    small[2:3, :] = jnp.sum(gnm * xhat, axis=0, keepdims=True)
    small[3:4, :] = jnp.sum(gnm, axis=0, keepdims=True)
    for part in range(3):
        cols = dmixed[:, part * width : (part + 1) * width].astype(F32)
        small[4 + part : 5 + part, :] = jnp.sum(cols, axis=0, keepdims=True)
    small[7:8, :] = jnp.sum(cot, axis=0, keepdims=True)


def weight_compute(own, other, normed, og, grads):
    half_m = own.shape[1] * 3 // 4
    both = jnp.concatenate([own, other], axis=0)
    grads[0:half_m, :] = mm_tn(both[:, :half_m], normed[...]).astype(BF16)
    grads[half_m:, :] = mm_tn(both[:, half_m:], og[...]).astype(BF16)


def finish_kernel(
    n_seq, n_blk, units1, units2, pieces,
    odq0, odq1, odq2, *refs,
):
    dkvs = [refs[j * pieces : (j + 1) * pieces] for j in range(PER_GROUP)]
    (
        grads1, out_part, gn_part, hid, og, og2, normed2, bins, again, mgain, wqkv, wdense, bdense, bout,
        cosw, sina, sinb,
        output, input_grad, small_out, final,
        odq_all, dkv_all, dkv_got, mout_got, gn_got, send, other, grads2, small, small_got,
        got1, got2, got3, out1, out2, sends, recvs, local_sem,
    ) = refs[PER_GROUP * pieces :]
    place = Place(n_seq, n_blk)
    wires = Wires(sends, recvs)
    odqs = (odq0, odq1, odq2)
    tokens, width = hid.shape
    n_rest = place.n_rest
    rows1 = grads1.shape[0]
    place.meet()
    sent = []

    def go(copy):
        copy.start()
        sent.append(copy)
        return copy

    mout_copy = go(wires.copy(out_part.at[pl.ds(tokens, tokens)], mout_got, place.flip(0)))
    gn_copy = go(wires.copy(gn_part.at[pl.ds(tokens, tokens)], gn_got, place.flip(0)))
    low_bits = place.n_low.bit_length() - 1
    stage_copies = []
    for j in range(PER_GROUP):
        half = pieces // 2
        stage_copies.append([
            go(wires.copy(dkvs[j][half + i], dkv_got.at[j, i], place.flip(0))) for i in range(half)
        ])
    home = []
    for j in range(PER_GROUP):
        for by in range(1, HEAD_GROUPS):
            home.append(go(wires.copy(odqs[j].at[by], odq_all.at[j, by], place.to_group(HEAD_GROUPS - by))))
    units = []
    at = 0
    for base, size, order in units1:
        units.append(Unit(
            place, wires, grads1, base, size, order,
            got1.at[pl.ds(at // 2, size // 2)], got2.at[pl.ds(at // 4, size // 4)],
            got3.at[pl.ds(at // 2, size // 2)], out1, final, base, local_sem.at[2 + len(units)],
        ))
        at += size
    units_b = []
    for base, size, order in units2:
        units_b.append(Unit(
            place, wires, grads2, base, size, order,
            got1.at[pl.ds(at // 2, size // 2)], got2.at[pl.ds(at // 4, size // 4)],
            got3.at[pl.ds(at // 2, size // 2)], out2, final, rows1 + base, None,
        ))
        at += size
    for unit in units:
        unit.stage0()

    slot = 0
    half = pieces // 2
    for bit in range(low_bits):
        after = slot + half
        for j in range(PER_GROUP):
            for copy in stage_copies[j]:
                copy.wait_recv()
            for i in range(half):
                mine = dkvs[j][i][...] if bit == 0 else dkv_got[j, slot - 2 * half + i]
                dkv_got[j, slot + i] = (mine.astype(F32) + dkv_got[j, slot + i].astype(F32)).astype(BF16)
            if half > 1:
                stage_copies[j] = [
                    go(wires.copy(dkv_got.at[j, slot + half // 2 + i], dkv_got.at[j, after + i], place.flip(bit + 1)))
                    for i in range(half // 2)
                ]
            else:
                for by in range(1, HEAD_GROUPS):
                    home.append(go(wires.copy(
                        dkv_got.at[j, slot, by], dkv_all.at[j, by], place.to_group(HEAD_GROUPS - by)
                    )))
                dkv_all[j, 0] = dkv_got[j, slot, 0]
        slot = after
        half //= 2
    for j in range(PER_GROUP):
        odq_all[j, 0] = odqs[j][0]
    for unit in units:
        unit.stage1()
    for copy in home:
        copy.wait_recv()
    mout_copy.wait_recv()
    gn_copy.wait_recv()
    mout = out_part[0:tokens, :] + mout_got[...]
    gnm = gn_part[0:tokens, :] + gn_got[...]
    tail_compute(
        odq_all, dkv_all, place.hi, hid, og, again, mgain, wqkv, wdense, bdense, bout, mout, gnm,
        cosw, sina, sinb, output, input_grad, send, small,
    )
    other_copy = go(wires.copy(send.at[1 - place.core], other, place.flip(0)))
    for unit in units:
        unit.stage2()
    other_copy.wait_recv()
    weight_compute(send[place.core], other[...], normed2, og2, grads2)
    for unit in units_b:
        unit.stage0()
    small[8:, :] = bins[...]
    for unit in units:
        unit.stage3()
    for unit in units_b:
        unit.stage1()
    order = [[place.flip(0)], [place.flip(1)], [place.to_seq()], [place.to_rest(by) for by in range(1, n_rest)]]
    slot = 0
    for devices in order:
        copies = [wires.copy(small, small_got.at[slot + i], device) for i, device in enumerate(devices)]
        for copy in copies:
            copy.start()
        for copy in copies:
            copy.wait()
        total = small[...]
        for i in range(len(devices)):
            total = total + small_got[slot + i]
        small[...] = total
        slot += len(devices)
    small_out[...] = small[...]
    for unit in units:
        unit.stage4()
    for unit in units_b:
        unit.stage2()
    for unit in units:
        unit.stage5()
    for unit in units_b:
        unit.stage3()
    for unit in units:
        unit.stage6()
    for unit in units_b:
        unit.stage4()
    for unit in units_b:
        unit.stage5()
    for unit in units_b:
        unit.stage6()
    keep1 = pltpu.make_async_copy(out1, final.at[place.core, pl.ds(0, rows1)], local_sem.at[0])
    keep2 = pltpu.make_async_copy(out2, final.at[place.core, pl.ds(rows1, grads2.shape[0])], local_sem.at[1])
    keep1.start()
    keep2.start()
    for unit in units + units_b:
        unit.finish()
    for copy in sent:
        copy.wait_send()
    keep1.wait()
    keep2.wait()


def finish(mesh, odqs, dkvs, grads1, out_part, gn_part, hid, og, og2, normed2, bins, again, mgain, wqkv, wdense, bdense, bout, tables):
    n_seq, n_blk = mesh.shape["seq"], mesh.shape["blk"]
    n_rest = n_blk // 4
    tokens, width = hid.shape
    pieces = len(dkvs[0])
    rows1, rows2 = grads1.shape[0], 2 * width
    fine = (rows1 // 4) % (4 * n_rest * 16) == 0
    parts = 4 if fine else 2
    units1 = [(i * rows1 // parts, rows1 // parts, "xy" if 2 * i < parts else "yx") for i in range(parts)]
    parts = 2 if fine else 1
    units2 = [(i * rows2 // parts, rows2 // parts, "xy" if 2 * i < parts else "yx") for i in range(parts)]
    total = rows1 + rows2
    copies = (len(units1) + len(units2)) * unit_copies(n_rest)
    copies += 3 + PER_GROUP * (2 * (HEAD_GROUPS - 1) + pieces - 1) + 3 + n_rest - 1
    line = (HEAD_GROUPS, tokens, 128)
    n_small = 8 + bins.shape[0]
    inputs = list(odqs) + [p for d in dkvs for p in d] + [
        grads1, out_part, gn_part, hid, og, og2, normed2, bins, again, mgain, wqkv, wdense, bdense, bout, *tables,
    ]
    return pl.pallas_call(
        functools.partial(finish_kernel, n_seq, n_blk, units1, units2, pieces),
        out_shape=[
            jax.ShapeDtypeStruct((tokens, width), BF16),
            jax.ShapeDtypeStruct((tokens, width), BF16),
            jax.ShapeDtypeStruct((n_small, width), F32),
            jax.ShapeDtypeStruct((2, total, width), BF16),
        ],
        in_specs=[pl.BlockSpec(memory_space=pl.ANY) if v is grads1 else IN_VMEM for v in inputs],
        out_specs=[IN_VMEM] * 3 + [pl.BlockSpec(memory_space=pl.ANY)],
        scratch_shapes=[
            pltpu.VMEM((PER_GROUP,) + line, BF16),
            pltpu.VMEM((PER_GROUP,) + line, BF16),
            pltpu.VMEM((PER_GROUP, pieces - 1) + line, BF16),
            pltpu.VMEM((tokens, width), F32),
            pltpu.VMEM((tokens, width), F32),
            pltpu.VMEM((2, tokens, 2 * width), BF16),
            pltpu.VMEM((tokens, 2 * width), BF16),
            pltpu.VMEM((rows2, width), BF16),
            pltpu.VMEM((n_small, width), F32),
            pltpu.VMEM((3 + n_rest - 1, n_small, width), F32),
            pltpu.VMEM((total // 2, width), BF16),
            pltpu.VMEM((total // 4, width), BF16),
            pltpu.VMEM((total // 2, width), BF16),
            pltpu.VMEM((rows1, width), BF16),
            pltpu.VMEM((rows2, width), BF16),
            pltpu.SemaphoreType.DMA((copies,)),
            pltpu.SemaphoreType.DMA((copies,)),
            pltpu.SemaphoreType.DMA((2 + len(units1),)),
        ],
        compiler_params=pltpu.CompilerParams(
            vmem_limit_bytes=VMEM_BYTES, collective_id=1, has_side_effects=True
        ),
        name="finish",
    )(*inputs)


def expand_kernel(marks, block, *outs):
    step = pl.program_id(0)
    for out, (first, last, turn) in zip(outs, marks):

        @pl.when((step >= first) & (step < last))
        def _(out=out, turn=turn):
            rows = block[0].astype(F32)
            out[...] = rows.T if turn else rows


def expand(final, sizes):
    width = final.shape[2]
    block = width // 2
    marks, specs, shapes, firsts = [], [], [], []
    first = offset = 0
    for rows, turn in sizes:
        each = rows // block
        marks.append((first, first + 2 * each, turn))
        firsts.append((first, each, offset))

        def at(i, first=first, count=2 * each):
            return jnp.clip(i - first, 0, count - 1)

        if turn:
            specs.append(pl.BlockSpec((width, block), lambda i, at=at: (0, at(i))))
            shapes.append(jax.ShapeDtypeStruct((width, 2 * rows), F32))
        else:
            specs.append(pl.BlockSpec((block, width), lambda i, at=at: (at(i), 0)))
            shapes.append(jax.ShapeDtypeStruct((2 * rows, width), F32))
        first += 2 * each
        offset += each

    def source(i):
        core, row = 0, 0
        for begin, each, offset in firsts:
            here = (i >= begin) & (i < begin + 2 * each)
            core = jnp.where(here, (i - begin) // each, core)
            row = jnp.where(here, offset + (i - begin) % each, row)
        return (core, row, 0)

    return pl.pallas_call(
        functools.partial(expand_kernel, marks),
        grid=(first,),
        in_specs=[pl.BlockSpec((1, block, width), source)],
        out_specs=specs,
        out_shape=shapes,
        compiler_params=params(),
        name="expand",
    )(final)


def half_rows(d):
    return pl.ds(pl.multiple_of(d * GROUP, GROUP), GROUP)


class Attention:
    def __init__(self, lines, devices, flags, kk, vv, kkt, vvt, sb, acc):
        self.lines, self.devices, self.flags = lines, devices, flags
        self.kk, self.vv, self.kkt, self.vvt = kk, vv, kkt, vvt
        self.sb, self.acc = sb, acc
        self.n = devices * GROUP

    def prepare(self, pieces):
        low_lanes = lax.broadcasted_iota(jnp.int32, (GROUP, 128), 1) < HEAD_DIM
        for p, ref in enumerate(pieces):

            def step(r, _, p=p, ref=ref):
                rows = half_rows(p * self.lines + r)
                low, high = ref[r, 0:GROUP, :], ref[r, GROUP : 2 * GROUP, :]
                lowt, hight = low.T, high.T
                low, high = low.astype(F32), high.astype(F32)
                self.kk[rows, :] = jnp.where(low_lanes, low, pltpu.roll(high, 64, 1)).astype(BF16)
                self.vv[rows, :] = jnp.where(low_lanes, pltpu.roll(low, 64, 1), high).astype(BF16)
                self.kkt[0:HEAD_DIM, rows] = lowt[0:HEAD_DIM]
                self.kkt[HEAD_DIM:128, rows] = hight[0:HEAD_DIM]
                self.vvt[0:HEAD_DIM, rows] = lowt[HEAD_DIM:128]
                self.vvt[HEAD_DIM:128, rows] = hight[HEAD_DIM:128]
                self.acc[0, rows, :] = jnp.zeros((GROUP, 128), F32)
                self.acc[1, rows, :] = jnp.zeros((GROUP, 128), F32)
                return 0

            lax.fori_loop(0, self.lines, step, 0, unroll=self.lines)

    def masks(self, i):
        all_flags = self.flags[...].reshape(self.devices, 16, 128)
        mine = all_flags[i : i + 1]
        one, nil = jnp.ones(mine.shape, BF16), jnp.zeros(mine.shape, BF16)
        low, high = [], []
        for d in range(self.devices):
            theirs = all_flags[d : d + 1]
            low.append(one if d == i else jnp.where(theirs < mine, one, nil))
            high.append(nil if d == i else jnp.where(theirs > mine, one, nil))
        return jnp.concatenate(low + [nil], axis=0), jnp.concatenate(high + [one], axis=0)

    def pair(self, first, qd_ref, odq_ref):
        n, blocks = self.n, self.devices + 1
        wide = 2 * GROUP
        lane = lax.broadcasted_iota(jnp.int32, (GROUP, 128), 1)
        krow = lax.broadcasted_iota(jnp.int32, (GROUP, wide), 0)
        qcol = lax.broadcasted_iota(jnp.int32, (GROUP, wide), 1)
        seen = krow <= qcol % GROUP
        sb, kk, vv = self.sb, self.kk, self.vv
        masks, low_t, high_t, keys_w, both_w = [], [], [], [], []
        for slot in range(2):
            masks.append(self.masks(first + slot))
            qd = qd_ref[first + slot]
            qdt = qd.T
            low_t.append(qdt[:, 0:GROUP])
            high_t.append(qdt[:, GROUP:wide])
            low, high = qd[0:GROUP], qd[GROUP:wide]
            zero = jnp.zeros_like(low)
            ql, qh = jnp.where(lane < HEAD_DIM, low, zero), jnp.where(lane < HEAD_DIM, high, zero)
            dl, dh = jnp.where(lane < HEAD_DIM, zero, low), jnp.where(lane < HEAD_DIM, zero, high)
            keys_w.append(jnp.concatenate([jnp.concatenate([ql, qh], axis=1), jnp.concatenate([dl, dh], axis=1)], axis=0))
            both_w.append((qh, dh))
        none = jnp.zeros((128, GROUP), BF16)

        def diagonal(rows):
            own = [jnp.concatenate([low_t[k][rows], high_t[k][rows]], axis=0) for k in range(2)]
            return jnp.concatenate(
                [jnp.concatenate([own[0], none], axis=1), jnp.concatenate([none, own[1]], axis=1)], axis=0
            )

        def highs(rows):
            got = jnp.concatenate([high_t[0][rows], high_t[1][rows]], axis=1)
            return jnp.concatenate([got, jnp.zeros_like(got)], axis=0)

        q_rows, d_rows = slice(0, HEAD_DIM), slice(HEAD_DIM, 128)
        w_score, w_dprob = diagonal(q_rows), diagonal(d_rows)
        h_score, h_dprob = highs(q_rows), highs(d_rows)
        dout_low = jnp.concatenate([low_t[0][d_rows], low_t[1][d_rows]], axis=1).astype(F32)
        dout_high = jnp.concatenate([high_t[0][d_rows], high_t[1][d_rows]], axis=1).astype(F32)
        weights_all = jnp.concatenate([both_w[0][0], both_w[1][0], both_w[0][1], both_w[1][1]], axis=0)
        less = jnp.concatenate([low.astype(F32)[:, 0:8] for low, _ in masks], axis=2)
        low_lanes = lax.broadcasted_iota(jnp.int32, (blocks, 16, 128), 2) < HEAD_DIM

        def rows_seen(held):
            found = []
            for slot, (low, high) in enumerate(masks):
                lanes = jnp.where(low_lanes, low.astype(F32), high.astype(F32)).astype(BF16)
                x = jnp.concatenate([held[...], held[half_rows(first + slot), :]], axis=0)
                x = x.reshape(blocks, GROUP // 16, 16, 128) * lanes[:, None]
                found.append(x.reshape(blocks * GROUP, 128))
            return jnp.concatenate(found, axis=1)

        def columns_seen(held):
            found = []
            for slot, pair in enumerate(masks):
                for half, mask in enumerate(pair):
                    rows = slice(half * HEAD_DIM, half * HEAD_DIM + HEAD_DIM)
                    x = jnp.concatenate([held[rows, :], held[rows, half_rows(first + slot)]], axis=1)
                    line = jnp.concatenate([mask[d] for d in range(blocks)], axis=1)
                    x = x.reshape(HEAD_DIM // 16, 16, blocks * GROUP) * line[None]
                    found.append(x.reshape(HEAD_DIM, blocks * GROUP))
            return jnp.concatenate(found, axis=0)

        own, rest = pl.ds(0, blocks * GROUP), pl.ds(blocks * GROUP, n)

        def cut(x):
            return x.reshape(x.shape[0] // GROUP, GROUP // 8, 8, wide)

        def spread(low, high):
            return jnp.where(less > 0, low, high)[:, None]

        s = cut(mm(rows_seen(kk), w_score))
        hide = cut(jnp.where(seen, 0.0, MASKED))
        left = cut(jnp.where(seen | (qcol >= GROUP), 0.0, MASKED))
        right = cut(jnp.where(seen | (qcol < GROUP), 0.0, MASKED))
        s = [s[:first], s[first : first + 1] + left, s[first + 1 : first + 2] + right, s[first + 2 : -1], s[blocks - 1 :] + hide]
        s = jnp.concatenate([x for x in s if x.shape[0]], axis=0)
        sb[own, :] = s.reshape(blocks * GROUP, wide)
        tops = jnp.max(s, axis=1)
        s = mm(kk[...], h_score)
        sb[rest, :] = s
        top_low = jnp.max(jnp.max(jnp.where(less > 0, tops, MASKED), axis=0), axis=0, keepdims=True)
        top_high = jnp.maximum(
            jnp.max(jnp.where(less > 0, MASKED, tops), axis=0), jnp.max(s.reshape(n // 8, 8, wide), axis=0)
        )
        top_high = jnp.max(top_high, axis=0, keepdims=True)

        e = jnp.exp(cut(sb[own, :]) - spread(top_low, top_high))
        sums = jnp.sum(e, axis=1)
        e = e.reshape(blocks * GROUP, wide)
        sb[own, :] = e
        out = mm(columns_seen(self.vvt), e.astype(BF16))
        e = jnp.exp(sb[rest, :] - top_high)
        sb[rest, :] = e
        out_high = mm(self.vvt[0:HEAD_DIM, :], e.astype(BF16))
        total_low = jnp.sum(jnp.sum(jnp.where(less > 0, sums, 0.0), axis=0), axis=0, keepdims=True)
        total_high = jnp.sum(jnp.where(less > 0, 0.0, sums), axis=0) + jnp.sum(e.reshape(n // 8, 8, wide), axis=0)
        total_high = jnp.sum(total_high, axis=0, keepdims=True)

        def parts(x):
            low = jnp.concatenate([x[0:64, 0:GROUP], x[128:192, GROUP:wide]], axis=1)
            high = jnp.concatenate([x[64:128, 0:GROUP], x[192:256, GROUP:wide]], axis=1)
            return low, high

        yield
        inv_low, inv_high = 1.0 / total_low, 1.0 / total_high
        out_low, more = parts(out)
        out_low, out_high = out_low * inv_low, (out_high + more) * inv_high
        delta_low = jnp.sum(out_low * dout_low, axis=0, keepdims=True)
        delta_high = jnp.sum(out_high * dout_high, axis=0, keepdims=True)

        p = cut(sb[own, :]) * spread(inv_low, inv_high)
        dp = cut(mm(rows_seen(vv), w_dprob))
        ds = (p * (dp - spread(delta_low, delta_high))).reshape(blocks * GROUP, wide).astype(BF16)
        p = p.reshape(blocks * GROUP, wide).astype(BF16)
        dq = mm(columns_seen(self.kkt), ds)
        for slot in range(2):
            cols = slice(slot * GROUP, slot * GROUP + GROUP)
            got = mm(jnp.concatenate([ds[:, cols], p[:, cols]], axis=1), keys_w[slot])
            here = less[:, :, cols][:, None] > 0
            got = got.reshape(blocks, GROUP // 8, 8, wide)
            low = jnp.where(here, got[..., 0:128], 0.0).reshape(blocks * GROUP, 128)
            high = jnp.where(here, 0.0, got[..., 128:256]).reshape(blocks * GROUP, 128)
            self.acc[0] += low[0:n]
            self.acc[1] += high[0:n]
            self.acc[1, half_rows(first + slot), :] += high[n:]
        p = sb[rest, :] * inv_high
        dp = mm(vv[...], h_dprob)
        ds = (p * (dp - delta_high)).astype(BF16)
        self.acc[0] += mm(jnp.concatenate([ds, p.astype(BF16)], axis=1), weights_all)
        dq_low, dq_high = parts(dq)
        dq_high = dq_high + mm(self.kkt[0:HEAD_DIM, :], ds)
        for slot in range(2):
            cols = slice(slot * GROUP, slot * GROUP + GROUP)
            scale = HEAD_DIM**-0.5
            low = jnp.concatenate([out_low[:, cols], dq_low[:, cols] * scale], axis=0).astype(BF16).T
            high = jnp.concatenate([out_high[:, cols], dq_high[:, cols] * scale], axis=0).astype(BF16).T
            odq_ref[first + slot] = jnp.concatenate([low, high], axis=0)

    def give(self, dkv_refs):
        for p, ref in enumerate(dkv_refs):

            def step(r, _, p=p, ref=ref):
                rows = half_rows(p * self.lines + r)
                ref[r, 0:GROUP, :] = self.acc[0, rows, :].astype(BF16)
                ref[r, GROUP : 2 * GROUP, :] = self.acc[1, rows, :].astype(BF16)
                return 0

            lax.fori_loop(0, self.lines, step, 0, unroll=2)


def attention_scratch(lines, devices):
    n = devices * GROUP
    more = n + GROUP
    return [
        pltpu.VMEM((n, 128), BF16),
        pltpu.VMEM((n, 128), BF16),
        pltpu.VMEM((128, n), BF16),
        pltpu.VMEM((128, n), BF16),
        pltpu.VMEM((n + more, 256), F32),
        pltpu.VMEM((2, n, 128), F32),
    ]


class Chain:
    def __init__(self, place, wires, data, base, size, order, got, final, final_base, free, keep):
        pairs = {
            "x": (place.x, place.flip(1)),
            "y": (place.s, place.to_seq()),
            "m": (place.rest % 2, place.flip(2)),
            "f": (place.rest // 2, place.flip(3)),
        }
        self.data, self.got, self.sizes, self.bases, self.bits = data, [], [size], [base], []
        at = 0
        self.down, self.up = [], []
        for level, name in enumerate(order):
            bit, device = pairs[name]
            half = self.sizes[-1] // 2
            got_here = got.at[pl.ds(at, half)]
            at += half
            source, start = (data, base) if level == 0 else (self.got[-1], 0)
            away = pl.ds(pl.multiple_of(start + (1 - bit) * half, 16), half)
            self.down.append(wires.copy(source.at[away], got_here, device))
            self.got.append(got_here)
            self.bits.append(bit)
            self.sizes.append(half)
            self.bases.append(self.bases[-1] + bit * half)
            kept = pl.ds(pl.multiple_of(self.bases[-1], 16), half)
            self.up.append(wires.copy(data.at[kept], data.at[kept], device))
        whole = pl.ds(base, size)
        self.up.insert(0, wires.copy(data.at[whole], final.at[place.core, pl.ds(final_base, size)], place.flip(0)))
        self.depth = len(order)
        self.keep = pltpu.make_async_copy(data.at[whole], final.at[place.core, pl.ds(final_base, size)], keep)
        self.free, self.first = free, pairs[order[0]][1]
        self.sent = []

    def start(self, copy):
        copy.start()
        self.sent.append(copy)

    def stage(self, number):
        depth = self.depth
        if number == 0:
            self.start(self.down[0])
        elif number <= depth:
            level = number - 1
            self.down[level].wait_recv()
            if level == 0:
                self.down[0].wait_send()
                self.sent.pop()
                pl.semaphore_signal(
                    self.free, inc=1, device_id=self.first, device_id_type=pl.DeviceIdType.MESH
                )
            half = self.sizes[number]
            source, start = (self.data, self.bases[0]) if level == 0 else (self.got[level - 1], 0)
            start = start + self.bits[level] * half
            if number < depth:
                add_rows(self.got[level], 0, [(source, start)], half)
                self.start(self.down[number])
            else:
                add_rows(self.got[level], 0, [(source, start)], half, self.data, self.bases[depth])
                self.start(self.up[depth])
        else:
            level = 2 * depth - number + 1
            self.up[level].wait_recv()
            if level == 2:
                pl.semaphore_wait(self.free, 1)
            self.start(self.up[level - 1])
            if level == 1:
                self.keep.start()

    def finish(self):
        self.up[0].wait_recv()
        self.keep.wait()
        for copy in self.sent:
            copy.wait_send()


SCHEDULE = (
    "front", "send0", "mlp0", "u0.0", "u3.0", "mlp1", "send1", "u4.0", "line0", "spread0", "mlp2", "u0.1", "send2",
    "u3.1", "line1", "fwd0", "spread1", "u5.0", "u2.0", "keys0", "a0", "u1.0", "u3.2", "u4.1", "a0", "a0", "u0.2",
    "u3.3", "fwd1", "a0", "keys1", "u5.1", "a1", "u0.3", "core0", "u3.4", "line2", "spread2", "u5.2", "u1.1", "u4.2",
    "a1", "u5.3", "u0.4", "a1", "u3.5", "plane0", "u2.1", "u5.4", "fwd2", "a1", "u3.6", "keys2", "a2", "u1.2", "u4.3",
    "core1", "u5.5", "u0.5", "home0", "a2", "part", "u3.7", "grad0", "u1.3", "u2.2", "a2", "u4.4", "u5.6", "plane1",
    "a2", "u4.5", "u0.6", "u2.3", "core2", "u5.7", "u1.4", "v1.1", "home1", "grad1", "u0.7", "v0.1", "plane2", "v0.2",
    "u2.4", "v3.1", "u4.6", "u1.5", "home2", "v2.1", "v1.2", "u3.8", "v3.2", "grad2", "u2.5", "u5.8", "v1.3", "u4.7",
    "v3.3", "u0.8", "u1.6", "v2.2", "u2.6", "tail", "v4.1", "v1.4", "v3.4", "u1.7", "v5.1", "vec0", "v2.3", "v1.5",
    "v0.3", "v3.5", "v4.2", "v5.2", "v2.4", "u2.7", "v0.4", "vec1", "v2.5", "v4.3", "v5.3", "v0.5", "v3.6", "u4.8",
    "v2.6", "v4.4", "v5.4", "v3.7", "v4.5", "u1.8", "v1.6", "v5.5", "v0.6", "v2.7", "u2.8", "v4.6", "v5.6", "v1.7",
    "vec2", "v0.7", "v3.8", "v4.7", "v2.8", "v5.7", "vec3", "v1.8", "v0.8", "v5.8", "v4.8",
)
FF_CHUNK = 256
ORDERS = ("xymf", "xmyf", "yxmf", "yxmf", "ymxf", "yxmf", "ymxf", "xmyf", "yxmf", "xmyf", "yxmf", "xmyf")


def runs_of(positions, n_blk):
    group = positions[0, 0] // GROUP
    mirror = 2 * n_blk - 1 - group
    turn = jnp.full((16, 128), (group - mirror).astype(F32), F32).astype(BF16) > 0
    return jnp.minimum(group, mirror), jnp.broadcast_to(turn[None], (GROUP // 16, 16, 128))


def rotary_rows(low_group, n_blk):
    shape = (2 * GROUP, 2 * HEAD_DIM)
    row = lax.broadcasted_iota(jnp.int32, shape, 0)
    lane = lax.broadcasted_iota(jnp.int32, shape, 1) % HEAD_DIM
    half = ROTARY // 2
    at = jnp.where(row < GROUP, low_group * GROUP + row, (2 * n_blk - 2 - low_group) * GROUP + row)
    inverse = jnp.zeros(shape, F32)
    for i in range(half):
        inverse = jnp.where(lane % half == i, float(np.float32(ROTARY_BASE ** (-2.0 * i / ROTARY))), inverse)
    angles = at.astype(F32) * inverse
    cosine, sine = jnp.cos(angles), jnp.sin(angles)
    return (
        jnp.where(lane < ROTARY, cosine, 1.0),
        jnp.where(lane < half, -sine, 0.0),
        jnp.where((lane >= half) & (lane < ROTARY), sine, 0.0),
    )


def joined_kernel(
    n_seq, n_blk, units1, units2,
    positions, hid, og, again, abias, mgain, mbias, bqkv, bdense, bout, bin_,
    wqkv_hbm, wdense_hbm, win_hbm, wout_hbm,
    output, input_grad, vec_out, final,
    wqkv, wdense, win, wout, cosw, sina, sinb, hid2, og2, normed2, normed_m, qd_msg, kv_msg, qd_line, keys, flags,
    kk, vv, kkt, vvt, sb, acc,
    dkv_got, odq_all, dkv_all, out_part, gn_part, mout_got, gn_got, mine, other, bins,
    grads1, grads2, got, small, small_got, sends, recvs, load_sem, chunk_sem, keep_sem, free_sem,
):
    def row(ref):
        return ref[...].astype(F32).reshape(1, ref.shape[0])

    place = Place(n_seq, n_blk)
    wires = Wires(sends, recvs)
    tokens, width = hid.shape
    n_rest = place.n_rest
    core, hi = place.core, place.hi
    half_ff = win_hbm.shape[1] // 2
    chunks = half_ff // FF_CHUNK
    rows1 = grads1.shape[0]
    pieces = place.n_low
    sent, waiting = [], {}
    todo = {}

    def go(name, src, dst, device):
        copy = wires.copy(src, dst, device)
        copy.start()
        sent.append(copy)
        waiting.setdefault(name, []).append(copy)

    def arrive(name):
        for copy in waiting.pop(name):
            copy.wait_recv()

    loads = [
        pltpu.make_async_copy(wqkv_hbm, wqkv, load_sem.at[0]),
        pltpu.make_async_copy(wdense_hbm, wdense, load_sem.at[1]),
    ]
    for load in loads:
        load.start()

    def chunk_loads(f):
        slot = f % 2
        at = pl.multiple_of(core * half_ff + f * FF_CHUNK, FF_CHUNK)
        return [
            pltpu.make_async_copy(win_hbm.at[:, pl.ds(at, FF_CHUNK)], win.at[slot], chunk_sem.at[0, slot]),
            pltpu.make_async_copy(wout_hbm.at[pl.ds(at, FF_CHUNK), :], wout.at[slot], chunk_sem.at[1, slot]),
        ]

    for f in range(2):
        for load in chunk_loads(f):
            load.start()

    low_group, turned_rows = runs_of(positions, n_blk)
    cut = (GROUP // 16, 16, 128)
    for src, dst in ((hid, hid2), (og, og2)):
        for at in range(0, width, 128):
            cols = slice(at, at + 128)
            one, two = src[0:GROUP, cols].reshape(cut), src[GROUP : 2 * GROUP, cols].reshape(cut)
            dst[0:GROUP, cols] = jnp.where(turned_rows, two, one).reshape(GROUP, 128)
            dst[GROUP : 2 * GROUP, cols] = jnp.where(turned_rows, one, two).reshape(GROUP, 128)
    flags[0, 0] = jnp.full((16, 128), low_group.astype(F32), F32).astype(BF16)
    cosw[...], sina[...], sinb[...] = rotary_rows(low_group, n_blk)
    place.meet()
    for by in range(1, HEAD_GROUPS):
        go("flags", flags.at[0, 0], flags.at[0, by], place.to_group(by))
    for ref in (hid2, og2):
        go("rows", ref.at[pl.ds(0, tokens)], ref.at[pl.ds(tokens, tokens)], place.flip(0))

    lane = lax.broadcasted_iota(jnp.int32, (tokens, 128), 1)
    low = lane < HEAD_DIM

    def front():
        xhat, _ = normalise(hid2[0:tokens, :].astype(F32))
        normed = (xhat * row(again) + row(abias)).astype(BF16)
        for load in loads:
            load.wait()
        mixed = mm(normed, wqkv[...]) + row(bqkv)
        datt = mm_nt(og2[0:tokens, :], wdense[...])
        ca, sa, sb_ = cosw[...], sina[...], sinb[...]

        def turned(u):
            return u * ca + pltpu.roll(u, 120, 1) * sa + pltpu.roll(u, 8, 1) * sb_

        for tile in range(HEADS // 2):
            at = tile * 128
            q = turned(mixed[:, at : at + 128]) * (HEAD_DIM**-0.5)
            k = turned(mixed[:, width + at : width + at + 128])
            v = mixed[:, 2 * width + at : 2 * width + at + 128]
            d = datt[:, at : at + 128]
            for msg, one, two in ((qd_msg, q, d), (kv_msg, k, v)):
                for odd in range(2):
                    head = 2 * tile + odd
                    if odd == 0:
                        packed = jnp.where(low, one, pltpu.roll(two, 64, 1))
                    else:
                        packed = jnp.where(low, pltpu.roll(one, 64, 1), two)
                    msg[head % PER_GROUP, head // PER_GROUP] = packed.astype(BF16)
        arrive("flags")
        go("flag_x", flags.at[0], flags.at[1], place.flip(1))
        go("flag_c", flags.at[0], flags.at[2], place.flip(0))

    def send(j):
        for msg, line, name in ((kv_msg, keys.at[j, 0], "line"), (qd_msg, qd_line.at[j], "query")):
            for by in range(1, HEAD_GROUPS):
                go(name + str(j), msg.at[j, (hi + by) % HEAD_GROUPS], line.at[by], place.to_group(by))
        keys[j, 0, 0] = kv_msg[j, hi]
        qd_line[j, 0] = qd_msg[j, hi]

    def mlp_group(g):
        if g == 0:
            arrive("rows")
            xhat, _ = normalise(hid2[...].astype(F32))
            normed_m[...] = (xhat * row(mgain) + row(mbias)).astype(BF16)
            normed2[...] = (xhat * row(again) + row(abias)).astype(BF16)
            out_part[...] = jnp.zeros_like(out_part)
            gn_part[...] = jnp.zeros_like(gn_part)
        per = chunks // 3

        def step(f, _):
            slot = f % 2
            for load in chunk_loads(f):
                load.wait()
            x, w1, w2 = normed_m[...], win[slot], wout[slot]
            at = pl.multiple_of(f * FF_CHUNK, FF_CHUNK)
            bias_at = pl.ds(pl.multiple_of(core * half_ff + f * FF_CHUNK, FF_CHUNK), FF_CHUNK)
            inner = mm(x, w1) + bin_[bias_at].astype(F32).reshape(1, FF_CHUNK)
            cdf = 0.5 * (1.0 + lax.erf(inner * (0.5**0.5)))
            act = (inner * cdf).astype(BF16)
            pdf = jnp.exp(-0.5 * inner * inner) * (0.5 * 2.0**0.5 * 3.141592653589793**-0.5)
            gact = mm_nt(og2[...], w2)
            ginner = (gact * (cdf + inner * pdf)).astype(BF16)
            bins[0:1, pl.ds(at, FF_CHUNK)] = jnp.sum(ginner.astype(F32), axis=0, keepdims=True)
            grads1[pl.ds(at, FF_CHUNK), :] = mm_tn(ginner, x).astype(BF16)
            grads1[pl.ds(pl.multiple_of(half_ff + at, FF_CHUNK), FF_CHUNK), :] = mm_tn(act, og2[...]).astype(BF16)
            out_part[...] += mm(act, w2)
            gn_part[...] += mm_nt(ginner, w1)

            @pl.when(f + 2 < chunks)
            def _():
                for load in chunk_loads(f + 2):
                    load.start()

            return 0

        lax.fori_loop(g * per, (g + 1) * per, step, 0)

    def part():
        go("part", out_part.at[pl.ds(tokens, tokens)], mout_got, place.flip(0))
        go("part", gn_part.at[pl.ds(tokens, tokens)], gn_got, place.flip(0))

    def spread(j):
        go("x" + str(j), keys.at[j, 0], keys.at[j, 1], place.flip(1))
        go("c" + str(j), keys.at[j, 0], keys.at[j, 2], place.flip(0))

    def forward(j):
        arrive("x" + str(j))
        go("c" + str(j), keys.at[j, 1], keys.at[j, 3], place.flip(0))
        if j == 0:
            arrive("flag_x")
            go("flag_c", flags.at[1], flags.at[3], place.flip(0))

    def keys_there(j):
        arrive("c" + str(j))
        arrive("query" + str(j))
        if j == 0:
            arrive("flag_c")

    attention = Attention(HEAD_GROUPS, HEAD_GROUPS * pieces, flags, kk, vv, kkt, vvt, sb, acc)

    def attend(j):
        sources = [keys.at[j, p] for p in range(pieces)]
        attention.prepare(sources)
        for first in range(0, HEAD_GROUPS, 2):
            yield from attention.pair(first, qd_line.at[j], qd_line.at[j])
            if first + 2 < HEAD_GROUPS:
                yield
        for copy in leaving[j]:
            copy.wait_send()
        attention.give(sources)
        for by in range(1, HEAD_GROUPS):
            go("home" + str(j), qd_line.at[j, by], odq_all.at[j, by], place.to_group(HEAD_GROUPS - by))
        for i in range(2):
            go("core" + str(j), keys.at[j, 2 + i], dkv_got.at[j, i], place.flip(0))
        yield

    leaving = {}

    def core_sum(j):
        arrive("core" + str(j))
        for i in range(2):
            dkv_got[j, i] = (keys[j, i].astype(F32) + dkv_got[j, i].astype(F32)).astype(BF16)
        go("plane" + str(j), dkv_got.at[j, 1], dkv_got.at[j, 2], place.flip(1))

    def plane_sum(j):
        arrive("plane" + str(j))
        dkv_got[j, 2] = (dkv_got[j, 0].astype(F32) + dkv_got[j, 2].astype(F32)).astype(BF16)
        for by in range(1, HEAD_GROUPS):
            go("home" + str(j), dkv_got.at[j, 2, by], dkv_all.at[j, by], place.to_group(HEAD_GROUPS - by))
        odq_all[j, 0] = qd_line[j, 0]
        dkv_all[j, 0] = dkv_got[j, 2, 0]

    def home(j):
        arrive("home" + str(j))
        ca, sa, sb_ = cosw[...], sina[...], sinb[...]

        def turned_back(g):
            return g * ca - pltpu.roll(g, 120, 1) * sa - pltpu.roll(g, 8, 1) * sb_

        for g in range(HEAD_GROUPS):
            at = (g - hi + HEAD_GROUPS) % HEAD_GROUPS
            a, b = odq_all[j, at].astype(F32), dkv_all[j, at].astype(F32)
            mine[j, g, :, 0:128] = jnp.where(low, a, turned_back(a)).astype(BF16)
            mine[j, g, :, 128:256] = jnp.where(low, turned_back(b), b).astype(BF16)
        half = HEAD_GROUPS // 2
        go("other" + str(j), mine.at[j, pl.ds((1 - core) * half, half)], other.at[j], place.flip(0))

    def grad(j):
        arrive("other" + str(j))
        half = HEAD_GROUPS // 2
        normed, cot = normed2[...], og2[...]
        from_out = lax.broadcasted_iota(jnp.int32, (128, width), 0) < HEAD_DIM
        for g in range(half):
            both = jnp.concatenate([mine[j, core * half + g], other[j, g]], axis=0)
            base = (j * half + g) * 256
            by_normed = mm_tn(both, normed)
            by_cot = mm_tn(both[:, 0:128], cot)
            grads2[base : base + 128, :] = jnp.where(from_out, by_cot, by_normed[0:128]).astype(BF16)
            grads2[base + 128 : base + 256, :] = by_normed[128:256].astype(BF16)
        per = len(units2) // PER_GROUP
        for unit in second[j * per : (j + 1) * per]:
            unit.stage(0)

    def tail():
        arrive("part")
        rows = hid2[0:tokens, :].astype(F32)

        def parts(a):
            return mine[a % PER_GROUP, a // PER_GROUP].astype(F32)

        outs, grads = [], [[], [], []]
        for tile in range(HEADS // 2):
            one, two = parts(2 * tile), parts(2 * tile + 1)
            a1, b1, a2, b2 = one[:, 0:128], one[:, 128:256], two[:, 0:128], two[:, 128:256]
            outs.append(jnp.where(low, a1, pltpu.roll(a2, 64, 1)).astype(BF16))
            grads[0].append(jnp.where(low, pltpu.roll(a1, 64, 1), a2).astype(BF16))
            grads[1].append(jnp.where(low, b1, pltpu.roll(b2, 64, 1)).astype(BF16))
            grads[2].append(jnp.where(low, pltpu.roll(b1, 64, 1), b2).astype(BF16))
        att = jnp.concatenate(outs, axis=1)
        dmixed = jnp.concatenate(grads[0] + grads[1] + grads[2], axis=1)
        branch = mm(att, wdense[...]) + row(bdense)
        mout = out_part[0:tokens, :] + mout_got[...]
        output[...] = (rows + branch + (mout + row(bout))).astype(BF16)
        gna = mm_nt(dmixed, wqkv[...])
        gnm = gn_part[0:tokens, :] + gn_got[...]
        xhat, scale = normalise(rows)
        cot = og2[0:tokens, :].astype(F32)
        input_grad[...] = (
            cot
            + norm_back(gna, xhat, scale, row(again))
            + norm_back(gnm, xhat, scale, row(mgain))
        ).astype(BF16)
        small[0:1, :] = jnp.sum(gna * xhat, axis=0, keepdims=True)
        small[1:2, :] = jnp.sum(gna, axis=0, keepdims=True)
        small[2:3, :] = jnp.sum(gnm * xhat, axis=0, keepdims=True)
        small[3:4, :] = jnp.sum(gnm, axis=0, keepdims=True)
        for k in range(3):
            cols = dmixed[:, k * width : (k + 1) * width].astype(F32)
            small[4 + k : 5 + k, :] = jnp.sum(cols, axis=0, keepdims=True)
        small[7:8, :] = jnp.sum(cot, axis=0, keepdims=True)
        per = half_ff // width
        for side in range(2):
            here = (1 - core if side == 0 else core).astype(F32)
            for k in range(per):
                at = 8 + side * per + k
                small[at : at + 1, :] = bins[0:1, k * width : (k + 1) * width] * here

    rounds = [
        [place.flip(0)],
        [place.flip(1)],
        [place.to_seq()],
        [place.to_rest(by) for by in range(1, n_rest)],
    ]

    def vec_start(r):
        for i, device in enumerate(rounds[r]):
            go("vec" + str(r), small.at[pl.ds(0, small.shape[0])] if r == 0 else small_got.at[8 + r], small_got.at[2 * r if r < 3 else 5 + i], device)

    def vec(r):
        if r == 0:
            vec_start(0)
            return
        arrive("vec" + str(r - 1))
        source = small[...] if r == 1 else small_got[8 + r - 1]
        small_got[8 + r] = source + small_got[2 * (r - 1)]
        vec_start(r)

    def vec_end():
        arrive("vec3")
        total = small_got[8 + 3]
        for i in range(n_rest - 1):
            total = total + small_got[5 + i]
        vec_out[...] = total

    first, second = [], []
    at = 0
    for found, units, data, offset in ((first, units1, grads1, 0), (second, units2, grads2, rows1)):
        for base, size, order in units:
            found.append(Chain(
                place, wires, data, base, size, order, got.at[pl.ds(at, size)], final, offset + base,
                free_sem.at[len(first) + len(second)], keep_sem.at[len(first) + len(second)],
            ))
            at += size

    todo = {"front": front, "part": part, "tail": tail}
    for g in range(3):
        todo["mlp" + str(g)] = functools.partial(mlp_group, g)
    for r in range(4):
        todo["vec" + str(r)] = functools.partial(vec, r)
    runs = {}
    for j in range(PER_GROUP):
        for name, action in (
            ("send", send), ("line", lambda j: arrive("line" + str(j))), ("spread", spread), ("fwd", forward),
            ("keys", keys_there), ("core", core_sum), ("plane", plane_sum), ("home", home), ("grad", grad),
        ):
            todo[name + str(j)] = functools.partial(action, j)
        runs[j] = attend(j)
        todo["a" + str(j)] = functools.partial(next, runs[j])
    for name, units in (("u", first), ("v", second)):
        for i, unit in enumerate(units):
            for stage in range(2 * unit.depth + 1):
                todo[name + str(i) + "." + str(stage)] = functools.partial(unit.stage, stage)
    for j in range(PER_GROUP):
        leaving[j] = []
    for token in SCHEDULE:
        before = len(sent)
        todo[token]()
        if token[:-1] in ("spread", "fwd"):
            leaving[int(token[-1])] += sent[before:]
            del sent[before:]
    vec_end()
    for unit in first + second:
        if unit.sent:
            unit.finish()
    for copy in sent:
        copy.wait_send()


def joined(mesh, positions, hid, og, again, abias, mgain, mbias, bqkv, bdense, bout, b_in, wqkv, wdense, win, wout):
    n_seq, n_blk = mesh.shape["seq"], mesh.shape["blk"]
    n_low, n_rest = n_blk // HEAD_GROUPS, n_blk // 4
    tokens, width = hid.shape
    half_ff = win.shape[1] // 2
    rows1, rows2 = 2 * half_ff, 2 * width
    size = half_ff // 3
    units1 = [(i * size, size, order) for i, order in enumerate(ORDERS[:6])]
    size = rows2 // 6
    units2 = [(i * size, size, order) for i, order in enumerate(ORDERS[6:])]
    total = rows1 + rows2
    copies = 9 * (len(units1) + len(units2)) + 128
    line = (HEAD_GROUPS, tokens, 128)
    n_small = 8 + 2 * half_ff // width
    devices = HEAD_GROUPS * n_low
    per = PER_GROUP
    inputs = [positions, hid, og, again, abias, mgain, mbias, bqkv, bdense, bout, b_in, wqkv, wdense, win, wout]
    return pl.pallas_call(
        functools.partial(joined_kernel, n_seq, n_blk, units1, units2),
        out_shape=[
            jax.ShapeDtypeStruct((tokens, width), BF16),
            jax.ShapeDtypeStruct((tokens, width), BF16),
            jax.ShapeDtypeStruct((n_small, width), F32),
            jax.ShapeDtypeStruct((2, total, width), BF16),
        ],
        in_specs=[IN_SMEM] + [IN_VMEM] * (len(inputs) - 5) + [pl.BlockSpec(memory_space=pl.ANY)] * 4,
        out_specs=[IN_VMEM] * 3 + [pl.BlockSpec(memory_space=pl.ANY)],
        scratch_shapes=[
            pltpu.VMEM(wqkv.shape, BF16),
            pltpu.VMEM(wdense.shape, BF16),
            pltpu.VMEM((2, width, FF_CHUNK), BF16),
            pltpu.VMEM((2, FF_CHUNK, width), BF16),
            pltpu.VMEM((tokens, 2 * HEAD_DIM), F32),
            pltpu.VMEM((tokens, 2 * HEAD_DIM), F32),
            pltpu.VMEM((tokens, 2 * HEAD_DIM), F32),
            pltpu.VMEM((2 * tokens, width), BF16),
            pltpu.VMEM((2 * tokens, width), BF16),
            pltpu.VMEM((2 * tokens, width), BF16),
            pltpu.VMEM((2 * tokens, width), BF16),
            pltpu.VMEM((per,) + line, BF16),
            pltpu.VMEM((per,) + line, BF16),
            pltpu.VMEM((per,) + line, BF16),
            pltpu.VMEM((per, n_low) + line, BF16),
            pltpu.VMEM((n_low, HEAD_GROUPS, 16, 128), BF16),
            *attention_scratch(HEAD_GROUPS, devices),
            pltpu.VMEM((per, 3) + line, BF16),
            pltpu.VMEM((per,) + line, BF16),
            pltpu.VMEM((per,) + line, BF16),
            pltpu.VMEM((2 * tokens, width), F32),
            pltpu.VMEM((2 * tokens, width), F32),
            pltpu.VMEM((tokens, width), F32),
            pltpu.VMEM((tokens, width), F32),
            pltpu.VMEM((per, HEAD_GROUPS, tokens, 256), BF16),
            pltpu.VMEM((per, HEAD_GROUPS // 2, tokens, 256), BF16),
            pltpu.VMEM((1, half_ff), F32),
            pltpu.VMEM((rows1, width), BF16),
            pltpu.VMEM((rows2, width), BF16),
            pltpu.VMEM((total, width), BF16),
            pltpu.VMEM((n_small, width), F32),
            pltpu.VMEM((12, n_small, width), F32),
            pltpu.SemaphoreType.DMA((copies,)),
            pltpu.SemaphoreType.DMA((copies,)),
            pltpu.SemaphoreType.DMA((2,)),
            pltpu.SemaphoreType.DMA((2, 2)),
            pltpu.SemaphoreType.DMA((len(units1) + len(units2),)),
            pltpu.SemaphoreType.REGULAR((len(units1) + len(units2),)),
        ],
        compiler_params=pltpu.CompilerParams(
            vmem_limit_bytes=VMEM_BYTES, collective_id=2, has_side_effects=True
        ),
        name="joined",
    )(*inputs)


def spread_kernel(
    n_blk, positions, final, vec, out_rows, grad_rows,
    output, input_grad, win, wout, wqkv, wdense, again, abias, mgain, mbias, bqkv, bdense, bin_, bout,
):
    half_ff = win.shape[1] // 2

    @pl.when(pl.program_id(0) == 0)
    def _():
        width = vec.shape[1]
        _, turned_rows = runs_of(positions, n_blk)
        cut = (GROUP // 16, 16, 128)
        for src, dst in ((out_rows, output), (grad_rows, input_grad)):
            for at in range(0, width, 128):
                cols = slice(at, at + 128)
                one, two = src[0:GROUP, cols].reshape(cut), src[GROUP : 2 * GROUP, cols].reshape(cut)
                dst[0:GROUP, cols] = jnp.where(turned_rows, two, one).reshape(GROUP, 128)
                dst[GROUP : 2 * GROUP, cols] = jnp.where(turned_rows, one, two).reshape(GROUP, 128)
        for ref, at in ((again, 0), (abias, 1), (mgain, 2), (mbias, 3), (bqkv, 4), (bdense, 7), (bout, 7), (bin_, 8)):
            for k in range(ref.shape[0] // width):
                ref[k * width : (k + 1) * width] = vec[at + k : at + k + 1, :].reshape(width)

    for core in range(2):
        win[:, core * half_ff : (core + 1) * half_ff] = final[core, 0:half_ff, :].T.astype(F32)
        wout[core * half_ff : (core + 1) * half_ff, :] = final[core, half_ff : 2 * half_ff, :].astype(F32)

    def segment(head, part):
        group, j = head // PER_GROUP, head % PER_GROUP
        half = HEAD_GROUPS // 2
        at = 2 * half_ff + (j * half + group % half) * 256 + part * HEAD_DIM
        return final[group // half, at : at + HEAD_DIM, :]

    width = wdense.shape[0]
    for tile in range(HEADS // 2):
        for part in range(4):
            both = jnp.concatenate([segment(2 * tile, part), segment(2 * tile + 1, part)], axis=0)
            if part == 0:
                wdense[tile * 128 : tile * 128 + 128, :] = both.astype(F32)
            else:
                at = (part - 1) * width + tile * 128
                wqkv[:, at : at + 128] = both.T.astype(F32)


def spread_out(n_blk, positions, final, vec, out_rows, grad_rows, ff):
    total, width = final.shape[1:]
    lanes = 384

    def whole(x):
        return pl.BlockSpec(x.shape, lambda i: (0,) * len(x.shape))

    vectors = [jax.ShapeDtypeStruct((n,), F32) for n in (width, width, width, width, 3 * width, width, ff, width)]
    rows = jax.ShapeDtypeStruct(out_rows.shape, BF16)
    return pl.pallas_call(
        functools.partial(spread_kernel, n_blk),
        grid=(width // lanes,),
        in_specs=[IN_SMEM, pl.BlockSpec((2, total, lanes), lambda i: (0, 0, i))]
        + [whole(x) for x in (vec, out_rows, grad_rows)],
        out_specs=[
            whole(rows),
            whole(rows),
            pl.BlockSpec((lanes, ff), lambda i: (i, 0)),
            pl.BlockSpec((ff, lanes), lambda i: (0, i)),
            pl.BlockSpec((lanes, 3 * width), lambda i: (i, 0)),
            pl.BlockSpec((width, lanes), lambda i: (0, i)),
        ]
        + [whole(x) for x in vectors],
        out_shape=[
            rows,
            rows,
            jax.ShapeDtypeStruct((width, ff), F32),
            jax.ShapeDtypeStruct((ff, width), F32),
            jax.ShapeDtypeStruct((width, 3 * width), F32),
            jax.ShapeDtypeStruct((width, width), F32),
        ]
        + vectors,
        compiler_params=params(),
        name="spread",
    )(positions, final, vec, out_rows, grad_rows)


def rotary_tables(positions):
    lane = jnp.arange(128, dtype=jnp.int32) % HEAD_DIM
    half = ROTARY // 2
    inverse = jnp.power(ROTARY_BASE, -2.0 * (lane % half).astype(F32) / ROTARY)
    angles = positions.astype(F32)[:, None] * inverse[None, :]
    cosine, sine = jnp.cos(angles), jnp.sin(angles)
    lane = lane[None, :]
    return (
        jnp.where(lane < ROTARY, cosine, 1.0),
        jnp.where(lane < half, -sine, 0.0),
        jnp.where((lane >= half) & (lane < ROTARY), sine, 0.0),
    )


def solution(mesh):
    n_seq, n_blk = mesh.shape["seq"], mesh.shape["blk"]
    n_low = n_blk // HEAD_GROUPS
    low_bits = n_low.bit_length() - 1
    def permute(x, target):
        return lax.ppermute(x, "blk", [(b, target(b)) for b in range(n_blk)])

    def to_group(x, by):
        return permute(x, lambda b: ((b // n_low + by) % HEAD_GROUPS) * n_low + b % n_low)

    def flip(x, bit):
        return permute(x, lambda b: b ^ (1 << bit))

    def on_device(
        hidden, positions, ln_attn_gain, ln_attn_bias, ln_mlp_gain, ln_mlp_bias,
        w_qkv, b_qkv, w_dense, b_dense, w_in, b_in, w_out, b_out, out_grad,
    ):
        hid, og, pos = hidden[0], out_grad[0], positions[0]
        again, abias = ln_attn_gain[None], ln_attn_bias[None]
        mgain, mbias = ln_mlp_gain[None], ln_mlp_bias[None]
        tokens, width = hid.shape
        if n_low == 4:
            output, input_grad, vec, final = joined(
                mesh, positions, hid, og, ln_attn_gain, ln_attn_bias, ln_mlp_gain, ln_mlp_bias, b_qkv, b_dense, b_out,
                b_in, w_qkv, w_dense, w_in, w_out,
            )
            output, input_grad, win, wout, wqkv, wdense, *vectors = spread_out(
                n_blk, positions, final, vec, output, input_grad, w_in.shape[1]
            )
            dgain, dbias, dmgain, dmbias, dbqkv, dbdense, dbin, dbout = vectors
            return (
                output[None], input_grad[None], dgain, dbias, dmgain, dmbias,
                wqkv, dbqkv, wdense, dbdense, win, dbin, wout, dbout,
            )
        b = lax.axis_index("blk")
        core = b % 2
        hi = b // n_low
        tables = rotary_tables(pos)

        own_runs = pos[::GROUP] // GROUP
        line_runs = jnp.concatenate(
            [own_runs] + [to_group(own_runs, by) for by in range(1, HEAD_GROUPS)]
        )
        key_runs = [line_runs]
        for bit in range(low_bits - 1, -1, -1):
            key_runs = key_runs + [flip(r, bit) for r in key_runs]
        n_query = line_runs.shape[0]
        rank = jnp.sum(line_runs[:, None] > line_runs[None, :], axis=1)
        slots = rank[None, :] == jnp.arange(n_query)[:, None]
        order = jnp.sum(jnp.where(slots, jnp.arange(n_query)[None, :], 0), axis=1)
        ordered = jnp.sum(jnp.where(slots, line_runs[None, :], 0), axis=1)
        tab = jnp.concatenate(key_runs + [order, ordered]).astype(jnp.int32)

        hid2 = jnp.concatenate([hid, flip(hid, 0)], axis=0)
        og2 = jnp.concatenate([og, flip(og, 0)], axis=0)

        msg = front(hid, og, again, abias, w_qkv, b_qkv[None], w_dense, tables)

        arrived = []
        for j in range(PER_GROUP):
            got = []
            for by in range(HEAD_GROUPS):
                part = lax.dynamic_index_in_dim(msg[j], lax.rem(hi + by, HEAD_GROUPS), 0, False)
                got.append(part if by == 0 else to_group(part, by))
            qd = jnp.stack([g[0] for g in got])
            pieces = [jnp.stack([g[1] for g in got])]
            for bit in range(low_bits - 1, -1, -1):
                pieces = pieces + [flip(piece, bit) for piece in pieces]
            arrived.append((qd, pieces))

        mlp_grads, bin_half, out_part, gn_part, normed2 = mlp(
            core[None].astype(jnp.int32), hid2, og2, again, abias, mgain, mbias, w_in, b_in[None], w_out
        )
        odqs, dkvs = [], []
        line = (HEAD_GROUPS, tokens, 128)
        for j in range(PER_GROUP):
            qd, pieces = arrived[j]
            runs = (HEAD_GROUPS * tokens // GROUP, GROUP, 128)
            odq, dkv = attention(tab, qd.reshape(runs), [p.reshape(runs) for p in pieces])
            odqs.append(odq.reshape(line))
            dkvs.append([d.reshape(line) for d in dkv])

        zero = jnp.zeros_like(bin_half)
        bins = jnp.where(
            core == 0, jnp.concatenate([bin_half, zero], 1), jnp.concatenate([zero, bin_half], 1)
        ).reshape(-1, width)
        half_ff = mlp_grads.shape[1]
        output, input_grad, vec, final = finish(
            mesh, odqs, dkvs, mlp_grads.reshape(2 * half_ff, width), out_part, gn_part, hid, og, og2,
            normed2, bins, again, mgain, w_qkv, w_dense, b_dense[None], b_out[None], tables,
        )
        win, wout, wqkv, wdense = expand(
            final, ((half_ff, True), (half_ff, False), (3 * width // 2, True), (width // 2, False))
        )
        return (
            output[None],
            input_grad[None],
            vec[0],
            vec[1],
            vec[2],
            vec[3],
            wqkv,
            vec[4:7].reshape(-1),
            wdense,
            vec[7],
            win,
            vec[8:].reshape(-1),
            wout,
            vec[7],
        )

    rows = P("seq", "blk", None)
    return jax.shard_map(
        on_device,
        mesh=mesh,
        in_specs=(rows, P("seq", "blk")) + (P(),) * 12 + (rows,),
        out_specs=(rows, rows) + (P(),) * 12,
        check_vma=False,
    )
```

```python
import functools

import jax
import jax.numpy as jnp
import numpy as np
from jax import lax
from jax.experimental import pallas as pl
from jax.experimental.pallas import tpu as pltpu
from jax.sharding import PartitionSpec as P

HEADS = 12
HEAD_DIM = 64
ROTARY = 16
GROUP = 128
HEAD_GROUPS = 4
PER_GROUP = HEADS // HEAD_GROUPS
NORM_EPSILON = 1e-05
ROTARY_BASE = 10000.0
MASKED = -1e30
VMEM_BYTES = 62 * 1024 * 1024

F32 = jnp.float32
BF16 = jnp.bfloat16
IN_VMEM = pl.BlockSpec(memory_space=pltpu.VMEM)
IN_SMEM = pl.BlockSpec(memory_space=pltpu.SMEM)


def mm(a, b):
    return lax.dot_general(a, b, (((1,), (0,)), ((), ())), preferred_element_type=F32)


def mm_nt(a, b):
    return lax.dot_general(a, b, (((1,), (1,)), ((), ())), preferred_element_type=F32)


def mm_tn(a, b):
    return lax.dot_general(a, b, (((0,), (0,)), ((), ())), preferred_element_type=F32)


def normalise(rows):
    centre = rows - jnp.mean(rows, axis=-1, keepdims=True)
    spread = jnp.mean(centre * centre, axis=-1, keepdims=True)
    scale = lax.rsqrt(spread + NORM_EPSILON)
    return centre * scale, scale


def norm_back(grad, xhat, scale, gain):
    eg = grad * gain
    return scale * (
        eg
        - jnp.mean(eg, axis=-1, keepdims=True)
        - xhat * jnp.mean(eg * xhat, axis=-1, keepdims=True)
    )


def params():
    return pltpu.CompilerParams(vmem_limit_bytes=VMEM_BYTES)


def front_kernel(hid, og, gain, bias, wqkv, bqkv, wdense, cosw, sina, sinb, msg):
    rows = hid[...].astype(F32)
    xhat, _ = normalise(rows)
    normed = (xhat * gain[...].astype(F32) + bias[...].astype(F32)).astype(BF16)
    mixed = mm(normed, wqkv[...]) + bqkv[...].astype(F32)
    datt = mm_nt(og[...], wdense[...])
    width = hid.shape[1]
    lane = lax.broadcasted_iota(jnp.int32, (rows.shape[0], 128), 1)
    low = lane < HEAD_DIM
    ca, sa, sb = cosw[...], sina[...], sinb[...]

    def turned(u):
        return u * ca + pltpu.roll(u, 120, 1) * sa + pltpu.roll(u, 8, 1) * sb

    for tile in range(HEADS // 2):
        at = tile * 128
        q = turned(mixed[:, at : at + 128]) * (HEAD_DIM**-0.5)
        k = turned(mixed[:, width + at : width + at + 128])
        v = mixed[:, 2 * width + at : 2 * width + at + 128]
        d = datt[:, at : at + 128]
        for part, (one, two) in enumerate(((q, d), (k, v))):
            for odd in range(2):
                head = 2 * tile + odd
                if odd == 0:
                    packed = jnp.where(low, one, pltpu.roll(two, 64, 1))
                else:
                    packed = jnp.where(low, pltpu.roll(one, 64, 1), two)
                msg[head % PER_GROUP, head // PER_GROUP, part] = packed.astype(BF16)


def front(hid, og, gain, bias, wqkv, bqkv, wdense, tables):
    rows = hid.shape[0]
    return pl.pallas_call(
        front_kernel,
        out_shape=jax.ShapeDtypeStruct((PER_GROUP, HEAD_GROUPS, 2, rows, 128), BF16),
        in_specs=[IN_VMEM] * 10,
        out_specs=IN_VMEM,
        compiler_params=params(),
        name="front",
    )(hid, og, gain, bias, wqkv, bqkv, wdense, *tables)


def mlp_kernel(
    core, hid, og, again, abias, mgain, mbias, win, bin_, wout,
    grads, bin_grad, out_part, gn_part, normed_attn, normed_s,
):
    step = pl.program_id(0)

    @pl.when(step == 0)
    def _():
        xhat, _ = normalise(hid[...].astype(F32))
        normed_s[...] = (xhat * mgain[...].astype(F32) + mbias[...].astype(F32)).astype(BF16)
        normed_attn[...] = (xhat * again[...].astype(F32) + abias[...].astype(F32)).astype(BF16)
        out_part[...] = jnp.zeros_like(out_part)
        gn_part[...] = jnp.zeros_like(gn_part)

    x = normed_s[...]
    w1 = win[...]
    w2 = wout[...]
    inner = mm(x, w1) + bin_[...].astype(F32)
    cdf = 0.5 * (1.0 + lax.erf(inner * (0.5**0.5)))
    act = (inner * cdf).astype(BF16)
    pdf = jnp.exp(-0.5 * inner * inner) * (0.5 * 2.0**0.5 * 3.141592653589793**-0.5)
    gact = mm_nt(og[...], w2)
    ginner = (gact * (cdf + inner * pdf)).astype(BF16)
    bin_grad[...] = jnp.sum(ginner.astype(F32), axis=0, keepdims=True)
    grads[0] = mm_tn(ginner, x).astype(BF16)
    grads[1] = mm_tn(act, og[...]).astype(BF16)
    out_part[...] += mm(act, w2)
    gn_part[...] += mm_nt(ginner, w1)


def mlp(core, hid, og, again, abias, mgain, mbias, win, b_in, wout):
    rows, width = hid.shape
    half = win.shape[1] // 2
    chunk = 512
    steps = half // chunk
    whole = lambda i, c: (0, 0)
    return pl.pallas_call(
        mlp_kernel,
        grid_spec=pltpu.PrefetchScalarGridSpec(
            num_scalar_prefetch=1,
            grid=(steps,),
            in_specs=[
                pl.BlockSpec((rows, width), whole),
                pl.BlockSpec((rows, width), whole),
                pl.BlockSpec((1, width), whole),
                pl.BlockSpec((1, width), whole),
                pl.BlockSpec((1, width), whole),
                pl.BlockSpec((1, width), whole),
                pl.BlockSpec((width, chunk), lambda i, c: (0, c[0] * steps + i)),
                pl.BlockSpec((1, chunk), lambda i, c: (0, c[0] * steps + i)),
                pl.BlockSpec((chunk, width), lambda i, c: (c[0] * steps + i, 0)),
            ],
            out_specs=[
                pl.BlockSpec((2, chunk, width), lambda i, c: (0, i, 0)),
                pl.BlockSpec((1, chunk), lambda i, c: (0, i)),
                pl.BlockSpec((rows, width), whole),
                pl.BlockSpec((rows, width), whole),
                pl.BlockSpec((rows, width), whole),
            ],
            scratch_shapes=[pltpu.VMEM((rows, width), BF16)],
        ),
        out_shape=[
            jax.ShapeDtypeStruct((2, half, width), BF16),
            jax.ShapeDtypeStruct((1, half), F32),
            jax.ShapeDtypeStruct((rows, width), F32),
            jax.ShapeDtypeStruct((rows, width), F32),
            jax.ShapeDtypeStruct((rows, width), BF16),
        ],
        compiler_params=params(),
        name="mlp",
    )(core, hid, og, again, abias, mgain, mbias, win, b_in, wout)


def attention_kernel(blocks, pieces, n_query, *refs):
    tab = refs[0]
    qd_ref = refs[1]
    kv_refs = refs[2 : 2 + pieces]
    odq_ref = refs[2 + pieces]
    dkv_refs = refs[3 + pieces : 3 + 2 * pieces]
    kvs, kvt, sbuf, acc = refs[3 + 2 * pieces :]
    kb_rows = blocks
    per_piece = kv_refs[0].shape[0]
    n_run = pieces * per_piece

    def group_rows(g):
        return pl.ds(pl.multiple_of(g * GROUP, GROUP), GROUP)

    for piece in range(pieces):

        def place(i, _, piece=piece):
            rows = group_rows(tab[piece * per_piece + i])
            blk = kv_refs[piece][i]
            kvs[rows, :] = blk
            kvt[:, rows] = blk.T
            acc[rows, :] = jnp.zeros((GROUP, 128), F32)
            return 0

        lax.fori_loop(0, per_piece, place, 0, unroll=4)

    lane = lax.broadcasted_iota(jnp.int32, (2 * GROUP, 128), 1)
    row = lax.broadcasted_iota(jnp.int32, (128, 2 * GROUP), 0)
    qcol = lax.broadcasted_iota(jnp.int32, (1, 2 * GROUP), 1)
    krow = lax.broadcasted_iota(jnp.int32, (kb_rows, 1), 0)

    def pair_step(pair, _):
        i0 = tab[n_run + 2 * pair]
        i1 = tab[n_run + 2 * pair + 1]
        g0 = tab[n_run + n_query + 2 * pair]
        g1 = tab[n_run + n_query + 2 * pair + 1]
        qd = jnp.concatenate([qd_ref[i0], qd_ref[i1]], axis=0)
        zero = jnp.zeros_like(qd)
        w_keys = jnp.concatenate(
            [jnp.where(lane < HEAD_DIM, qd, zero), jnp.where(lane >= HEAD_DIM, qd, zero)], axis=0
        )
        qdt = qd.T
        zero_t = jnp.zeros_like(qdt)
        w_score = jnp.where(row < HEAD_DIM, qdt, zero_t)
        w_dprob = jnp.where(row >= HEAD_DIM, qdt, zero_t)
        qpos = jnp.where(qcol < GROUP, g0 * GROUP + qcol, (g1 - 1) * GROUP + qcol)
        n_full = (g0 * GROUP) // kb_rows
        n_all = (g1 * GROUP) // kb_rows + 1

        def block_rows(kb):
            return pl.ds(pl.multiple_of(kb * kb_rows, kb_rows), kb_rows)

        def score_step(kb, top, masked):
            rows = block_rows(kb)
            s = mm(kvs[rows, :], w_score)
            if masked:
                s = jnp.where(kb * kb_rows + krow <= qpos, s, MASKED)
            sbuf[rows, :] = s
            return jnp.maximum(top, jnp.max(s.reshape(kb_rows // 8, 8, 2 * GROUP), axis=0))

        top = jnp.full((8, 2 * GROUP), MASKED, F32)
        top = lax.fori_loop(0, n_full, lambda kb, c: score_step(kb, c, False), top)
        top = lax.fori_loop(n_full, n_all, lambda kb, c: score_step(kb, c, True), top)
        top = jnp.max(top, axis=0, keepdims=True)

        def value_step(kb, carry):
            total, out = carry
            rows = block_rows(kb)
            e = jnp.exp(sbuf[rows, :] - top)
            sbuf[rows, :] = e
            total = total + jnp.sum(e.reshape(kb_rows // 8, 8, 2 * GROUP), axis=0)
            return total, out + mm(kvt[HEAD_DIM:128, rows], e.astype(BF16))

        total, out = lax.fori_loop(
            0,
            n_all,
            value_step,
            (jnp.zeros((8, 2 * GROUP), F32), jnp.zeros((HEAD_DIM, 2 * GROUP), F32)),
        )
        inv = 1.0 / jnp.sum(total, axis=0, keepdims=True)
        out = out * inv
        delta = jnp.sum(out * qdt[HEAD_DIM:128, :].astype(F32), axis=0, keepdims=True)

        def grad_step(kb, dq):
            rows = block_rows(kb)
            p = sbuf[rows, :] * inv
            dp = mm(kvs[rows, :], w_dprob)
            ds = (p * (dp - delta)).astype(BF16)
            acc[rows, :] += mm(jnp.concatenate([ds, p.astype(BF16)], axis=1), w_keys)
            return dq + mm(kvt[0:HEAD_DIM, rows], ds)

        dq = lax.fori_loop(0, n_all, grad_step, jnp.zeros((HEAD_DIM, 2 * GROUP), F32))
        odq = jnp.concatenate([out, dq * (HEAD_DIM**-0.5)], axis=0).astype(BF16).T
        odq_ref[i0] = odq[:GROUP]
        odq_ref[i1] = odq[GROUP:]
        return 0

    lax.fori_loop(0, n_query // 2, pair_step, 0)

    for piece in range(pieces):

        def give(i, _, piece=piece):
            dkv_refs[piece][i] = acc[group_rows(tab[piece * per_piece + i]), :].astype(BF16)
            return 0

        lax.fori_loop(0, per_piece, give, 0, unroll=4)


def attention(tab, qd, kvs):
    pieces = len(kvs)
    n_query = qd.shape[0]
    n_key = pieces * kvs[0].shape[0] * GROUP
    blocks = 1024
    run = jax.ShapeDtypeStruct(kvs[0].shape, BF16)
    outs = pl.pallas_call(
        functools.partial(attention_kernel, blocks, pieces, n_query),
        out_shape=[jax.ShapeDtypeStruct(qd.shape, BF16)] + [run] * pieces,
        in_specs=[IN_SMEM] + [IN_VMEM] * (1 + pieces),
        out_specs=[IN_VMEM] * (1 + pieces),
        scratch_shapes=[
            pltpu.VMEM((n_key, 128), BF16),
            pltpu.VMEM((128, n_key), BF16),
            pltpu.VMEM((n_key, 2 * GROUP), F32),
            pltpu.VMEM((n_key, 128), F32),
        ],
        compiler_params=params(),
        name="attention",
    )(tab, qd, *kvs)
    return outs[0], outs[1:]


class Place:
    def __init__(self, n_seq, n_blk):
        self.n_seq, self.n_blk = n_seq, n_blk
        self.n_low = n_blk // HEAD_GROUPS
        self.n_rest = n_blk // 4
        self.s = lax.axis_index("seq")
        self.b = lax.axis_index("blk")
        self.core = self.b % 2
        self.x = (self.b // 2) % 2
        self.rest = self.b // 4
        self.hi = self.b // self.n_low

    def flip(self, bit):
        step = 1 << bit
        return (self.s, self.b + step - 2 * step * ((self.b // step) % 2))

    def to_seq(self):
        return ((self.s + 1) % self.n_seq, self.b)

    def to_rest(self, by):
        return (self.s, ((self.rest + by) % self.n_rest) * 4 + self.b % 4)

    def to_group(self, by):
        return (self.s, ((self.hi + by) % HEAD_GROUPS) * self.n_low + self.b % self.n_low)

    def partners(self):
        found = [self.flip(bit) for bit in range(self.n_low.bit_length() - 1)]
        found += [self.to_seq()]
        found += [self.to_rest(by) for by in range(1, self.n_rest)]
        if self.n_low != 4:
            found += [self.to_group(by) for by in range(1, HEAD_GROUPS)]
        return found

    def meet(self):
        barrier = pltpu.get_barrier_semaphore()
        partners = self.partners()
        for device in partners:
            pl.semaphore_signal(
                barrier, inc=1, device_id=device, device_id_type=pl.DeviceIdType.MESH
            )
        pl.semaphore_wait(barrier, len(partners))


class Wires:
    def __init__(self, sends, recvs):
        self.sends, self.recvs, self.used = sends, recvs, 0

    def copy(self, src, dst, device):
        at = self.used
        self.used += 1
        return pltpu.make_async_remote_copy(
            src_ref=src,
            dst_ref=dst,
            send_sem=self.sends.at[at],
            recv_sem=self.recvs.at[at],
            device_id=device,
            device_id_type=pl.DeviceIdType.MESH,
        )


def add_rows(dst, dst_at, others, count, out=None, out_at=0, lanes=slice(None), got_lanes=slice(None)):
    block = 16
    for size in (96, 64, 48, 32):
        if count % size == 0:
            block = size
            break
    out = dst if out is None else out

    def step(i, _):
        total = dst[pl.ds(pl.multiple_of(dst_at + i * block, 16), block), lanes].astype(F32)
        for ref, start in others:
            rows = pl.ds(pl.multiple_of(start + i * block, 16), block)
            total = total + ref[rows, got_lanes].astype(F32)
        out[pl.ds(pl.multiple_of(out_at + i * block, 16), block), lanes] = total.astype(BF16)
        return 0

    lax.fori_loop(0, count // block, step, 0)


def unit_copies(n_rest):
    return 2 * (2 + n_rest - 1) + 1


class Unit:
    def __init__(self, place, wires, data, base, size, order, got1, got2, got3, out, final, final_base, local):
        pairs = {"x": (place.x, place.flip(1)), "y": (place.s, place.to_seq())}
        (self.bit1, self.dev1), (self.bit2, self.dev2) = pairs[order[0]], pairs[order[1]]
        self.place, self.data, self.out = place, data, out
        self.base, self.size = base, size
        self.h, self.q = size // 2, size // 4
        n = place.n_rest
        self.cuts = 1 if (self.q // n) % 16 == 0 else 2
        self.e = self.q * self.cuts // n
        self.w = data.shape[1] // self.cuts
        self.base1 = base + self.bit1 * self.h
        self.base2 = self.base1 + self.bit2 * self.q
        self.got1, self.got2, self.got3 = got1, got2, got3
        self.fetch = None
        if local is not None:
            kept = pl.ds(pl.multiple_of(self.base1, 16), self.h)
            self.fetch = pltpu.make_async_copy(data.at[kept], out.at[kept], local)
        z = place.rest

        def cell(ref, start, index):
            at = pl.multiple_of(start + (index // self.cuts) * self.e, 16)
            if self.cuts == 1:
                return ref.at[pl.ds(at, self.e)]
            return ref.at[
                pl.ds(at, self.e), pl.ds(pl.multiple_of((index % self.cuts) * self.w, 128), self.w)
            ]

        def landing(by):
            slot = pl.ds((by - 1) * self.e, self.e)
            return got3.at[slot] if self.cuts == 1 else got3.at[slot, pl.ds(0, self.w)]

        def rows(ref, start, count):
            return ref.at[pl.ds(pl.multiple_of(start, 16), count)]

        self.rs1 = [wires.copy(rows(data, base + (1 - self.bit1) * self.h, self.h), got1, self.dev1)]
        self.rs2 = [wires.copy(rows(got1, (1 - self.bit2) * self.q, self.q), got2, self.dev2)]
        self.rs3 = [
            wires.copy(cell(got2, 0, (z + by) % n), landing(by), place.to_rest(by))
            for by in range(1, n)
        ]
        self.ag3 = [
            wires.copy(cell(out, self.base2, z), cell(out, self.base2, z), place.to_rest(by))
            for by in range(1, n)
        ]
        self.ag2 = [wires.copy(rows(out, self.base2, self.q), rows(out, self.base2, self.q), self.dev2)]
        self.ag1 = [wires.copy(rows(out, self.base1, self.h), rows(out, self.base1, self.h), self.dev1)]
        self.agc = [
            wires.copy(
                rows(out, base, size),
                final.at[place.core, pl.ds(final_base, size)],
                place.flip(0),
            )
        ]
        self.sent = []

    def start(self, copies):
        for copy in copies:
            copy.start()
        self.sent = self.sent + copies

    def arrive(self, copies):
        for copy in copies:
            copy.wait_recv()

    def stage0(self):
        self.start(self.rs1)
        if self.fetch is not None:
            self.fetch.start()

    def stage1(self):
        self.arrive(self.rs1)
        for copy in self.rs1:
            copy.wait_send()
        self.sent = [copy for copy in self.sent if not any(copy is gone for gone in self.rs1)]
        if self.fetch is not None:
            self.fetch.wait()
        add_rows(self.got1, 0, [(self.data if self.fetch is None else self.out, self.base1)], self.h)
        self.start(self.rs2)

    def stage2(self):
        self.arrive(self.rs2)
        add_rows(self.got2, 0, [(self.got1, self.bit2 * self.q)], self.q)
        self.start(self.rs3)

    def stage3(self):
        self.arrive(self.rs3)
        others = [(self.got3, k * self.e) for k in range(self.place.n_rest - 1)]
        z = self.place.rest
        at = (z // self.cuts) * self.e
        lanes = got_lanes = slice(None)
        if self.cuts > 1:
            lanes = pl.ds(pl.multiple_of((z % self.cuts) * self.w, 128), self.w)
            got_lanes = pl.ds(0, self.w)
        add_rows(self.got2, at, others, self.e, self.out, self.base2 + at, lanes, got_lanes)
        self.start(self.ag3)

    def stage4(self):
        self.arrive(self.ag3)
        self.start(self.ag2)

    def stage5(self):
        self.arrive(self.ag2)
        self.start(self.ag1)

    def stage6(self):
        self.arrive(self.ag1)
        self.start(self.agc)

    def finish(self):
        self.arrive(self.agc)
        for copy in self.sent:
            copy.wait_send()


def tail_compute(
    odq, dkv, hi, hid, og, again, mgain, wqkv, wdense, bdense, bout, mout, gnm,
    cosw, sina, sinb, output, input_grad, send, small,
):
    rows = hid[...].astype(F32)
    count, width = rows.shape
    lane = lax.broadcasted_iota(jnp.int32, (count, 128), 1)
    low = lane < HEAD_DIM
    ca, sa, sb = cosw[...], sina[...], sinb[...]

    def turned_back(g):
        return g * ca - pltpu.roll(g, 120, 1) * sa - pltpu.roll(g, 8, 1) * sb

    def head(ref, a):
        at = (a // PER_GROUP - hi + HEAD_GROUPS) % HEAD_GROUPS
        return ref[a % PER_GROUP, at].astype(F32)

    outs, grads = [], [[], [], []]
    for tile in range(HEADS // 2):
        one, two = head(odq, 2 * tile), head(odq, 2 * tile + 1)
        outs.append(jnp.where(low, one, pltpu.roll(two, 64, 1)).astype(BF16))
        grads[0].append(turned_back(jnp.where(low, pltpu.roll(one, 64, 1), two)).astype(BF16))
        one, two = head(dkv, 2 * tile), head(dkv, 2 * tile + 1)
        grads[1].append(
            turned_back(jnp.where(low, one, pltpu.roll(two, 64, 1))).astype(BF16)
        )
        grads[2].append(jnp.where(low, pltpu.roll(one, 64, 1), two).astype(BF16))
    att = jnp.concatenate(outs, axis=1)
    dmixed = jnp.concatenate(grads[0] + grads[1] + grads[2], axis=1)
    half_m, half_a = dmixed.shape[1] // 2, width // 2
    for side in range(2):
        send[side, :, :half_m] = dmixed[:, side * half_m : (side + 1) * half_m]
        send[side, :, half_m:] = att[:, side * half_a : (side + 1) * half_a]
    branch = mm(att, wdense[...]) + bdense[...].astype(F32)
    output[...] = (rows + branch + (mout + bout[...].astype(F32))).astype(BF16)
    gna = mm_nt(dmixed, wqkv[...])
    xhat, scale = normalise(rows)
    cot = og[...].astype(F32)
    input_grad[...] = (
        cot
        + norm_back(gna, xhat, scale, again[...].astype(F32))
        + norm_back(gnm, xhat, scale, mgain[...].astype(F32))
    ).astype(BF16)
    small[0:1, :] = jnp.sum(gna * xhat, axis=0, keepdims=True)
    small[1:2, :] = jnp.sum(gna, axis=0, keepdims=True)
    small[2:3, :] = jnp.sum(gnm * xhat, axis=0, keepdims=True)
    small[3:4, :] = jnp.sum(gnm, axis=0, keepdims=True)
    for part in range(3):
        cols = dmixed[:, part * width : (part + 1) * width].astype(F32)
        small[4 + part : 5 + part, :] = jnp.sum(cols, axis=0, keepdims=True)
    small[7:8, :] = jnp.sum(cot, axis=0, keepdims=True)


def weight_compute(own, other, normed, og, grads):
    half_m = own.shape[1] * 3 // 4
    both = jnp.concatenate([own, other], axis=0)
    grads[0:half_m, :] = mm_tn(both[:, :half_m], normed[...]).astype(BF16)
    grads[half_m:, :] = mm_tn(both[:, half_m:], og[...]).astype(BF16)


def finish_kernel(
    n_seq, n_blk, units1, units2, pieces,
    odq0, odq1, odq2, *refs,
):
    dkvs = [refs[j * pieces : (j + 1) * pieces] for j in range(PER_GROUP)]
    (
        grads1, out_part, gn_part, hid, og, og2, normed2, bins, again, mgain, wqkv, wdense, bdense, bout,
        cosw, sina, sinb,
        output, input_grad, small_out, final,
        odq_all, dkv_all, dkv_got, mout_got, gn_got, send, other, grads2, small, small_got,
        got1, got2, got3, out1, out2, sends, recvs, local_sem,
    ) = refs[PER_GROUP * pieces :]
    place = Place(n_seq, n_blk)
    wires = Wires(sends, recvs)
    odqs = (odq0, odq1, odq2)
    tokens, width = hid.shape
    n_rest = place.n_rest
    rows1 = grads1.shape[0]
    place.meet()
    sent = []

    def go(copy):
        copy.start()
        sent.append(copy)
        return copy

    mout_copy = go(wires.copy(out_part.at[pl.ds(tokens, tokens)], mout_got, place.flip(0)))
    gn_copy = go(wires.copy(gn_part.at[pl.ds(tokens, tokens)], gn_got, place.flip(0)))
    low_bits = place.n_low.bit_length() - 1
    stage_copies = []
    for j in range(PER_GROUP):
        half = pieces // 2
        stage_copies.append([
            go(wires.copy(dkvs[j][half + i], dkv_got.at[j, i], place.flip(0))) for i in range(half)
        ])
    home = []
    for j in range(PER_GROUP):
        for by in range(1, HEAD_GROUPS):
            home.append(go(wires.copy(odqs[j].at[by], odq_all.at[j, by], place.to_group(HEAD_GROUPS - by))))
    units = []
    at = 0
    for base, size, order in units1:
        units.append(Unit(
            place, wires, grads1, base, size, order,
            got1.at[pl.ds(at // 2, size // 2)], got2.at[pl.ds(at // 4, size // 4)],
            got3.at[pl.ds(at // 2, size // 2)], out1, final, base, local_sem.at[2 + len(units)],
        ))
        at += size
    units_b = []
    for base, size, order in units2:
        units_b.append(Unit(
            place, wires, grads2, base, size, order,
            got1.at[pl.ds(at // 2, size // 2)], got2.at[pl.ds(at // 4, size // 4)],
            got3.at[pl.ds(at // 2, size // 2)], out2, final, rows1 + base, None,
        ))
        at += size
    for unit in units:
        unit.stage0()

    slot = 0
    half = pieces // 2
    for bit in range(low_bits):
        after = slot + half
        for j in range(PER_GROUP):
            for copy in stage_copies[j]:
                copy.wait_recv()
            for i in range(half):
                mine = dkvs[j][i][...] if bit == 0 else dkv_got[j, slot - 2 * half + i]
                dkv_got[j, slot + i] = (mine.astype(F32) + dkv_got[j, slot + i].astype(F32)).astype(BF16)
            if half > 1:
                stage_copies[j] = [
                    go(wires.copy(dkv_got.at[j, slot + half // 2 + i], dkv_got.at[j, after + i], place.flip(bit + 1)))
                    for i in range(half // 2)
                ]
            else:
                for by in range(1, HEAD_GROUPS):
                    home.append(go(wires.copy(
                        dkv_got.at[j, slot, by], dkv_all.at[j, by], place.to_group(HEAD_GROUPS - by)
                    )))
                dkv_all[j, 0] = dkv_got[j, slot, 0]
        slot = after
        half //= 2
    for j in range(PER_GROUP):
        odq_all[j, 0] = odqs[j][0]
    for unit in units:
        unit.stage1()
    for copy in home:
        copy.wait_recv()
    mout_copy.wait_recv()
    gn_copy.wait_recv()
    mout = out_part[0:tokens, :] + mout_got[...]
    gnm = gn_part[0:tokens, :] + gn_got[...]
    tail_compute(
        odq_all, dkv_all, place.hi, hid, og, again, mgain, wqkv, wdense, bdense, bout, mout, gnm,
        cosw, sina, sinb, output, input_grad, send, small,
    )
    other_copy = go(wires.copy(send.at[1 - place.core], other, place.flip(0)))
    for unit in units:
        unit.stage2()
    other_copy.wait_recv()
    weight_compute(send[place.core], other[...], normed2, og2, grads2)
    for unit in units_b:
        unit.stage0()
    small[8:, :] = bins[...]
    for unit in units:
        unit.stage3()
    for unit in units_b:
        unit.stage1()
    order = [[place.flip(0)], [place.flip(1)], [place.to_seq()], [place.to_rest(by) for by in range(1, n_rest)]]
    slot = 0
    for devices in order:
        copies = [wires.copy(small, small_got.at[slot + i], device) for i, device in enumerate(devices)]
        for copy in copies:
            copy.start()
        for copy in copies:
            copy.wait()
        total = small[...]
        for i in range(len(devices)):
            total = total + small_got[slot + i]
        small[...] = total
        slot += len(devices)
    small_out[...] = small[...]
    for unit in units:
        unit.stage4()
    for unit in units_b:
        unit.stage2()
    for unit in units:
        unit.stage5()
    for unit in units_b:
        unit.stage3()
    for unit in units:
        unit.stage6()
    for unit in units_b:
        unit.stage4()
    for unit in units_b:
        unit.stage5()
    for unit in units_b:
        unit.stage6()
    keep1 = pltpu.make_async_copy(out1, final.at[place.core, pl.ds(0, rows1)], local_sem.at[0])
    keep2 = pltpu.make_async_copy(out2, final.at[place.core, pl.ds(rows1, grads2.shape[0])], local_sem.at[1])
    keep1.start()
    keep2.start()
    for unit in units + units_b:
        unit.finish()
    for copy in sent:
        copy.wait_send()
    keep1.wait()
    keep2.wait()


def finish(mesh, odqs, dkvs, grads1, out_part, gn_part, hid, og, og2, normed2, bins, again, mgain, wqkv, wdense, bdense, bout, tables):
    n_seq, n_blk = mesh.shape["seq"], mesh.shape["blk"]
    n_rest = n_blk // 4
    tokens, width = hid.shape
    pieces = len(dkvs[0])
    rows1, rows2 = grads1.shape[0], 2 * width
    fine = (rows1 // 4) % (4 * n_rest * 16) == 0
    parts = 4 if fine else 2
    units1 = [(i * rows1 // parts, rows1 // parts, "xy" if 2 * i < parts else "yx") for i in range(parts)]
    parts = 2 if fine else 1
    units2 = [(i * rows2 // parts, rows2 // parts, "xy" if 2 * i < parts else "yx") for i in range(parts)]
    total = rows1 + rows2
    copies = (len(units1) + len(units2)) * unit_copies(n_rest)
    copies += 3 + PER_GROUP * (2 * (HEAD_GROUPS - 1) + pieces - 1) + 3 + n_rest - 1
    line = (HEAD_GROUPS, tokens, 128)
    n_small = 8 + bins.shape[0]
    inputs = list(odqs) + [p for d in dkvs for p in d] + [
        grads1, out_part, gn_part, hid, og, og2, normed2, bins, again, mgain, wqkv, wdense, bdense, bout, *tables,
    ]
    return pl.pallas_call(
        functools.partial(finish_kernel, n_seq, n_blk, units1, units2, pieces),
        out_shape=[
            jax.ShapeDtypeStruct((tokens, width), BF16),
            jax.ShapeDtypeStruct((tokens, width), BF16),
            jax.ShapeDtypeStruct((n_small, width), F32),
            jax.ShapeDtypeStruct((2, total, width), BF16),
        ],
        in_specs=[pl.BlockSpec(memory_space=pl.ANY) if v is grads1 else IN_VMEM for v in inputs],
        out_specs=[IN_VMEM] * 3 + [pl.BlockSpec(memory_space=pl.ANY)],
        scratch_shapes=[
            pltpu.VMEM((PER_GROUP,) + line, BF16),
            pltpu.VMEM((PER_GROUP,) + line, BF16),
            pltpu.VMEM((PER_GROUP, pieces - 1) + line, BF16),
            pltpu.VMEM((tokens, width), F32),
            pltpu.VMEM((tokens, width), F32),
            pltpu.VMEM((2, tokens, 2 * width), BF16),
            pltpu.VMEM((tokens, 2 * width), BF16),
            pltpu.VMEM((rows2, width), BF16),
            pltpu.VMEM((n_small, width), F32),
            pltpu.VMEM((3 + n_rest - 1, n_small, width), F32),
            pltpu.VMEM((total // 2, width), BF16),
            pltpu.VMEM((total // 4, width), BF16),
            pltpu.VMEM((total // 2, width), BF16),
            pltpu.VMEM((rows1, width), BF16),
            pltpu.VMEM((rows2, width), BF16),
            pltpu.SemaphoreType.DMA((copies,)),
            pltpu.SemaphoreType.DMA((copies,)),
            pltpu.SemaphoreType.DMA((2 + len(units1),)),
        ],
        compiler_params=pltpu.CompilerParams(
            vmem_limit_bytes=VMEM_BYTES, collective_id=1, has_side_effects=True
        ),
        name="finish",
    )(*inputs)


def expand_kernel(marks, block, *outs):
    step = pl.program_id(0)
    for out, (first, last, turn) in zip(outs, marks):

        @pl.when((step >= first) & (step < last))
        def _(out=out, turn=turn):
            rows = block[0].astype(F32)
            out[...] = rows.T if turn else rows


def expand(final, sizes):
    width = final.shape[2]
    block = width // 2
    marks, specs, shapes, firsts = [], [], [], []
    first = offset = 0
    for rows, turn in sizes:
        each = rows // block
        marks.append((first, first + 2 * each, turn))
        firsts.append((first, each, offset))

        def at(i, first=first, count=2 * each):
            return jnp.clip(i - first, 0, count - 1)

        if turn:
            specs.append(pl.BlockSpec((width, block), lambda i, at=at: (0, at(i))))
            shapes.append(jax.ShapeDtypeStruct((width, 2 * rows), F32))
        else:
            specs.append(pl.BlockSpec((block, width), lambda i, at=at: (at(i), 0)))
            shapes.append(jax.ShapeDtypeStruct((2 * rows, width), F32))
        first += 2 * each
        offset += each

    def source(i):
        core, row = 0, 0
        for begin, each, offset in firsts:
            here = (i >= begin) & (i < begin + 2 * each)
            core = jnp.where(here, (i - begin) // each, core)
            row = jnp.where(here, offset + (i - begin) % each, row)
        return (core, row, 0)

    return pl.pallas_call(
        functools.partial(expand_kernel, marks),
        grid=(first,),
        in_specs=[pl.BlockSpec((1, block, width), source)],
        out_specs=specs,
        out_shape=shapes,
        compiler_params=params(),
        name="expand",
    )(final)


def half_rows(d):
    return pl.ds(pl.multiple_of(d * GROUP, GROUP), GROUP)


class Attention:
    def __init__(self, lines, devices, flags, kk, vv, kkt, vvt, sb, acc):
        self.lines, self.devices, self.flags = lines, devices, flags
        self.kk, self.vv, self.kkt, self.vvt = kk, vv, kkt, vvt
        self.sb, self.acc = sb, acc
        self.n = devices * GROUP

    def prepare(self, pieces):
        low_lanes = lax.broadcasted_iota(jnp.int32, (GROUP, 128), 1) < HEAD_DIM
        for p, ref in enumerate(pieces):

            def step(r, _, p=p, ref=ref):
                rows = half_rows(p * self.lines + r)
                low, high = ref[r, 0:GROUP, :], ref[r, GROUP : 2 * GROUP, :]
                lowt, hight = low.T, high.T
                low, high = low.astype(F32), high.astype(F32)
                self.kk[rows, :] = jnp.where(low_lanes, low, pltpu.roll(high, 64, 1)).astype(BF16)
                self.vv[rows, :] = jnp.where(low_lanes, pltpu.roll(low, 64, 1), high).astype(BF16)
                self.kkt[0:HEAD_DIM, rows] = lowt[0:HEAD_DIM]
                self.kkt[HEAD_DIM:128, rows] = hight[0:HEAD_DIM]
                self.vvt[0:HEAD_DIM, rows] = lowt[HEAD_DIM:128]
                self.vvt[HEAD_DIM:128, rows] = hight[HEAD_DIM:128]
                self.acc[0, rows, :] = jnp.zeros((GROUP, 128), F32)
                self.acc[1, rows, :] = jnp.zeros((GROUP, 128), F32)
                return 0

            lax.fori_loop(0, self.lines, step, 0, unroll=self.lines)

    def masks(self, i):
        all_flags = self.flags[...].reshape(self.devices, 16, 128)
        mine = all_flags[i : i + 1]
        one, nil = jnp.ones(mine.shape, BF16), jnp.zeros(mine.shape, BF16)
        low, high = [], []
        for d in range(self.devices):
            theirs = all_flags[d : d + 1]
            low.append(one if d == i else jnp.where(theirs < mine, one, nil))
            high.append(nil if d == i else jnp.where(theirs > mine, one, nil))
        return jnp.concatenate(low + [nil], axis=0), jnp.concatenate(high + [one], axis=0)

    def pair(self, first, qd_ref, odq_ref):
        n, blocks = self.n, self.devices + 1
        wide = 2 * GROUP
        lane = lax.broadcasted_iota(jnp.int32, (GROUP, 128), 1)
        krow = lax.broadcasted_iota(jnp.int32, (GROUP, wide), 0)
        qcol = lax.broadcasted_iota(jnp.int32, (GROUP, wide), 1)
        seen = krow <= qcol % GROUP
        sb, kk, vv = self.sb, self.kk, self.vv
        masks, low_t, high_t, keys_w, both_w = [], [], [], [], []
        for slot in range(2):
            masks.append(self.masks(first + slot))
            qd = qd_ref[first + slot]
            qdt = qd.T
            low_t.append(qdt[:, 0:GROUP])
            high_t.append(qdt[:, GROUP:wide])
            low, high = qd[0:GROUP], qd[GROUP:wide]
            zero = jnp.zeros_like(low)
            ql, qh = jnp.where(lane < HEAD_DIM, low, zero), jnp.where(lane < HEAD_DIM, high, zero)
            dl, dh = jnp.where(lane < HEAD_DIM, zero, low), jnp.where(lane < HEAD_DIM, zero, high)
            keys_w.append(jnp.concatenate([jnp.concatenate([ql, qh], axis=1), jnp.concatenate([dl, dh], axis=1)], axis=0))
            both_w.append((qh, dh))
        none = jnp.zeros((128, GROUP), BF16)

        def diagonal(rows):
            own = [jnp.concatenate([low_t[k][rows], high_t[k][rows]], axis=0) for k in range(2)]
            return jnp.concatenate(
                [jnp.concatenate([own[0], none], axis=1), jnp.concatenate([none, own[1]], axis=1)], axis=0
            )

        def highs(rows):
            got = jnp.concatenate([high_t[0][rows], high_t[1][rows]], axis=1)
            return jnp.concatenate([got, jnp.zeros_like(got)], axis=0)

        q_rows, d_rows = slice(0, HEAD_DIM), slice(HEAD_DIM, 128)
        w_score, w_dprob = diagonal(q_rows), diagonal(d_rows)
        h_score, h_dprob = highs(q_rows), highs(d_rows)
        dout_low = jnp.concatenate([low_t[0][d_rows], low_t[1][d_rows]], axis=1).astype(F32)
        dout_high = jnp.concatenate([high_t[0][d_rows], high_t[1][d_rows]], axis=1).astype(F32)
        weights_all = jnp.concatenate([both_w[0][0], both_w[1][0], both_w[0][1], both_w[1][1]], axis=0)
        less = jnp.concatenate([low.astype(F32)[:, 0:8] for low, _ in masks], axis=2)
        low_lanes = lax.broadcasted_iota(jnp.int32, (blocks, 16, 128), 2) < HEAD_DIM

        def rows_seen(held):
            found = []
            for slot, (low, high) in enumerate(masks):
                lanes = jnp.where(low_lanes, low.astype(F32), high.astype(F32)).astype(BF16)
                x = jnp.concatenate([held[...], held[half_rows(first + slot), :]], axis=0)
                x = x.reshape(blocks, GROUP // 16, 16, 128) * lanes[:, None]
                found.append(x.reshape(blocks * GROUP, 128))
            return jnp.concatenate(found, axis=1)

        def columns_seen(held):
            found = []
            for slot, pair in enumerate(masks):
                for half, mask in enumerate(pair):
                    rows = slice(half * HEAD_DIM, half * HEAD_DIM + HEAD_DIM)
                    x = jnp.concatenate([held[rows, :], held[rows, half_rows(first + slot)]], axis=1)
                    line = jnp.concatenate([mask[d] for d in range(blocks)], axis=1)
                    x = x.reshape(HEAD_DIM // 16, 16, blocks * GROUP) * line[None]
                    found.append(x.reshape(HEAD_DIM, blocks * GROUP))
            return jnp.concatenate(found, axis=0)

        own, rest = pl.ds(0, blocks * GROUP), pl.ds(blocks * GROUP, n)

        def cut(x):
            return x.reshape(x.shape[0] // GROUP, GROUP // 8, 8, wide)

        def spread(low, high):
            return jnp.where(less > 0, low, high)[:, None]

        s = cut(mm(rows_seen(kk), w_score))
        hide = cut(jnp.where(seen, 0.0, MASKED))
        left = cut(jnp.where(seen | (qcol >= GROUP), 0.0, MASKED))
        right = cut(jnp.where(seen | (qcol < GROUP), 0.0, MASKED))
        s = [s[:first], s[first : first + 1] + left, s[first + 1 : first + 2] + right, s[first + 2 : -1], s[blocks - 1 :] + hide]
        s = jnp.concatenate([x for x in s if x.shape[0]], axis=0)
        sb[own, :] = s.reshape(blocks * GROUP, wide)
        tops = jnp.max(s, axis=1)
        s = mm(kk[...], h_score)
        sb[rest, :] = s
        top_low = jnp.max(jnp.max(jnp.where(less > 0, tops, MASKED), axis=0), axis=0, keepdims=True)
        top_high = jnp.maximum(
            jnp.max(jnp.where(less > 0, MASKED, tops), axis=0), jnp.max(s.reshape(n // 8, 8, wide), axis=0)
        )
        top_high = jnp.max(top_high, axis=0, keepdims=True)

        e = jnp.exp(cut(sb[own, :]) - spread(top_low, top_high))
        sums = jnp.sum(e, axis=1)
        e = e.reshape(blocks * GROUP, wide)
        sb[own, :] = e
        out = mm(columns_seen(self.vvt), e.astype(BF16))
        e = jnp.exp(sb[rest, :] - top_high)
        sb[rest, :] = e
        out_high = mm(self.vvt[0:HEAD_DIM, :], e.astype(BF16))
        total_low = jnp.sum(jnp.sum(jnp.where(less > 0, sums, 0.0), axis=0), axis=0, keepdims=True)
        total_high = jnp.sum(jnp.where(less > 0, 0.0, sums), axis=0) + jnp.sum(e.reshape(n // 8, 8, wide), axis=0)
        total_high = jnp.sum(total_high, axis=0, keepdims=True)

        def parts(x):
            low = jnp.concatenate([x[0:64, 0:GROUP], x[128:192, GROUP:wide]], axis=1)
            high = jnp.concatenate([x[64:128, 0:GROUP], x[192:256, GROUP:wide]], axis=1)
            return low, high

        yield
        inv_low, inv_high = 1.0 / total_low, 1.0 / total_high
        out_low, more = parts(out)
        out_low, out_high = out_low * inv_low, (out_high + more) * inv_high
        delta_low = jnp.sum(out_low * dout_low, axis=0, keepdims=True)
        delta_high = jnp.sum(out_high * dout_high, axis=0, keepdims=True)

        p = cut(sb[own, :]) * spread(inv_low, inv_high)
        dp = cut(mm(rows_seen(vv), w_dprob))
        ds = (p * (dp - spread(delta_low, delta_high))).reshape(blocks * GROUP, wide).astype(BF16)
        p = p.reshape(blocks * GROUP, wide).astype(BF16)
        dq = mm(columns_seen(self.kkt), ds)
        for slot in range(2):
            cols = slice(slot * GROUP, slot * GROUP + GROUP)
            got = mm(jnp.concatenate([ds[:, cols], p[:, cols]], axis=1), keys_w[slot])
            here = less[:, :, cols][:, None] > 0
            got = got.reshape(blocks, GROUP // 8, 8, wide)
            low = jnp.where(here, got[..., 0:128], 0.0).reshape(blocks * GROUP, 128)
            high = jnp.where(here, 0.0, got[..., 128:256]).reshape(blocks * GROUP, 128)
            self.acc[0] += low[0:n]
            self.acc[1] += high[0:n]
            self.acc[1, half_rows(first + slot), :] += high[n:]
        p = sb[rest, :] * inv_high
        dp = mm(vv[...], h_dprob)
        ds = (p * (dp - delta_high)).astype(BF16)
        self.acc[0] += mm(jnp.concatenate([ds, p.astype(BF16)], axis=1), weights_all)
        dq_low, dq_high = parts(dq)
        dq_high = dq_high + mm(self.kkt[0:HEAD_DIM, :], ds)
        for slot in range(2):
            cols = slice(slot * GROUP, slot * GROUP + GROUP)
            scale = HEAD_DIM**-0.5
            low = jnp.concatenate([out_low[:, cols], dq_low[:, cols] * scale], axis=0).astype(BF16).T
            high = jnp.concatenate([out_high[:, cols], dq_high[:, cols] * scale], axis=0).astype(BF16).T
            odq_ref[first + slot] = jnp.concatenate([low, high], axis=0)

    def give(self, dkv_refs):
        for p, ref in enumerate(dkv_refs):

            def step(r, _, p=p, ref=ref):
                rows = half_rows(p * self.lines + r)
                ref[r, 0:GROUP, :] = self.acc[0, rows, :].astype(BF16)
                ref[r, GROUP : 2 * GROUP, :] = self.acc[1, rows, :].astype(BF16)
                return 0

            lax.fori_loop(0, self.lines, step, 0, unroll=2)


def attention_scratch(lines, devices):
    n = devices * GROUP
    more = n + GROUP
    return [
        pltpu.VMEM((n, 128), BF16),
        pltpu.VMEM((n, 128), BF16),
        pltpu.VMEM((128, n), BF16),
        pltpu.VMEM((128, n), BF16),
        pltpu.VMEM((n + more, 256), F32),
        pltpu.VMEM((2, n, 128), F32),
    ]


class Chain:
    def __init__(self, place, wires, data, base, size, order, got, final, final_base, free, keep):
        pairs = {
            "x": (place.x, place.flip(1)),
            "y": (place.s, place.to_seq()),
            "m": (place.rest % 2, place.flip(2)),
            "f": (place.rest // 2, place.flip(3)),
        }
        self.data, self.got, self.sizes, self.bases, self.bits = data, [], [size], [base], []
        at = 0
        self.down, self.up = [], []
        for level, name in enumerate(order):
            bit, device = pairs[name]
            half = self.sizes[-1] // 2
            got_here = got.at[pl.ds(at, half)]
            at += half
            source, start = (data, base) if level == 0 else (self.got[-1], 0)
            away = pl.ds(pl.multiple_of(start + (1 - bit) * half, 16), half)
            self.down.append(wires.copy(source.at[away], got_here, device))
            self.got.append(got_here)
            self.bits.append(bit)
            self.sizes.append(half)
            self.bases.append(self.bases[-1] + bit * half)
            kept = pl.ds(pl.multiple_of(self.bases[-1], 16), half)
            self.up.append(wires.copy(data.at[kept], data.at[kept], device))
        whole = pl.ds(base, size)

        def across(start):
            rows = pl.ds(pl.multiple_of(start, 16), size // 2)
            there = pl.ds(pl.multiple_of(start + final_base - base, 16), size // 2)
            return wires.copy(data.at[rows], final.at[place.core, there], place.flip(0))

        self.near = across(self.bases[1])
        self.up.insert(0, across(base + (1 - self.bits[0]) * (size // 2)))
        self.depth = len(order)
        self.keep = pltpu.make_async_copy(data.at[whole], final.at[place.core, pl.ds(final_base, size)], keep)
        self.free, self.first = free, pairs[order[0]][1]
        self.sent = []

    def start(self, copy):
        copy.start()
        self.sent.append(copy)

    def stage(self, number):
        depth = self.depth
        if number == 0:
            self.start(self.down[0])
        elif number <= depth:
            level = number - 1
            self.down[level].wait_recv()
            if level == 0:
                self.down[0].wait_send()
                self.sent.pop()
                pl.semaphore_signal(
                    self.free, inc=1, device_id=self.first, device_id_type=pl.DeviceIdType.MESH
                )
            half = self.sizes[number]
            source, start = (self.data, self.bases[0]) if level == 0 else (self.got[level - 1], 0)
            start = start + self.bits[level] * half
            if number < depth:
                add_rows(self.got[level], 0, [(source, start)], half)
                self.start(self.down[number])
            else:
                add_rows(self.got[level], 0, [(source, start)], half, self.data, self.bases[depth])
                self.start(self.up[depth])
        else:
            level = 2 * depth - number + 1
            self.up[level].wait_recv()
            if level == 2:
                pl.semaphore_wait(self.free, 1)
            self.start(self.up[level - 1])
            if level == 2:
                self.start(self.near)
            if level == 1:
                self.keep.start()

    def finish(self):
        self.near.wait_recv()
        self.up[0].wait_recv()
        self.keep.wait()
        for copy in self.sent:
            copy.wait_send()


SCHEDULE = (
    "front", "send0", "mlp0", "u0.0", "u3.0", "mlp1", "send1", "u4.0", "line0", "spread0", "mlp2", "u0.1", "send2",
    "u3.1", "line1", "fwd0", "spread1", "u5.0", "u2.0", "keys0", "a0", "u1.0", "u3.2", "u4.1", "a0", "a0", "u0.2",
    "u3.3", "fwd1", "a0", "keys1", "u5.1", "a1", "u0.3", "core0", "u3.4", "line2", "spread2", "u5.2", "u1.1", "u4.2",
    "a1", "u5.3", "u0.4", "a1", "u3.5", "plane0", "u2.1", "u5.4", "fwd2", "a1", "u3.6", "keys2", "a2", "u1.2", "u4.3",
    "core1", "u5.5", "u0.5", "home0", "a2", "part", "u3.7", "grad0", "u1.3", "u2.2", "a2", "u4.4", "u5.6", "plane1",
    "a2", "u4.5", "u0.6", "u2.3", "core2", "u5.7", "u1.4", "v1.1", "home1", "grad1", "u0.7", "v0.1", "plane2", "v0.2",
    "u2.4", "v3.1", "u4.6", "u1.5", "home2", "v2.1", "v1.2", "u3.8", "v3.2", "grad2", "u2.5", "u5.8", "v1.3", "u4.7",
    "v3.3", "u0.8", "u1.6", "v2.2", "u2.6", "tail", "v4.1", "v1.4", "v3.4", "u1.7", "v5.1", "vec0", "v2.3", "v1.5",
    "v0.3", "v3.5", "v4.2", "v5.2", "v2.4", "u2.7", "v0.4", "vec1", "v2.5", "v4.3", "v5.3", "v0.5", "v3.6", "u4.8",
    "v2.6", "v4.4", "v5.4", "v3.7", "v4.5", "u1.8", "v1.6", "v5.5", "v0.6", "v2.7", "u2.8", "v4.6", "v5.6", "v1.7",
    "vec2", "v0.7", "v3.8", "v4.7", "v2.8", "v5.7", "vec3", "v1.8", "v0.8", "v5.8", "v4.8",
)
FF_CHUNK = 256
ORDERS = ("xymf", "xmyf", "yxmf", "yxmf", "ymxf", "yxmf", "ymxf", "xmyf", "yxmf", "xmyf", "yxmf", "xmyf")


def runs_of(positions, n_blk):
    group = positions[0, 0] // GROUP
    mirror = 2 * n_blk - 1 - group
    turn = jnp.full((16, 128), (group - mirror).astype(F32), F32).astype(BF16) > 0
    return jnp.minimum(group, mirror), jnp.broadcast_to(turn[None], (GROUP // 16, 16, 128))


def rotary_rows(low_group, n_blk):
    shape = (2 * GROUP, 2 * HEAD_DIM)
    row = lax.broadcasted_iota(jnp.int32, shape, 0)
    lane = lax.broadcasted_iota(jnp.int32, shape, 1) % HEAD_DIM
    half = ROTARY // 2
    at = jnp.where(row < GROUP, low_group * GROUP + row, (2 * n_blk - 2 - low_group) * GROUP + row)
    inverse = jnp.zeros(shape, F32)
    for i in range(half):
        inverse = jnp.where(lane % half == i, float(np.float32(ROTARY_BASE ** (-2.0 * i / ROTARY))), inverse)
    angles = at.astype(F32) * inverse
    cosine, sine = jnp.cos(angles), jnp.sin(angles)
    return (
        jnp.where(lane < ROTARY, cosine, 1.0),
        jnp.where(lane < half, -sine, 0.0),
        jnp.where((lane >= half) & (lane < ROTARY), sine, 0.0),
    )


def joined_kernel(
    n_seq, n_blk, units1, units2,
    positions, hid, og, again, abias, mgain, mbias, bqkv, bdense, bout, bin_,
    wqkv_hbm, wdense_hbm, win_hbm, wout_hbm,
    output, input_grad, vec_out, final,
    wqkv, wdense, win, wout, cosw, sina, sinb, hid2, og2, normed2, normed_m, qd_msg, kv_msg, qd_line, keys, flags,
    kk, vv, kkt, vvt, sb, acc,
    dkv_got, odq_all, dkv_all, out_part, gn_part, mout_got, gn_got, mine, other, bins,
    grads1, grads2, got, small, small_got, sends, recvs, load_sem, chunk_sem, keep_sem, free_sem,
):
    def row(ref):
        return ref[...].astype(F32).reshape(1, ref.shape[0])

    place = Place(n_seq, n_blk)
    wires = Wires(sends, recvs)
    tokens, width = hid.shape
    n_rest = place.n_rest
    core, hi = place.core, place.hi
    half_ff = win_hbm.shape[1] // 2
    chunks = half_ff // FF_CHUNK
    rows1 = grads1.shape[0]
    pieces = place.n_low
    sent, waiting = [], {}
    todo = {}

    def go(name, src, dst, device):
        copy = wires.copy(src, dst, device)
        copy.start()
        sent.append(copy)
        waiting.setdefault(name, []).append(copy)

    def arrive(name):
        for copy in waiting.pop(name):
            copy.wait_recv()

    loads = [
        pltpu.make_async_copy(wqkv_hbm, wqkv, load_sem.at[0]),
        pltpu.make_async_copy(wdense_hbm, wdense, load_sem.at[1]),
    ]
    for load in loads:
        load.start()

    def chunk_loads(f):
        slot = f % 2
        at = pl.multiple_of(core * half_ff + f * FF_CHUNK, FF_CHUNK)
        return [
            pltpu.make_async_copy(win_hbm.at[:, pl.ds(at, FF_CHUNK)], win.at[slot], chunk_sem.at[0, slot]),
            pltpu.make_async_copy(wout_hbm.at[pl.ds(at, FF_CHUNK), :], wout.at[slot], chunk_sem.at[1, slot]),
        ]

    for f in range(2):
        for load in chunk_loads(f):
            load.start()

    low_group, turned_rows = runs_of(positions, n_blk)
    cut = (GROUP // 16, 16, 128)
    for src, dst in ((hid, hid2), (og, og2)):
        for at in range(0, width, 128):
            cols = slice(at, at + 128)
            one, two = src[0:GROUP, cols].reshape(cut), src[GROUP : 2 * GROUP, cols].reshape(cut)
            dst[0:GROUP, cols] = jnp.where(turned_rows, two, one).reshape(GROUP, 128)
            dst[GROUP : 2 * GROUP, cols] = jnp.where(turned_rows, one, two).reshape(GROUP, 128)
    flags[0, 0] = jnp.full((16, 128), low_group.astype(F32), F32).astype(BF16)
    cosw[...], sina[...], sinb[...] = rotary_rows(low_group, n_blk)
    place.meet()
    for by in range(1, HEAD_GROUPS):
        go("flags", flags.at[0, 0], flags.at[0, by], place.to_group(by))
    for ref in (hid2, og2):
        go("rows", ref.at[pl.ds(0, tokens)], ref.at[pl.ds(tokens, tokens)], place.flip(0))

    lane = lax.broadcasted_iota(jnp.int32, (tokens, 128), 1)
    low = lane < HEAD_DIM

    def front():
        xhat, _ = normalise(hid2[0:tokens, :].astype(F32))
        normed = (xhat * row(again) + row(abias)).astype(BF16)
        for load in loads:
            load.wait()
        mixed = mm(normed, wqkv[...]) + row(bqkv)
        datt = mm_nt(og2[0:tokens, :], wdense[...])
        ca, sa, sb_ = cosw[...], sina[...], sinb[...]

        def turned(u):
            return u * ca + pltpu.roll(u, 120, 1) * sa + pltpu.roll(u, 8, 1) * sb_

        for tile in range(HEADS // 2):
            at = tile * 128
            q = turned(mixed[:, at : at + 128]) * (HEAD_DIM**-0.5)
            k = turned(mixed[:, width + at : width + at + 128])
            v = mixed[:, 2 * width + at : 2 * width + at + 128]
            d = datt[:, at : at + 128]
            for msg, one, two in ((qd_msg, q, d), (kv_msg, k, v)):
                for odd in range(2):
                    head = 2 * tile + odd
                    if odd == 0:
                        packed = jnp.where(low, one, pltpu.roll(two, 64, 1))
                    else:
                        packed = jnp.where(low, pltpu.roll(one, 64, 1), two)
                    msg[head % PER_GROUP, head // PER_GROUP] = packed.astype(BF16)
        arrive("flags")
        go("flag_x", flags.at[0], flags.at[1], place.flip(1))
        go("flag_c", flags.at[0], flags.at[2], place.flip(0))

    def send(j):
        for msg, line, name in ((kv_msg, keys.at[j, 0], "line"), (qd_msg, qd_line.at[j], "query")):
            for by in range(1, HEAD_GROUPS):
                go(name + str(j), msg.at[j, (hi + by) % HEAD_GROUPS], line.at[by], place.to_group(by))
        keys[j, 0, 0] = kv_msg[j, hi]
        qd_line[j, 0] = qd_msg[j, hi]

    def mlp_group(g):
        if g == 0:
            arrive("rows")
            xhat, _ = normalise(hid2[...].astype(F32))
            normed_m[...] = (xhat * row(mgain) + row(mbias)).astype(BF16)
            normed2[...] = (xhat * row(again) + row(abias)).astype(BF16)
            out_part[...] = jnp.zeros_like(out_part)
            gn_part[...] = jnp.zeros_like(gn_part)
        per = chunks // 3

        def step(f, _):
            slot = f % 2
            for load in chunk_loads(f):
                load.wait()
            x, w1, w2 = normed_m[...], win[slot], wout[slot]
            at = pl.multiple_of(f * FF_CHUNK, FF_CHUNK)
            bias_at = pl.ds(pl.multiple_of(core * half_ff + f * FF_CHUNK, FF_CHUNK), FF_CHUNK)
            inner = mm(x, w1) + bin_[bias_at].astype(F32).reshape(1, FF_CHUNK)
            cdf = 0.5 * (1.0 + lax.erf(inner * (0.5**0.5)))
            act = (inner * cdf).astype(BF16)
            pdf = jnp.exp(-0.5 * inner * inner) * (0.5 * 2.0**0.5 * 3.141592653589793**-0.5)
            gact = mm_nt(og2[...], w2)
            ginner = (gact * (cdf + inner * pdf)).astype(BF16)
            bins[0:1, pl.ds(at, FF_CHUNK)] = jnp.sum(ginner.astype(F32), axis=0, keepdims=True)
            grads1[pl.ds(at, FF_CHUNK), :] = mm_tn(ginner, x).astype(BF16)
            grads1[pl.ds(pl.multiple_of(half_ff + at, FF_CHUNK), FF_CHUNK), :] = mm_tn(act, og2[...]).astype(BF16)
            out_part[...] += mm(act, w2)
            gn_part[...] += mm_nt(ginner, w1)

            @pl.when(f + 2 < chunks)
            def _():
                for load in chunk_loads(f + 2):
                    load.start()

            return 0

        lax.fori_loop(g * per, (g + 1) * per, step, 0)

    def part():
        go("part", out_part.at[pl.ds(tokens, tokens)], mout_got, place.flip(0))
        go("part", gn_part.at[pl.ds(tokens, tokens)], gn_got, place.flip(0))

    def spread(j):
        go("x" + str(j), keys.at[j, 0], keys.at[j, 1], place.flip(1))
        go("c" + str(j), keys.at[j, 0], keys.at[j, 2], place.flip(0))

    def forward(j):
        arrive("x" + str(j))
        go("c" + str(j), keys.at[j, 1], keys.at[j, 3], place.flip(0))
        if j == 0:
            arrive("flag_x")
            go("flag_c", flags.at[1], flags.at[3], place.flip(0))

    def keys_there(j):
        arrive("c" + str(j))
        arrive("query" + str(j))
        if j == 0:
            arrive("flag_c")

    attention = Attention(HEAD_GROUPS, HEAD_GROUPS * pieces, flags, kk, vv, kkt, vvt, sb, acc)

    def attend(j):
        sources = [keys.at[j, p] for p in range(pieces)]
        attention.prepare(sources)
        for first in range(0, HEAD_GROUPS, 2):
            yield from attention.pair(first, qd_line.at[j], qd_line.at[j])
            if first + 2 < HEAD_GROUPS:
                yield
        for copy in leaving[j]:
            copy.wait_send()
        attention.give(sources)
        for by in range(1, HEAD_GROUPS):
            go("home" + str(j), qd_line.at[j, by], odq_all.at[j, by], place.to_group(HEAD_GROUPS - by))
        for i in range(2):
            go("core" + str(j), keys.at[j, 2 + i], dkv_got.at[j, i], place.flip(0))
        yield

    leaving = {}

    def core_sum(j):
        arrive("core" + str(j))
        for i in range(2):
            dkv_got[j, i] = (keys[j, i].astype(F32) + dkv_got[j, i].astype(F32)).astype(BF16)
        go("plane" + str(j), dkv_got.at[j, 1], dkv_got.at[j, 2], place.flip(1))

    def plane_sum(j):
        arrive("plane" + str(j))
        dkv_got[j, 2] = (dkv_got[j, 0].astype(F32) + dkv_got[j, 2].astype(F32)).astype(BF16)
        for by in range(1, HEAD_GROUPS):
            go("home" + str(j), dkv_got.at[j, 2, by], dkv_all.at[j, by], place.to_group(HEAD_GROUPS - by))
        odq_all[j, 0] = qd_line[j, 0]
        dkv_all[j, 0] = dkv_got[j, 2, 0]

    def home(j):
        arrive("home" + str(j))
        ca, sa, sb_ = cosw[...], sina[...], sinb[...]

        def turned_back(g):
            return g * ca - pltpu.roll(g, 120, 1) * sa - pltpu.roll(g, 8, 1) * sb_

        for g in range(HEAD_GROUPS):
            at = (g - hi + HEAD_GROUPS) % HEAD_GROUPS
            a, b = odq_all[j, at].astype(F32), dkv_all[j, at].astype(F32)
            mine[j, g, :, 0:128] = jnp.where(low, a, turned_back(a)).astype(BF16)
            mine[j, g, :, 128:256] = jnp.where(low, turned_back(b), b).astype(BF16)
        half = HEAD_GROUPS // 2
        go("other" + str(j), mine.at[j, pl.ds((1 - core) * half, half)], other.at[j], place.flip(0))

    def grad(j):
        arrive("other" + str(j))
        half = HEAD_GROUPS // 2
        normed, cot = normed2[...], og2[...]
        from_out = lax.broadcasted_iota(jnp.int32, (128, width), 0) < HEAD_DIM
        for g in range(half):
            both = jnp.concatenate([mine[j, core * half + g], other[j, g]], axis=0)
            base = (j * half + g) * 256
            by_normed = mm_tn(both, normed)
            by_cot = mm_tn(both[:, 0:128], cot)
            grads2[base : base + 128, :] = jnp.where(from_out, by_cot, by_normed[0:128]).astype(BF16)
            grads2[base + 128 : base + 256, :] = by_normed[128:256].astype(BF16)
        per = len(units2) // PER_GROUP
        for unit in second[j * per : (j + 1) * per]:
            unit.stage(0)

    def tail():
        arrive("part")
        rows = hid2[0:tokens, :].astype(F32)

        def parts(a):
            return mine[a % PER_GROUP, a // PER_GROUP].astype(F32)

        outs, grads = [], [[], [], []]
        for tile in range(HEADS // 2):
            one, two = parts(2 * tile), parts(2 * tile + 1)
            a1, b1, a2, b2 = one[:, 0:128], one[:, 128:256], two[:, 0:128], two[:, 128:256]
            outs.append(jnp.where(low, a1, pltpu.roll(a2, 64, 1)).astype(BF16))
            grads[0].append(jnp.where(low, pltpu.roll(a1, 64, 1), a2).astype(BF16))
            grads[1].append(jnp.where(low, b1, pltpu.roll(b2, 64, 1)).astype(BF16))
            grads[2].append(jnp.where(low, pltpu.roll(b1, 64, 1), b2).astype(BF16))
        att = jnp.concatenate(outs, axis=1)
        dmixed = jnp.concatenate(grads[0] + grads[1] + grads[2], axis=1)
        branch = mm(att, wdense[...]) + row(bdense)
        mout = out_part[0:tokens, :] + mout_got[...]
        output[...] = (rows + branch + (mout + row(bout))).astype(BF16)
        gna = mm_nt(dmixed, wqkv[...])
        gnm = gn_part[0:tokens, :] + gn_got[...]
        xhat, scale = normalise(rows)
        cot = og2[0:tokens, :].astype(F32)
        input_grad[...] = (
            cot
            + norm_back(gna, xhat, scale, row(again))
            + norm_back(gnm, xhat, scale, row(mgain))
        ).astype(BF16)
        small[0:1, :] = jnp.sum(gna * xhat, axis=0, keepdims=True)
        small[1:2, :] = jnp.sum(gna, axis=0, keepdims=True)
        small[2:3, :] = jnp.sum(gnm * xhat, axis=0, keepdims=True)
        small[3:4, :] = jnp.sum(gnm, axis=0, keepdims=True)
        for k in range(3):
            cols = dmixed[:, k * width : (k + 1) * width].astype(F32)
            small[4 + k : 5 + k, :] = jnp.sum(cols, axis=0, keepdims=True)
        small[7:8, :] = jnp.sum(cot, axis=0, keepdims=True)
        per = half_ff // width
        for side in range(2):
            here = (1 - core if side == 0 else core).astype(F32)
            for k in range(per):
                at = 8 + side * per + k
                small[at : at + 1, :] = bins[0:1, k * width : (k + 1) * width] * here

    rounds = [
        [place.flip(0)],
        [place.flip(1)],
        [place.to_seq()],
        [place.to_rest(by) for by in range(1, n_rest)],
    ]

    def vec_start(r):
        for i, device in enumerate(rounds[r]):
            go("vec" + str(r), small.at[pl.ds(0, small.shape[0])] if r == 0 else small_got.at[8 + r], small_got.at[2 * r if r < 3 else 5 + i], device)

    def vec(r):
        if r == 0:
            vec_start(0)
            return
        arrive("vec" + str(r - 1))
        source = small[...] if r == 1 else small_got[8 + r - 1]
        small_got[8 + r] = source + small_got[2 * (r - 1)]
        vec_start(r)

    def vec_end():
        arrive("vec3")
        total = small_got[8 + 3]
        for i in range(n_rest - 1):
            total = total + small_got[5 + i]
        vec_out[...] = total

    first, second = [], []
    at = 0
    for found, units, data, offset in ((first, units1, grads1, 0), (second, units2, grads2, rows1)):
        for base, size, order in units:
            found.append(Chain(
                place, wires, data, base, size, order, got.at[pl.ds(at, size)], final, offset + base,
                free_sem.at[len(first) + len(second)], keep_sem.at[len(first) + len(second)],
            ))
            at += size

    todo = {"front": front, "part": part, "tail": tail}
    for g in range(3):
        todo["mlp" + str(g)] = functools.partial(mlp_group, g)
    for r in range(4):
        todo["vec" + str(r)] = functools.partial(vec, r)
    runs = {}
    for j in range(PER_GROUP):
        for name, action in (
            ("send", send), ("line", lambda j: arrive("line" + str(j))), ("spread", spread), ("fwd", forward),
            ("keys", keys_there), ("core", core_sum), ("plane", plane_sum), ("home", home), ("grad", grad),
        ):
            todo[name + str(j)] = functools.partial(action, j)
        runs[j] = attend(j)
        todo["a" + str(j)] = functools.partial(next, runs[j])
    for name, units in (("u", first), ("v", second)):
        for i, unit in enumerate(units):
            for stage in range(2 * unit.depth + 1):
                todo[name + str(i) + "." + str(stage)] = functools.partial(unit.stage, stage)
    for j in range(PER_GROUP):
        leaving[j] = []
    for token in SCHEDULE:
        before = len(sent)
        todo[token]()
        if token[:-1] in ("spread", "fwd"):
            leaving[int(token[-1])] += sent[before:]
            del sent[before:]
    vec_end()
    for unit in first + second:
        if unit.sent:
            unit.finish()
    for copy in sent:
        copy.wait_send()


def joined(mesh, positions, hid, og, again, abias, mgain, mbias, bqkv, bdense, bout, b_in, wqkv, wdense, win, wout):
    n_seq, n_blk = mesh.shape["seq"], mesh.shape["blk"]
    n_low, n_rest = n_blk // HEAD_GROUPS, n_blk // 4
    tokens, width = hid.shape
    half_ff = win.shape[1] // 2
    rows1, rows2 = 2 * half_ff, 2 * width
    size = half_ff // 3
    units1 = [(i * size, size, order) for i, order in enumerate(ORDERS[:6])]
    size = rows2 // 6
    units2 = [(i * size, size, order) for i, order in enumerate(ORDERS[6:])]
    total = rows1 + rows2
    copies = 10 * (len(units1) + len(units2)) + 128
    line = (HEAD_GROUPS, tokens, 128)
    n_small = 8 + 2 * half_ff // width
    devices = HEAD_GROUPS * n_low
    per = PER_GROUP
    inputs = [positions, hid, og, again, abias, mgain, mbias, bqkv, bdense, bout, b_in, wqkv, wdense, win, wout]
    return pl.pallas_call(
        functools.partial(joined_kernel, n_seq, n_blk, units1, units2),
        out_shape=[
            jax.ShapeDtypeStruct((tokens, width), BF16),
            jax.ShapeDtypeStruct((tokens, width), BF16),
            jax.ShapeDtypeStruct((n_small, width), F32),
            jax.ShapeDtypeStruct((2, total, width), BF16),
        ],
        in_specs=[IN_SMEM] + [IN_VMEM] * (len(inputs) - 5) + [pl.BlockSpec(memory_space=pl.ANY)] * 4,
        out_specs=[IN_VMEM] * 3 + [pl.BlockSpec(memory_space=pl.ANY)],
        scratch_shapes=[
            pltpu.VMEM(wqkv.shape, BF16),
            pltpu.VMEM(wdense.shape, BF16),
            pltpu.VMEM((2, width, FF_CHUNK), BF16),
            pltpu.VMEM((2, FF_CHUNK, width), BF16),
            pltpu.VMEM((tokens, 2 * HEAD_DIM), F32),
            pltpu.VMEM((tokens, 2 * HEAD_DIM), F32),
            pltpu.VMEM((tokens, 2 * HEAD_DIM), F32),
            pltpu.VMEM((2 * tokens, width), BF16),
            pltpu.VMEM((2 * tokens, width), BF16),
            pltpu.VMEM((2 * tokens, width), BF16),
            pltpu.VMEM((2 * tokens, width), BF16),
            pltpu.VMEM((per,) + line, BF16),
            pltpu.VMEM((per,) + line, BF16),
            pltpu.VMEM((per,) + line, BF16),
            pltpu.VMEM((per, n_low) + line, BF16),
            pltpu.VMEM((n_low, HEAD_GROUPS, 16, 128), BF16),
            *attention_scratch(HEAD_GROUPS, devices),
            pltpu.VMEM((per, 3) + line, BF16),
            pltpu.VMEM((per,) + line, BF16),
            pltpu.VMEM((per,) + line, BF16),
            pltpu.VMEM((2 * tokens, width), F32),
            pltpu.VMEM((2 * tokens, width), F32),
            pltpu.VMEM((tokens, width), F32),
            pltpu.VMEM((tokens, width), F32),
            pltpu.VMEM((per, HEAD_GROUPS, tokens, 256), BF16),
            pltpu.VMEM((per, HEAD_GROUPS // 2, tokens, 256), BF16),
            pltpu.VMEM((1, half_ff), F32),
            pltpu.VMEM((rows1, width), BF16),
            pltpu.VMEM((rows2, width), BF16),
            pltpu.VMEM((total, width), BF16),
            pltpu.VMEM((n_small, width), F32),
            pltpu.VMEM((12, n_small, width), F32),
            pltpu.SemaphoreType.DMA((copies,)),
            pltpu.SemaphoreType.DMA((copies,)),
            pltpu.SemaphoreType.DMA((2,)),
            pltpu.SemaphoreType.DMA((2, 2)),
            pltpu.SemaphoreType.DMA((len(units1) + len(units2),)),
            pltpu.SemaphoreType.REGULAR((len(units1) + len(units2),)),
        ],
        compiler_params=pltpu.CompilerParams(
            vmem_limit_bytes=VMEM_BYTES, collective_id=2, has_side_effects=True
        ),
        name="joined",
    )(*inputs)


def spread_kernel(
    n_blk, positions, final, vec, out_rows, grad_rows,
    output, input_grad, win, wout, wqkv, wdense, again, abias, mgain, mbias, bqkv, bdense, bin_, bout,
):
    half_ff = win.shape[1] // 2

    @pl.when(pl.program_id(0) == 0)
    def _():
        width = vec.shape[1]
        _, turned_rows = runs_of(positions, n_blk)
        cut = (GROUP // 16, 16, 128)
        for src, dst in ((out_rows, output), (grad_rows, input_grad)):
            for at in range(0, width, 128):
                cols = slice(at, at + 128)
                one, two = src[0:GROUP, cols].reshape(cut), src[GROUP : 2 * GROUP, cols].reshape(cut)
                dst[0:GROUP, cols] = jnp.where(turned_rows, two, one).reshape(GROUP, 128)
                dst[GROUP : 2 * GROUP, cols] = jnp.where(turned_rows, one, two).reshape(GROUP, 128)
        for ref, at in ((again, 0), (abias, 1), (mgain, 2), (mbias, 3), (bqkv, 4), (bdense, 7), (bout, 7), (bin_, 8)):
            for k in range(ref.shape[0] // width):
                ref[k * width : (k + 1) * width] = vec[at + k : at + k + 1, :].reshape(width)

    for core in range(2):
        win[:, core * half_ff : (core + 1) * half_ff] = final[core, 0:half_ff, :].T.astype(F32)
        wout[core * half_ff : (core + 1) * half_ff, :] = final[core, half_ff : 2 * half_ff, :].astype(F32)

    def segment(head, part):
        group, j = head // PER_GROUP, head % PER_GROUP
        half = HEAD_GROUPS // 2
        at = 2 * half_ff + (j * half + group % half) * 256 + part * HEAD_DIM
        return final[group // half, at : at + HEAD_DIM, :]

    width = wdense.shape[0]
    for tile in range(HEADS // 2):
        for part in range(4):
            both = jnp.concatenate([segment(2 * tile, part), segment(2 * tile + 1, part)], axis=0)
            if part == 0:
                wdense[tile * 128 : tile * 128 + 128, :] = both.astype(F32)
            else:
                at = (part - 1) * width + tile * 128
                wqkv[:, at : at + 128] = both.T.astype(F32)


def spread_out(n_blk, positions, final, vec, out_rows, grad_rows, ff):
    total, width = final.shape[1:]
    lanes = 384

    def whole(x):
        return pl.BlockSpec(x.shape, lambda i: (0,) * len(x.shape))

    vectors = [jax.ShapeDtypeStruct((n,), F32) for n in (width, width, width, width, 3 * width, width, ff, width)]
    rows = jax.ShapeDtypeStruct(out_rows.shape, BF16)
    return pl.pallas_call(
        functools.partial(spread_kernel, n_blk),
        grid=(width // lanes,),
        in_specs=[IN_SMEM, pl.BlockSpec((2, total, lanes), lambda i: (0, 0, i))]
        + [whole(x) for x in (vec, out_rows, grad_rows)],
        out_specs=[
            whole(rows),
            whole(rows),
            pl.BlockSpec((lanes, ff), lambda i: (i, 0)),
            pl.BlockSpec((ff, lanes), lambda i: (0, i)),
            pl.BlockSpec((lanes, 3 * width), lambda i: (i, 0)),
            pl.BlockSpec((width, lanes), lambda i: (0, i)),
        ]
        + [whole(x) for x in vectors],
        out_shape=[
            rows,
            rows,
            jax.ShapeDtypeStruct((width, ff), F32),
            jax.ShapeDtypeStruct((ff, width), F32),
            jax.ShapeDtypeStruct((width, 3 * width), F32),
            jax.ShapeDtypeStruct((width, width), F32),
        ]
        + vectors,
        compiler_params=params(),
        name="spread",
    )(positions, final, vec, out_rows, grad_rows)


def rotary_tables(positions):
    lane = jnp.arange(128, dtype=jnp.int32) % HEAD_DIM
    half = ROTARY // 2
    inverse = jnp.power(ROTARY_BASE, -2.0 * (lane % half).astype(F32) / ROTARY)
    angles = positions.astype(F32)[:, None] * inverse[None, :]
    cosine, sine = jnp.cos(angles), jnp.sin(angles)
    lane = lane[None, :]
    return (
        jnp.where(lane < ROTARY, cosine, 1.0),
        jnp.where(lane < half, -sine, 0.0),
        jnp.where((lane >= half) & (lane < ROTARY), sine, 0.0),
    )


def solution(mesh):
    n_seq, n_blk = mesh.shape["seq"], mesh.shape["blk"]
    n_low = n_blk // HEAD_GROUPS
    low_bits = n_low.bit_length() - 1
    def permute(x, target):
        return lax.ppermute(x, "blk", [(b, target(b)) for b in range(n_blk)])

    def to_group(x, by):
        return permute(x, lambda b: ((b // n_low + by) % HEAD_GROUPS) * n_low + b % n_low)

    def flip(x, bit):
        return permute(x, lambda b: b ^ (1 << bit))

    def on_device(
        hidden, positions, ln_attn_gain, ln_attn_bias, ln_mlp_gain, ln_mlp_bias,
        w_qkv, b_qkv, w_dense, b_dense, w_in, b_in, w_out, b_out, out_grad,
    ):
        hid, og, pos = hidden[0], out_grad[0], positions[0]
        again, abias = ln_attn_gain[None], ln_attn_bias[None]
        mgain, mbias = ln_mlp_gain[None], ln_mlp_bias[None]
        tokens, width = hid.shape
        if n_low == 4:
            output, input_grad, vec, final = joined(
                mesh, positions, hid, og, ln_attn_gain, ln_attn_bias, ln_mlp_gain, ln_mlp_bias, b_qkv, b_dense, b_out,
                b_in, w_qkv, w_dense, w_in, w_out,
            )
            output, input_grad, win, wout, wqkv, wdense, *vectors = spread_out(
                n_blk, positions, final, vec, output, input_grad, w_in.shape[1]
            )
            dgain, dbias, dmgain, dmbias, dbqkv, dbdense, dbin, dbout = vectors
            return (
                output[None], input_grad[None], dgain, dbias, dmgain, dmbias,
                wqkv, dbqkv, wdense, dbdense, win, dbin, wout, dbout,
            )
        b = lax.axis_index("blk")
        core = b % 2
        hi = b // n_low
        tables = rotary_tables(pos)

        own_runs = pos[::GROUP] // GROUP
        line_runs = jnp.concatenate(
            [own_runs] + [to_group(own_runs, by) for by in range(1, HEAD_GROUPS)]
        )
        key_runs = [line_runs]
        for bit in range(low_bits - 1, -1, -1):
            key_runs = key_runs + [flip(r, bit) for r in key_runs]
        n_query = line_runs.shape[0]
        rank = jnp.sum(line_runs[:, None] > line_runs[None, :], axis=1)
        slots = rank[None, :] == jnp.arange(n_query)[:, None]
        order = jnp.sum(jnp.where(slots, jnp.arange(n_query)[None, :], 0), axis=1)
        ordered = jnp.sum(jnp.where(slots, line_runs[None, :], 0), axis=1)
        tab = jnp.concatenate(key_runs + [order, ordered]).astype(jnp.int32)

        hid2 = jnp.concatenate([hid, flip(hid, 0)], axis=0)
        og2 = jnp.concatenate([og, flip(og, 0)], axis=0)

        msg = front(hid, og, again, abias, w_qkv, b_qkv[None], w_dense, tables)

        arrived = []
        for j in range(PER_GROUP):
            got = []
            for by in range(HEAD_GROUPS):
                part = lax.dynamic_index_in_dim(msg[j], lax.rem(hi + by, HEAD_GROUPS), 0, False)
                got.append(part if by == 0 else to_group(part, by))
            qd = jnp.stack([g[0] for g in got])
            pieces = [jnp.stack([g[1] for g in got])]
            for bit in range(low_bits - 1, -1, -1):
                pieces = pieces + [flip(piece, bit) for piece in pieces]
            arrived.append((qd, pieces))

        mlp_grads, bin_half, out_part, gn_part, normed2 = mlp(
            core[None].astype(jnp.int32), hid2, og2, again, abias, mgain, mbias, w_in, b_in[None], w_out
        )
        odqs, dkvs = [], []
        line = (HEAD_GROUPS, tokens, 128)
        for j in range(PER_GROUP):
            qd, pieces = arrived[j]
            runs = (HEAD_GROUPS * tokens // GROUP, GROUP, 128)
            odq, dkv = attention(tab, qd.reshape(runs), [p.reshape(runs) for p in pieces])
            odqs.append(odq.reshape(line))
            dkvs.append([d.reshape(line) for d in dkv])

        zero = jnp.zeros_like(bin_half)
        bins = jnp.where(
            core == 0, jnp.concatenate([bin_half, zero], 1), jnp.concatenate([zero, bin_half], 1)
        ).reshape(-1, width)
        half_ff = mlp_grads.shape[1]
        output, input_grad, vec, final = finish(
            mesh, odqs, dkvs, mlp_grads.reshape(2 * half_ff, width), out_part, gn_part, hid, og, og2,
            normed2, bins, again, mgain, w_qkv, w_dense, b_dense[None], b_out[None], tables,
        )
        win, wout, wqkv, wdense = expand(
            final, ((half_ff, True), (half_ff, False), (3 * width // 2, True), (width // 2, False))
        )
        return (
            output[None],
            input_grad[None],
            vec[0],
            vec[1],
            vec[2],
            vec[3],
            wqkv,
            vec[4:7].reshape(-1),
            wdense,
            vec[7],
            win,
            vec[8:].reshape(-1),
            wout,
            vec[7],
        )

    rows = P("seq", "blk", None)
    return jax.shard_map(
        on_device,
        mesh=mesh,
        in_specs=(rows, P("seq", "blk")) + (P(),) * 12 + (rows,),
        out_specs=(rows, rows) + (P(),) * 12,
        check_vma=False,
    )
```
